32 devices in a mesh: dp: 8 (over y, x, core), seq: 4 (over z).
Axes of the slice: x: 2, y: 2, z: 4, core: 2. Of those that a mesh axis runs over, the one named last changes fastest.
Arguments:
- image_tokens: bfloat16 [8, 1024, 1536], P('dp', 'seq'), may hold values from -6 to 6
- text_tokens: bfloat16 [8, 308, 1536], P('dp', 'seq'), may hold values from -6 to 6
- text_lengths: int32 [8, 4], P('dp', 'seq'), may hold values from 1 to 77, 154 in all within a row
- conditioning: bfloat16 [8, 1536], P('dp'), may hold values from -6 to 6
- ada_weight: bfloat16 [1536, 2, 9216], P('dp', None, 'seq'), may hold values from -0.15625 to 0.15625
- ada_bias: bfloat16 [2, 9216], P(None, 'seq'), may hold values from -3 to 3
- qkv_weight: bfloat16 [1536, 2, 3, 1536], P('dp', None, None, 'seq'), may hold values from -1 to 1
- qv_bias: bfloat16 [2, 2, 1536], P(None, None, 'seq'), may hold values from -3 to 3
- proj_weight: bfloat16 [1536, 2, 1536], P('seq', None, 'dp'), may hold values from -1.75 to 1.75
- proj_bias: bfloat16 [2, 1536], P(None, 'seq'), may hold values from -3 to 3
- fc1_weight: bfloat16 [1536, 2, 6144], P('dp', None, 'seq'), may hold values from -0.15625 to 0.15625
- fc1_bias: bfloat16 [2, 6144], P(None, 'seq'), may hold values from -3 to 3
- fc2_weight: bfloat16 [6144, 2, 1536], P('seq', None, 'dp'), may hold values from -0.078125 to 0.078125
- fc2_bias: bfloat16 [2, 1536], P(None, 'seq'), may hold values from -3 to 3
- image_cotangent: bfloat16 [8, 1024, 1536], P('dp', 'seq'), may hold values from -6 to 6
- text_cotangent: bfloat16 [8, 308, 1536], P('dp', 'seq'), may hold values from -6 to 6
Outputs:
- image_out: bfloat16 [8, 1024, 1536], P('dp', 'seq')
- text_out: bfloat16 [8, 308, 1536], P('dp', 'seq')
- image_grad: float32 [8, 1024, 1536], P('dp', 'seq')
- text_grad: float32 [8, 308, 1536], P('dp', 'seq')
- cond_grad: float32 [8, 1536], P('dp')
- ada_weight_grad: float32 [1536, 2, 9216], P('dp', None, 'seq')
- ada_bias_grad: float32 [2, 9216], P(None, 'seq')
- qkv_weight_grad: float32 [1536, 2, 3, 1536], P('dp', None, None, 'seq')
- qv_bias_grad: float32 [2, 2, 1536], P(None, None, 'seq')
- proj_weight_grad: float32 [1536, 2, 1536], P('seq', None, 'dp')
- proj_bias_grad: float32 [2, 1536], P(None, 'seq')
- fc1_weight_grad: float32 [1536, 2, 6144], P('dp', None, 'seq')
- fc1_bias_grad: float32 [2, 6144], P(None, 'seq')
- fc2_weight_grad: float32 [6144, 2, 1536], P('seq', None, 'dp')
- fc2_bias_grad: float32 [2, 1536], P(None, 'seq')
The draws below stay inside these ranges and needn't reach their ends.
Inputs may be any that keep to these rules, and one draw needn't show every extreme that they name: The first text_lengths slots of a device's 77 are live; the live slots of one sequence add up to 154, and in each sequence some device has all 77 live.
All inputs are finite; a program needn't handle non-finite values.
Results may differ from the reference program's by a relative error of at most 0.025.
The reference program's roundings to bfloat16 on the way count: a program that leaves them out, or rounds other values in their place, can miss the bound.
Values may be sent and summed in bfloat16 or wider, within the bound.
A program may use at most 320 MiB of HBM per device.

```python
import math
import jax
import jax.numpy as jnp
import numpy as np
from jax import lax

D = 1536
H = 24
HD = 64
FF = 6144
IMG = 1024
TXT = 154
SEQS = 8
CAP = 77
N_SEQ = 4


def draw_qkv_weight(key, part):
    base_key = jax.random.fold_in(jax.random.fold_in(key, 17), 0)
    result = jax.random.truncated_normal(base_key, -6.0, 6.0, (D, 2, 3, D), jnp.float32) * D ** (-0.5)
    return result.astype(jnp.bfloat16)


def block_scale(rng, shape, pieces, smallest, high):
    def one(position, shards_of):
        heights = jax.random.uniform(jax.random.fold_in(jax.random.fold_in(rng, 6), position), (shards_of,), jnp.float32, smallest / len(pieces), high / len(pieces))
        return jnp.repeat(jnp.exp(heights), shape[position] // shards_of).reshape((-1,) + (1,) * (len(shape) - position - 1))

    loudness = one(*pieces[0])
    for cut in pieces[1:]:
        loudness = loudness * one(*cut)
    return loudness


def length_profile(amount, total, bound, slope):
    weights = [(1 << 20) // math.isqrt(rank ** slope) + 1 for rank in range(2, amount + 1)]
    rest, holding = total - bound - (amount - 1), [1] * (amount - 1)
    while rest > 0:
        free = [i for i in range(amount - 1) if holding[i] < bound]
        mass, left = sum([weights[i] for i in free]), rest
        for i in free:
            addition = min(bound - holding[i], max(1, left * weights[i] // mass), rest)
            holding[i] = holding[i] + addition
            rest = rest - addition
    return np.array([bound] + holding)


def uneven(rng, count, total, most, skew):
    if count == 2:
        one = jax.random.randint(rng, (), max(1, total - most), min(most, total - 1) + 1)
        return jnp.stack([one, total - one])
    lengths = jnp.asarray(length_profile(count, total, most, skew), jnp.int32)
    couples = (count - 1) // 2
    giver, taker = lengths[1:1 + 2 * couples:2], lengths[2:2 + 2 * couples:2]
    margin = jnp.minimum(giver - 1, most - taker)
    shifted = jax.random.randint(jax.random.fold_in(rng, 1), (couples,), 0, 1 << 20) % (margin + 1)
    lengths = lengths.at[1:1 + 2 * couples:2].set(giver - shifted).at[2:2 + 2 * couples:2].set(taker + shifted)
    return lengths[jax.random.permutation(jax.random.fold_in(rng, 2), count)]


def bell_draw(key, extent, spread, most, shards=(), kind=jnp.bfloat16):
    loudness = block_scale(key, extent, shards, -0.22, 0.18) if shards else 1.0
    entries = jax.random.normal(key, extent, jnp.float32) * spread * loudness
    return jnp.minimum(jnp.maximum(entries, -most), most).astype(kind)


def setup_inputs(seed: int = 0) -> dict:
    splits = jax.random.split(jax.random.key(seed), 17)
    image_tokens = bell_draw(splits[0], (SEQS, IMG, D), 1.0, 6.0, ((0, 8), (1, 4)))
    text_tokens = bell_draw(splits[1], (SEQS, N_SEQ * CAP, D), 1.0, 6.0, ((0, 8), (1, 4)))
    text_lengths = jax.vmap(lambda own: uneven(own, N_SEQ, TXT, CAP, 2))(jax.random.split(splits[2], SEQS)).reshape((SEQS, N_SEQ)).astype(jnp.int32)
    conditioning = bell_draw(splits[3], (SEQS, D), 1.0, 6.0, ((0, 8),))
    ada_weight = bell_draw(splits[4], (D, 2, 6 * D), D ** -0.5, 0.15625, ((0, 8), (2, 4)))
    ada_bias = bell_draw(splits[5], (2, 6 * D), 0.5, 3.0, ((1, 4),))
    qkv_weight = draw_qkv_weight(jax.random.fold_in(splits[16], 71), 0)
    qv_bias = bell_draw(splits[7], (2, 2, D), 0.5, 3.0, ((2, 4),))
    proj_weight = bell_draw(splits[8], (D, 2, D), (max(D // 128, 1)) ** -0.5, 1.75, ((0, 4), (2, 8)))
    proj_bias = bell_draw(splits[9], (2, D), 0.5, 3.0, ((1, 4),))
    fc1_weight = bell_draw(splits[10], (D, 2, FF), D ** -0.5, 0.15625, ((0, 8), (2, 4)))
    fc1_bias = bell_draw(splits[11], (2, FF), 0.5, 3.0, ((1, 4),))
    fc2_weight = bell_draw(splits[12], (FF, 2, D), FF ** -0.5, 0.078125, ((0, 4), (2, 8)))
    fc2_bias = bell_draw(splits[13], (2, D), 0.5, 3.0, ((1, 4),))
    image_cotangent = bell_draw(splits[14], (SEQS, IMG, D), 1.0, 6.0, ((0, 8), (1, 4)))
    text_cotangent = bell_draw(splits[15], (SEQS, N_SEQ * CAP, D), 1.0, 6.0, ((0, 8), (1, 4)))
    return {"image_tokens": image_tokens, "text_tokens": text_tokens, "text_lengths": text_lengths, "conditioning": conditioning, "ada_weight": ada_weight, "ada_bias": ada_bias, "qkv_weight": qkv_weight, "qv_bias": qv_bias, "proj_weight": proj_weight, "proj_bias": proj_bias, "fc1_weight": fc1_weight, "fc1_bias": fc1_bias, "fc2_weight": fc2_weight, "fc2_bias": fc2_bias, "image_cotangent": image_cotangent, "text_cotangent": text_cotangent}


EPSILON = 1e-06
GELU_ROOT = math.sqrt(2.0 / math.pi)
GELU_CUBE = 0.044715
MASKED = -1e+30

def layer_norm(values):
    center = values - lax.optimization_barrier(jnp.mean(values, axis=-1, keepdims=True))
    inv_std = lax.rsqrt(lax.optimization_barrier(jnp.mean(center * center, axis=-1, keepdims=True)) + EPSILON)
    return (center * inv_std, inv_std)

def norm_back(normed, inv_std, upstream):
    first = lax.optimization_barrier(jnp.mean(upstream, axis=-1, keepdims=True))
    second = lax.optimization_barrier(jnp.mean(upstream * normed, axis=-1, keepdims=True))
    return inv_std * (upstream - first - normed * second)

def gelu_tanh(values):
    inner = GELU_ROOT * (values + GELU_CUBE * values * values * values)
    return 0.5 * values * (1.0 + jnp.tanh(inner))

def gelu_slope(values):
    inner = GELU_ROOT * (values + GELU_CUBE * values * values * values)
    tangent = jnp.tanh(inner)
    return 0.5 * (1.0 + tangent) + 0.5 * values * (1.0 - tangent * tangent) * GELU_ROOT * (1.0 + 3.0 * GELU_CUBE * values * values)

def silu_slope(values):
    sigma = jax.nn.sigmoid(values)
    return sigma + values * sigma * (1.0 - sigma)

def attend(queries, key_rows, value_rows, live_keys):
    score_scale = 1.0 / math.sqrt(HD)
    scores = jnp.einsum('qhd,khd->hqk', queries.astype(jnp.float32), key_rows.astype(jnp.float32)) * score_scale
    scores = jnp.where(live_keys[None, None, :], scores, MASKED)
    maxima = lax.optimization_barrier(jnp.max(scores, axis=-1, keepdims=True))
    raised = jnp.exp(scores - maxima)
    totals = lax.optimization_barrier(jnp.sum(raised, axis=-1, keepdims=True))
    weights = (raised / totals).astype(jnp.bfloat16)
    mixture = jnp.einsum('hqk,khd->qhd', weights.astype(jnp.float32), value_rows.astype(jnp.float32)).astype(jnp.bfloat16)
    return (mixture, (maxima + jnp.log(totals))[..., 0])

def attend_back(queries, key_rows, value_rows, mixture, grad_mix, log_total, live_keys):
    score_scale = 1.0 / math.sqrt(HD)
    scores = jnp.einsum('qhd,khd->hqk', queries.astype(jnp.float32), key_rows.astype(jnp.float32)) * score_scale
    scores = jnp.where(live_keys[None, None, :], scores, MASKED)
    probs = jnp.exp(scores - log_total[..., None])
    prob_half = probs.astype(jnp.bfloat16)
    grad_prob = jnp.einsum('qhd,khd->hqk', grad_mix.astype(jnp.float32), value_rows.astype(jnp.float32))
    offset = lax.optimization_barrier(jnp.sum(grad_mix.astype(jnp.float32) * mixture.astype(jnp.float32), axis=-1)).T
    grad_score = (probs * (grad_prob - offset[:, :, None]) * score_scale).astype(jnp.bfloat16)
    grad_query = jnp.einsum('hqk,khd->qhd', grad_score.astype(jnp.float32), key_rows.astype(jnp.float32))
    grad_key = jnp.einsum('hqk,qhd->khd', grad_score.astype(jnp.float32), queries.astype(jnp.float32))
    grad_value = jnp.einsum('hqk,qhd->khd', prob_half.astype(jnp.float32), grad_mix.astype(jnp.float32))
    return (grad_query, grad_key, grad_value)

def reference(image_tokens, text_tokens, text_lengths, conditioning, ada_weight, ada_bias, qkv_weight, qv_bias, proj_weight, proj_bias, fc1_weight, fc1_bias, fc2_weight, fc2_bias, image_cotangent, text_cotangent):
    slot_index = jnp.arange(N_SEQ * CAP, dtype=jnp.int32)
    live_text = (slot_index % CAP)[None, :] < jnp.repeat(text_lengths, CAP, axis=1)
    zero_grads = (jnp.zeros((D, 2, 6 * D), jnp.float32), jnp.zeros((2, 6 * D), jnp.float32), jnp.zeros((D, 2, 3, D), jnp.float32), jnp.zeros((2, 2, D), jnp.float32), jnp.zeros((D, 2, D), jnp.float32), jnp.zeros((2, D), jnp.float32), jnp.zeros((D, 2, FF), jnp.float32), jnp.zeros((2, FF), jnp.float32), jnp.zeros((FF, 2, D), jnp.float32), jnp.zeros((2, D), jnp.float32))

    def one_sequence(running, inputs):
        image_row, text_row, live_row, cond_row, image_cot, text_cot = inputs
        cond_float = cond_row.astype(jnp.float32)
        cond_act = jax.nn.silu(cond_float).astype(jnp.bfloat16)
        residual_in = (image_row.astype(jnp.float32), text_row.astype(jnp.float32))
        row_masks = (jnp.ones((IMG, 1), jnp.float32), live_row.astype(jnp.float32)[:, None])
        cotangents = (image_cot, text_cot)
        modulation = []
        first_norm = []
        attn_inputs = []
        qkv_rows = []
        for stream in range(2):
            shifts = jnp.dot(cond_act[None, :], ada_weight[:, stream, :], preferred_element_type=jnp.float32)[0]
            shifts = (shifts + ada_bias[stream].astype(jnp.float32)).reshape(6, D)
            normed, inv_std = layer_norm(residual_in[stream])
            attn_in = (normed * (1.0 + shifts[1]) + shifts[0]).astype(jnp.bfloat16)
            projected = jnp.dot(attn_in, qkv_weight[:, stream].reshape(D, 3 * D), preferred_element_type=jnp.float32).reshape(-1, 3, D)
            bias_rows = jnp.stack([qv_bias[stream, 0].astype(jnp.float32), jnp.zeros((D,), jnp.float32), qv_bias[stream, 1].astype(jnp.float32)])
            modulation.append(shifts)
            first_norm.append((normed, inv_std))
            attn_inputs.append(attn_in)
            qkv_rows.append((projected + bias_rows).astype(jnp.bfloat16))
        joint_rows = jnp.concatenate(qkv_rows, axis=0).reshape(-1, 3, H, HD)
        live_keys = jnp.concatenate([jnp.ones((IMG,), jnp.bool_), live_row])
        mixture, log_total = attend(joint_rows[:, 0], joint_rows[:, 1], joint_rows[:, 2], live_keys)
        mixture_rows = mixture.reshape(-1, D)
        mix_parts = (mixture_rows[:IMG], mixture_rows[IMG:])
        outputs = []
        grad_middles = []
        gate_ones = []
        shift_twos = []
        scale_twos = []
        gate_twos = []
        grad_mix_parts = []
        new_grads = {}
        for stream in range(2):
            shifts = modulation[stream]
            attn_out = jnp.dot(mix_parts[stream], proj_weight[:, stream], preferred_element_type=jnp.float32) + proj_bias[stream].astype(jnp.float32)
            middle = residual_in[stream] + shifts[2] * attn_out
            normed_two, inv_two = layer_norm(middle)
            mlp_in = (normed_two * (1.0 + shifts[4]) + shifts[3]).astype(jnp.bfloat16)
            pre_act = jnp.dot(mlp_in, fc1_weight[:, stream], preferred_element_type=jnp.float32) + fc1_bias[stream].astype(jnp.float32)
            hidden = gelu_tanh(pre_act).astype(jnp.bfloat16)
            mlp_out = jnp.dot(hidden, fc2_weight[:, stream], preferred_element_type=jnp.float32) + fc2_bias[stream].astype(jnp.float32)
            outputs.append(((middle + shifts[5] * mlp_out) * row_masks[stream]).astype(jnp.bfloat16))
            upstream = cotangents[stream].astype(jnp.float32) * row_masks[stream]
            grad_mlp_full = shifts[5] * upstream
            gate_twos.append(lax.optimization_barrier(jnp.sum(upstream * mlp_out, axis=0)))
            grad_mlp = grad_mlp_full.astype(jnp.bfloat16)
            new_grads['fc2', stream] = jnp.dot(hidden.T, grad_mlp, preferred_element_type=jnp.float32)
            new_grads['fc2b', stream] = lax.optimization_barrier(jnp.sum(grad_mlp_full, axis=0))
            grad_hidden = jnp.dot(grad_mlp, fc2_weight[:, stream].T, preferred_element_type=jnp.float32) * gelu_slope(pre_act)
            new_grads['fc1b', stream] = lax.optimization_barrier(jnp.sum(grad_hidden, axis=0))
            grad_hidden_half = grad_hidden.astype(jnp.bfloat16)
            new_grads['fc1', stream] = jnp.dot(mlp_in.T, grad_hidden_half, preferred_element_type=jnp.float32)
            grad_mlp_in = jnp.dot(grad_hidden_half, fc1_weight[:, stream].T, preferred_element_type=jnp.float32)
            scale_twos.append(lax.optimization_barrier(jnp.sum(grad_mlp_in * normed_two, axis=0)))
            shift_twos.append(lax.optimization_barrier(jnp.sum(grad_mlp_in, axis=0)))
            grad_middle = upstream + norm_back(normed_two, inv_two, grad_mlp_in * (1.0 + shifts[4]))
            grad_middles.append(grad_middle)
            grad_attn_full = shifts[2] * grad_middle
            gate_ones.append(lax.optimization_barrier(jnp.sum(grad_middle * attn_out, axis=0)))
            new_grads['projb', stream] = lax.optimization_barrier(jnp.sum(grad_attn_full, axis=0))
            grad_attn = grad_attn_full.astype(jnp.bfloat16)
            new_grads['proj', stream] = jnp.dot(mix_parts[stream].T, grad_attn, preferred_element_type=jnp.float32)
            grad_mix_parts.append(jnp.dot(grad_attn, proj_weight[:, stream].T, preferred_element_type=jnp.float32).astype(jnp.bfloat16))
        grad_mix = jnp.concatenate(grad_mix_parts, axis=0).reshape(-1, H, HD)
        grad_query, grad_key, grad_value = attend_back(joint_rows[:, 0], joint_rows[:, 1], joint_rows[:, 2], mixture, grad_mix, log_total, live_keys)
        grad_joint = jnp.stack([grad_query, grad_key, grad_value], axis=1).reshape(-1, 3, D)
        joint_parts = (grad_joint[:IMG], grad_joint[IMG:])
        input_grads = []
        mod_list = []
        for stream in range(2):
            shifts = modulation[stream]
            rows_grad = joint_parts[stream]
            new_grads['qvb', stream] = jnp.stack([lax.optimization_barrier(jnp.sum(rows_grad[:, 0], axis=0)), lax.optimization_barrier(jnp.sum(rows_grad[:, 2], axis=0))])
            rows_half = rows_grad.astype(jnp.bfloat16).reshape(-1, 3 * D)
            new_grads['qkv', stream] = jnp.dot(attn_inputs[stream].T, rows_half, preferred_element_type=jnp.float32).reshape(D, 3, D)
            grad_attn_in = jnp.dot(rows_half, qkv_weight[:, stream].reshape(D, 3 * D).T, preferred_element_type=jnp.float32)
            normed, inv_std = first_norm[stream]
            scale_one = lax.optimization_barrier(jnp.sum(grad_attn_in * normed, axis=0))
            shift_one = lax.optimization_barrier(jnp.sum(grad_attn_in, axis=0))
            input_grads.append((grad_middles[stream] + norm_back(normed, inv_std, grad_attn_in * (1.0 + shifts[1]))) * row_masks[stream])
            mod_list.append(jnp.stack([shift_one, scale_one, gate_ones[stream], shift_twos[stream], scale_twos[stream], gate_twos[stream]]).reshape(6 * D))
        mod_grads = jnp.stack(mod_list)
        mod_half = mod_grads.astype(jnp.bfloat16)
        grad_act = jnp.zeros((D,), jnp.float32)
        ada_parts = []
        for stream in range(2):
            grad_act = grad_act + jnp.dot(mod_half[stream][None, :], ada_weight[:, stream, :].T, preferred_element_type=jnp.float32)[0]
            ada_parts.append(jnp.dot(cond_act[:, None], mod_half[stream][None, :], preferred_element_type=jnp.float32))
        cond_grad = grad_act * silu_slope(cond_float)
        increments = (jnp.stack(ada_parts, axis=1), mod_grads, jnp.stack([new_grads['qkv', 0], new_grads['qkv', 1]], axis=1), jnp.stack([new_grads['qvb', 0], new_grads['qvb', 1]]), jnp.stack([new_grads['proj', 0], new_grads['proj', 1]], axis=1), jnp.stack([new_grads['projb', 0], new_grads['projb', 1]]), jnp.stack([new_grads['fc1', 0], new_grads['fc1', 1]], axis=1), jnp.stack([new_grads['fc1b', 0], new_grads['fc1b', 1]]), jnp.stack([new_grads['fc2', 0], new_grads['fc2', 1]], axis=1), jnp.stack([new_grads['fc2b', 0], new_grads['fc2b', 1]]))
        running = tuple((total + extra for total, extra in zip(running, increments)))
        return (running, (outputs[0], outputs[1], input_grads[0], input_grads[1], cond_grad))
    totals, stacked = lax.scan(one_sequence, zero_grads, (image_tokens, text_tokens, live_text, conditioning, image_cotangent, text_cotangent))
    return (stacked[0], stacked[1], stacked[2], stacked[3], stacked[4], totals[0], totals[1], totals[2], totals[3], totals[4], totals[5], totals[6], totals[7], totals[8], totals[9])
```

```python
import functools
import math

import jax
import jax.numpy as jnp
from jax import lax
from jax.experimental import pallas as pl
from jax.experimental.pallas import tpu as pltpu
from jax.sharding import PartitionSpec as P

HD = 64
LANES = 128
EPSILON = 1e-06
GELU_ROOT = math.sqrt(2.0 / math.pi)
GELU_CUBE = 0.044715
MASKED = -1e30
SINGLE = jnp.float32
HALF = jnp.bfloat16
MEGA = 2**20


def up(value, multiple):
    return -(-value // multiple) * multiple


def params(limit=56):
    return pltpu.CompilerParams(
        dimension_semantics=None, vmem_limit_bytes=limit * MEGA
    )


def cost(flops, nbytes, trans=0):
    return pl.CostEstimate(flops=int(flops), bytes_accessed=int(nbytes), transcendentals=int(trans))


def nt_dot(a, b):
    return lax.dot_general(a, b, (((1,), (1,)), ((), ())), preferred_element_type=SINGLE)


def tn_dot(a, b):
    return lax.dot_general(a, b, (((0,), (0,)), ((), ())), preferred_element_type=SINGLE)


def nn_dot(a, b):
    return jnp.dot(a, b, preferred_element_type=SINGLE)


def layer_norm(values):
    center = values - jnp.mean(values, axis=-1, keepdims=True)
    inv_std = lax.rsqrt(jnp.mean(center * center, axis=-1, keepdims=True) + EPSILON)
    return (center * inv_std, inv_std)


def norm_back(normed, inv_std, upstream):
    first = jnp.mean(upstream, axis=-1, keepdims=True)
    second = jnp.mean(upstream * normed, axis=-1, keepdims=True)
    return inv_std * (upstream - first - normed * second)


def gelu_both(values):
    square = values * values
    inner = GELU_ROOT * (values + GELU_CUBE * square * values)
    tangent = jnp.tanh(inner)
    half = 0.5 * (1.0 + tangent)
    slope = half + 0.5 * values * (1.0 - tangent * tangent) * GELU_ROOT * (
        1.0 + 3.0 * GELU_CUBE * square
    )
    return values * half, slope


def silu_slope(values):
    sigma = jax.nn.sigmoid(values)
    return sigma + values * sigma * (1.0 - sigma)


def whole(shape, single=False):
    zeros = (0,) * len(shape)
    if single:
        return pl.BlockSpec(shape, lambda *_: zeros, pipeline_mode=pl.Buffered(1))
    return pl.BlockSpec(shape, lambda *_: zeros)


def rows_spec(rows, width):
    return pl.BlockSpec((1, rows, width), lambda s: (s, 0, 0))


def qkv_kernel(img, x_ref, mod_ref, w_ref, b_ref, a_ref, o_ref):
    wide = o_ref.shape[2]
    for t, sl in ((0, slice(0, img)), (1, slice(img, x_ref.shape[1]))):
        normed, _ = layer_norm(x_ref[0, sl].astype(SINGLE))
        a = (normed * (1.0 + mod_ref[t, 1:2]) + mod_ref[t, 0:1]).astype(HALF)
        a_ref[0, sl] = a
        o_ref[0, sl] = (
            nn_dot(a, w_ref[:, t * wide : (t + 1) * wide]) + b_ref[t : t + 1]
        ).astype(HALF)


def project_qkv(n, img, x_all, mods, weight, bias):
    _, rows, width = x_all.shape
    wide = weight.shape[1] // 2
    return pl.pallas_call(
        functools.partial(qkv_kernel, img),
        grid=(n,),
        in_specs=[rows_spec(rows, width), whole(mods.shape), whole(weight.shape, True), whole(bias.shape)],
        out_specs=[rows_spec(rows, width), rows_spec(rows, wide)],
        out_shape=[
            jax.ShapeDtypeStruct((n, rows, width), HALF),
            jax.ShapeDtypeStruct((n, rows, wide), HALF),
        ],
        compiler_params=params(),
        cost_estimate=cost(2 * n * rows * width * wide, 30 * MEGA),
        name="project_qkv",
    )(x_all, mods, weight, bias)


def halves(shape):
    lane = lax.broadcasted_iota(jnp.int32, shape, len(shape) - 1)
    return lane < HD


def attn_kernel(q_ref, k_ref, v_ref, mask_ref, o_ref, lse_ref):
    n, rows, _ = k_ref.shape
    queries = q_ref[0] * HALF(1.0 / math.sqrt(HD))
    keys = k_ref[...].reshape(n * rows, LANES)
    values = v_ref[...].reshape(n * rows, LANES)
    first = halves(queries.shape)
    outs, logs = [], []
    for head in range(2):
        own = first if head == 0 else jnp.logical_not(first)
        scores = nt_dot(jnp.where(own, queries, HALF(0)), keys) + mask_ref[...]
        maxima = jnp.max(scores, axis=-1, keepdims=True)
        raised = jnp.exp(scores - maxima)
        totals = jnp.sum(raised, axis=-1, keepdims=True)
        weights = (raised * (1.0 / totals)).astype(HALF)
        outs.append(nn_dot(weights, values))
        logs.append(maxima + jnp.log(totals))
    o_ref[0] = jnp.where(first, outs[0], outs[1]).astype(HALF)
    lse_ref[0] = jnp.where(first, logs[0], logs[1])


def attend(n, qkv, mask):
    _, rows, wide = qkv.shape
    pairs = wide // 3 // LANES
    total = n * rows
    block = pl.BlockSpec((1, rows, LANES), lambda h, s: (s, 0, h))
    return pl.pallas_call(
        attn_kernel,
        grid=(pairs, n),
        in_specs=[
            block,
            pl.BlockSpec((n, rows, LANES), lambda h, s: (0, 0, pairs + h)),
            pl.BlockSpec((n, rows, LANES), lambda h, s: (0, 0, 2 * pairs + h)),
            whole(mask.shape),
        ],
        out_specs=[block, block],
        out_shape=[
            jax.ShapeDtypeStruct((n, rows, pairs * LANES), HALF),
            jax.ShapeDtypeStruct((n, rows, pairs * LANES), SINGLE),
        ],
        compiler_params=params(),
        cost_estimate=cost(2 * 2 * 4 * pairs * total * total * LANES, 20 * MEGA, 2 * pairs * total * total),
        name="attend",
    )(qkv, qkv, qkv, mask)


def attn_back_kernel(
    q_ref, k_ref, v_ref, o_ref, g_ref, lse_ref, mask_ref, dq_ref, dk_ref, dv_ref, qb_ref, vb_ref,
    acc_ref, lse_row, delta_row,
):
    step = pl.program_id(1)
    last = pl.num_programs(1) - 1
    n, rows, _ = q_ref.shape
    total = n * rows
    grads = g_ref[...].reshape(total, LANES)
    queries = q_ref[...].reshape(total, LANES) * HALF(1.0 / math.sqrt(HD))

    @pl.when(step == 0)
    def _():
        acc_ref[...] = jnp.zeros_like(acc_ref)
        product = grads.astype(SINGLE) * o_ref[...].reshape(total, LANES).astype(SINGLE)
        turned = product.T
        logs = lse_ref[...].reshape(total, LANES).T
        for head in range(2):
            delta_row[head : head + 1] = jnp.sum(
                turned[head * HD : (head + 1) * HD], axis=0, keepdims=True
            )
            lse_row[head : head + 1] = logs[head * HD : head * HD + 1]
        vb_ref[0] = jnp.zeros_like(vb_ref[0])

    keys, values = k_ref[0], v_ref[0]
    first = halves(keys.shape)
    mask = mask_ref[0][:, 0:1]
    dks, dvs = [], []
    for head in range(2):
        own = first if head == 0 else jnp.logical_not(first)
        key_own = jnp.where(own, keys, HALF(0))
        scores = nt_dot(key_own, queries)
        probs = jnp.exp((scores - lse_row[head : head + 1]) + mask)
        grad_prob = nt_dot(jnp.where(own, values, HALF(0)), grads)
        grad_score = (probs * (grad_prob - delta_row[head : head + 1])).astype(HALF)
        dvs.append(nn_dot(probs.astype(HALF), grads))
        dks.append(nn_dot(grad_score, queries))
        acc_ref[...] += tn_dot(grad_score, key_own)
    dk_ref[0] = jnp.where(first, dks[0], dks[1]).astype(HALF)
    dv = jnp.where(first, dvs[0], dvs[1])
    dv_ref[0] = dv.astype(HALF)
    img = mask_ref.shape[2]
    vb_ref[0, 0:1] += jnp.sum(dv[:img], axis=0, keepdims=True)
    vb_ref[0, 1:2] += jnp.sum(dv[img:], axis=0, keepdims=True)

    @pl.when(step == last)
    def _():
        dq = (acc_ref[...] * (1.0 / math.sqrt(HD))).reshape(n, rows, LANES)
        dq_ref[...] = dq.astype(HALF)
        qb_ref[0, 0:1] = jnp.sum(jnp.sum(dq[:, :img], axis=0), axis=0, keepdims=True)
        qb_ref[0, 1:2] = jnp.sum(jnp.sum(dq[:, img:], axis=0), axis=0, keepdims=True)


def attend_back(n, img, qkv, mixture, grad_mix, lse, mask_col):
    _, rows, wide = qkv.shape
    pairs = wide // 3 // LANES
    total = n * rows
    full = pl.BlockSpec((n, rows, LANES), lambda h, s: (0, 0, h))
    block = pl.BlockSpec((1, rows, LANES), lambda h, s: (s, 0, h))
    bias = pl.BlockSpec((1, 2, LANES), lambda h, s: (h, 0, 0))
    lw = pairs * LANES
    return pl.pallas_call(
        attn_back_kernel,
        grid=(pairs, n),
        in_specs=[
            full,
            pl.BlockSpec((1, rows, LANES), lambda h, s: (s, 0, pairs + h)),
            pl.BlockSpec((1, rows, LANES), lambda h, s: (s, 0, 2 * pairs + h)),
            full,
            full,
            full,
            pl.BlockSpec((1, rows, img), lambda h, s: (s, 0, 0)),
        ],
        out_specs=[full, block, block, bias, bias],
        out_shape=[jax.ShapeDtypeStruct((n, rows, lw), HALF)] * 3
        + [jax.ShapeDtypeStruct((pairs, 2, LANES), SINGLE)] * 2,
        scratch_shapes=[
            pltpu.VMEM((total, LANES), SINGLE),
            pltpu.VMEM((2, total), SINGLE),
            pltpu.VMEM((2, total), SINGLE),
        ],
        compiler_params=params(),
        cost_estimate=cost(2 * 5 * 4 * pairs * total * total * LANES, 30 * MEGA, 2 * pairs * total * total),
        name="attend_back",
    )(qkv, qkv, qkv, mixture, grad_mix, lse, mask_col)


def middle_kernel(img, mix_ref, x_ref, w_ref, b_ref, mod_ref, y_ref, m_ref, o_ref):
    width = x_ref.shape[1]
    for t, sl in ((0, slice(0, img)), (1, slice(img, x_ref.shape[0]))):
        attn = nt_dot(mix_ref[sl], w_ref[:, t * width : (t + 1) * width]) + b_ref[t : t + 1]
        y_ref[sl] = attn
        middle = x_ref[sl].astype(SINGLE) + mod_ref[t, 2:3] * attn
        m_ref[sl] = middle
        normed, _ = layer_norm(middle)
        o_ref[sl] = (normed * (1.0 + mod_ref[t, 4:5]) + mod_ref[t, 3:4]).astype(HALF)


def middle_rows(img, mixture, x_loc, weight, bias, mods):
    rows, width = x_loc.shape
    return pl.pallas_call(
        functools.partial(middle_kernel, img),
        out_shape=[
            jax.ShapeDtypeStruct((rows, width), SINGLE),
            jax.ShapeDtypeStruct((rows, width), SINGLE),
            jax.ShapeDtypeStruct((rows, width), HALF),
        ],
        compiler_params=params(),
        cost_estimate=cost(2 * rows * width * width, 16 * MEGA),
        name="middle_rows",
    )(mixture, x_loc, weight, bias, mods)


def mlp_kernel(img, tile, b_ref, e_ref, mod_ref, w1_ref, b1_ref, w2_ref, g_ref, dz_ref, dy_ref, db_ref, sum_ref, acc_ref):
    step = pl.program_id(0)
    units = g_ref.shape[2]

    @pl.when(step == 0)
    def _():
        sum_ref[...] = jnp.zeros_like(sum_ref)

    for t, sl in ((0, slice(0, img)), (1, slice(img, b_ref.shape[1]))):
        rows = b_ref[0, sl]
        grad = (mod_ref[t, 5:6] * e_ref[0, sl].astype(SINGLE)).astype(HALF)
        dy_ref[0, sl] = grad

        for k in range(units // tile):
            here = slice(k * tile, (k + 1) * tile)
            cols = slice(t * units + k * tile, t * units + (k + 1) * tile)
            w1 = w1_ref[:, cols]
            pre = nn_dot(rows, w1) + b1_ref[t : t + 1, here]
            hidden, slope = gelu_both(pre)
            g_ref[0, sl, here] = hidden.astype(HALF)
            dz = nn_dot(grad, w2_ref[:, cols]) * slope
            sum_ref[t : t + 1, here] += jnp.sum(dz, axis=0, keepdims=True)
            dzh = dz.astype(HALF)
            dz_ref[0, sl, here] = dzh
            part = nt_dot(dzh, w1)
            if k == 0:
                acc_ref[sl] = part
            else:
                acc_ref[sl] += part
        db_ref[0, sl] = acc_ref[sl].astype(HALF)


def feed_forward(n, img, mlp_in, cot, mods, w1, b1, w2):
    rows, width = mlp_in.shape[1:]
    units = w1.shape[1] // 2
    tile = min(512, units)
    while units % tile:
        tile -= LANES
    return pl.pallas_call(
        functools.partial(mlp_kernel, img, tile),
        grid=(n,),
        in_specs=[
            rows_spec(rows, width),
            rows_spec(rows, width),
            whole(mods.shape),
            whole(w1.shape, True),
            whole(b1.shape),
            whole(w2.shape, True),
        ],
        out_specs=[
            rows_spec(rows, units),
            rows_spec(rows, units),
            rows_spec(rows, width),
            rows_spec(rows, width),
            whole((2, units)),
        ],
        out_shape=[
            jax.ShapeDtypeStruct((n, rows, units), HALF),
            jax.ShapeDtypeStruct((n, rows, units), HALF),
            jax.ShapeDtypeStruct((n, rows, width), HALF),
            jax.ShapeDtypeStruct((n, rows, width), HALF),
            jax.ShapeDtypeStruct((2, units), SINGLE),
        ],
        scratch_shapes=[pltpu.VMEM((rows, width), SINGLE)],
        compiler_params=params(),
        cost_estimate=cost(6 * n * rows * width * units, 50 * MEGA, n * rows * units),
        name="feed_forward",
    )(mlp_in, cot, mods, w1, b1, w2)


def out_kernel(img, g_ref, e_ref, w2_ref, y_ref, sum_ref):
    units = g_ref.shape[2]

    @pl.when(pl.program_id(0) == 0)
    def _():
        sum_ref[...] = jnp.zeros_like(sum_ref)

    for t, sl in ((0, slice(0, img)), (1, slice(img, g_ref.shape[1]))):
        part = nt_dot(g_ref[0, sl], w2_ref[:, t * units : (t + 1) * units])
        y_ref[0, sl] = part.astype(HALF)
        sum_ref[t : t + 1] += jnp.sum(part * e_ref[0, sl].astype(SINGLE), axis=0, keepdims=True)


def feed_out(n, img, hidden, cot, w2):
    _, rows, units = hidden.shape
    width = w2.shape[0]
    return pl.pallas_call(
        functools.partial(out_kernel, img),
        grid=(n,),
        in_specs=[rows_spec(rows, units), rows_spec(rows, width), whole(w2.shape, True)],
        out_specs=[rows_spec(rows, width), whole((2, width))],
        out_shape=[
            jax.ShapeDtypeStruct((n, rows, width), HALF),
            jax.ShapeDtypeStruct((2, width), SINGLE),
        ],
        compiler_params=params(),
        cost_estimate=cost(2 * n * rows * width * units, 20 * MEGA),
        name="feed_out",
    )(hidden, cot, w2)


def grad_kernel(img, l_ref, r_ref, o_ref):
    n = l_ref.shape[0]
    stream = pl.program_id(0)
    for t, sl in ((0, slice(0, img)), (1, slice(img, l_ref.shape[1]))):

        @pl.when(stream == t)
        def _():
            left = l_ref[:, sl].reshape(-1, l_ref.shape[2])
            right = r_ref[:, sl].reshape(-1, r_ref.shape[2])
            o_ref[...] = tn_dot(left, right).astype(HALF)


def weight_grad(n, img, left, right, name):
    rows, depth = left.shape[1:]
    wide = right.shape[2]
    tile = 384 if wide % 384 == 0 else (256 if wide % 256 == 0 else LANES)
    tiles = wide // tile
    return pl.pallas_call(
        functools.partial(grad_kernel, img),
        grid=(2, tiles),
        in_specs=[
            whole((n, rows, depth), True),
            pl.BlockSpec((n, rows, tile), lambda t, k: (0, 0, k)),
        ],
        out_specs=pl.BlockSpec((depth, tile), lambda t, k: (0, t * tiles + k)),
        out_shape=jax.ShapeDtypeStruct((depth, 2 * wide), HALF),
        compiler_params=params(),
        cost_estimate=cost(2 * n * rows * depth * wide, 20 * MEGA),
        name=name,
    )(left, right)


def middle_back_kernel(img, db_ref, m_ref, y_ref, e_ref, w_ref, mod_ref, dm_ref, dy_ref, do_ref, sum_ref):
    width = m_ref.shape[1]
    for t, sl in ((0, slice(0, img)), (1, slice(img, m_ref.shape[0]))):
        grad_in = db_ref[sl]
        normed, inv_std = layer_norm(m_ref[sl])
        upstream = e_ref[sl].astype(SINGLE)
        grad_middle = upstream + norm_back(normed, inv_std, grad_in * (1.0 + mod_ref[t, 4:5]))
        dm_ref[sl] = grad_middle
        grad_attn = mod_ref[t, 2:3] * grad_middle
        half = grad_attn.astype(HALF)
        dy_ref[sl] = half
        do_ref[sl] = nn_dot(half, w_ref[:, t * width : (t + 1) * width]).astype(HALF)

        def total(value):
            return jnp.sum(value, axis=0, keepdims=True)

        sum_ref[t, 0:1] = total(grad_middle * y_ref[sl])
        sum_ref[t, 1:2] = total(grad_in)
        sum_ref[t, 2:3] = total(grad_in * normed)
        sum_ref[t, 3:4] = total(grad_attn)
        sum_ref[t, 4:5] = total(upstream)


def middle_back(img, grad_in, middle, attn_out, cot, weight, mods):
    rows, width = middle.shape
    return pl.pallas_call(
        functools.partial(middle_back_kernel, img),
        out_shape=[
            jax.ShapeDtypeStruct((rows, width), SINGLE),
            jax.ShapeDtypeStruct((rows, width), HALF),
            jax.ShapeDtypeStruct((rows, width), HALF),
            jax.ShapeDtypeStruct((2, 8, width), SINGLE),
        ],
        compiler_params=params(),
        cost_estimate=cost(2 * rows * width * width, 20 * MEGA),
        name="middle_back",
    )(grad_in, middle, attn_out, cot, weight, mods)


def attn_in_kernel(img, dq_ref, dk_ref, dv_ref, x_ref, w_ref, da_ref, sum_ref):
    lw = dq_ref.shape[2]

    @pl.when(pl.program_id(0) == 0)
    def _():
        sum_ref[...] = jnp.zeros_like(sum_ref)

    for t, sl in ((0, slice(0, img)), (1, slice(img, x_ref.shape[1]))):
        part = None
        for c, ref in enumerate((dq_ref, dk_ref, dv_ref)):
            start = (3 * t + c) * lw
            term = nt_dot(ref[0, sl], w_ref[:, start : start + lw])
            part = term if part is None else part + term
        da_ref[0, sl] = part.astype(HALF)
        normed, _ = layer_norm(x_ref[0, sl].astype(SINGLE))
        sum_ref[t, 0:1] += jnp.sum(part, axis=0, keepdims=True)
        sum_ref[t, 1:2] += jnp.sum(part * normed, axis=0, keepdims=True)


def attn_in_back(n, img, dq, dk, dv, x_all, weight):
    _, rows, lw = dq.shape
    width = x_all.shape[2]
    return pl.pallas_call(
        functools.partial(attn_in_kernel, img),
        grid=(n,),
        in_specs=[rows_spec(rows, lw)] * 3 + [rows_spec(rows, width), whole(weight.shape, True)],
        out_specs=[rows_spec(rows, width), whole((2, 2, width))],
        out_shape=[
            jax.ShapeDtypeStruct((n, rows, width), HALF),
            jax.ShapeDtypeStruct((2, 2, width), SINGLE),
        ],
        compiler_params=params(),
        cost_estimate=cost(6 * n * rows * width * lw, 30 * MEGA),
        name="attn_in_back",
    )(dq, dk, dv, x_all, weight)


def hops(n):
    return [(a, a + 1) for a in range(n - 1)], [(a + 1, a) for a in range(n - 1)]


def line_gather(rows, n):
    me = lax.axis_index("seq")
    right, left = hops(n)
    held = jnp.zeros((n + 1,) + rows.shape, rows.dtype)
    held = lax.dynamic_update_index_in_dim(held, rows, me, 0)
    from_left = from_right = rows
    for k in range(1, n):
        from_left = lax.ppermute(from_left, "seq", right)
        from_right = lax.ppermute(from_right, "seq", left)
        held = lax.dynamic_update_index_in_dim(
            held, from_left, jnp.where(me >= k, me - k, n), 0
        )
        held = lax.dynamic_update_index_in_dim(
            held, from_right, jnp.where(me + k < n, me + k, n), 0
        )
    return held


def line_sum(parts, n):
    me = lax.axis_index("seq")
    right, left = hops(n)

    def term(s):
        return lax.dynamic_index_in_dim(parts, jnp.clip(s, 0, n - 1), 0, keepdims=False).astype(
            SINGLE
        )

    result = term(me)
    for sign, pattern in ((1, right), (-1, left)):
        carry = None
        for k in range(n - 1, 0, -1):
            value = term(me + sign * k)
            if carry is not None:
                value = value + carry.astype(SINGLE)
            carry = lax.ppermute(value.astype(HALF), "seq", pattern)
        result = result + carry.astype(SINGLE)
    return result


def swap(parts, n):
    me = lax.axis_index("seq")
    held = jnp.zeros_like(parts)
    held = lax.dynamic_update_index_in_dim(
        held, lax.dynamic_index_in_dim(parts, me, 0, keepdims=False), me, 0
    )
    for k in range(1, n):
        piece = lax.dynamic_index_in_dim(parts, lax.rem(me + k, n), 0, keepdims=False)
        got = lax.ppermute(piece, "seq", [(a, (a + k) % n) for a in range(n)])
        held = lax.dynamic_update_index_in_dim(held, got, lax.rem(me + n - k, n), 0)
    return held


def body(
    image_tokens,
    text_tokens,
    text_lengths,
    conditioning,
    ada_weight,
    ada_bias,
    qkv_weight,
    qv_bias,
    proj_weight,
    proj_bias,
    fc1_weight,
    fc1_bias,
    fc2_weight,
    fc2_bias,
    image_cotangent,
    text_cotangent,
):
    n = lax.axis_size("seq")
    dp = lax.axis_size("dp")
    img, width = image_tokens.shape[1:]
    slots = text_tokens.shape[1]
    pad = up(slots, 16)
    rows = img + pad
    depth = qkv_weight.shape[0]
    lw = qkv_weight.shape[3]
    lwp = up(lw, LANES)
    units = fc1_weight.shape[2]
    mod_cols = ada_weight.shape[2]
    my_seq = lax.axis_index("dp")

    def stacked(image, text):
        return jnp.concatenate([image, jnp.pad(text, ((0, pad - slots), (0, 0)))], axis=0)

    length = text_lengths[0, 0]
    live_text = (jnp.arange(slots, dtype=jnp.int32) < length)[:, None]
    x_loc = stacked(image_tokens[0], text_tokens[0])
    e_loc = stacked(
        image_cotangent[0], jnp.where(live_text, text_cotangent[0], jnp.zeros((), HALF))
    )
    x_all = line_gather(x_loc, n)

    qkv_local = jnp.pad(qkv_weight, ((0, 0), (0, 0), (0, 0), (0, lwp - lw))).reshape(depth, 6 * lwp)
    qkv_full = lax.all_gather(qkv_local, "dp", axis=0, tiled=True)
    share = proj_weight.shape[0]
    proj_turned = proj_weight.transpose(2, 1, 0)
    proj_line = lax.all_gather(proj_turned, "seq", axis=2, tiled=True).reshape(depth, 2 * width)
    proj_full = lax.all_gather(proj_line, "dp", axis=0, tiled=True)
    fc1_full = lax.all_gather(fc1_weight.reshape(depth, 2 * units), "dp", axis=0, tiled=True)
    fc2_turned = fc2_weight.transpose(2, 1, 0).reshape(depth, 2 * units)
    fc2_full = lax.all_gather(fc2_turned, "dp", axis=0, tiled=True)

    cond_float = conditioning.astype(SINGLE)
    cond_act = jax.nn.silu(cond_float).astype(HALF)
    act_all = lax.all_gather(cond_act, "dp", axis=0, tiled=True)
    act_slice = lax.dynamic_slice_in_dim(act_all, my_seq * depth, depth, axis=1)
    ada_flat = ada_weight.reshape(depth, 2 * mod_cols)
    mod_part = jnp.dot(act_slice, ada_flat, preferred_element_type=SINGLE)
    mod_local = lax.psum_scatter(mod_part, "dp", scatter_dimension=0, tiled=True).reshape(
        2, mod_cols
    ) + ada_bias.astype(SINGLE)
    side = jnp.concatenate(
        [
            mod_local.reshape(-1),
            proj_bias.astype(SINGLE).reshape(-1),
            fc2_bias.astype(SINGLE).reshape(-1),
            jnp.full((LANES,), length.astype(SINGLE)),
        ]
    )
    side_all = lax.all_gather(side, "seq", axis=0, tiled=False)
    bias_cols = proj_bias.shape[1]
    cut = 2 * mod_cols

    def columns(start, cols):
        return side_all[:, start : start + 2 * cols].reshape(n, 2, cols).transpose(1, 0, 2)

    mods = jnp.pad(
        columns(0, mod_cols).reshape(2, 6, width), ((0, 0), (0, 2), (0, 0))
    )
    proj_shift = columns(cut, bias_cols).reshape(2, width)
    fc2_shift = columns(cut + 2 * bias_cols, bias_cols).reshape(2, width)
    lengths_all = side_all[:, cut + 4 * bias_cols]

    slot = jnp.arange(rows, dtype=SINGLE)[None, :] - img
    live = jnp.logical_or(slot < 0, jnp.logical_and(slot < lengths_all[:, None], slot < slots))
    mask = jnp.where(live, SINGLE(0), SINGLE(MASKED))
    mask_row = mask.reshape(1, n * rows)
    mask_col = jnp.broadcast_to(mask[:, :, None], (n, rows, img))
    live_loc = jnp.concatenate(
        [jnp.ones((img, 1), SINGLE), jnp.pad(live_text.astype(SINGLE), ((0, pad - slots), (0, 0)))]
    )

    bias_rows = jnp.stack(
        [qv_bias[:, 0], jnp.zeros_like(qv_bias[:, 0]), qv_bias[:, 1]], axis=1
    ).astype(SINGLE)
    bias_rows = jnp.pad(bias_rows, ((0, 0), (0, 0), (0, lwp - lw))).reshape(2, 3 * lwp)
    attn_in, qkv_rows = project_qkv(n, img, x_all, mods, qkv_full, bias_rows)
    mixture, lse = attend(n, qkv_rows, mask_row)
    e_all = line_gather(e_loc, n)
    mix_loc = swap(mixture[:, :, :lw], n).transpose(1, 0, 2).reshape(rows, width)

    attn_out, middle, mlp_loc = middle_rows(img, mix_loc, x_loc, proj_full, proj_shift, mods)
    mlp_in = line_gather(mlp_loc, n)
    hidden, grad_pre, grad_mlp, mlp_in_part, fc1_bias_part = feed_forward(
        n, img, mlp_in, e_all, mods, fc1_full, fc1_bias.astype(SINGLE), fc2_full
    )
    grad_mlp_in = line_sum(mlp_in_part, n)
    fc1_part = weight_grad(n, img, mlp_in, grad_pre, "fc1_grad")
    fc1_sum = lax.psum_scatter(fc1_part, "dp", scatter_dimension=0, tiled=True)
    fc2_part = weight_grad(n, img, grad_mlp, hidden, "fc2_grad")
    fc2_sum = lax.psum_scatter(fc2_part, "dp", scatter_dimension=0, tiled=True)
    mlp_out_part, gate_two_part = feed_out(n, img, hidden, e_all, fc2_full)

    grad_middle, grad_attn, grad_mix_loc, sums = middle_back(
        img, grad_mlp_in, middle, attn_out, e_loc, proj_full, mods
    )
    grad_mix = swap(grad_mix_loc.reshape(rows, n, lw).transpose(1, 0, 2), n)
    grad_mix = jnp.pad(grad_mix, ((0, 0), (0, 0), (0, lwp - lw)))
    mlp_sum = line_sum(mlp_out_part, n)
    proj_part = weight_grad(1, img, grad_attn[None], mix_loc[None], "proj_grad")
    proj_sum = lax.psum_scatter(proj_part, "dp", scatter_dimension=0, tiled=True)
    proj_own = lax.psum_scatter(
        proj_sum.reshape(depth, 2, n, share).transpose(2, 0, 1, 3).astype(SINGLE),
        "seq",
        scatter_dimension=0,
        tiled=False,
    )
    grad_q, grad_k, grad_v, q_bias_part, v_bias_part = attend_back(
        n, img, qkv_rows, mixture, grad_mix, lse, mask_col
    )
    attn_in_part, mod_one = attn_in_back(n, img, grad_q, grad_k, grad_v, x_all, qkv_full)
    grad_attn_in = line_sum(attn_in_part, n)
    qkv_part = weight_grad(
        n, img, attn_in, jnp.concatenate([grad_q, grad_k, grad_v], axis=2), "qkv_grad"
    )
    qkv_sum = lax.psum_scatter(qkv_part, "dp", scatter_dimension=0, tiled=True)

    def by_row(vectors):
        return jnp.concatenate(
            [
                jnp.broadcast_to(vectors[0:1], (img, width)),
                jnp.broadcast_to(vectors[1:2], (pad, width)),
            ]
        )

    block_out = (
        (middle + by_row(mods[:, 5]) * (mlp_sum + by_row(fc2_shift))) * live_loc
    ).astype(HALF)
    normed, inv_std = layer_norm(x_loc.astype(SINGLE))
    input_grad = (
        grad_middle + norm_back(normed, inv_std, grad_attn_in * (1.0 + by_row(mods[:, 1])))
    ) * live_loc

    upstream_sum = sums[:, 4]
    gate_two = gate_two_part + fc2_shift * upstream_sum
    mod_grads = jnp.stack(
        [mod_one[:, 0], mod_one[:, 1], sums[:, 0], sums[:, 1], sums[:, 2], gate_two], axis=1
    ).reshape(2, n, mod_cols)
    rest = jnp.stack([sums[:, 3], mods[:, 5] * upstream_sum]).reshape(4, n, bias_cols)
    packed = jnp.concatenate(
        [
            mod_grads.transpose(1, 0, 2).reshape(n, -1),
            rest.transpose(1, 0, 2).reshape(n, -1),
        ],
        axis=1,
    )
    own = lax.psum_scatter(packed, "seq", scatter_dimension=0, tiled=False)
    q_bias = q_bias_part.transpose(1, 0, 2).reshape(2, lwp)[:, :lw]
    v_bias = v_bias_part.transpose(1, 0, 2).reshape(2, lwp)[:, :lw]
    qv_part = jnp.stack([q_bias, v_bias], axis=1)
    wide_row = jnp.concatenate([own, qv_part.reshape(-1), fc1_bias_part.reshape(-1)])
    every = lax.all_gather(wide_row, "dp", axis=0, tiled=False)
    total = jnp.sum(every, axis=0)
    mod_half = every[:, :cut].astype(HALF).reshape(dp, 2, mod_cols)
    ada_grad = jnp.einsum("nd,ntc->dtc", act_slice, mod_half, preferred_element_type=SINGLE)
    ada_bias_grad = total[:cut].reshape(2, mod_cols)
    proj_bias_grad = total[cut : cut + 2 * bias_cols].reshape(2, bias_cols)
    fc2_bias_grad = total[cut + 2 * bias_cols : cut + 4 * bias_cols].reshape(2, bias_cols)
    after = cut + 4 * bias_cols
    qv_bias_grad = total[after : after + 4 * lw].reshape(2, 2, lw)
    fc1_bias_grad = total[after + 4 * lw :].reshape(2, units)
    cond_part = jnp.einsum(
        "nc,dc->nd", mod_half.reshape(dp, cut), ada_flat, preferred_element_type=SINGLE
    )
    cond_cols = lax.psum(cond_part, "seq")
    cond_all = lax.all_gather(cond_cols, "dp", axis=1, tiled=True)
    cond_grad = lax.dynamic_slice_in_dim(cond_all, my_seq, 1, axis=0) * silu_slope(cond_float)

    def streams(flat, last):
        return flat.astype(SINGLE).reshape(depth, 2, last)

    qkv_grad = qkv_sum.astype(SINGLE).reshape(depth, 2, 3, lwp)[..., :lw]
    fc2_grad = streams(fc2_sum, units).transpose(2, 1, 0)
    proj_grad = proj_own.transpose(2, 1, 0)
    return (
        block_out[None, :img],
        block_out[None, img : img + slots],
        input_grad[None, :img],
        input_grad[None, img : img + slots],
        cond_grad,
        ada_grad,
        ada_bias_grad,
        qkv_grad,
        qv_bias_grad,
        proj_grad,
        proj_bias_grad,
        streams(fc1_sum, units),
        fc1_bias_grad,
        fc2_grad,
        fc2_bias_grad,
    )


def solution(mesh):
    in_specs = (
        P("dp", "seq", None),
        P("dp", "seq", None),
        P("dp", "seq"),
        P("dp", None),
        P("dp", None, "seq"),
        P(None, "seq"),
        P("dp", None, None, "seq"),
        P(None, None, "seq"),
        P("seq", None, "dp"),
        P(None, "seq"),
        P("dp", None, "seq"),
        P(None, "seq"),
        P("seq", None, "dp"),
        P(None, "seq"),
        P("dp", "seq", None),
        P("dp", "seq", None),
    )
    out_specs = (
        P("dp", "seq", None),
        P("dp", "seq", None),
        P("dp", "seq", None),
        P("dp", "seq", None),
        P("dp", None),
        P("dp", None, "seq"),
        P(None, "seq"),
        P("dp", None, None, "seq"),
        P(None, None, "seq"),
        P("seq", None, "dp"),
        P(None, "seq"),
        P("dp", None, "seq"),
        P(None, "seq"),
        P("seq", None, "dp"),
        P(None, "seq"),
    )
    return jax.shard_map(body, mesh=mesh, in_specs=in_specs, out_specs=out_specs, check_vma=False)
```

```python
import functools
import math

import jax
import jax.numpy as jnp
from jax import lax
from jax.experimental import pallas as pl
from jax.experimental.pallas import tpu as pltpu
from jax.sharding import PartitionSpec as P

HD = 64
LANES = 128
EPSILON = 1e-06
GELU_ROOT = math.sqrt(2.0 / math.pi)
GELU_CUBE = 0.044715
MASKED = -1e30
SINGLE = jnp.float32
HALF = jnp.bfloat16
MEGA = 2**20


def up(value, multiple):
    return -(-value // multiple) * multiple


def params(limit=56):
    return pltpu.CompilerParams(vmem_limit_bytes=limit * MEGA)


def remote(collective, limit=56):
    return pltpu.CompilerParams(
        collective_id=collective, has_side_effects=True, vmem_limit_bytes=limit * MEGA
    )


def cost(flops, nbytes, trans=0):
    return pl.CostEstimate(flops=int(flops), bytes_accessed=int(nbytes), transcendentals=int(trans))


def nt_dot(a, b):
    return lax.dot_general(a, b, (((1,), (1,)), ((), ())), preferred_element_type=SINGLE)


def tn_dot(a, b):
    return lax.dot_general(a, b, (((0,), (0,)), ((), ())), preferred_element_type=SINGLE)


def nn_dot(a, b):
    return jnp.dot(a, b, preferred_element_type=SINGLE)


def layer_norm(values):
    center = values - jnp.mean(values, axis=-1, keepdims=True)
    inv_std = lax.rsqrt(jnp.mean(center * center, axis=-1, keepdims=True) + EPSILON)
    return (center * inv_std, inv_std)


def norm_back(normed, inv_std, upstream):
    first = jnp.mean(upstream, axis=-1, keepdims=True)
    second = jnp.mean(upstream * normed, axis=-1, keepdims=True)
    return inv_std * (upstream - first - normed * second)


def gelu_both(values):
    square = values * values
    inner = GELU_ROOT * (values + GELU_CUBE * square * values)
    tangent = jnp.tanh(inner)
    half = 0.5 * (1.0 + tangent)
    slope = half + 0.5 * values * (1.0 - tangent * tangent) * GELU_ROOT * (
        1.0 + 3.0 * GELU_CUBE * square
    )
    return values * half, slope


def silu_slope(values):
    sigma = jax.nn.sigmoid(values)
    return sigma + values * sigma * (1.0 - sigma)


def whole(shape, single=False):
    zeros = (0,) * len(shape)
    if single:
        return pl.BlockSpec(shape, lambda *_: zeros, pipeline_mode=pl.Buffered(1))
    return pl.BlockSpec(shape, lambda *_: zeros)


def rows_spec(rows, width):
    return pl.BlockSpec((1, rows, width), lambda s: (s, 0, 0))


MESH = pl.DeviceIdType.MESH


def on_line(position):
    return {"seq": position}


def both(first, second):
    return jnp.logical_and(first, second)


def flip(value, mask):
    bit = 1
    while bit <= mask:
        if mask & bit:
            value = value + bit - 2 * bit * lax.rem(lax.div(value, bit), 2)
        bit *= 2
    return value


def greet(n, line=None, group=None):
    me, my = lax.axis_index("seq"), lax.axis_index("dp")
    dp = lax.axis_size("dp")
    barrier = pltpu.get_barrier_semaphore()
    peers = []
    if line == "all":
        peers += [on_line(lax.rem(me + offset, n)) for offset in range(1, n)]
    if group == "all":
        peers += [{"dp": lax.rem(my + offset, dp)} for offset in range(1, dp)]
    if group == "paths":
        peers += [{"dp": flip(my, 1)}] + [{"dp": flip(my, mask)} for mask in masks_of(dp)]
    for peer in peers:
        pl.semaphore_signal(barrier, inc=1, device_id=peer, device_id_type=MESH)
    if line == "near":
        for sign in (1, -1):
            near = me + sign

            @pl.when(both(near >= 0, near < n))
            def _():
                pl.semaphore_signal(barrier, inc=1, device_id=on_line(near), device_id_type=MESH)

    count = len(peers)
    if line == "near":
        count = count + lax.min(me, 1) + lax.min(n - 1 - me, 1)
    pl.semaphore_wait(barrier, count)


def masks_of(dp):
    masks, bit = [], 2
    while bit < dp:
        masks.append(bit)
        bit *= 2
    return masks


class GroupGather:
    def __init__(self, src, out, send, recv, pass_send, pass_recv, local):
        self.src, self.out = src, out
        self.send, self.recv, self.local = send, recv, local
        self.pass_send, self.pass_recv = pass_send, pass_recv
        self.my = lax.axis_index("dp")
        masks = masks_of(out.shape[0])
        self.orders = (masks, masks[::-1])
        self.phases = len(masks)

    @staticmethod
    def scratch(dp):
        return [pltpu.SemaphoreType.DMA((2, dp // 2)) for _ in range(4)] + [
            pltpu.SemaphoreType.DMA
        ]

    def span(self, half, count):
        mask = 0
        for k in range(self.phases):
            if count >> k & 1:
                mask |= self.orders[half][k]
        return mask

    def copy(self, half, phase, count, block):
        src = self.src.at[half] if count == 0 else self.out.at[block, half]
        index = 2**phase - 1 + count
        return pltpu.make_async_remote_copy(
            src_ref=src,
            dst_ref=self.out.at[block, half],
            send_sem=self.send.at[half, index],
            recv_sem=self.recv.at[half, index],
            device_id={"dp": flip(self.my, self.orders[half][phase])},
            device_id_type=MESH,
        )

    def hand(self, half, index, block, own=False):
        src = self.src.at[half] if own else self.out.at[block, half]
        return pltpu.make_async_remote_copy(
            src_ref=src,
            dst_ref=self.out.at[block, half],
            send_sem=self.pass_send.at[half, index],
            recv_sem=self.pass_recv.at[half, index],
            device_id={"dp": flip(self.my, 1)},
            device_id_type=MESH,
        )

    def begin(self):
        for half in range(2):
            self.copy(half, 0, 0, self.my).start()
        for half in range(2):
            self.hand(half, 0, self.my, True).start()
        pltpu.make_async_copy(self.src, self.out.at[self.my], self.local).start()

    def arrive(self, phase):
        for half in range(2):
            mask = self.orders[half][phase]
            for count in range(2**phase):
                block = flip(self.my, mask ^ self.span(half, count))
                self.copy(half, phase, count, block).wait_recv()
            if phase + 1 < self.phases:
                for count in range(2 ** (phase + 1)):
                    block = flip(self.my, self.span(half, count))
                    self.copy(half, phase + 1, count, block).start()
            for count in range(2**phase):
                block = flip(self.my, mask ^ self.span(half, count))
                self.hand(half, 2**phase + count, block).start()

    def finish(self):
        pltpu.make_async_copy(self.src, self.out.at[self.my], self.local).wait()
        other = flip(self.my, 1)
        for half in range(2):
            self.hand(half, 0, other, True).wait()
            for phase in range(self.phases):
                mask = self.orders[half][phase]
                for count in range(2**phase):
                    self.copy(half, phase, count, self.my).wait_send()
                    block = flip(other, mask ^ self.span(half, count))
                    self.hand(half, 2**phase + count, block).wait()


class LineGather:
    def __init__(self, n, src, out, send, recv, local, first=0, stop=None, land=None):
        self.n, self.src, self.out, self.land = n, src, out, land
        self.send, self.recv, self.local = send, recv, local
        self.first, self.stop = first, n - 1 if stop is None else stop
        self.me = lax.axis_index("seq")

    @staticmethod
    def scratch(n):
        return [
            pltpu.SemaphoreType.DMA((2, n - 1)),
            pltpu.SemaphoreType.DMA((2, n - 1)),
            pltpu.SemaphoreType.DMA,
        ]

    def inside(self, position):
        return both(position >= 0, position < self.n)

    def copy(self, way, hop, block, near):
        if hop > self.first:
            src = self.out.at[block]
        else:
            src = self.src if hop == 0 else self.src.at[way]
        return pltpu.make_async_remote_copy(
            src_ref=src,
            dst_ref=self.out.at[block] if self.land is None else self.land.at[way],
            send_sem=self.send.at[way, hop],
            recv_sem=self.recv.at[way, hop],
            device_id=on_line(near),
            device_id_type=MESH,
        )

    def each(self, hop):
        for way, sign in ((0, 1), (1, -1)):
            yield way, sign, self.me - sign * hop, self.me + sign

    def begin(self):
        self.launch(self.first)

    def launch(self, hop):
        for way, sign, block, near in self.each(hop):

            @pl.when(both(self.inside(block), self.inside(near)))
            def _():
                self.copy(way, hop, block, near).start()

    def keep(self):
        return pltpu.make_async_copy(self.src, self.out.at[self.me], self.local)

    def arrive(self, hop):
        for way, sign, block, near in self.each(hop + 1):

            @pl.when(self.inside(block))
            def _():
                self.copy(way, hop, block, near).wait_recv()

        if hop + 1 < self.stop:
            self.launch(hop + 1)

    def finish(self):
        for hop in range(self.first, self.stop):
            for way, sign, block, near in self.each(hop):

                @pl.when(both(self.inside(block), self.inside(near)))
                def _():
                    self.copy(way, hop, block, near).wait_send()


class LineSum:
    def __init__(self, n, part, out, got, mine, passed, send, recv, load, first=0, stop=None, tail=None, prev=None):
        self.n, self.part, self.out = n, part, out
        self.got, self.mine, self.passed = got, mine, passed
        self.send, self.recv, self.load = send, recv, load
        self.first, self.stop = first, n - 1 if stop is None else stop
        self.tail, self.prev = tail, prev
        self.me = lax.axis_index("seq")

    @staticmethod
    def scratch(n, rows, width, first=0, stop=None):
        stop = n - 1 if stop is None else stop
        return [
            pltpu.VMEM((2, stop - first + (first > 0), rows, width), HALF),
            pltpu.VMEM((2, rows, width), HALF),
            pltpu.VMEM((2, max(stop - max(first, 1), 1), rows, width), HALF),
            pltpu.SemaphoreType.DMA((2, n - 1)),
            pltpu.SemaphoreType.DMA((2, n - 1)),
            pltpu.SemaphoreType.DMA((2, 2)),
        ]

    def inside(self, position):
        return both(position >= 0, position < self.n)

    def each(self, step):
        reach = self.n - 1 - step
        for way, sign in ((0, 1), (1, -1)):
            yield way, self.me + sign * reach, self.me + sign, self.me - sign

    def slot(self, way, step):
        return self.passed.at[way, max(step - max(self.first, 1), 0)]

    def copy(self, way, step, src, near):
        if self.tail is not None and step == self.stop - 1:
            dst = self.tail.at[way]
        else:
            dst = self.got.at[way, step - self.first]
        return pltpu.make_async_remote_copy(
            src_ref=src,
            dst_ref=dst,
            send_sem=self.send.at[way, step],
            recv_sem=self.recv.at[way, step],
            device_id=on_line(near),
            device_id_type=MESH,
        )

    def round(self, step):
        for way, owner, near, behind in self.each(step):
            if step == 0:

                @pl.when(self.inside(owner))
                def _():
                    self.copy(way, step, self.part(owner), near).start()

                continue

            @pl.when(both(self.inside(owner), jnp.logical_not(self.inside(behind))))
            def _():
                self.copy(way, step, self.part(owner), near).start()

            @pl.when(both(self.inside(owner), self.inside(behind)))
            def _():
                fetch = pltpu.make_async_copy(
                    self.part(owner), self.mine.at[way], self.load.at[way, 0]
                )
                fetch.start()
                slot = self.slot(way, step)
                if step == self.first:
                    index = self.stop - self.first
                    held = pltpu.make_async_copy(
                        self.prev.at[way], self.got.at[way, index], self.load.at[way, 1]
                    )
                    held.start()
                    held.wait()
                else:
                    index = step - 1 - self.first
                    self.copy(way, step - 1, slot, near).wait_recv()
                fetch.wait()
                total = self.mine[way].astype(SINGLE) + self.got[way, index].astype(SINGLE)
                self.passed[way, step - max(self.first, 1)] = total.astype(HALF)
                self.copy(way, step, slot, near).start()

    def sent(self):
        for step in range(self.first, self.stop):
            for way, owner, near, behind in self.each(step):

                @pl.when(self.inside(owner))
                def _():
                    self.copy(way, step, self.slot(way, step), near).wait_send()

    def close(self):
        last = self.stop - 1
        for way, owner, near, behind in self.each(last + 1):

            @pl.when(both(self.inside(owner), self.inside(behind)))
            def _():
                self.copy(way, last, self.slot(way, last), near).wait_recv()

        self.sent()

    def finish(self):
        last = self.n - 2
        fetch = pltpu.make_async_copy(self.part(self.me), self.mine.at[0], self.load.at[0, 0])
        fetch.start()
        fetch.wait()
        self.out[...] = self.mine[0].astype(SINGLE)
        for way, owner, near, behind in self.each(last):

            @pl.when(self.inside(behind))
            def _():
                self.copy(way, last, self.slot(way, last), near).wait_recv()
                self.out[...] += self.got[way, last - self.first].astype(SINGLE)

        self.sent()


def at_rows(ref):
    return lambda owner: ref.at[owner]


def at_step(step, when, action):
    @pl.when(step == when)
    def _():
        action()


def to_group(my, dp, offset, src, dst, send, recv):
    peer = lax.rem(my + offset, dp)
    return pltpu.make_async_remote_copy(
        src_ref=src if src.shape == dst.shape[1:] else src.at[peer],
        dst_ref=dst.at[my],
        send_sem=send.at[offset - 1],
        recv_sem=recv.at[offset - 1],
        device_id={"dp": peer},
        device_id_type=MESH,
    )


def to_line(me, n, offset, src, dst, send, recv):
    peer = lax.rem(me + offset, n)
    return pltpu.make_async_remote_copy(
        src_ref=src if src.shape == dst.shape[1:] else src.at[peer],
        dst_ref=dst.at[me],
        send_sem=send.at[offset - 1],
        recv_sem=recv.at[offset - 1],
        device_id=on_line(peer),
        device_id_type=MESH,
    )


def start_kernel(
    n, dp, x_ref, act_ref, ada_ref, side_ref, qkv_ref, fc1_ref, x_all, side_all, acts, qkv_all, fc1_all,
    part, parts, row, a_send, a_recv, p_send, p_recv, s_send, s_recv, *sems,
):
    me, my = lax.axis_index("seq"), lax.axis_index("dp")
    depth, cols = ada_ref.shape
    greet(n, "all", "all")
    gather = LineGather(n, x_ref, x_all, *sems[:3])
    qkv = GroupGather(qkv_ref, qkv_all, *sems[3:8])
    fc1 = GroupGather(fc1_ref, fc1_all, *sems[8:13])
    gather.begin()
    others = range(1, dp)
    act_go = [to_group(my, dp, k, act_ref, acts, a_send, a_recv) for k in others]
    for copy in act_go:
        copy.start()
    gather.keep().start()
    acts[my] = act_ref[my]
    for copy in act_go:
        copy.wait_recv()
    product = nn_dot(acts[:, 0, :depth].astype(HALF), ada_ref[...])
    for k in range(dp):
        part[k] = product[k : k + 1]
    part_go = [to_group(my, dp, k, part, parts, p_send, p_recv) for k in others]
    for copy in part_go:
        copy.start()
    qkv.begin()
    fc1.begin()
    parts[my] = part[my]
    for copy in part_go:
        copy.wait_recv()
    row[...] = side_ref[...]
    row[:, :cols] += jnp.sum(parts[...], axis=0)
    row_go = [to_line(me, n, k, row, side_all, s_send, s_recv) for k in range(1, n)]
    for copy in row_go:
        copy.start()
    side_all[me] = row[...]
    for hop in range(max(n - 1, qkv.phases)):
        if hop < n - 1:
            gather.arrive(hop)
        if hop < qkv.phases:
            qkv.arrive(hop)
            fc1.arrive(hop)
    for copy in row_go:
        copy.wait()
    for copy in act_go + part_go:
        copy.wait_send()
    gather.keep().wait()
    gather.finish()
    qkv.finish()
    fc1.finish()


def start(n, dp, x_loc, act_parts, ada, side, qkv, fc1):
    rows, width = x_loc.shape
    cols = ada.shape[1]
    anywhere = pl.BlockSpec(memory_space=pl.ANY)
    inner = pl.BlockSpec(memory_space=pltpu.VMEM)
    return pl.pallas_call(
        functools.partial(start_kernel, n, dp),
        in_specs=[anywhere, inner, inner, inner, anywhere, anywhere],
        out_specs=[anywhere, inner, inner, anywhere, anywhere],
        out_shape=[
            jax.ShapeDtypeStruct((n, rows, width), HALF),
            jax.ShapeDtypeStruct((n,) + side.shape, SINGLE),
            jax.ShapeDtypeStruct(act_parts.shape, SINGLE),
            jax.ShapeDtypeStruct((dp,) + qkv.shape, HALF),
            jax.ShapeDtypeStruct((dp,) + fc1.shape, HALF),
        ],
        scratch_shapes=[
            pltpu.VMEM((dp, 1, cols), SINGLE),
            pltpu.VMEM((dp, 1, cols), SINGLE),
            pltpu.VMEM(side.shape, SINGLE),
            pltpu.SemaphoreType.DMA((dp - 1,)),
            pltpu.SemaphoreType.DMA((dp - 1,)),
            pltpu.SemaphoreType.DMA((dp - 1,)),
            pltpu.SemaphoreType.DMA((dp - 1,)),
            pltpu.SemaphoreType.DMA((n - 1,)),
            pltpu.SemaphoreType.DMA((n - 1,)),
        ]
        + LineGather.scratch(n)
        + GroupGather.scratch(dp)
        + GroupGather.scratch(dp),
        compiler_params=remote(1),
        cost_estimate=cost(10**6, 100 * MEGA),
        name="start",
    )(x_loc, act_parts, ada, side, qkv, fc1)


def qkv_kernel(n, img, x_ref, mod_ref, w_ref, b_ref, p_ref, a_ref, o_ref, p_line, *sems):
    step = pl.program_id(0)
    wide = o_ref.shape[2]
    gather = LineGather(n, p_ref, p_line, *sems)

    def begin():
        greet(n, "near")
        gather.begin()
        gather.keep().start()

    at_step(step, 0, begin)
    for t, sl in ((0, slice(0, img)), (1, slice(img, x_ref.shape[1]))):
        normed, _ = layer_norm(x_ref[0, sl].astype(SINGLE))
        a = (normed * (1.0 + mod_ref[t, 1:2]) + mod_ref[t, 0:1]).astype(HALF)
        a_ref[0, sl] = a
        o_ref[0, sl] = (
            nn_dot(a, w_ref[:, t * wide : (t + 1) * wide]) + b_ref[t : t + 1]
        ).astype(HALF)
    for hop in range(n - 1):
        at_step(step, min(n - 1, 2 * hop + 1), functools.partial(gather.arrive, hop))

    def finish():
        gather.keep().wait()
        gather.finish()

    at_step(step, n - 1, finish)


def project_qkv(n, img, x_all, mods, weight, bias, proj):
    _, rows, width = x_all.shape
    wide = weight.shape[1] // 2
    anywhere = pl.BlockSpec(memory_space=pl.ANY)
    return pl.pallas_call(
        functools.partial(qkv_kernel, n, img),
        grid=(n,),
        in_specs=[
            rows_spec(rows, width),
            whole(mods.shape),
            whole(weight.shape, True),
            whole(bias.shape),
            anywhere,
        ],
        out_specs=[rows_spec(rows, width), rows_spec(rows, wide), anywhere],
        out_shape=[
            jax.ShapeDtypeStruct((n, rows, width), HALF),
            jax.ShapeDtypeStruct((n, rows, wide), HALF),
            jax.ShapeDtypeStruct((n,) + proj.shape, HALF),
        ],
        scratch_shapes=LineGather.scratch(n),
        compiler_params=remote(8),
        cost_estimate=cost(2 * n * rows * width * wide, 30 * MEGA),
        name="project_qkv",
    )(x_all, mods, weight, bias, proj)


def halves(shape):
    lane = lax.broadcasted_iota(jnp.int32, shape, len(shape) - 1)
    return lane < HD


def attn_kernel(
    n, q_ref, k_ref, v_ref, mask_ref, e_ref, p_ref, o_ref, lse_ref, e_near, mix_ref, p_all,
    o_buf, o_send, o_recv, o_local, *sems,
):
    pair, block = pl.program_id(0), pl.program_id(1)
    pairs = pl.num_programs(0)
    step = pair * n + block
    me = lax.axis_index("seq")
    count, rows, _ = k_ref.shape
    gather = LineGather(n, e_ref, None, *sems[:3], first=0, stop=1, land=e_near)
    proj = GroupGather(p_ref, p_all, *sems[3:])

    def begin():
        greet(n, "all", "paths")
        gather.begin()
        proj.begin()

    at_step(step, 0, begin)
    queries = q_ref[0] * HALF(1.0 / math.sqrt(HD))
    keys = k_ref[...].reshape(n * rows, LANES)
    values = v_ref[...].reshape(n * rows, LANES)
    first = halves(queries.shape)
    outs, logs = [], []
    for head in range(2):
        own = first if head == 0 else jnp.logical_not(first)
        scores = nt_dot(jnp.where(own, queries, HALF(0)), keys) + mask_ref[...]
        maxima = jnp.max(scores, axis=-1, keepdims=True)
        raised = jnp.exp(scores - maxima)
        totals = jnp.sum(raised, axis=-1, keepdims=True)
        weights = (raised * (1.0 / totals)).astype(HALF)
        outs.append(nn_dot(weights, values))
        logs.append(maxima + jnp.log(totals))
    mixed = jnp.where(first, outs[0], outs[1]).astype(HALF)
    o_ref[0] = mixed
    o_buf[pair, block] = mixed
    lse_ref[0] = jnp.where(first, logs[0], logs[1])
    static_pairs = o_buf.shape[0]

    def columns(sender, which):
        start = (sender * static_pairs + which) * LANES
        return mix_ref.at[:, pl.ds(pl.multiple_of(start, LANES), LANES)]

    def away(which, offset):
        peer = lax.rem(me + offset, n)
        return pltpu.make_async_remote_copy(
            src_ref=o_buf.at[which, peer],
            dst_ref=columns(me, which),
            send_sem=o_send.at[which, offset - 1],
            recv_sem=o_recv.at[which, offset - 1],
            device_id=on_line(peer),
            device_id_type=MESH,
        )

    for offset in range(1, n):

        @pl.when(block == lax.rem(me + offset, n))
        def _():
            away(pair, offset).start()

    @pl.when(block == me)
    def _():
        pltpu.make_async_copy(o_buf.at[pair, me], columns(me, pair), o_local.at[pair]).start()

    last = static_pairs * n - 1
    for phase in range(proj.phases):
        at_step(step, min(last, 5 * phase + 5), functools.partial(proj.arrive, phase))

    def finish():
        gather.arrive(0)
        proj.finish()
        for which in range(static_pairs):
            pltpu.make_async_copy(o_buf.at[which, me], columns(me, which), o_local.at[which]).wait()
            for offset in range(1, n):
                away(which, offset).wait()
        gather.finish()

    at_step(step, last, finish)


def attend(n, dp, qkv, mask, e_loc, proj):
    _, rows, wide = qkv.shape
    width = e_loc.shape[1]
    pairs = wide // 3 // LANES
    total = n * rows
    block = pl.BlockSpec((1, rows, LANES), lambda h, s: (s, 0, h))
    anywhere = pl.BlockSpec(memory_space=pl.ANY)
    return pl.pallas_call(
        functools.partial(attn_kernel, n),
        grid=(pairs, n),
        in_specs=[
            block,
            pl.BlockSpec((n, rows, LANES), lambda h, s: (0, 0, pairs + h)),
            pl.BlockSpec((n, rows, LANES), lambda h, s: (0, 0, 2 * pairs + h)),
            whole(mask.shape),
            anywhere,
            anywhere,
        ],
        out_specs=[block, block, anywhere, anywhere, anywhere],
        out_shape=[
            jax.ShapeDtypeStruct((n, rows, pairs * LANES), HALF),
            jax.ShapeDtypeStruct((n, rows, pairs * LANES), SINGLE),
            jax.ShapeDtypeStruct((2, rows, width), HALF),
            jax.ShapeDtypeStruct((rows, n * pairs * LANES), HALF),
            jax.ShapeDtypeStruct((dp,) + proj.shape, HALF),
        ],
        scratch_shapes=[
            pltpu.VMEM((pairs, n, rows, LANES), HALF),
            pltpu.SemaphoreType.DMA((pairs, n - 1)),
            pltpu.SemaphoreType.DMA((pairs, n - 1)),
            pltpu.SemaphoreType.DMA((pairs,)),
        ]
        + LineGather.scratch(n)
        + GroupGather.scratch(dp),
        compiler_params=remote(2),
        cost_estimate=cost(2 * 2 * 4 * pairs * total * total * LANES, 20 * MEGA, 2 * pairs * total * total),
        name="attend",
    )(qkv, qkv, qkv, mask, e_loc, proj)


def attn_back_kernel(
    lines, img, pairs, q_ref, k_ref, v_ref, o_ref, g_ref, lse_ref, mask_ref, y_ref, l_ref, r_ref,
    dq_ref, dk_ref, dv_ref, qb_ref, vb_ref, sum_ref, p_ref,
    acc_ref, lse_row, delta_row, turned, *line_scratch,
):
    linear = pl.program_id(0)
    attn_steps = pairs * lines
    step = lax.rem(linear, lines)
    n, rows, _ = q_ref.shape
    total = n * rows
    line = LineSum(lines, at_rows(y_ref), sum_ref, *line_scratch)

    def begin():
        greet(lines, "near")
        line.round(0)

    at_step(linear, 0, begin)

    @pl.when(linear < attn_steps)
    def _():
        grads = g_ref[...].reshape(total, LANES)
        queries = q_ref[...].reshape(total, LANES) * HALF(1.0 / math.sqrt(HD))

        @pl.when(step == 0)
        def _():
            acc_ref[...] = jnp.zeros_like(acc_ref)
            product = grads.astype(SINGLE) * o_ref[...].reshape(total, LANES).astype(SINGLE)
            flipped = product.T
            logs = lse_ref[...].reshape(total, LANES).T
            for head in range(2):
                delta_row[head : head + 1] = jnp.sum(
                    flipped[head * HD : (head + 1) * HD], axis=0, keepdims=True
                )
                lse_row[head : head + 1] = logs[head * HD : head * HD + 1]
            vb_ref[0] = jnp.zeros_like(vb_ref[0])

        keys, values = k_ref[0], v_ref[0]
        first = halves(keys.shape)
        mask = mask_ref[0][:, 0:1]
        dks, dvs = [], []
        for head in range(2):
            own = first if head == 0 else jnp.logical_not(first)
            key_own = jnp.where(own, keys, HALF(0))
            scores = nt_dot(key_own, queries)
            probs = jnp.exp((scores - lse_row[head : head + 1]) + mask)
            grad_prob = nt_dot(jnp.where(own, values, HALF(0)), grads)
            grad_score = (probs * (grad_prob - delta_row[head : head + 1])).astype(HALF)
            dvs.append(nn_dot(probs.astype(HALF), grads))
            dks.append(nn_dot(grad_score, queries))
            acc_ref[...] += tn_dot(grad_score, key_own)
        dk_ref[0] = jnp.where(first, dks[0], dks[1]).astype(HALF)
        dv = jnp.where(first, dvs[0], dvs[1])
        dv_ref[0] = dv.astype(HALF)
        vb_ref[0, 0:1] += jnp.sum(dv[:img], axis=0, keepdims=True)
        vb_ref[0, 1:2] += jnp.sum(dv[img:], axis=0, keepdims=True)

        @pl.when(step == lines - 1)
        def _():
            dq = (acc_ref[...] * (1.0 / math.sqrt(HD))).reshape(n, rows, LANES)
            dq_ref[...] = dq.astype(HALF)
            qb_ref[0, 0:1] = jnp.sum(jnp.sum(dq[:, :img], axis=0), axis=0, keepdims=True)
            qb_ref[0, 1:2] = jnp.sum(jnp.sum(dq[:, img:], axis=0), axis=0, keepdims=True)

    for t, sl in ((0, slice(0, img)), (1, slice(img, rows))):

        @pl.when(linear == attn_steps)
        def _():
            turned[:, sl] = l_ref[sl].T

        @pl.when(both(linear >= attn_steps, lax.rem(linear - attn_steps, 2) == t))
        def _():
            p_ref[...] = nn_dot(turned[:, sl], r_ref[sl]).astype(HALF)

    for hop in range(1, lines - 1):
        at_step(linear, 6 * hop, functools.partial(line.round, hop))
    at_step(linear, attn_steps + 2 * lines - 1, line.finish)


def attend_back(n, img, qkv, mixture, grad_mix, lse, mask_col, out_parts, grad_attn, mix_loc):
    _, rows, wide = qkv.shape
    pairs = wide // 3 // LANES
    total = n * rows
    lw = pairs * LANES
    steps = pairs * n
    width = out_parts.shape[2]

    def head(k):
        return lax.min(lax.div(k, n), pairs - 1)

    def place(k):
        return lax.select(k < steps, lax.rem(k, n), n - 1)

    def later(k):
        return lax.max(k - steps, 0)

    full = pl.BlockSpec((n, rows, LANES), lambda k: (0, 0, head(k)))

    def block(base):
        return pl.BlockSpec((1, rows, LANES), lambda k: (place(k), 0, base + head(k)))

    bias = pl.BlockSpec((1, 2, LANES), lambda k: (head(k), 0, 0))
    anywhere = pl.BlockSpec(memory_space=pl.ANY)
    return pl.pallas_call(
        functools.partial(attn_back_kernel, n, img, pairs),
        grid=(steps + 2 * n,),
        in_specs=[
            full,
            block(pairs),
            block(2 * pairs),
            full,
            full,
            full,
            pl.BlockSpec((1, rows, LANES), lambda k: (place(k), 0, 0)),
            anywhere,
            whole(grad_attn.shape, True),
            pl.BlockSpec((rows, lw), lambda k: (0, lax.div(later(k), 2))),
        ],
        out_specs=[
            full,
            block(0),
            block(0),
            bias,
            bias,
            whole(out_parts.shape[1:], True),
            pl.BlockSpec((width, lw), lambda k: (0, later(k))),
        ],
        out_shape=[jax.ShapeDtypeStruct((n, rows, lw), HALF)] * 3
        + [jax.ShapeDtypeStruct((pairs, 2, LANES), SINGLE)] * 2
        + [
            jax.ShapeDtypeStruct(out_parts.shape[1:], SINGLE),
            jax.ShapeDtypeStruct((width, 2 * n * lw), HALF),
        ],
        scratch_shapes=[
            pltpu.VMEM((total, LANES), SINGLE),
            pltpu.VMEM((2, total), SINGLE),
            pltpu.VMEM((2, total), SINGLE),
            pltpu.VMEM((width, rows), HALF),
        ]
        + LineSum.scratch(n, rows, width),
        compiler_params=remote(3, 60),
        cost_estimate=cost(2 * 5 * 4 * pairs * total * total * LANES, 30 * MEGA, 2 * pairs * total * total),
        name="attend_back",
    )(qkv, qkv, qkv, mixture, grad_mix, lse, mask_col, out_parts, grad_attn, mix_loc)


def proj_columns(w_ref, z, t):
    dp, n, depth, cols = w_ref.shape
    half = cols // 2
    return w_ref[:, z, :, t * half : (t + 1) * half].reshape(dp * depth, half)


def middle_kernel(
    n, img, mix_ref, x_ref, w_ref, b_ref, mod_ref, fc2_ref, y_ref, m_ref, all_ref, fc2_all, own, *sems
):
    greet(n, "near", "paths")
    fc2 = GroupGather(fc2_ref, fc2_all, *sems[3:])
    fc2.begin()
    lw = mix_ref.shape[1] // n
    heads = w_ref.shape[3] // 2
    for t, sl in ((0, slice(0, img)), (1, slice(img, x_ref.shape[0]))):
        attn = b_ref[t : t + 1]
        for z in range(n):
            attn = attn + nt_dot(mix_ref[sl, z * lw : z * lw + heads], proj_columns(w_ref, z, t))
        y_ref[sl] = attn
        middle = x_ref[sl].astype(SINGLE) + mod_ref[t, 2:3] * attn
        m_ref[sl] = middle
        normed, _ = layer_norm(middle)
        own[sl] = (normed * (1.0 + mod_ref[t, 4:5]) + mod_ref[t, 3:4]).astype(HALF)
    gather = LineGather(n, own, all_ref, *sems[:3])
    gather.begin()
    gather.keep().start()
    for hop in range(max(n - 1, fc2.phases)):
        if hop < fc2.phases:
            fc2.arrive(hop)
        if hop < n - 1:
            gather.arrive(hop)
    gather.keep().wait()
    gather.finish()
    fc2.finish()


def middle_rows(n, dp, img, mixture, x_loc, weight, bias, mods, fc2):
    rows, width = x_loc.shape
    inner = pl.BlockSpec(memory_space=pltpu.VMEM)
    anywhere = pl.BlockSpec(memory_space=pl.ANY)
    return pl.pallas_call(
        functools.partial(middle_kernel, n, img),
        in_specs=[inner] * 5 + [anywhere],
        out_specs=[inner, inner, anywhere, anywhere],
        out_shape=[
            jax.ShapeDtypeStruct((rows, width), SINGLE),
            jax.ShapeDtypeStruct((rows, width), SINGLE),
            jax.ShapeDtypeStruct((n, rows, width), HALF),
            jax.ShapeDtypeStruct((dp,) + fc2.shape, HALF),
        ],
        scratch_shapes=[pltpu.VMEM((rows, width), HALF)]
        + LineGather.scratch(n)
        + GroupGather.scratch(dp),
        compiler_params=remote(4),
        cost_estimate=cost(2 * rows * width * width, 100 * MEGA),
        name="middle_rows",
    )(mixture, x_loc, weight, bias, mods, fc2)


def by_distance(me, n, count):
    low = lax.min(me, n - 1 - me)
    near = lax.select(lax.rem(count, 2) == 1, lax.div(count + 1, 2), -lax.div(count, 2))
    far = lax.select(me < n - 1 - me, count - low, low - count)
    return me + lax.select(count <= 2 * low, near, far)


def mlp_kernel(n, img, tile, b_ref, e_loc, e_near, mod_ref, w1_ref, b1_ref, w2_ref,
    g_ref, dz_ref, dy_ref, db_ref, y_ref, sum_ref, gate_ref, acc_ref, out_ref, e_all, near_sem, *sems):
    step = pl.program_id(0)
    me = lax.axis_index("seq")
    owner = by_distance(me, n, step)
    e_ref = e_all.at[pl.ds(owner, 1)]
    gather = LineGather(n, e_near, e_all, *sems, first=1)
    own = pltpu.make_async_copy(e_loc, e_all.at[me], near_sem.at[2])

    def nears(action):
        for way, sign in ((0, 1), (1, -1)):
            block = me - sign

            @pl.when(both(block >= 0, block < n))
            def _():
                action(
                    pltpu.make_async_copy(e_near.at[way], e_all.at[block], near_sem.at[way])
                )

    def begin():
        greet(n, "near")
        gather.begin()
        own.start()
        nears(lambda copy: copy.start())
        own.wait()
        nears(lambda copy: copy.wait())

    at_step(step, 0, begin)
    for hop in range(1, n - 1):
        at_step(step, hop + 1, functools.partial(gather.arrive, hop))
    at_step(step, n - 1, gather.finish)
    units = g_ref.shape[2]

    @pl.when(step == 0)
    def _():
        sum_ref[...] = jnp.zeros_like(sum_ref)
        gate_ref[...] = jnp.zeros_like(gate_ref)

    for t, sl in ((0, slice(0, img)), (1, slice(img, b_ref.shape[1]))):
        rows = b_ref[0, sl]
        grad = (mod_ref[t, 5:6] * e_ref[0, sl].astype(SINGLE)).astype(HALF)
        dy_ref[0, sl] = grad

        for k in range(units // tile):
            here = slice(k * tile, (k + 1) * tile)
            cols = slice(t * units + k * tile, t * units + (k + 1) * tile)
            w1 = w1_ref[:, cols]
            pre = nn_dot(rows, w1) + b1_ref[t : t + 1, here]
            hidden, slope = gelu_both(pre)
            hidden = hidden.astype(HALF)
            g_ref[0, sl, here] = hidden
            w2 = w2_ref[:, cols]
            out = nt_dot(hidden, w2)
            dz = nn_dot(grad, w2) * slope
            sum_ref[t : t + 1, here] += jnp.sum(dz, axis=0, keepdims=True)
            dzh = dz.astype(HALF)
            dz_ref[0, sl, here] = dzh
            part = nt_dot(dzh, w1)
            if k == 0:
                acc_ref[sl] = part
                out_ref[sl] = out
            else:
                acc_ref[sl] += part
                out_ref[sl] += out
        db_ref[0, sl] = acc_ref[sl].astype(HALF)
        out = out_ref[sl]
        y_ref[0, sl] = out.astype(HALF)
        gate_ref[t : t + 1] += jnp.sum(out * e_ref[0, sl].astype(SINGLE), axis=0, keepdims=True)


def feed_forward(n, img, mlp_in, e_loc, e_near, mods, w1, b1, w2):
    rows, width = mlp_in.shape[1:]
    units = w1.shape[1] // 2
    tile = min(512, units)
    while units % tile:
        tile -= LANES

    def owned(columns):
        return pl.BlockSpec(
            (1, rows, columns), lambda k: (by_distance(lax.axis_index("seq"), n, k), 0, 0)
        )

    return pl.pallas_call(
        functools.partial(mlp_kernel, n, img, tile),
        grid=(n,),
        in_specs=[
            owned(width),
            pl.BlockSpec(memory_space=pl.ANY),
            pl.BlockSpec(memory_space=pl.ANY),
            whole(mods.shape),
            whole(w1.shape, True),
            whole(b1.shape),
            whole(w2.shape, True),
        ],
        out_specs=[
            owned(units),
            owned(units),
            owned(width),
            owned(width),
            owned(width),
            whole((2, units)),
            whole((2, width)),
        ],
        out_shape=[
            jax.ShapeDtypeStruct((n, rows, units), HALF),
            jax.ShapeDtypeStruct((n, rows, units), HALF),
            jax.ShapeDtypeStruct((n, rows, width), HALF),
            jax.ShapeDtypeStruct((n, rows, width), HALF),
            jax.ShapeDtypeStruct((n, rows, width), HALF),
            jax.ShapeDtypeStruct((2, units), SINGLE),
            jax.ShapeDtypeStruct((2, width), SINGLE),
        ],
        scratch_shapes=[
            pltpu.VMEM((rows, width), SINGLE),
            pltpu.VMEM((rows, width), SINGLE),
            pltpu.VMEM((n, rows, width), HALF),
            pltpu.SemaphoreType.DMA((3,)),
        ]
        + LineGather.scratch(n),
        compiler_params=remote(9, 60),
        cost_estimate=cost(6 * n * rows * width * units, 50 * MEGA, n * rows * units),
        name="feed_forward",
    )(mlp_in, e_loc, e_near, mods, w1, b1, w2)


def grads_kernel(n, img, plan, rounds, *refs):
    lefts = max(p[0] for p in plan) + 1
    rights = max(p[1] for p in plan) + 1
    l_refs, r_refs = refs[:lefts], refs[lefts : lefts + rights]
    rest = refs[lefts + rights :]
    step = pl.program_id(0)
    if rounds:
        parts, o_ref, tail, turned = rest[:4]
        line = LineSum(n, at_rows(parts), None, *rest[4:], stop=n - 2, tail=tail)

        def begin():
            greet(n, "near")
            line.round(0)

        at_step(step, 0, begin)
    else:
        o_ref, turned = rest
    tile = o_ref.shape[1]
    before = None
    for k, (left, right, stream, column) in enumerate(plan):

        @pl.when(step == k)
        def _():
            l_ref, r_ref = l_refs[left], r_refs[right]
            count, rows, _ = l_ref.shape
            sl = slice(0, img) if stream == 0 else slice(img, rows)
            size = count * (sl.stop - sl.start)
            if before != (left, stream):
                turned[:, :size] = l_ref[:, sl].reshape(size, l_ref.shape[2]).T
            values = r_ref[:, sl, column : column + tile].reshape(size, tile)
            o_ref[...] = nn_dot(turned[:, :size], values).astype(HALF)

        before = (left, stream)
    if rounds:
        for hop, when in enumerate(rounds):
            at_step(step, when, functools.partial(line.round, hop + 1))
        at_step(step, len(plan) - 1, line.close)


def weight_grads(n, img, lefts, rights, plan, tile, name, rounds=(), parts=None, collective=None):
    rows, depth = lefts[0].shape[1:]
    in_specs = [whole(a.shape, True) for a in (*lefts, *rights)]
    out_specs = [pl.BlockSpec((depth, tile), lambda k: (0, k))]
    out_shape = [jax.ShapeDtypeStruct((depth, len(plan) * tile), HALF)]
    longest = max(up(n * img, LANES), up(n * (rows - img), LANES))
    scratch = [pltpu.VMEM((depth, longest), HALF)]
    arrays = (*lefts, *rights)
    if rounds:
        anywhere = pl.BlockSpec(memory_space=pl.ANY)
        in_specs.append(anywhere)
        out_specs.append(anywhere)
        out_shape.append(jax.ShapeDtypeStruct((2,) + parts.shape[1:], HALF))
        scratch += LineSum.scratch(n, *parts.shape[1:], stop=n - 2)
        arrays += (parts,)
    return pl.pallas_call(
        functools.partial(grads_kernel, n, img, plan, rounds),
        grid=(len(plan),),
        in_specs=in_specs,
        out_specs=out_specs,
        out_shape=out_shape,
        scratch_shapes=scratch,
        compiler_params=remote(collective, 60) if rounds else params(60),
        cost_estimate=cost(2 * n * rows * depth * len(plan) * tile // 2, 60 * MEGA),
        name=name,
    )(*arrays)


def middle_back_kernel(
    n, img, part_ref, prev_ref, m_ref, y_ref, e_ref, w_ref, mod_ref, dm_ref, dy_ref, sum_ref, all_ref,
    db_ref, mix, send, recv, local, *line_scratch,
):
    me = lax.axis_index("seq")
    rows, width = m_ref.shape
    heads = w_ref.shape[3] // 2
    streams = ((0, slice(0, img)), (1, slice(img, rows)))
    greet(n, "all")
    line = LineSum(n, at_rows(part_ref), db_ref, *line_scratch, first=n - 2, prev=prev_ref)
    line.round(n - 2)
    if mix.shape[2] > heads:
        mix[...] = jnp.zeros_like(mix)
    line.finish()
    for t, sl in streams:
        grad_in = db_ref[sl]
        normed, inv_std = layer_norm(m_ref[sl])
        upstream = e_ref[sl].astype(SINGLE)
        grad_middle = upstream + norm_back(normed, inv_std, grad_in * (1.0 + mod_ref[t, 4:5]))
        dm_ref[sl] = grad_middle
        grad_attn = mod_ref[t, 2:3] * grad_middle
        dy_ref[sl] = grad_attn.astype(HALF)

        def total(value):
            return jnp.sum(value, axis=0, keepdims=True)

        sum_ref[t, 0:1] = total(grad_middle * y_ref[sl])
        sum_ref[t, 1:2] = total(grad_in)
        sum_ref[t, 2:3] = total(grad_in * normed)
        sum_ref[t, 3:4] = total(grad_attn)
        sum_ref[t, 4:5] = total(upstream)

    def exchange(peer, block):
        return pltpu.make_async_remote_copy(
            src_ref=mix.at[peer],
            dst_ref=all_ref.at[block],
            send_sem=send.at[peer],
            recv_sem=recv.at[block],
            device_id=on_line(peer),
            device_id_type=MESH,
        )

    keep = pltpu.make_async_copy(mix.at[me], all_ref.at[me], local)
    for peer in range(n):
        for t, sl in streams:
            mix[peer, sl, :heads] = nn_dot(dy_ref[sl], proj_columns(w_ref, peer, t)).astype(HALF)

        @pl.when(peer != me)
        def _():
            exchange(peer, me).start()

        @pl.when(peer == me)
        def _():
            keep.start()

    for peer in range(n):

        @pl.when(peer != me)
        def _():
            exchange(peer, peer).wait()

    keep.wait()


def middle_back(n, img, parts, prev, middle, attn_out, cot, weight, mods, lwp):
    rows, width = middle.shape
    inner = pl.BlockSpec(memory_space=pltpu.VMEM)
    anywhere = pl.BlockSpec(memory_space=pl.ANY)
    return pl.pallas_call(
        functools.partial(middle_back_kernel, n, img),
        in_specs=[anywhere, anywhere] + [inner] * 5,
        out_specs=[inner, inner, inner, anywhere],
        out_shape=[
            jax.ShapeDtypeStruct((rows, width), SINGLE),
            jax.ShapeDtypeStruct((rows, width), HALF),
            jax.ShapeDtypeStruct((2, 8, width), SINGLE),
            jax.ShapeDtypeStruct((n, rows, lwp), HALF),
        ],
        scratch_shapes=[
            pltpu.VMEM((rows, width), SINGLE),
            pltpu.VMEM((n, rows, lwp), HALF),
            pltpu.SemaphoreType.DMA((n,)),
            pltpu.SemaphoreType.DMA((n,)),
            pltpu.SemaphoreType.DMA,
        ]
        + LineSum.scratch(n, rows, width, first=n - 2),
        compiler_params=remote(5),
        cost_estimate=cost(2 * rows * width * width, 60 * MEGA),
        name="middle_back",
    )(parts, prev, middle, attn_out, cot, weight, mods)


def attn_in_kernel(img, dq_ref, dk_ref, dv_ref, x_ref, w_ref, da_ref, sum_ref):
    lw = dq_ref.shape[2]

    @pl.when(pl.program_id(0) == 0)
    def _():
        sum_ref[...] = jnp.zeros_like(sum_ref)

    for t, sl in ((0, slice(0, img)), (1, slice(img, x_ref.shape[1]))):
        part = None
        for c, ref in enumerate((dq_ref, dk_ref, dv_ref)):
            start = (3 * t + c) * lw
            term = nt_dot(ref[0, sl], w_ref[:, start : start + lw])
            part = term if part is None else part + term
        da_ref[0, sl] = part.astype(HALF)
        normed, _ = layer_norm(x_ref[0, sl].astype(SINGLE))
        sum_ref[t, 0:1] += jnp.sum(part, axis=0, keepdims=True)
        sum_ref[t, 1:2] += jnp.sum(part * normed, axis=0, keepdims=True)


def attn_in_back(n, img, dq, dk, dv, x_all, weight):
    _, rows, lw = dq.shape
    width = x_all.shape[2]
    return pl.pallas_call(
        functools.partial(attn_in_kernel, img),
        grid=(n,),
        in_specs=[rows_spec(rows, lw)] * 3 + [rows_spec(rows, width), whole(weight.shape, True)],
        out_specs=[rows_spec(rows, width), whole((2, 2, width))],
        out_shape=[
            jax.ShapeDtypeStruct((n, rows, width), HALF),
            jax.ShapeDtypeStruct((2, 2, width), SINGLE),
        ],
        compiler_params=params(),
        cost_estimate=cost(6 * n * rows * width * lw, 30 * MEGA),
        name="attn_in_back",
    )(dq, dk, dv, x_all, weight)


def end_kernel(
    n, dp, cut, parts, packed, extra, ada_ref, sum_ref, every, cond_ref,
    z_got, row, c_part, c_got, c_all, z_send, z_recv, e_send, e_recv, c_send, c_recv, a_send, a_recv,
    *line_scratch,
):
    me, my = lax.axis_index("seq"), lax.axis_index("dp")
    depth = ada_ref.shape[0]
    span = packed.shape[2]
    greet(n, "all", "all")
    line = LineSum(n, at_rows(parts), sum_ref, *line_scratch)
    line.round(0)
    mates, others = range(1, n), range(1, dp)
    z_go = [to_line(me, n, k, packed, z_got, z_send, z_recv) for k in mates]
    for copy in z_go:
        copy.start()
    z_got[me] = packed[me]
    for copy in z_go:
        copy.wait_recv()
    row[:, :span] = jnp.sum(z_got[...], axis=0)
    row[:, span:] = extra[...]
    e_go = [to_group(my, dp, k, row, every, e_send, e_recv) for k in others]
    for copy in e_go:
        copy.start()
    every[my] = row[...]
    for copy in e_go:
        copy.wait_recv()
    product = nt_dot(every[:, 0, :cut].astype(HALF), ada_ref[...])
    c_part[...] = jnp.zeros_like(c_part)
    for k in range(dp):
        c_part[k, :, :depth] = product[k : k + 1]
    c_go = [to_group(my, dp, k, c_part, c_got, c_send, c_recv) for k in others]
    for copy in c_go:
        copy.start()
    c_got[my] = c_part[my]
    for copy in c_go:
        copy.wait_recv()
    a_go = [to_line(me, n, k, c_got, c_all, a_send, a_recv) for k in mates]
    for copy in a_go:
        copy.start()
    c_all[me] = c_got[...]
    for hop in range(1, n - 1):
        line.round(hop)
    for copy in a_go:
        copy.wait_recv()
    cond_ref[...] = jnp.sum(c_all[...], axis=0)
    for copy in z_go + e_go + c_go + a_go:
        copy.wait_send()
    line.finish()


def end(n, dp, cut, parts, packed, extra, ada):
    rows, width = parts.shape[1:]
    depth = up(ada.shape[0], LANES)
    span = packed.shape[2] + extra.shape[1]
    inner = pl.BlockSpec(memory_space=pltpu.VMEM)
    sems = [n - 1, n - 1, dp - 1, dp - 1, dp - 1, dp - 1, n - 1, n - 1]
    return pl.pallas_call(
        functools.partial(end_kernel, n, dp, cut),
        in_specs=[pl.BlockSpec(memory_space=pl.ANY), inner, inner, inner],
        out_specs=[inner] * 3,
        out_shape=[
            jax.ShapeDtypeStruct((rows, width), SINGLE),
            jax.ShapeDtypeStruct((dp, 1, span), SINGLE),
            jax.ShapeDtypeStruct((dp, 1, depth), SINGLE),
        ],
        scratch_shapes=[
            pltpu.VMEM(packed.shape, SINGLE),
            pltpu.VMEM((1, span), SINGLE),
            pltpu.VMEM((dp, 1, depth), SINGLE),
            pltpu.VMEM((dp, 1, depth), SINGLE),
            pltpu.VMEM((n, dp, 1, depth), SINGLE),
        ]
        + [pltpu.SemaphoreType.DMA((k,)) for k in sems]
        + LineSum.scratch(n, rows, width),
        compiler_params=remote(7),
        cost_estimate=cost(10**6, 100 * MEGA),
        name="end",
    )(parts, packed, extra, ada)


def proj_sum_kernel(n, wide, parts, sum_ref, *line_scratch):
    greet(n, "near")

    def part(owner):
        return parts.at[:, pl.ds(pl.multiple_of(owner * wide, LANES), wide)]

    line = LineSum(n, part, sum_ref, *line_scratch)
    for hop in range(n - 1):
        line.round(hop)
    line.finish()


def sum_proj(n, parts):
    depth, wide = parts.shape[0], parts.shape[1] // n
    return pl.pallas_call(
        functools.partial(proj_sum_kernel, n, wide),
        in_specs=[pl.BlockSpec(memory_space=pl.ANY)],
        out_specs=pl.BlockSpec(memory_space=pltpu.VMEM),
        out_shape=jax.ShapeDtypeStruct((depth, wide), SINGLE),
        scratch_shapes=LineSum.scratch(n, depth, wide),
        compiler_params=remote(10, 32),
        cost_estimate=cost(10**6, 20 * MEGA),
        name="sum_proj",
    )(parts)


def body(
    image_tokens,
    text_tokens,
    text_lengths,
    conditioning,
    ada_weight,
    ada_bias,
    qkv_weight,
    qv_bias,
    proj_weight,
    proj_bias,
    fc1_weight,
    fc1_bias,
    fc2_weight,
    fc2_bias,
    image_cotangent,
    text_cotangent,
):
    n = lax.axis_size("seq")
    dp = lax.axis_size("dp")
    img, width = image_tokens.shape[1:]
    slots = text_tokens.shape[1]
    pad = up(slots, 16)
    rows = img + pad
    depth = qkv_weight.shape[0]
    lw = qkv_weight.shape[3]
    lwp = up(lw, LANES)
    units = fc1_weight.shape[2]
    mod_cols = ada_weight.shape[2]
    my_seq = lax.axis_index("dp")

    def stacked(image, text):
        return jnp.concatenate([image, jnp.pad(text, ((0, pad - slots), (0, 0)))], axis=0)

    length = text_lengths[0, 0]
    live_text = (jnp.arange(slots, dtype=jnp.int32) < length)[:, None]
    x_loc = stacked(image_tokens[0], text_tokens[0])
    e_loc = stacked(
        image_cotangent[0], jnp.where(live_text, text_cotangent[0], jnp.zeros((), HALF))
    )

    def split(shard):
        return shard.reshape(2, -1, shard.shape[-1])

    qkv_local = jnp.pad(qkv_weight, ((0, 0), (0, 0), (0, 0), (0, lwp - lw))).reshape(depth, 6 * lwp)
    share = proj_weight.shape[0]
    proj_turned = proj_weight.transpose(2, 1, 0).reshape(depth, 2 * share)
    fc1_local = fc1_weight.reshape(depth, 2 * units)
    fc2_turned = fc2_weight.transpose(2, 1, 0).reshape(depth, 2 * units)

    cond_float = conditioning.astype(SINGLE)
    cond_act = jax.nn.silu(cond_float).astype(HALF)
    act_parts = jnp.pad(
        cond_act.astype(SINGLE).reshape(dp, 1, depth), ((0, 0), (0, 0), (0, up(depth, LANES) - depth))
    )
    ada_flat = ada_weight.reshape(depth, 2 * mod_cols)
    bias_cols = proj_bias.shape[1]
    cut = 2 * mod_cols
    side = jnp.concatenate(
        [
            ada_bias.astype(SINGLE).reshape(-1),
            proj_bias.astype(SINGLE).reshape(-1),
            fc2_bias.astype(SINGLE).reshape(-1),
            jnp.full((LANES,), length.astype(SINGLE)),
        ]
    )[None]
    x_all, side_all, acts, qkv_full, fc1_full = start(
        n, dp, x_loc, act_parts, ada_flat, side, split(qkv_local), split(fc1_local)
    )
    qkv_full = qkv_full.reshape(width, 6 * lwp)
    fc1_full = fc1_full.reshape(width, 2 * units)
    act_slice = acts[:, 0, :depth].astype(HALF)
    side_all = side_all[:, 0]

    def columns(begin, cols):
        return side_all[:, begin : begin + 2 * cols].reshape(n, 2, cols).transpose(1, 0, 2)

    mods = jnp.pad(columns(0, mod_cols).reshape(2, 6, width), ((0, 0), (0, 2), (0, 0)))
    proj_shift = columns(cut, bias_cols).reshape(2, width)
    fc2_shift = columns(cut + 2 * bias_cols, bias_cols).reshape(2, width)
    lengths_all = side_all[:, cut + 4 * bias_cols]

    slot = jnp.arange(rows, dtype=SINGLE)[None, :] - img
    live = jnp.logical_or(slot < 0, jnp.logical_and(slot < lengths_all[:, None], slot < slots))
    mask = jnp.where(live, SINGLE(0), SINGLE(MASKED))
    mask_row = mask.reshape(1, n * rows)
    mask_col = jnp.broadcast_to(mask[:, :, None], (n, rows, LANES))
    live_loc = jnp.concatenate(
        [jnp.ones((img, 1), SINGLE), jnp.pad(live_text.astype(SINGLE), ((0, pad - slots), (0, 0)))]
    )

    bias_rows = jnp.stack(
        [qv_bias[:, 0], jnp.zeros_like(qv_bias[:, 0]), qv_bias[:, 1]], axis=1
    ).astype(SINGLE)
    bias_rows = jnp.pad(bias_rows, ((0, 0), (0, 0), (0, lwp - lw))).reshape(2, 3 * lwp)
    attn_in, qkv_rows, proj_line = project_qkv(
        n, img, x_all, mods, qkv_full, bias_rows, proj_turned
    )
    mixture, lse, e_near, mix_loc, proj_full = attend(
        n, dp, qkv_rows, mask_row, e_loc, split(proj_line)
    )
    proj_full = proj_full.reshape(dp, n, depth, 2 * share)

    attn_out, middle, mlp_in, fc2_full = middle_rows(
        n, dp, img, mix_loc, x_loc, proj_full, proj_shift, mods, split(fc2_turned)
    )
    fc2_full = fc2_full.reshape(width, 2 * units)
    hidden, grad_pre, grad_mlp, mlp_in_part, mlp_out_part, fc1_bias_part, gate_two_part = (
        feed_forward(
            n, img, mlp_in, e_loc, e_near, mods, fc1_full, fc1_bias.astype(SINGLE), fc2_full
        )
    )
    tile = units // 4 if units % (4 * LANES) == 0 else units // 2
    tiles = units // tile
    fc_plan = [(w, w, t, k * tile) for w in range(2) for t in range(2) for k in range(tiles)]
    fc_rounds = [(k + 1) * 4 * tiles * 2 // (3 * (n - 2)) for k in range(n - 3)]
    fc_part, running = weight_grads(
        n, img, (mlp_in, grad_mlp), (grad_pre, hidden), fc_plan, tile, "fc_grads", fc_rounds, mlp_in_part, 6
    )
    fc_sum = lax.psum_scatter(fc_part, "dp", scatter_dimension=0, tiled=True)

    grad_middle, grad_attn, sums, grad_mix = middle_back(
        n, img, mlp_in_part, running, middle, attn_out, e_loc, proj_full, mods, lwp
    )
    grad_q, grad_k, grad_v, q_bias_part, v_bias_part, mlp_sum, proj_part = attend_back(
        n, img, qkv_rows, mixture, grad_mix, lse, mask_col, mlp_out_part, grad_attn, mix_loc
    )
    proj_part, fc_sum = lax.optimization_barrier((proj_part, fc_sum))
    proj_half = lax.psum_scatter(proj_part, "dp", scatter_dimension=0, tiled=True)
    attn_in_part, mod_one = attn_in_back(n, img, grad_q, grad_k, grad_v, x_all, qkv_full)
    qkv_plan = [(0, c, t, 0) for t in range(2) for c in range(3)]
    (qkv_part,) = weight_grads(
        n, img, (attn_in,), (grad_q, grad_k, grad_v), qkv_plan, lwp, "qkv_grad"
    )
    qkv_part, fc_sum = lax.optimization_barrier((qkv_part, fc_sum))
    qkv_sum = lax.psum_scatter(qkv_part, "dp", scatter_dimension=0, tiled=True)
    fc1_sum, fc2_sum = fc_sum[:, : 2 * units], fc_sum[:, 2 * units :]
    proj_own = sum_proj(n, proj_half)

    upstream_sum = sums[:, 4]
    gate_two = gate_two_part + fc2_shift * upstream_sum
    mod_grads = jnp.stack(
        [mod_one[:, 0], mod_one[:, 1], sums[:, 0], sums[:, 1], sums[:, 2], gate_two], axis=1
    ).reshape(2, n, mod_cols)
    rest = jnp.stack([sums[:, 3], mods[:, 5] * upstream_sum]).reshape(4, n, bias_cols)
    packed = jnp.concatenate(
        [
            mod_grads.transpose(1, 0, 2).reshape(n, -1),
            rest.transpose(1, 0, 2).reshape(n, -1),
        ],
        axis=1,
    )
    q_bias = q_bias_part.transpose(1, 0, 2).reshape(2, lwp)[:, :lw]
    v_bias = v_bias_part.transpose(1, 0, 2).reshape(2, lwp)[:, :lw]
    extra = jnp.concatenate(
        [jnp.stack([q_bias, v_bias], axis=1).reshape(-1), fc1_bias_part.reshape(-1)]
    )
    grad_attn_in, every, cond_sum = end(
        n, dp, cut, attn_in_part, packed[:, None], extra[None], ada_flat
    )
    every = every[:, 0]
    total = jnp.sum(every, axis=0)

    def by_row(vectors):
        return jnp.concatenate(
            [
                jnp.broadcast_to(vectors[0:1], (img, width)),
                jnp.broadcast_to(vectors[1:2], (pad, width)),
            ]
        )

    block_out = (
        (middle + by_row(mods[:, 5]) * (mlp_sum + by_row(fc2_shift))) * live_loc
    ).astype(HALF)
    normed, inv_std = layer_norm(x_loc.astype(SINGLE))
    input_grad = (
        grad_middle + norm_back(normed, inv_std, grad_attn_in * (1.0 + by_row(mods[:, 1])))
    ) * live_loc

    mod_half = every[:, :cut].astype(HALF).reshape(dp, 2, mod_cols)
    ada_grad = jnp.einsum("nd,ntc->dtc", act_slice, mod_half, preferred_element_type=SINGLE)
    ada_bias_grad = total[:cut].reshape(2, mod_cols)
    proj_bias_grad = total[cut : cut + 2 * bias_cols].reshape(2, bias_cols)
    fc2_bias_grad = total[cut + 2 * bias_cols : cut + 4 * bias_cols].reshape(2, bias_cols)
    after = cut + 4 * bias_cols
    qv_bias_grad = total[after : after + 4 * lw].reshape(2, 2, lw)
    fc1_bias_grad = total[after + 4 * lw :].reshape(2, units)
    cond_grad = cond_sum[:, 0, :depth].reshape(1, width) * silu_slope(cond_float)

    def streams(flat, last):
        return flat.astype(SINGLE).reshape(depth, 2, last)

    qkv_grad = qkv_sum.astype(SINGLE).reshape(depth, 2, 3, lwp)[..., :lw]
    fc2_grad = streams(fc2_sum, units).transpose(2, 1, 0)
    proj_grad = proj_own.reshape(depth, 2, lwp)[..., :share].transpose(2, 1, 0)
    return (
        block_out[None, :img],
        block_out[None, img : img + slots],
        input_grad[None, :img],
        input_grad[None, img : img + slots],
        cond_grad,
        ada_grad,
        ada_bias_grad,
        qkv_grad,
        qv_bias_grad,
        proj_grad,
        proj_bias_grad,
        streams(fc1_sum, units),
        fc1_bias_grad,
        fc2_grad,
        fc2_bias_grad,
    )


def solution(mesh):
    in_specs = (
        P("dp", "seq", None),
        P("dp", "seq", None),
        P("dp", "seq"),
        P("dp", None),
        P("dp", None, "seq"),
        P(None, "seq"),
        P("dp", None, None, "seq"),
        P(None, None, "seq"),
        P("seq", None, "dp"),
        P(None, "seq"),
        P("dp", None, "seq"),
        P(None, "seq"),
        P("seq", None, "dp"),
        P(None, "seq"),
        P("dp", "seq", None),
        P("dp", "seq", None),
    )
    out_specs = (
        P("dp", "seq", None),
        P("dp", "seq", None),
        P("dp", "seq", None),
        P("dp", "seq", None),
        P("dp", None),
        P("dp", None, "seq"),
        P(None, "seq"),
        P("dp", None, None, "seq"),
        P(None, None, "seq"),
        P("seq", None, "dp"),
        P(None, "seq"),
        P("dp", None, "seq"),
        P(None, "seq"),
        P("seq", None, "dp"),
        P(None, "seq"),
    )
    return jax.shard_map(body, mesh=mesh, in_specs=in_specs, out_specs=out_specs, check_vma=False)
```

```python
import functools
import math

import jax
import jax.numpy as jnp
from jax import lax
from jax.experimental import pallas as pl
from jax.experimental.pallas import tpu as pltpu
from jax.sharding import PartitionSpec as P

HD = 64
LANES = 128
EPSILON = 1e-06
GELU_ROOT = math.sqrt(2.0 / math.pi)
GELU_CUBE = 0.044715
MASKED = -1e30
SINGLE = jnp.float32
HALF = jnp.bfloat16
MEGA = 2**20


def up(value, multiple):
    return -(-value // multiple) * multiple


def params(limit=56):
    return pltpu.CompilerParams(vmem_limit_bytes=limit * MEGA)


def remote(collective, limit=56):
    return pltpu.CompilerParams(
        collective_id=collective, has_side_effects=True, vmem_limit_bytes=limit * MEGA
    )


def cost(flops, nbytes, trans=0):
    return pl.CostEstimate(flops=int(flops), bytes_accessed=int(nbytes), transcendentals=int(trans))


def nt_dot(a, b):
    return lax.dot_general(a, b, (((1,), (1,)), ((), ())), preferred_element_type=SINGLE)


def tn_dot(a, b):
    return lax.dot_general(a, b, (((0,), (0,)), ((), ())), preferred_element_type=SINGLE)


def nn_dot(a, b):
    return jnp.dot(a, b, preferred_element_type=SINGLE)


def layer_norm(values):
    center = values - jnp.mean(values, axis=-1, keepdims=True)
    inv_std = lax.rsqrt(jnp.mean(center * center, axis=-1, keepdims=True) + EPSILON)
    return (center * inv_std, inv_std)


def norm_back(normed, inv_std, upstream):
    first = jnp.mean(upstream, axis=-1, keepdims=True)
    second = jnp.mean(upstream * normed, axis=-1, keepdims=True)
    return inv_std * (upstream - first - normed * second)


def gelu_both(values):
    square = values * values
    inner = GELU_ROOT * (values + GELU_CUBE * square * values)
    tangent = jnp.tanh(inner)
    half = 0.5 * (1.0 + tangent)
    slope = half + 0.5 * values * (1.0 - tangent * tangent) * GELU_ROOT * (
        1.0 + 3.0 * GELU_CUBE * square
    )
    return values * half, slope


def silu_slope(values):
    sigma = jax.nn.sigmoid(values)
    return sigma + values * sigma * (1.0 - sigma)


def whole(shape, single=False):
    zeros = (0,) * len(shape)
    if single:
        return pl.BlockSpec(shape, lambda *_: zeros, pipeline_mode=pl.Buffered(1))
    return pl.BlockSpec(shape, lambda *_: zeros)


def rows_spec(rows, width):
    return pl.BlockSpec((1, rows, width), lambda s: (s, 0, 0))


MESH = pl.DeviceIdType.MESH


def on_line(position):
    return {"seq": position}


def both(first, second):
    return jnp.logical_and(first, second)


def flip(value, mask):
    bit = 1
    while bit <= mask:
        if mask & bit:
            value = value + bit - 2 * bit * lax.rem(lax.div(value, bit), 2)
        bit *= 2
    return value


def greet(n, line=None, group=None):
    me, my = lax.axis_index("seq"), lax.axis_index("dp")
    dp = lax.axis_size("dp")
    barrier = pltpu.get_barrier_semaphore()
    peers = []
    if line == "all":
        peers += [on_line(lax.rem(me + offset, n)) for offset in range(1, n)]
    if group == "all":
        peers += [{"dp": lax.rem(my + offset, dp)} for offset in range(1, dp)]
    if group == "paths":
        peers += [{"dp": flip(my, 1)}] + [{"dp": flip(my, mask)} for mask in masks_of(dp)]
    for peer in peers:
        pl.semaphore_signal(barrier, inc=1, device_id=peer, device_id_type=MESH)
    if line == "near":
        for sign in (1, -1):
            near = me + sign

            @pl.when(both(near >= 0, near < n))
            def _():
                pl.semaphore_signal(barrier, inc=1, device_id=on_line(near), device_id_type=MESH)

    count = len(peers)
    if line == "near":
        count = count + lax.min(me, 1) + lax.min(n - 1 - me, 1)
    pl.semaphore_wait(barrier, count)


def masks_of(dp):
    masks, bit = [], 2
    while bit < dp:
        masks.append(bit)
        bit *= 2
    return masks


class GroupGather:
    def __init__(self, src, out, send, recv, pass_send, pass_recv, local):
        self.src, self.out = src, out
        self.send, self.recv, self.local = send, recv, local
        self.pass_send, self.pass_recv = pass_send, pass_recv
        self.my = lax.axis_index("dp")
        masks = masks_of(out.shape[0])
        self.orders = (masks, masks[::-1])
        self.phases = len(masks)

    @staticmethod
    def scratch(dp):
        return [pltpu.SemaphoreType.DMA((2, dp // 2)) for _ in range(4)] + [
            pltpu.SemaphoreType.DMA
        ]

    def span(self, half, count):
        mask = 0
        for k in range(self.phases):
            if count >> k & 1:
                mask |= self.orders[half][k]
        return mask

    def copy(self, half, phase, count, block):
        src = self.src.at[half] if count == 0 else self.out.at[block, half]
        index = 2**phase - 1 + count
        return pltpu.make_async_remote_copy(
            src_ref=src,
            dst_ref=self.out.at[block, half],
            send_sem=self.send.at[half, index],
            recv_sem=self.recv.at[half, index],
            device_id={"dp": flip(self.my, self.orders[half][phase])},
            device_id_type=MESH,
        )

    def hand(self, half, index, block, own=False):
        src = self.src.at[half] if own else self.out.at[block, half]
        return pltpu.make_async_remote_copy(
            src_ref=src,
            dst_ref=self.out.at[block, half],
            send_sem=self.pass_send.at[half, index],
            recv_sem=self.pass_recv.at[half, index],
            device_id={"dp": flip(self.my, 1)},
            device_id_type=MESH,
        )

    def begin(self):
        for phase in range(self.phases):
            for half in range(2):
                self.copy(half, phase, 0, self.my).start()
        for half in range(2):
            self.hand(half, 0, self.my, True).start()
        pltpu.make_async_copy(self.src, self.out.at[self.my], self.local).start()

    def arrive(self, phase):
        for half in range(2):
            mask = self.orders[half][phase]
            for count in range(2**phase):
                block = flip(self.my, mask ^ self.span(half, count))
                self.copy(half, phase, count, block).wait_recv()
            if phase + 1 < self.phases:
                for count in range(1, 2 ** (phase + 1)):
                    block = flip(self.my, self.span(half, count))
                    self.copy(half, phase + 1, count, block).start()
            for count in range(2**phase):
                block = flip(self.my, mask ^ self.span(half, count))
                self.hand(half, 2**phase + count, block).start()

    def finish(self):
        pltpu.make_async_copy(self.src, self.out.at[self.my], self.local).wait()
        other = flip(self.my, 1)
        for half in range(2):
            self.hand(half, 0, other, True).wait()
            for phase in range(self.phases):
                mask = self.orders[half][phase]
                for count in range(2**phase):
                    self.copy(half, phase, count, self.my).wait_send()
                    block = flip(other, mask ^ self.span(half, count))
                    self.hand(half, 2**phase + count, block).wait()


class GroupSum:
    def __init__(self, part, got, hold, passed, came, pass_send, pass_recv, send, recv, load):
        self.part, self.got, self.hold, self.passed, self.came = part, got, hold, passed, came
        self.pass_send, self.pass_recv = pass_send, pass_recv
        self.send, self.recv, self.load = send, recv, load
        self.my = lax.axis_index("dp")
        self.dp = part.shape[0]
        masks = masks_of(self.dp)
        self.orders = (masks, masks[::-1])
        self.phases = len(masks)

    @staticmethod
    def scratch(dp, rows, width):
        half = dp // 2
        return [
            pltpu.VMEM((2, half, rows, width), HALF),
            pltpu.VMEM((2, half, rows, width), HALF),
            pltpu.VMEM((2, half - 1, rows, width), HALF),
            pltpu.VMEM((2, half - 1, rows, width), HALF),
        ] + [pltpu.SemaphoreType.DMA((2, half)) for _ in range(5)]

    @staticmethod
    def scratch_inner(dp, rows, width):
        full = GroupSum.scratch(dp, rows, width)
        return full[:1] + full[2:8]

    def span(self, half, count):
        mask = 0
        for k in range(self.phases):
            if count >> k & 1:
                mask |= self.orders[half][k]
        return mask

    def hand(self, half, count):
        block = flip(self.my, 1 ^ self.span(half, count))
        return pltpu.make_async_remote_copy(
            src_ref=self.part.at[block, half],
            dst_ref=self.got.at[half, count],
            send_sem=self.pass_send.at[half, count],
            recv_sem=self.pass_recv.at[half, count],
            device_id={"dp": flip(self.my, 1)},
            device_id_type=MESH,
        )

    def fetch(self, half, count):
        block = flip(self.my, self.span(half, count))
        return pltpu.make_async_copy(
            self.part.at[block, half], self.hold.at[half, count], self.load.at[half, count]
        )

    def copy(self, half, phase, index):
        return pltpu.make_async_remote_copy(
            src_ref=self.passed.at[half, 2**phase + index - 1],
            dst_ref=self.came.at[half, 2**phase - 1 + index],
            send_sem=self.send.at[half, 2**phase - 1 + index],
            recv_sem=self.recv.at[half, 2**phase - 1 + index],
            device_id={"dp": flip(self.my, self.orders[half][phase])},
            device_id_type=MESH,
        )

    def every(self):
        return [(half, count) for half in range(2) for count in range(self.dp // 2)]

    def begin(self):
        for half, count in self.every():
            self.hand(half, count).start()
            if self.hold is not None:
                self.fetch(half, count).start()

    def value(self, half, count, phase):
        if self.hold is None:
            mine = self.part[flip(self.my, self.span(half, count)), half]
        else:
            mine = self.hold[half, count]
        total = mine.astype(SINGLE) + self.got[half, count].astype(SINGLE)
        for later in range(phase, self.phases):
            total = total + self.came[half, 2**later - 1 + count].astype(SINGLE)
        return total

    def step(self, number):
        if number == 0:
            for half, count in self.every():
                if self.hold is not None:
                    self.fetch(half, count).wait()
                self.hand(half, count).wait_recv()
        else:
            self.took(self.phases - number)
        phase = self.phases - 1 - number
        for half in range(2):
            for index in range(2**phase):
                count = 2**phase + index
                self.passed[half, count - 1] = self.value(half, count, phase + 1).astype(HALF)
                self.copy(half, phase, index).start()

    def took(self, phase):
        for half in range(2):
            for index in range(2**phase):
                self.copy(half, phase, index).wait_recv()

    def finish(self, out):
        self.took(0)
        for half in range(2):
            out[half] = self.value(half, 0, 0).astype(out.dtype)
        self.sent(0)

    def close(self, rest):
        self.took(1)
        for half in range(2):
            for count in range(2):
                rest[half, count] = self.value(half, count, 1).astype(rest.dtype)
        self.sent(1)

    def sent(self, first):
        for half, count in self.every():
            self.hand(half, count).wait_send()
        for phase in range(first, self.phases):
            for half in range(2):
                for index in range(2**phase):
                    self.copy(half, phase, index).wait_send()


class GroupLast:
    def __init__(self, rest, came, send, recv):
        self.rest, self.came, self.send, self.recv = rest, came, send, recv
        masks = masks_of(lax.axis_size("dp"))
        self.partners = [flip(lax.axis_index("dp"), mask) for mask in (masks[0], masks[-1])]

    @staticmethod
    def scratch(rows, width):
        return [pltpu.VMEM((2, rows, width), HALF)] + [pltpu.SemaphoreType.DMA((2,))] * 2

    def copy(self, half):
        return pltpu.make_async_remote_copy(
            src_ref=self.rest.at[half, 1],
            dst_ref=self.came.at[half],
            send_sem=self.send.at[half],
            recv_sem=self.recv.at[half],
            device_id={"dp": self.partners[half]},
            device_id_type=MESH,
        )

    def begin(self):
        for half in range(2):
            self.copy(half).start()

    def finish(self, store):
        for half in range(2):
            self.copy(half).wait()
            store(half, self.rest[half, 0].astype(SINGLE) + self.came[half].astype(SINGLE))


class LineGather:
    def __init__(self, n, src, out, send, recv, local, first=0, stop=None, land=None):
        self.n, self.src, self.out, self.land = n, src, out, land
        self.send, self.recv, self.local = send, recv, local
        self.first, self.stop = first, n - 1 if stop is None else stop
        self.me = lax.axis_index("seq")

    @staticmethod
    def scratch(n):
        return [
            pltpu.SemaphoreType.DMA((2, n - 1)),
            pltpu.SemaphoreType.DMA((2, n - 1)),
            pltpu.SemaphoreType.DMA,
        ]

    def inside(self, position):
        return both(position >= 0, position < self.n)

    def copy(self, way, hop, block, near):
        if hop > self.first:
            src = self.out.at[block]
        else:
            src = self.src if hop == 0 else self.src.at[way]
        return pltpu.make_async_remote_copy(
            src_ref=src,
            dst_ref=self.out.at[block] if self.land is None else self.land.at[way],
            send_sem=self.send.at[way, hop],
            recv_sem=self.recv.at[way, hop],
            device_id=on_line(near),
            device_id_type=MESH,
        )

    def each(self, hop):
        for way, sign in ((0, 1), (1, -1)):
            yield way, sign, self.me - sign * hop, self.me + sign

    def begin(self):
        self.launch(self.first)

    def launch(self, hop):
        for way, sign, block, near in self.each(hop):

            @pl.when(both(self.inside(block), self.inside(near)))
            def _():
                self.copy(way, hop, block, near).start()

    def keep(self):
        return pltpu.make_async_copy(self.src, self.out.at[self.me], self.local)

    def arrive(self, hop):
        for way, sign, block, near in self.each(hop + 1):

            @pl.when(self.inside(block))
            def _():
                self.copy(way, hop, block, near).wait_recv()

        if hop + 1 < self.stop:
            self.launch(hop + 1)

    def finish(self):
        for hop in range(self.first, self.stop):
            for way, sign, block, near in self.each(hop):

                @pl.when(both(self.inside(block), self.inside(near)))
                def _():
                    self.copy(way, hop, block, near).wait_send()


class LineSum:
    def __init__(self, n, part, out, got, mine, passed, send, recv, load, first=0, stop=None, tail=None, prev=None):
        self.n, self.part, self.out = n, part, out
        self.got, self.mine, self.passed = got, mine, passed
        self.send, self.recv, self.load = send, recv, load
        self.first, self.stop = first, n - 1 if stop is None else stop
        self.tail, self.prev = tail, prev
        self.me = lax.axis_index("seq")

    @staticmethod
    def scratch(n, rows, width, first=0, stop=None):
        stop = n - 1 if stop is None else stop
        return [
            pltpu.VMEM((2, stop - first + (first > 0), rows, width), HALF),
            pltpu.VMEM((2, rows, width), HALF),
            pltpu.VMEM((2, max(stop - max(first, 1), 1), rows, width), HALF),
            pltpu.SemaphoreType.DMA((2, n - 1)),
            pltpu.SemaphoreType.DMA((2, n - 1)),
            pltpu.SemaphoreType.DMA((2, 2)),
        ]

    def inside(self, position):
        return both(position >= 0, position < self.n)

    def each(self, step):
        reach = self.n - 1 - step
        for way, sign in ((0, 1), (1, -1)):
            yield way, self.me + sign * reach, self.me + sign, self.me - sign

    def slot(self, way, step):
        return self.passed.at[way, max(step - max(self.first, 1), 0)]

    def copy(self, way, step, src, near):
        if self.tail is not None and step == self.stop - 1:
            dst = self.tail.at[way]
        else:
            dst = self.got.at[way, step - self.first]
        return pltpu.make_async_remote_copy(
            src_ref=src,
            dst_ref=dst,
            send_sem=self.send.at[way, step],
            recv_sem=self.recv.at[way, step],
            device_id=on_line(near),
            device_id_type=MESH,
        )

    def round(self, step):
        for way, owner, near, behind in self.each(step):
            if step == 0:

                @pl.when(self.inside(owner))
                def _():
                    self.copy(way, step, self.part(owner), near).start()

                continue

            @pl.when(both(self.inside(owner), jnp.logical_not(self.inside(behind))))
            def _():
                self.copy(way, step, self.part(owner), near).start()

            @pl.when(both(self.inside(owner), self.inside(behind)))
            def _():
                fetch = pltpu.make_async_copy(
                    self.part(owner), self.mine.at[way], self.load.at[way, 0]
                )
                fetch.start()
                slot = self.slot(way, step)
                if step == self.first:
                    index = self.stop - self.first
                    held = pltpu.make_async_copy(
                        self.prev.at[way], self.got.at[way, index], self.load.at[way, 1]
                    )
                    held.start()
                    held.wait()
                else:
                    index = step - 1 - self.first
                    self.copy(way, step - 1, slot, near).wait_recv()
                fetch.wait()
                total = self.mine[way].astype(SINGLE) + self.got[way, index].astype(SINGLE)
                self.passed[way, step - max(self.first, 1)] = total.astype(HALF)
                self.copy(way, step, slot, near).start()

    def sent(self):
        for step in range(self.first, self.stop):
            for way, owner, near, behind in self.each(step):

                @pl.when(self.inside(owner))
                def _():
                    self.copy(way, step, self.slot(way, step), near).wait_send()

    def close(self):
        last = self.stop - 1
        for way, owner, near, behind in self.each(last + 1):

            @pl.when(both(self.inside(owner), self.inside(behind)))
            def _():
                self.copy(way, last, self.slot(way, last), near).wait_recv()

        self.sent()

    def finish(self):
        last = self.n - 2
        fetch = pltpu.make_async_copy(self.part(self.me), self.mine.at[0], self.load.at[0, 0])
        fetch.start()
        fetch.wait()
        self.out[...] = self.mine[0].astype(SINGLE)
        for way, owner, near, behind in self.each(last):

            @pl.when(self.inside(behind))
            def _():
                self.copy(way, last, self.slot(way, last), near).wait_recv()
                self.out[...] += self.got[way, last - self.first].astype(SINGLE)

        self.sent()


def at_rows(ref):
    return lambda owner: ref.at[owner]


def at_step(step, when, action):
    @pl.when(step == when)
    def _():
        action()


def to_group(my, dp, offset, src, dst, send, recv):
    peer = lax.rem(my + offset, dp)
    return pltpu.make_async_remote_copy(
        src_ref=src if src.shape == dst.shape[1:] else src.at[peer],
        dst_ref=dst.at[my],
        send_sem=send.at[offset - 1],
        recv_sem=recv.at[offset - 1],
        device_id={"dp": peer},
        device_id_type=MESH,
    )


def to_line(me, n, offset, src, dst, send, recv):
    peer = lax.rem(me + offset, n)
    return pltpu.make_async_remote_copy(
        src_ref=src if src.shape == dst.shape[1:] else src.at[peer],
        dst_ref=dst.at[me],
        send_sem=send.at[offset - 1],
        recv_sem=recv.at[offset - 1],
        device_id=on_line(peer),
        device_id_type=MESH,
    )


def start_kernel(
    n, dp, x_ref, act_ref, ada_ref, side_ref, qkv_ref, fc1_ref, x_all, side_all, acts, qkv_all, fc1_all,
    part, parts, row, a_send, a_recv, p_send, p_recv, s_send, s_recv, *sems,
):
    me, my = lax.axis_index("seq"), lax.axis_index("dp")
    depth, cols = ada_ref.shape
    greet(n, "all", "all")
    gather = LineGather(n, x_ref, x_all, *sems[:3])
    qkv = GroupGather(qkv_ref, qkv_all, *sems[3:8])
    fc1 = GroupGather(fc1_ref, fc1_all, *sems[8:13])
    gather.begin()
    others = range(1, dp)
    act_go = [to_group(my, dp, k, act_ref, acts, a_send, a_recv) for k in others]
    for copy in act_go:
        copy.start()
    gather.keep().start()
    acts[my] = act_ref[my]
    for copy in act_go:
        copy.wait_recv()
    product = nn_dot(acts[:, 0, :depth].astype(HALF), ada_ref[...])
    for k in range(dp):
        part[k] = product[k : k + 1]
    part_go = [to_group(my, dp, k, part, parts, p_send, p_recv) for k in others]
    for copy in part_go:
        copy.start()
    parts[my] = part[my]
    for copy in part_go:
        copy.wait_recv()
    qkv.begin()
    fc1.begin()
    row[...] = side_ref[...]
    row[:, :cols] += jnp.sum(parts[...], axis=0)
    row_go = [to_line(me, n, k, row, side_all, s_send, s_recv) for k in range(1, n)]
    for copy in row_go:
        copy.start()
    side_all[me] = row[...]
    for hop in range(max(n - 1, qkv.phases)):
        if hop < n - 1:
            gather.arrive(hop)
        if hop < qkv.phases:
            qkv.arrive(hop)
            fc1.arrive(hop)
    for copy in row_go:
        copy.wait()
    for copy in act_go + part_go:
        copy.wait_send()
    gather.keep().wait()
    gather.finish()
    qkv.finish()
    fc1.finish()


def start(n, dp, x_loc, act_parts, ada, side, qkv, fc1):
    rows, width = x_loc.shape
    cols = ada.shape[1]
    anywhere = pl.BlockSpec(memory_space=pl.ANY)
    inner = pl.BlockSpec(memory_space=pltpu.VMEM)
    return pl.pallas_call(
        functools.partial(start_kernel, n, dp),
        in_specs=[inner] * 6,
        out_specs=[anywhere, inner, inner, anywhere, anywhere],
        out_shape=[
            jax.ShapeDtypeStruct((n, rows, width), HALF),
            jax.ShapeDtypeStruct((n,) + side.shape, SINGLE),
            jax.ShapeDtypeStruct(act_parts.shape, SINGLE),
            jax.ShapeDtypeStruct((dp,) + qkv.shape, HALF),
            jax.ShapeDtypeStruct((dp,) + fc1.shape, HALF),
        ],
        scratch_shapes=[
            pltpu.VMEM((dp, 1, cols), SINGLE),
            pltpu.VMEM((dp, 1, cols), SINGLE),
            pltpu.VMEM(side.shape, SINGLE),
            pltpu.SemaphoreType.DMA((dp - 1,)),
            pltpu.SemaphoreType.DMA((dp - 1,)),
            pltpu.SemaphoreType.DMA((dp - 1,)),
            pltpu.SemaphoreType.DMA((dp - 1,)),
            pltpu.SemaphoreType.DMA((n - 1,)),
            pltpu.SemaphoreType.DMA((n - 1,)),
        ]
        + LineGather.scratch(n)
        + GroupGather.scratch(dp)
        + GroupGather.scratch(dp),
        compiler_params=remote(1),
        cost_estimate=cost(10**6, 100 * MEGA),
        name="start",
    )(x_loc, act_parts, ada, side, qkv, fc1)


def qkv_kernel(img, x_ref, mod_ref, w_ref, b_ref, a_ref, o_ref):
    wide = o_ref.shape[2]
    for t, sl in ((0, slice(0, img)), (1, slice(img, x_ref.shape[1]))):
        normed, _ = layer_norm(x_ref[0, sl].astype(SINGLE))
        a = (normed * (1.0 + mod_ref[t, 1:2]) + mod_ref[t, 0:1]).astype(HALF)
        a_ref[0, sl] = a
        o_ref[0, sl] = (
            nn_dot(a, w_ref[:, t * wide : (t + 1) * wide]) + b_ref[t : t + 1]
        ).astype(HALF)


def project_qkv(n, img, x_all, mods, weight, bias):
    _, rows, width = x_all.shape
    wide = weight.shape[1] // 2
    return pl.pallas_call(
        functools.partial(qkv_kernel, img),
        grid=(n,),
        in_specs=[
            rows_spec(rows, width),
            whole(mods.shape),
            whole(weight.shape, True),
            whole(bias.shape),
        ],
        out_specs=[rows_spec(rows, width), rows_spec(rows, wide)],
        out_shape=[
            jax.ShapeDtypeStruct((n, rows, width), HALF),
            jax.ShapeDtypeStruct((n, rows, wide), HALF),
        ],
        compiler_params=params(),
        cost_estimate=cost(2 * n * rows * width * wide, 30 * MEGA),
        name="project_qkv",
    )(x_all, mods, weight, bias)


def halves(shape):
    lane = lax.broadcasted_iota(jnp.int32, shape, len(shape) - 1)
    return lane < HD


def attn_kernel(
    n, q_ref, k_ref, v_ref, mask_ref, e_ref, p_ref, o_ref, lse_ref, e_near, mix_ref, p_all,
    o_buf, o_send, o_recv, o_local, *sems,
):
    pair, block = pl.program_id(0), pl.program_id(1)
    pairs = pl.num_programs(0)
    step = pair * n + block
    me = lax.axis_index("seq")
    count, rows, _ = k_ref.shape
    gather = LineGather(n, e_ref, None, *sems[:3], first=0, stop=1, land=e_near)
    proj = GroupGather(p_ref, p_all, *sems[3:])

    def begin():
        greet(n, "all", "paths")
        gather.begin()
        proj.begin()

    at_step(step, 0, begin)
    queries = q_ref[0] * HALF(1.0 / math.sqrt(HD))
    keys = k_ref[...].reshape(n * rows, LANES)
    values = v_ref[...].reshape(n * rows, LANES)
    first = halves(queries.shape)
    outs, logs = [], []
    for head in range(2):
        own = first if head == 0 else jnp.logical_not(first)
        scores = nt_dot(jnp.where(own, queries, HALF(0)), keys) + mask_ref[...]
        maxima = jnp.max(scores, axis=-1, keepdims=True)
        raised = jnp.exp(scores - maxima)
        totals = jnp.sum(raised, axis=-1, keepdims=True)
        weights = (raised * (1.0 / totals)).astype(HALF)
        outs.append(nn_dot(weights, values))
        logs.append(maxima + jnp.log(totals))
    mixed = jnp.where(first, outs[0], outs[1]).astype(HALF)
    o_ref[0] = mixed
    o_buf[pair, block] = mixed
    lse_ref[0] = jnp.where(first, logs[0], logs[1])
    static_pairs = o_buf.shape[0]

    def columns(sender, which):
        start = (sender * static_pairs + which) * LANES
        return mix_ref.at[:, pl.ds(pl.multiple_of(start, LANES), LANES)]

    def away(which, offset):
        peer = lax.rem(me + offset, n)
        return pltpu.make_async_remote_copy(
            src_ref=o_buf.at[which, peer],
            dst_ref=columns(me, which),
            send_sem=o_send.at[which, offset - 1],
            recv_sem=o_recv.at[which, offset - 1],
            device_id=on_line(peer),
            device_id_type=MESH,
        )

    for offset in range(1, n):

        @pl.when(block == lax.rem(me + offset, n))
        def _():
            away(pair, offset).start()

    @pl.when(block == me)
    def _():
        pltpu.make_async_copy(o_buf.at[pair, me], columns(me, pair), o_local.at[pair]).start()

    last = static_pairs * n - 1
    for phase in range(proj.phases):
        at_step(step, min(last, 5 * phase + 5), functools.partial(proj.arrive, phase))

    def finish():
        gather.arrive(0)
        proj.finish()
        for which in range(static_pairs):
            pltpu.make_async_copy(o_buf.at[which, me], columns(me, which), o_local.at[which]).wait()
            for offset in range(1, n):
                away(which, offset).wait()
        gather.finish()

    at_step(step, last, finish)


def attend(n, dp, qkv, mask, e_loc, proj):
    _, rows, wide = qkv.shape
    width = e_loc.shape[1]
    pairs = wide // 3 // LANES
    total = n * rows
    block = pl.BlockSpec((1, rows, LANES), lambda h, s: (s, 0, h))
    anywhere = pl.BlockSpec(memory_space=pl.ANY)
    return pl.pallas_call(
        functools.partial(attn_kernel, n),
        grid=(pairs, n),
        in_specs=[
            block,
            pl.BlockSpec((n, rows, LANES), lambda h, s: (0, 0, pairs + h)),
            pl.BlockSpec((n, rows, LANES), lambda h, s: (0, 0, 2 * pairs + h)),
            whole(mask.shape),
            anywhere,
            whole(proj.shape, True),
        ],
        out_specs=[block, block, anywhere, anywhere, anywhere],
        out_shape=[
            jax.ShapeDtypeStruct((n, rows, pairs * LANES), HALF),
            jax.ShapeDtypeStruct((n, rows, pairs * LANES), SINGLE),
            jax.ShapeDtypeStruct((2, rows, width), HALF),
            jax.ShapeDtypeStruct((rows, n * pairs * LANES), HALF),
            jax.ShapeDtypeStruct((dp,) + proj.shape, HALF),
        ],
        scratch_shapes=[
            pltpu.VMEM((pairs, n, rows, LANES), HALF),
            pltpu.SemaphoreType.DMA((pairs, n - 1)),
            pltpu.SemaphoreType.DMA((pairs, n - 1)),
            pltpu.SemaphoreType.DMA((pairs,)),
        ]
        + LineGather.scratch(n)
        + GroupGather.scratch(dp),
        compiler_params=remote(2),
        cost_estimate=cost(2 * 2 * 4 * pairs * total * total * LANES, 20 * MEGA, 2 * pairs * total * total),
        name="attend",
    )(qkv, qkv, qkv, mask, e_loc, proj)


def attn_back_kernel(
    lines, img, pairs, q_ref, k_ref, v_ref, o_ref, g_ref, lse_ref, mask_ref, y_ref, l_ref, r_ref,
    dq_ref, dk_ref, dv_ref, qb_ref, vb_ref, p_rest, tail,
    acc_ref, lse_row, delta_row, turned, p_part, *scratch,
):
    linear = pl.program_id(0)
    ahead = 2 * lines
    attn_steps = pairs * lines
    last = ahead + attn_steps - 1
    step = lax.rem(lax.max(linear - ahead, 0), lines)
    n, rows, _ = q_ref.shape
    total = n * rows
    line = LineSum(lines, at_rows(y_ref), None, *scratch[:6], stop=lines - 2, tail=tail)
    group = GroupSum(p_part, scratch[6], None, *scratch[7:], None)

    def begin():
        greet(lines, "near", "paths")
        line.round(0)

    at_step(linear, 0, begin)
    tile = r_ref.shape[1]
    for t, sl in ((0, slice(0, img)), (1, slice(img, rows))):

        @pl.when(linear == 0)
        def _():
            turned[:, sl] = l_ref[sl].T

        @pl.when(both(linear < ahead, lax.rem(linear, 2) == t))
        def _():
            column = pl.ds(pl.multiple_of(linear * tile, LANES), tile)
            product = nn_dot(turned[:, sl], r_ref[sl]).astype(HALF)
            p_part[:, :, :, column] = product.reshape(p_part.shape[:3] + (tile,))

    at_step(linear, ahead, group.begin)

    @pl.when(linear >= ahead)
    def _():
        grads = g_ref[...].reshape(total, LANES)
        queries = q_ref[...].reshape(total, LANES) * HALF(1.0 / math.sqrt(HD))

        @pl.when(step == 0)
        def _():
            acc_ref[...] = jnp.zeros_like(acc_ref)
            product = grads.astype(SINGLE) * o_ref[...].reshape(total, LANES).astype(SINGLE)
            flipped = product.T
            logs = lse_ref[...].reshape(total, LANES).T
            for head in range(2):
                delta_row[head : head + 1] = jnp.sum(
                    flipped[head * HD : (head + 1) * HD], axis=0, keepdims=True
                )
                lse_row[head : head + 1] = logs[head * HD : head * HD + 1]
            vb_ref[0] = jnp.zeros_like(vb_ref[0])

        keys, values = k_ref[0], v_ref[0]
        first = halves(keys.shape)
        mask = mask_ref[0][:, 0:1]
        dks, dvs = [], []
        for head in range(2):
            own = first if head == 0 else jnp.logical_not(first)
            key_own = jnp.where(own, keys, HALF(0))
            scores = nt_dot(key_own, queries)
            probs = jnp.exp((scores - lse_row[head : head + 1]) + mask)
            grad_prob = nt_dot(jnp.where(own, values, HALF(0)), grads)
            grad_score = (probs * (grad_prob - delta_row[head : head + 1])).astype(HALF)
            dvs.append(nn_dot(probs.astype(HALF), grads))
            dks.append(nn_dot(grad_score, queries))
            acc_ref[...] += tn_dot(grad_score, key_own)
        dk_ref[0] = jnp.where(first, dks[0], dks[1]).astype(HALF)
        dv = jnp.where(first, dvs[0], dvs[1])
        dv_ref[0] = dv.astype(HALF)
        vb_ref[0, 0:1] += jnp.sum(dv[:img], axis=0, keepdims=True)
        vb_ref[0, 1:2] += jnp.sum(dv[img:], axis=0, keepdims=True)

        @pl.when(step == lines - 1)
        def _():
            dq = (acc_ref[...] * (1.0 / math.sqrt(HD))).reshape(n, rows, LANES)
            dq_ref[...] = dq.astype(HALF)
            qb_ref[0, 0:1] = jnp.sum(jnp.sum(dq[:, :img], axis=0), axis=0, keepdims=True)
            qb_ref[0, 1:2] = jnp.sum(jnp.sum(dq[:, img:], axis=0), axis=0, keepdims=True)

    for hop in range(1, lines - 2):
        at_step(linear, min(last, ahead + 5 * hop), functools.partial(line.round, hop))

    for number in range(group.phases - 1):
        at_step(linear, min(last, ahead + 2 + 4 * number), functools.partial(group.step, number))

    def finish():
        line.close()
        group.close(p_rest)

    at_step(linear, last, finish)


def attend_back(n, dp, img, qkv, mixture, grad_mix, lse, mask_col, out_parts, grad_attn, mix_loc):
    _, rows, wide = qkv.shape
    pairs = wide // 3 // LANES
    total = n * rows
    lw = pairs * LANES
    ahead = 2 * n
    steps = pairs * n
    width = out_parts.shape[2]
    depth = width // dp // 2

    def place(k):
        return lax.rem(lax.max(k - ahead, 0), n)

    def head(k):
        return lax.div(lax.max(k - ahead, 0), n)

    full = pl.BlockSpec((n, rows, LANES), lambda k: (0, 0, head(k)))

    def block(base):
        return pl.BlockSpec((1, rows, LANES), lambda k: (place(k), 0, base + head(k)))

    bias = pl.BlockSpec((1, 2, LANES), lambda k: (head(k), 0, 0))
    anywhere = pl.BlockSpec(memory_space=pl.ANY)
    return pl.pallas_call(
        functools.partial(attn_back_kernel, n, img, pairs),
        grid=(ahead + steps,),
        in_specs=[
            full,
            block(pairs),
            block(2 * pairs),
            full,
            full,
            full,
            pl.BlockSpec((1, rows, LANES), lambda k: (place(k), 0, 0)),
            anywhere,
            whole(grad_attn.shape, True),
            pl.BlockSpec((rows, lw), lambda k: (0, lax.min(lax.div(k, 2), n - 1))),
        ],
        out_specs=[
            full,
            block(0),
            block(0),
            bias,
            bias,
            whole((2, 2, depth, 2 * n * lw), True),
            anywhere,
        ],
        out_shape=[jax.ShapeDtypeStruct((n, rows, lw), HALF)] * 3
        + [jax.ShapeDtypeStruct((pairs, 2, LANES), SINGLE)] * 2
        + [
            jax.ShapeDtypeStruct((2, 2, depth, 2 * n * lw), HALF),
            jax.ShapeDtypeStruct((2, rows, width), HALF),
        ],
        scratch_shapes=[
            pltpu.VMEM((total, LANES), SINGLE),
            pltpu.VMEM((2, total), SINGLE),
            pltpu.VMEM((2, total), SINGLE),
            pltpu.VMEM((width, rows), HALF),
            pltpu.VMEM((dp, 2, depth, 2 * n * lw), HALF),
        ]
        + LineSum.scratch(n, rows, width, stop=n - 2)
        + GroupSum.scratch_inner(dp, depth, 2 * n * lw),
        compiler_params=remote(3, 62),
        cost_estimate=cost(2 * 5 * 4 * pairs * total * total * LANES, 30 * MEGA, 2 * pairs * total * total),
        name="attend_back",
    )(qkv, qkv, qkv, mixture, grad_mix, lse, mask_col, out_parts, grad_attn, mix_loc)


def proj_columns(w_ref, z, t):
    dp, n, depth, cols = w_ref.shape
    half = cols // 2
    return w_ref[:, z, :, t * half : (t + 1) * half].reshape(dp * depth, half)


def middle_kernel(
    n, img, mix_ref, x_ref, w_ref, b_ref, mod_ref, fc2_ref, y_ref, m_ref, all_ref, fc2_all, own, *sems
):
    greet(n, "near", "paths")
    fc2 = GroupGather(fc2_ref, fc2_all, *sems[3:])
    fc2.begin()
    lw = mix_ref.shape[1] // n
    heads = w_ref.shape[3] // 2
    for t, sl in ((0, slice(0, img)), (1, slice(img, x_ref.shape[0]))):
        attn = b_ref[t : t + 1]
        for z in range(n):
            attn = attn + nt_dot(mix_ref[sl, z * lw : z * lw + heads], proj_columns(w_ref, z, t))
        y_ref[sl] = attn
        middle = x_ref[sl].astype(SINGLE) + mod_ref[t, 2:3] * attn
        m_ref[sl] = middle
        normed, _ = layer_norm(middle)
        own[sl] = (normed * (1.0 + mod_ref[t, 4:5]) + mod_ref[t, 3:4]).astype(HALF)
    gather = LineGather(n, own, all_ref, *sems[:3])
    gather.begin()
    gather.keep().start()
    for hop in range(max(n - 1, fc2.phases)):
        if hop < fc2.phases:
            fc2.arrive(hop)
        if hop < n - 1:
            gather.arrive(hop)
    gather.keep().wait()
    gather.finish()
    fc2.finish()


def middle_rows(n, dp, img, mixture, x_loc, weight, bias, mods, fc2):
    rows, width = x_loc.shape
    inner = pl.BlockSpec(memory_space=pltpu.VMEM)
    anywhere = pl.BlockSpec(memory_space=pl.ANY)
    return pl.pallas_call(
        functools.partial(middle_kernel, n, img),
        in_specs=[inner] * 6,
        out_specs=[inner, inner, anywhere, anywhere],
        out_shape=[
            jax.ShapeDtypeStruct((rows, width), SINGLE),
            jax.ShapeDtypeStruct((rows, width), SINGLE),
            jax.ShapeDtypeStruct((n, rows, width), HALF),
            jax.ShapeDtypeStruct((dp,) + fc2.shape, HALF),
        ],
        scratch_shapes=[pltpu.VMEM((rows, width), HALF)]
        + LineGather.scratch(n)
        + GroupGather.scratch(dp),
        compiler_params=remote(4),
        cost_estimate=cost(2 * rows * width * width, 100 * MEGA),
        name="middle_rows",
    )(mixture, x_loc, weight, bias, mods, fc2)


def by_distance(me, n, count):
    low = lax.min(me, n - 1 - me)
    near = lax.select(lax.rem(count, 2) == 1, lax.div(count + 1, 2), -lax.div(count, 2))
    far = lax.select(me < n - 1 - me, count - low, low - count)
    return me + lax.select(count <= 2 * low, near, far)


def mlp_kernel(n, img, tile, b_ref, e_loc, e_near, mod_ref, w1_ref, b1_ref, w2_ref,
    g_ref, dz_ref, dy_ref, db_ref, y_ref, sum_ref, gate_ref, acc_ref, out_ref, e_all, near_sem, *sems):
    step = pl.program_id(0)
    me = lax.axis_index("seq")
    owner = by_distance(me, n, step)
    e_ref = e_all.at[pl.ds(owner, 1)]
    gather = LineGather(n, e_near, e_all, *sems, first=1)
    own = pltpu.make_async_copy(e_loc, e_all.at[me], near_sem.at[2])

    def nears(action):
        for way, sign in ((0, 1), (1, -1)):
            block = me - sign

            @pl.when(both(block >= 0, block < n))
            def _():
                action(
                    pltpu.make_async_copy(e_near.at[way], e_all.at[block], near_sem.at[way])
                )

    def begin():
        greet(n, "near")
        gather.begin()
        own.start()
        nears(lambda copy: copy.start())
        own.wait()
        nears(lambda copy: copy.wait())

    at_step(step, 0, begin)
    for hop in range(1, n - 1):
        at_step(step, hop + 1, functools.partial(gather.arrive, hop))
    at_step(step, n - 1, gather.finish)
    units = g_ref.shape[2]

    @pl.when(step == 0)
    def _():
        sum_ref[...] = jnp.zeros_like(sum_ref)
        gate_ref[...] = jnp.zeros_like(gate_ref)

    for t, sl in ((0, slice(0, img)), (1, slice(img, b_ref.shape[1]))):
        rows = b_ref[0, sl]
        grad = (mod_ref[t, 5:6] * e_ref[0, sl].astype(SINGLE)).astype(HALF)
        dy_ref[0, sl] = grad

        for k in range(units // tile):
            here = slice(k * tile, (k + 1) * tile)
            cols = slice(t * units + k * tile, t * units + (k + 1) * tile)
            w1 = w1_ref[:, cols]
            pre = nn_dot(rows, w1) + b1_ref[t : t + 1, here]
            hidden, slope = gelu_both(pre)
            hidden = hidden.astype(HALF)
            g_ref[0, sl, here] = hidden
            w2 = w2_ref[:, cols]
            out = nt_dot(hidden, w2)
            dz = nn_dot(grad, w2) * slope
            sum_ref[t : t + 1, here] += jnp.sum(dz, axis=0, keepdims=True)
            dzh = dz.astype(HALF)
            dz_ref[0, sl, here] = dzh
            part = nt_dot(dzh, w1)
            if k == 0:
                acc_ref[sl] = part
                out_ref[sl] = out
            else:
                acc_ref[sl] += part
                out_ref[sl] += out
        db_ref[0, sl] = acc_ref[sl].astype(HALF)
        out = out_ref[sl]
        y_ref[0, sl] = out.astype(HALF)
        gate_ref[t : t + 1] += jnp.sum(out * e_ref[0, sl].astype(SINGLE), axis=0, keepdims=True)


def feed_forward(n, img, mlp_in, e_loc, e_near, mods, w1, b1, w2):
    rows, width = mlp_in.shape[1:]
    units = w1.shape[1] // 2
    tile = min(512, units)
    while units % tile:
        tile -= LANES

    def owned(columns):
        return pl.BlockSpec(
            (1, rows, columns), lambda k: (by_distance(lax.axis_index("seq"), n, k), 0, 0)
        )

    return pl.pallas_call(
        functools.partial(mlp_kernel, n, img, tile),
        grid=(n,),
        in_specs=[
            owned(width),
            pl.BlockSpec(memory_space=pl.ANY),
            pl.BlockSpec(memory_space=pl.ANY),
            whole(mods.shape),
            whole(w1.shape, True),
            whole(b1.shape),
            whole(w2.shape, True),
        ],
        out_specs=[
            owned(units),
            owned(units),
            owned(width),
            owned(width),
            owned(width),
            whole((2, units)),
            whole((2, width)),
        ],
        out_shape=[
            jax.ShapeDtypeStruct((n, rows, units), HALF),
            jax.ShapeDtypeStruct((n, rows, units), HALF),
            jax.ShapeDtypeStruct((n, rows, width), HALF),
            jax.ShapeDtypeStruct((n, rows, width), HALF),
            jax.ShapeDtypeStruct((n, rows, width), HALF),
            jax.ShapeDtypeStruct((2, units), SINGLE),
            jax.ShapeDtypeStruct((2, width), SINGLE),
        ],
        scratch_shapes=[
            pltpu.VMEM((rows, width), SINGLE),
            pltpu.VMEM((rows, width), SINGLE),
            pltpu.VMEM((n, rows, width), HALF),
            pltpu.SemaphoreType.DMA((3,)),
        ]
        + LineGather.scratch(n),
        compiler_params=remote(9, 60),
        cost_estimate=cost(6 * n * rows * width * units, 50 * MEGA, n * rows * units),
        name="feed_forward",
    )(mlp_in, e_loc, e_near, mods, w1, b1, w2)


def grads_kernel(n, img, plan, rounds, *refs):
    lefts = max(p[0] for p in plan) + 1
    rights = max(p[1] for p in plan) + 1
    l_refs, r_refs = refs[:lefts], refs[lefts : lefts + rights]
    rest = refs[lefts + rights :]
    step = pl.program_id(0)
    if rounds:
        parts, o_ref, tail, turned = rest[:4]
        line = LineSum(n, at_rows(parts), None, *rest[4:], stop=n - 2, tail=tail)

        def begin():
            greet(n, "near")
            line.round(0)

        at_step(step, 0, begin)
    else:
        o_ref, turned = rest
    tile = o_ref.shape[1]
    before = None
    for k, (left, right, stream, column) in enumerate(plan):

        @pl.when(step == k)
        def _():
            l_ref, r_ref = l_refs[left], r_refs[right]
            count, rows, _ = l_ref.shape
            sl = slice(0, img) if stream == 0 else slice(img, rows)
            size = count * (sl.stop - sl.start)
            if before != (left, stream):
                turned[:, :size] = l_ref[:, sl].reshape(size, l_ref.shape[2]).T
            values = r_ref[:, sl, column : column + tile].reshape(size, tile)
            o_ref[...] = nn_dot(turned[:, :size], values).astype(HALF)

        before = (left, stream)
    if rounds:
        for hop, when in enumerate(rounds):
            at_step(step, when, functools.partial(line.round, hop + 1))
        at_step(step, len(plan) - 1, line.close)


def weight_grads(n, img, lefts, rights, plan, tile, name, rounds=(), parts=None, collective=None):
    rows, depth = lefts[0].shape[1:]
    in_specs = [whole(a.shape, True) for a in (*lefts, *rights)]
    out_specs = [pl.BlockSpec((depth, tile), lambda k: (0, k))]
    out_shape = [jax.ShapeDtypeStruct((depth, len(plan) * tile), HALF)]
    longest = max(up(n * img, LANES), up(n * (rows - img), LANES))
    scratch = [pltpu.VMEM((depth, longest), HALF)]
    arrays = (*lefts, *rights)
    if rounds:
        anywhere = pl.BlockSpec(memory_space=pl.ANY)
        in_specs.append(anywhere)
        out_specs.append(anywhere)
        out_shape.append(jax.ShapeDtypeStruct((2,) + parts.shape[1:], HALF))
        scratch += LineSum.scratch(n, *parts.shape[1:], stop=n - 2)
        arrays += (parts,)
    return pl.pallas_call(
        functools.partial(grads_kernel, n, img, plan, rounds),
        grid=(len(plan),),
        in_specs=in_specs,
        out_specs=out_specs,
        out_shape=out_shape,
        scratch_shapes=scratch,
        compiler_params=remote(collective, 60) if rounds else params(60),
        cost_estimate=cost(2 * n * rows * depth * len(plan) * tile // 2, 60 * MEGA),
        name=name,
    )(*arrays)


def middle_back_kernel(
    n, img, part_ref, prev_ref, m_ref, y_ref, e_ref, w_ref, mod_ref, dm_ref, dy_ref, sum_ref, all_ref,
    db_ref, mix, send, recv, local, *line_scratch,
):
    me = lax.axis_index("seq")
    rows, width = m_ref.shape
    heads = w_ref.shape[3] // 2
    streams = ((0, slice(0, img)), (1, slice(img, rows)))
    greet(n, "all")
    line = LineSum(n, at_rows(part_ref), db_ref, *line_scratch, first=n - 2, prev=prev_ref)
    line.round(n - 2)
    if mix.shape[2] > heads:
        mix[...] = jnp.zeros_like(mix)
    line.finish()
    for t, sl in streams:
        grad_in = db_ref[sl]
        normed, inv_std = layer_norm(m_ref[sl])
        upstream = e_ref[sl].astype(SINGLE)
        grad_middle = upstream + norm_back(normed, inv_std, grad_in * (1.0 + mod_ref[t, 4:5]))
        dm_ref[sl] = grad_middle
        grad_attn = mod_ref[t, 2:3] * grad_middle
        dy_ref[sl] = grad_attn.astype(HALF)

        def total(value):
            return jnp.sum(value, axis=0, keepdims=True)

        sum_ref[t, 0:1] = total(grad_middle * y_ref[sl])
        sum_ref[t, 1:2] = total(grad_in)
        sum_ref[t, 2:3] = total(grad_in * normed)
        sum_ref[t, 3:4] = total(grad_attn)
        sum_ref[t, 4:5] = total(upstream)

    def exchange(peer, block):
        return pltpu.make_async_remote_copy(
            src_ref=mix.at[peer],
            dst_ref=all_ref.at[block],
            send_sem=send.at[peer],
            recv_sem=recv.at[block],
            device_id=on_line(peer),
            device_id_type=MESH,
        )

    keep = pltpu.make_async_copy(mix.at[me], all_ref.at[me], local)
    for peer in range(n):
        for t, sl in streams:
            mix[peer, sl, :heads] = nn_dot(dy_ref[sl], proj_columns(w_ref, peer, t)).astype(HALF)

        @pl.when(peer != me)
        def _():
            exchange(peer, me).start()

        @pl.when(peer == me)
        def _():
            keep.start()

    for peer in range(n):

        @pl.when(peer != me)
        def _():
            exchange(peer, peer).wait()

    keep.wait()


def middle_back(n, img, parts, prev, middle, attn_out, cot, weight, mods, lwp):
    rows, width = middle.shape
    inner = pl.BlockSpec(memory_space=pltpu.VMEM)
    anywhere = pl.BlockSpec(memory_space=pl.ANY)
    return pl.pallas_call(
        functools.partial(middle_back_kernel, n, img),
        in_specs=[anywhere, anywhere] + [inner] * 5,
        out_specs=[inner, inner, inner, anywhere],
        out_shape=[
            jax.ShapeDtypeStruct((rows, width), SINGLE),
            jax.ShapeDtypeStruct((rows, width), HALF),
            jax.ShapeDtypeStruct((2, 8, width), SINGLE),
            jax.ShapeDtypeStruct((n, rows, lwp), HALF),
        ],
        scratch_shapes=[
            pltpu.VMEM((rows, width), SINGLE),
            pltpu.VMEM((n, rows, lwp), HALF),
            pltpu.SemaphoreType.DMA((n,)),
            pltpu.SemaphoreType.DMA((n,)),
            pltpu.SemaphoreType.DMA,
        ]
        + LineSum.scratch(n, rows, width, first=n - 2),
        compiler_params=remote(5),
        cost_estimate=cost(2 * rows * width * width, 60 * MEGA),
        name="middle_back",
    )(parts, prev, middle, attn_out, cot, weight, mods)


def attn_in_kernel(
    n, img, dq_ref, dk_ref, dv_ref, x_ref, a_ref, w_ref, y_ref, prev_ref, p_ref,
    da_ref, sum_ref, g_ref, y_sum, p_sum, turned, p_own, *scratch,
):
    step = pl.program_id(0)
    count, rows, lw = dq_ref.shape
    line = LineSum(n, at_rows(y_ref), y_sum, *scratch[:6], first=n - 2, prev=prev_ref)
    wide = p_sum.shape[1]
    proj = LineSum(
        n,
        lambda owner: p_own.at[:, pl.ds(pl.multiple_of(owner * wide, LANES), wide)],
        p_sum,
        *scratch[6:12],
    )
    group = GroupLast(p_ref, *scratch[12:])
    streams = ((0, slice(0, img)), (1, slice(img, rows)))

    def begin():
        greet(n, "near", "paths")
        group.begin()
        line.round(n - 2)
        sum_ref[...] = jnp.zeros_like(sum_ref)

    at_step(step, 0, begin)

    @pl.when(step < n)
    def _():
        here = lax.min(step, n - 1)
        for t, sl in streams:
            part = None
            for c, ref in enumerate((dq_ref, dk_ref, dv_ref)):
                start = (3 * t + c) * lw
                term = nt_dot(ref[here, sl], w_ref[:, start : start + lw])
                part = term if part is None else part + term
            da_ref[0, sl] = part.astype(HALF)
            normed, _ = layer_norm(x_ref[0, sl].astype(SINGLE))
            sum_ref[t, 0:1] += jnp.sum(part, axis=0, keepdims=True)
            sum_ref[t, 1:2] += jnp.sum(part * normed, axis=0, keepdims=True)

    for t, sl in streams:
        size = count * (sl.stop - sl.start)
        for c, ref in enumerate((dq_ref, dk_ref, dv_ref)):

            @pl.when(step == n + 3 * t + c)
            def _():
                if c == 0:
                    turned[:, :size] = a_ref[:, sl].reshape(size, a_ref.shape[2]).T
                g_ref[...] = nn_dot(turned[:, :size], ref[:, sl].reshape(size, lw)).astype(HALF)

    half_rows = p_ref.shape[2]

    def store(half, value):
        p_own[half * half_rows : (half + 1) * half_rows] = value.astype(HALF)

    def hand_on():
        group.finish(store)
        proj.round(0)

    at_step(step, n - 1, hand_on)
    for hop in range(1, n - 1):
        at_step(step, min(n + 5, n - 1 + 3 * hop), functools.partial(proj.round, hop))

    def finish():
        line.finish()
        proj.finish()

    at_step(step, n + 5, finish)


def attn_in_back(n, img, dq, dk, dv, x_all, attn_in, weight, out_parts, running, proj):
    _, rows, lw = dq.shape
    width = x_all.shape[2]
    anywhere = pl.BlockSpec(memory_space=pl.ANY)
    row = pl.BlockSpec((1, rows, width), lambda k: (lax.min(k, n - 1), 0, 0))
    tall, wide = 2 * proj.shape[2], proj.shape[3] // n
    longest = max(up(n * img, LANES), up(n * (rows - img), LANES))
    return pl.pallas_call(
        functools.partial(attn_in_kernel, n, img),
        grid=(n + 6,),
        in_specs=[whole(dq.shape, True)] * 3
        + [row, whole(attn_in.shape, True), whole(weight.shape, True)]
        + [anywhere, anywhere, whole(proj.shape, True)],
        out_specs=[
            row,
            whole((2, 2, width)),
            pl.BlockSpec((width, lw), lambda k: (0, lax.max(k - n, 0))),
            whole((rows, width), True),
            whole((tall, wide), True),
        ],
        out_shape=[
            jax.ShapeDtypeStruct((n, rows, width), HALF),
            jax.ShapeDtypeStruct((2, 2, width), SINGLE),
            jax.ShapeDtypeStruct((width, 6 * lw), HALF),
            jax.ShapeDtypeStruct((rows, width), SINGLE),
            jax.ShapeDtypeStruct((tall, wide), SINGLE),
        ],
        scratch_shapes=[
            pltpu.VMEM((width, longest), HALF),
            pltpu.VMEM((tall, n * wide), HALF),
        ]
        + LineSum.scratch(n, rows, width, first=n - 2)
        + LineSum.scratch(n, tall, wide)
        + GroupLast.scratch(*proj.shape[2:]),
        compiler_params=remote(10, 62),
        cost_estimate=cost(12 * n * rows * width * lw, 30 * MEGA),
        name="attn_in_back",
    )(dq, dk, dv, x_all, attn_in, weight, out_parts, running, proj)


def end_kernel(
    n, dp, cut, parts, qkv_part, packed, extra, ada_ref,
    sum_ref, qkv_sum, every, cond_ref,
    z_got, row, c_part, c_got, c_all, z_send, z_recv, e_send, e_recv, c_send, c_recv, a_send, a_recv,
    *scratch,
):
    me, my = lax.axis_index("seq"), lax.axis_index("dp")
    depth = ada_ref.shape[0]
    span = packed.shape[2]
    greet(n, "all", "all")
    line = LineSum(n, at_rows(parts), sum_ref, *scratch[:6])
    group = GroupSum(qkv_part, *scratch[6:])
    mates, others = range(1, n), range(1, dp)
    z_go = [to_line(me, n, k, packed, z_got, z_send, z_recv) for k in mates]
    for copy in z_go:
        copy.start()
    group.begin()
    line.round(0)
    z_got[me] = packed[me]
    for copy in z_go:
        copy.wait_recv()
    row[:, :span] = jnp.sum(z_got[...], axis=0)
    row[:, span:] = extra[...]
    e_go = [to_group(my, dp, k, row, every, e_send, e_recv) for k in others]
    for copy in e_go:
        copy.start()
    every[my] = row[...]
    group.step(0)
    for copy in e_go:
        copy.wait_recv()
    product = nt_dot(every[:, 0, :cut].astype(HALF), ada_ref[...])
    c_part[...] = jnp.zeros_like(c_part)
    for k in range(dp):
        c_part[k, :, :depth] = product[k : k + 1]
    c_go = [to_group(my, dp, k, c_part, c_got, c_send, c_recv) for k in others]
    for copy in c_go:
        copy.start()
    c_got[my] = c_part[my]
    a_go = [to_line(me, n, k, c_got, c_all, a_send, a_recv) for k in mates]
    for hop in range(1, n - 1):
        line.round(hop)
        if hop == 1:
            for copy in c_go:
                copy.wait_recv()
            for copy in a_go:
                copy.start()
            c_all[me] = c_got[...]
        if hop < group.phases:
            group.step(hop)
    for number in range(max(n - 1, 1), group.phases):
        group.step(number)
    for copy in a_go:
        copy.wait_recv()
    cond_ref[...] = jnp.sum(c_all[...], axis=0)
    group.finish(qkv_sum)
    line.finish()
    for copy in z_go + e_go + c_go + a_go:
        copy.wait_send()


def end(n, dp, cut, parts, qkv_part, packed, extra, ada):
    rows, width = parts.shape[1:]
    depth = up(ada.shape[0], LANES)
    span = packed.shape[2] + extra.shape[1]
    inner = pl.BlockSpec(memory_space=pltpu.VMEM)
    anywhere = pl.BlockSpec(memory_space=pl.ANY)
    sems = [n - 1, n - 1, dp - 1, dp - 1, dp - 1, dp - 1, n - 1, n - 1]
    return pl.pallas_call(
        functools.partial(end_kernel, n, dp, cut),
        in_specs=[anywhere, anywhere, inner, inner, inner],
        out_specs=[inner] * 4,
        out_shape=[
            jax.ShapeDtypeStruct((rows, width), SINGLE),
            jax.ShapeDtypeStruct(qkv_part.shape[1:], SINGLE),
            jax.ShapeDtypeStruct((dp, 1, span), SINGLE),
            jax.ShapeDtypeStruct((dp, 1, depth), SINGLE),
        ],
        scratch_shapes=[
            pltpu.VMEM(packed.shape, SINGLE),
            pltpu.VMEM((1, span), SINGLE),
            pltpu.VMEM((dp, 1, depth), SINGLE),
            pltpu.VMEM((dp, 1, depth), SINGLE),
            pltpu.VMEM((n, dp, 1, depth), SINGLE),
        ]
        + [pltpu.SemaphoreType.DMA((k,)) for k in sems]
        + LineSum.scratch(n, rows, width)
        + GroupSum.scratch(dp, *qkv_part.shape[2:]),
        compiler_params=remote(7, 60),
        cost_estimate=cost(10**6, 100 * MEGA),
        name="end",
    )(parts, qkv_part, packed, extra, ada)


def rows_kernel(img, slots, da_ref, dm_ref, x_ref, m_ref, y_ref, mod_ref, shift_ref, live_ref, io_ref, to_ref, ig_ref, tg_ref):
    for t, sl, out_ref, grad_ref in (
        (0, slice(0, img), io_ref, ig_ref),
        (1, slice(img, x_ref.shape[0]), to_ref, tg_ref),
    ):
        keep = out_ref.shape[1]
        live = live_ref[sl]
        value = m_ref[sl] + mod_ref[t, 5:6] * (y_ref[sl] + shift_ref[t : t + 1])
        out_ref[0] = (value * live).astype(HALF)[:keep]
        normed, inv_std = layer_norm(x_ref[sl].astype(SINGLE))
        grad = dm_ref[sl] + norm_back(normed, inv_std, da_ref[sl] * (1.0 + mod_ref[t, 1:2]))
        grad_ref[0] = (grad * live)[:keep]


def rows_out(img, slots, grad_attn_in, grad_middle, x_loc, middle, mlp_sum, mods, fc2_shift, live):
    width = x_loc.shape[1]
    return pl.pallas_call(
        functools.partial(rows_kernel, img, slots),
        out_shape=[
            jax.ShapeDtypeStruct((1, img, width), HALF),
            jax.ShapeDtypeStruct((1, slots, width), HALF),
            jax.ShapeDtypeStruct((1, img, width), SINGLE),
            jax.ShapeDtypeStruct((1, slots, width), SINGLE),
        ],
        compiler_params=params(),
        cost_estimate=cost(10**6, 14 * MEGA),
        name="rows_out",
    )(grad_attn_in, grad_middle, x_loc, middle, mlp_sum, mods, fc2_shift, live)


def body(
    image_tokens,
    text_tokens,
    text_lengths,
    conditioning,
    ada_weight,
    ada_bias,
    qkv_weight,
    qv_bias,
    proj_weight,
    proj_bias,
    fc1_weight,
    fc1_bias,
    fc2_weight,
    fc2_bias,
    image_cotangent,
    text_cotangent,
):
    n = lax.axis_size("seq")
    dp = lax.axis_size("dp")
    img, width = image_tokens.shape[1:]
    slots = text_tokens.shape[1]
    pad = up(slots, 16)
    rows = img + pad
    depth = qkv_weight.shape[0]
    lw = qkv_weight.shape[3]
    lwp = up(lw, LANES)
    units = fc1_weight.shape[2]
    mod_cols = ada_weight.shape[2]
    my_seq = lax.axis_index("dp")

    def stacked(image, text):
        return jnp.concatenate([image, jnp.pad(text, ((0, pad - slots), (0, 0)))], axis=0)

    length = text_lengths[0, 0]
    live_text = (jnp.arange(slots, dtype=jnp.int32) < length)[:, None]
    x_loc = stacked(image_tokens[0], text_tokens[0])
    e_loc = stacked(
        image_cotangent[0], jnp.where(live_text, text_cotangent[0], jnp.zeros((), HALF))
    )

    def split(shard):
        return shard.reshape(2, -1, shard.shape[-1])

    qkv_local = jnp.pad(qkv_weight, ((0, 0), (0, 0), (0, 0), (0, lwp - lw))).reshape(depth, 6 * lwp)
    share = proj_weight.shape[0]
    proj_turned = proj_weight.transpose(2, 1, 0).reshape(depth, 2 * share)
    fc1_local = fc1_weight.reshape(depth, 2 * units)
    fc2_turned = fc2_weight.transpose(2, 1, 0).reshape(depth, 2 * units)

    cond_float = conditioning.astype(SINGLE)
    cond_act = jax.nn.silu(cond_float).astype(HALF)
    act_parts = jnp.pad(
        cond_act.astype(SINGLE).reshape(dp, 1, depth), ((0, 0), (0, 0), (0, up(depth, LANES) - depth))
    )
    ada_flat = ada_weight.reshape(depth, 2 * mod_cols)
    bias_cols = proj_bias.shape[1]
    cut = 2 * mod_cols
    side = jnp.concatenate(
        [
            ada_bias.astype(SINGLE).reshape(-1),
            proj_bias.astype(SINGLE).reshape(-1),
            fc2_bias.astype(SINGLE).reshape(-1),
            jnp.full((LANES,), length.astype(SINGLE)),
        ]
    )[None]
    proj_line = lax.all_gather(proj_turned, "seq", axis=0, tiled=False)
    x_all, side_all, acts, qkv_full, fc1_full = start(
        n, dp, x_loc, act_parts, ada_flat, side, split(qkv_local), split(fc1_local)
    )
    qkv_full = qkv_full.reshape(width, 6 * lwp)
    fc1_full = fc1_full.reshape(width, 2 * units)
    act_slice = acts[:, 0, :depth].astype(HALF)
    side_all = side_all[:, 0]

    def columns(begin, cols):
        return side_all[:, begin : begin + 2 * cols].reshape(n, 2, cols).transpose(1, 0, 2)

    mods = jnp.pad(columns(0, mod_cols).reshape(2, 6, width), ((0, 0), (0, 2), (0, 0)))
    proj_shift = columns(cut, bias_cols).reshape(2, width)
    fc2_shift = columns(cut + 2 * bias_cols, bias_cols).reshape(2, width)
    lengths_all = side_all[:, cut + 4 * bias_cols]

    slot = jnp.arange(rows, dtype=SINGLE)[None, :] - img
    live = jnp.logical_or(slot < 0, jnp.logical_and(slot < lengths_all[:, None], slot < slots))
    mask = jnp.where(live, SINGLE(0), SINGLE(MASKED))
    mask_row = mask.reshape(1, n * rows)
    mask_col = jnp.broadcast_to(mask[:, :, None], (n, rows, LANES))
    live_loc = jnp.concatenate(
        [jnp.ones((img, 1), SINGLE), jnp.pad(live_text.astype(SINGLE), ((0, pad - slots), (0, 0)))]
    )

    bias_rows = jnp.stack(
        [qv_bias[:, 0], jnp.zeros_like(qv_bias[:, 0]), qv_bias[:, 1]], axis=1
    ).astype(SINGLE)
    bias_rows = jnp.pad(bias_rows, ((0, 0), (0, 0), (0, lwp - lw))).reshape(2, 3 * lwp)
    attn_in, qkv_rows = project_qkv(n, img, x_all, mods, qkv_full, bias_rows)
    mixture, lse, e_near, mix_loc, proj_full = attend(
        n, dp, qkv_rows, mask_row, e_loc, split(proj_line)
    )
    proj_full = proj_full.reshape(dp, n, depth, 2 * share)

    attn_out, middle, mlp_in, fc2_full = middle_rows(
        n, dp, img, mix_loc, x_loc, proj_full, proj_shift, mods, split(fc2_turned)
    )
    fc2_full = fc2_full.reshape(width, 2 * units)
    hidden, grad_pre, grad_mlp, mlp_in_part, mlp_out_part, fc1_bias_part, gate_two_part = (
        feed_forward(
            n, img, mlp_in, e_loc, e_near, mods, fc1_full, fc1_bias.astype(SINGLE), fc2_full
        )
    )
    tile = units // 4 if units % (4 * LANES) == 0 else units // 2
    tiles = units // tile
    fc_plan = [(w, w, t, k * tile) for w in range(2) for t in range(2) for k in range(tiles)]
    fc_rounds = [(k + 1) * 4 * tiles * 2 // (3 * (n - 2)) for k in range(n - 3)]
    fc_part, running = weight_grads(
        n, img, (mlp_in, grad_mlp), (grad_pre, hidden), fc_plan, tile, "fc_grads", fc_rounds, mlp_in_part, 6
    )
    fc_sum = lax.psum_scatter(fc_part, "dp", scatter_dimension=0, tiled=True)

    grad_middle, grad_attn, sums, grad_mix = middle_back(
        n, img, mlp_in_part, running, middle, attn_out, e_loc, proj_full, mods, lwp
    )
    grad_q, grad_k, grad_v, q_bias_part, v_bias_part, proj_rest, out_running = attend_back(
        n, dp, img, qkv_rows, mixture, grad_mix, lse, mask_col, mlp_out_part, grad_attn, mix_loc
    )
    attn_in_part, mod_one, qkv_part, mlp_sum, proj_own = attn_in_back(
        n,
        img,
        grad_q,
        grad_k,
        grad_v,
        x_all,
        attn_in,
        qkv_full,
        mlp_out_part,
        out_running,
        proj_rest,
    )
    fc1_sum, fc2_sum = fc_sum[:, : 2 * units], fc_sum[:, 2 * units :]

    upstream_sum = sums[:, 4]
    gate_two = gate_two_part + fc2_shift * upstream_sum
    mod_grads = jnp.stack(
        [mod_one[:, 0], mod_one[:, 1], sums[:, 0], sums[:, 1], sums[:, 2], gate_two], axis=1
    ).reshape(2, n, mod_cols)
    rest = jnp.stack([sums[:, 3], mods[:, 5] * upstream_sum]).reshape(4, n, bias_cols)
    packed = jnp.concatenate(
        [
            mod_grads.transpose(1, 0, 2).reshape(n, -1),
            rest.transpose(1, 0, 2).reshape(n, -1),
        ],
        axis=1,
    )
    q_bias = q_bias_part.transpose(1, 0, 2).reshape(2, lwp)[:, :lw]
    v_bias = v_bias_part.transpose(1, 0, 2).reshape(2, lwp)[:, :lw]
    extra = jnp.concatenate(
        [jnp.stack([q_bias, v_bias], axis=1).reshape(-1), fc1_bias_part.reshape(-1)]
    )
    grad_attn_in, qkv_sum, every, cond_sum = end(
        n,
        dp,
        cut,
        attn_in_part,
        qkv_part.reshape(dp, 2, depth // 2, 6 * lwp),
        packed[:, None],
        extra[None],
        ada_flat,
    )
    every = every[:, 0]
    total = jnp.sum(every, axis=0)

    image_out, text_out, image_grad, text_grad = rows_out(
        img, slots, grad_attn_in, grad_middle, x_loc, middle, mlp_sum, mods, fc2_shift, live_loc
    )

    mod_half = every[:, :cut].astype(HALF).reshape(dp, 2, mod_cols)
    ada_grad = jnp.einsum("nd,ntc->dtc", act_slice, mod_half, preferred_element_type=SINGLE)
    ada_bias_grad = total[:cut].reshape(2, mod_cols)
    proj_bias_grad = total[cut : cut + 2 * bias_cols].reshape(2, bias_cols)
    fc2_bias_grad = total[cut + 2 * bias_cols : cut + 4 * bias_cols].reshape(2, bias_cols)
    after = cut + 4 * bias_cols
    qv_bias_grad = total[after : after + 4 * lw].reshape(2, 2, lw)
    fc1_bias_grad = total[after + 4 * lw :].reshape(2, units)
    cond_grad = cond_sum[:, 0, :depth].reshape(1, width) * silu_slope(cond_float)

    def streams(flat, last):
        return flat.astype(SINGLE).reshape(depth, 2, last)

    qkv_grad = qkv_sum.reshape(depth, 2, 3, lwp)[..., :lw]
    fc2_grad = streams(fc2_sum, units).transpose(2, 1, 0)
    proj_grad = proj_own.reshape(depth, 2, lwp)[..., :share].transpose(2, 1, 0)
    return (
        image_out,
        text_out,
        image_grad,
        text_grad,
        cond_grad,
        ada_grad,
        ada_bias_grad,
        qkv_grad,
        qv_bias_grad,
        proj_grad,
        proj_bias_grad,
        streams(fc1_sum, units),
        fc1_bias_grad,
        fc2_grad,
        fc2_bias_grad,
    )


def solution(mesh):
    in_specs = (
        P("dp", "seq", None),
        P("dp", "seq", None),
        P("dp", "seq"),
        P("dp", None),
        P("dp", None, "seq"),
        P(None, "seq"),
        P("dp", None, None, "seq"),
        P(None, None, "seq"),
        P("seq", None, "dp"),
        P(None, "seq"),
        P("dp", None, "seq"),
        P(None, "seq"),
        P("seq", None, "dp"),
        P(None, "seq"),
        P("dp", "seq", None),
        P("dp", "seq", None),
    )
    out_specs = (
        P("dp", "seq", None),
        P("dp", "seq", None),
        P("dp", "seq", None),
        P("dp", "seq", None),
        P("dp", None),
        P("dp", None, "seq"),
        P(None, "seq"),
        P("dp", None, None, "seq"),
        P(None, None, "seq"),
        P("seq", None, "dp"),
        P(None, "seq"),
        P("dp", None, "seq"),
        P(None, "seq"),
        P("seq", None, "dp"),
        P(None, "seq"),
    )
    return jax.shard_map(body, mesh=mesh, in_specs=in_specs, out_specs=out_specs, check_vma=False)
```

```python
import functools
import math

import jax
import jax.numpy as jnp
from jax import lax
from jax.experimental import pallas as pl
from jax.experimental.pallas import tpu as pltpu
from jax.sharding import PartitionSpec as P

HD = 64
LANES = 128
EPSILON = 1e-06
GELU_ROOT = math.sqrt(2.0 / math.pi)
GELU_CUBE = 0.044715
MASKED = -1e30
SINGLE = jnp.float32
HALF = jnp.bfloat16
MEGA = 2**20


def up(value, multiple):
    return -(-value // multiple) * multiple


def params(limit=56):
    return pltpu.CompilerParams(vmem_limit_bytes=limit * MEGA)


def remote(collective, limit=56):
    return pltpu.CompilerParams(
        collective_id=collective, has_side_effects=True, vmem_limit_bytes=limit * MEGA
    )


def cost(flops, nbytes, trans=0):
    return pl.CostEstimate(flops=int(flops), bytes_accessed=int(nbytes), transcendentals=int(trans))


def nt_dot(a, b):
    return lax.dot_general(a, b, (((1,), (1,)), ((), ())), preferred_element_type=SINGLE)


def tn_dot(a, b):
    return lax.dot_general(a, b, (((0,), (0,)), ((), ())), preferred_element_type=SINGLE)


def nn_dot(a, b):
    return jnp.dot(a, b, preferred_element_type=SINGLE)


def layer_norm(values):
    center = values - jnp.mean(values, axis=-1, keepdims=True)
    inv_std = lax.rsqrt(jnp.mean(center * center, axis=-1, keepdims=True) + EPSILON)
    return (center * inv_std, inv_std)


def norm_back(normed, inv_std, upstream):
    first = jnp.mean(upstream, axis=-1, keepdims=True)
    second = jnp.mean(upstream * normed, axis=-1, keepdims=True)
    return inv_std * (upstream - first - normed * second)


def gelu_both(values):
    square = values * values
    inner = GELU_ROOT * (values + GELU_CUBE * square * values)
    tangent = jnp.tanh(inner)
    half = 0.5 * (1.0 + tangent)
    slope = half + 0.5 * values * (1.0 - tangent * tangent) * GELU_ROOT * (
        1.0 + 3.0 * GELU_CUBE * square
    )
    return values * half, slope


def silu_slope(values):
    sigma = jax.nn.sigmoid(values)
    return sigma + values * sigma * (1.0 - sigma)


def whole(shape, single=False):
    zeros = (0,) * len(shape)
    if single:
        return pl.BlockSpec(shape, lambda *_: zeros, pipeline_mode=pl.Buffered(1))
    return pl.BlockSpec(shape, lambda *_: zeros)


def rows_spec(rows, width):
    return pl.BlockSpec((1, rows, width), lambda s: (s, 0, 0))


MESH = pl.DeviceIdType.MESH


def on_line(position):
    return {"seq": position}


def both(first, second):
    return jnp.logical_and(first, second)


def flip(value, mask):
    bit = 1
    while bit <= mask:
        if mask & bit:
            value = value + bit - 2 * bit * lax.rem(lax.div(value, bit), 2)
        bit *= 2
    return value


def greet(n, line=None, group=None):
    me, my = lax.axis_index("seq"), lax.axis_index("dp")
    dp = lax.axis_size("dp")
    barrier = pltpu.get_barrier_semaphore()
    peers = []
    if line == "all":
        peers += [on_line(lax.rem(me + offset, n)) for offset in range(1, n)]
    if group == "all":
        peers += [{"dp": lax.rem(my + offset, dp)} for offset in range(1, dp)]
    if group == "paths":
        peers += [{"dp": flip(my, 1)}] + [{"dp": flip(my, mask)} for mask in masks_of(dp)]
    for peer in peers:
        pl.semaphore_signal(barrier, inc=1, device_id=peer, device_id_type=MESH)
    if line == "near":
        for sign in (1, -1):
            near = me + sign

            @pl.when(both(near >= 0, near < n))
            def _():
                pl.semaphore_signal(barrier, inc=1, device_id=on_line(near), device_id_type=MESH)

    count = len(peers)
    if line == "near":
        count = count + lax.min(me, 1) + lax.min(n - 1 - me, 1)
    pl.semaphore_wait(barrier, count)


def masks_of(dp):
    masks, bit = [], 2
    while bit < dp:
        masks.append(bit)
        bit *= 2
    return masks


class GroupGather:
    def __init__(self, src, out, send, recv, pass_send, pass_recv, local):
        self.src, self.out = src, out
        self.send, self.recv, self.local = send, recv, local
        self.pass_send, self.pass_recv = pass_send, pass_recv
        self.my = lax.axis_index("dp")
        masks = masks_of(out.shape[0])
        self.orders = (masks, masks[::-1])
        self.phases = len(masks)

    @staticmethod
    def scratch(dp):
        return [pltpu.SemaphoreType.DMA((2, dp // 2)) for _ in range(4)] + [
            pltpu.SemaphoreType.DMA
        ]

    def span(self, half, count):
        mask = 0
        for k in range(self.phases):
            if count >> k & 1:
                mask |= self.orders[half][k]
        return mask

    def copy(self, half, phase, count, block):
        src = self.src.at[half] if count == 0 else self.out.at[block, half]
        index = 2**phase - 1 + count
        return pltpu.make_async_remote_copy(
            src_ref=src,
            dst_ref=self.out.at[block, half],
            send_sem=self.send.at[half, index],
            recv_sem=self.recv.at[half, index],
            device_id={"dp": flip(self.my, self.orders[half][phase])},
            device_id_type=MESH,
        )

    def hand(self, half, index, block, own=False):
        src = self.src.at[half] if own else self.out.at[block, half]
        return pltpu.make_async_remote_copy(
            src_ref=src,
            dst_ref=self.out.at[block, half],
            send_sem=self.pass_send.at[half, index],
            recv_sem=self.pass_recv.at[half, index],
            device_id={"dp": flip(self.my, 1)},
            device_id_type=MESH,
        )

    def begin(self):
        for phase in range(self.phases):
            for half in range(2):
                self.copy(half, phase, 0, self.my).start()
        for half in range(2):
            self.hand(half, 0, self.my, True).start()
        pltpu.make_async_copy(self.src, self.out.at[self.my], self.local).start()

    def arrive(self, phase):
        for half in range(2):
            mask = self.orders[half][phase]
            for count in range(2**phase):
                block = flip(self.my, mask ^ self.span(half, count))
                self.copy(half, phase, count, block).wait_recv()
            if phase + 1 < self.phases:
                for count in range(1, 2 ** (phase + 1)):
                    block = flip(self.my, self.span(half, count))
                    self.copy(half, phase + 1, count, block).start()
            for count in range(2**phase):
                block = flip(self.my, mask ^ self.span(half, count))
                self.hand(half, 2**phase + count, block).start()

    def finish(self):
        pltpu.make_async_copy(self.src, self.out.at[self.my], self.local).wait()
        other = flip(self.my, 1)
        for half in range(2):
            self.hand(half, 0, other, True).wait()
            for phase in range(self.phases):
                mask = self.orders[half][phase]
                for count in range(2**phase):
                    self.copy(half, phase, count, self.my).wait_send()
                    block = flip(other, mask ^ self.span(half, count))
                    self.hand(half, 2**phase + count, block).wait()


class GroupSum:
    def __init__(self, part, got, hold, passed, came, pass_send, pass_recv, send, recv, load):
        self.part, self.got, self.hold, self.passed, self.came = part, got, hold, passed, came
        self.pass_send, self.pass_recv = pass_send, pass_recv
        self.send, self.recv, self.load = send, recv, load
        self.my = lax.axis_index("dp")
        self.dp = part.shape[0]
        masks = masks_of(self.dp)
        self.orders = (masks, masks[::-1])
        self.phases = len(masks)

    @staticmethod
    def scratch(dp, rows, width):
        half = dp // 2
        return [
            pltpu.VMEM((2, half, rows, width), HALF),
            pltpu.VMEM((2, half, rows, width), HALF),
            pltpu.VMEM((2, half - 1, rows, width), HALF),
            pltpu.VMEM((2, half - 1, rows, width), HALF),
        ] + [pltpu.SemaphoreType.DMA((2, half)) for _ in range(5)]

    @staticmethod
    def scratch_inner(dp, rows, width):
        full = GroupSum.scratch(dp, rows, width)
        return full[:1] + full[2:8]

    def span(self, half, count):
        mask = 0
        for k in range(self.phases):
            if count >> k & 1:
                mask |= self.orders[half][k]
        return mask

    def hand(self, half, count):
        block = flip(self.my, 1 ^ self.span(half, count))
        return pltpu.make_async_remote_copy(
            src_ref=self.part.at[block, half],
            dst_ref=self.got.at[half, count],
            send_sem=self.pass_send.at[half, count],
            recv_sem=self.pass_recv.at[half, count],
            device_id={"dp": flip(self.my, 1)},
            device_id_type=MESH,
        )

    def fetch(self, half, count):
        block = flip(self.my, self.span(half, count))
        return pltpu.make_async_copy(
            self.part.at[block, half], self.hold.at[half, count], self.load.at[half, count]
        )

    def copy(self, half, phase, index):
        return pltpu.make_async_remote_copy(
            src_ref=self.passed.at[half, 2**phase + index - 1],
            dst_ref=self.came.at[half, 2**phase - 1 + index],
            send_sem=self.send.at[half, 2**phase - 1 + index],
            recv_sem=self.recv.at[half, 2**phase - 1 + index],
            device_id={"dp": flip(self.my, self.orders[half][phase])},
            device_id_type=MESH,
        )

    def every(self):
        return [(half, count) for half in range(2) for count in range(self.dp // 2)]

    def begin(self):
        for half, count in self.every():
            self.hand(half, count).start()
            if self.hold is not None:
                self.fetch(half, count).start()

    def value(self, half, count, phase):
        if self.hold is None:
            mine = self.part[flip(self.my, self.span(half, count)), half]
        else:
            mine = self.hold[half, count]
        total = mine.astype(SINGLE) + self.got[half, count].astype(SINGLE)
        for later in range(phase, self.phases):
            total = total + self.came[half, 2**later - 1 + count].astype(SINGLE)
        return total

    def step(self, number):
        if number == 0:
            for half, count in self.every():
                if self.hold is not None:
                    self.fetch(half, count).wait()
                self.hand(half, count).wait_recv()
        else:
            self.took(self.phases - number)
        phase = self.phases - 1 - number
        for half in range(2):
            for index in range(2**phase):
                count = 2**phase + index
                self.passed[half, count - 1] = self.value(half, count, phase + 1).astype(HALF)
                self.copy(half, phase, index).start()

    def took(self, phase):
        for half in range(2):
            for index in range(2**phase):
                self.copy(half, phase, index).wait_recv()

    def finish(self, out):
        self.took(0)
        for half in range(2):
            out[half] = self.value(half, 0, 0).astype(out.dtype)
        self.sent(0)

    def close(self, rest):
        self.took(1)
        for half in range(2):
            for count in range(2):
                rest[half, count] = self.value(half, count, 1).astype(rest.dtype)
        self.sent(1)

    def sent(self, first):
        for half, count in self.every():
            self.hand(half, count).wait_send()
        for phase in range(first, self.phases):
            for half in range(2):
                for index in range(2**phase):
                    self.copy(half, phase, index).wait_send()


class GroupLast:
    def __init__(self, rest, came, send, recv):
        self.rest, self.came, self.send, self.recv = rest, came, send, recv
        masks = masks_of(lax.axis_size("dp"))
        self.partners = [flip(lax.axis_index("dp"), mask) for mask in (masks[0], masks[-1])]

    @staticmethod
    def scratch(rows, width):
        return [pltpu.VMEM((2, rows, width), HALF)] + [pltpu.SemaphoreType.DMA((2,))] * 2

    def copy(self, half):
        return pltpu.make_async_remote_copy(
            src_ref=self.rest.at[half, 1],
            dst_ref=self.came.at[half],
            send_sem=self.send.at[half],
            recv_sem=self.recv.at[half],
            device_id={"dp": self.partners[half]},
            device_id_type=MESH,
        )

    def begin(self):
        for half in range(2):
            self.copy(half).start()

    def finish(self, store):
        for half in range(2):
            self.copy(half).wait()
            store(half, self.rest[half, 0].astype(SINGLE) + self.came[half].astype(SINGLE))


class LineGather:
    def __init__(self, n, src, out, send, recv, local, first=0, stop=None, land=None):
        self.n, self.src, self.out, self.land = n, src, out, land
        self.send, self.recv, self.local = send, recv, local
        self.first, self.stop = first, n - 1 if stop is None else stop
        self.me = lax.axis_index("seq")

    @staticmethod
    def scratch(n):
        return [
            pltpu.SemaphoreType.DMA((2, n - 1)),
            pltpu.SemaphoreType.DMA((2, n - 1)),
            pltpu.SemaphoreType.DMA,
        ]

    def inside(self, position):
        return both(position >= 0, position < self.n)

    def copy(self, way, hop, block, near):
        if hop > self.first:
            src = self.out.at[block]
        else:
            src = self.src if hop == 0 else self.src.at[way]
        return pltpu.make_async_remote_copy(
            src_ref=src,
            dst_ref=self.out.at[block] if self.land is None else self.land.at[way],
            send_sem=self.send.at[way, hop],
            recv_sem=self.recv.at[way, hop],
            device_id=on_line(near),
            device_id_type=MESH,
        )

    def each(self, hop):
        for way, sign in ((0, 1), (1, -1)):
            yield way, sign, self.me - sign * hop, self.me + sign

    def begin(self):
        self.launch(self.first)

    def launch(self, hop):
        for way, sign, block, near in self.each(hop):

            @pl.when(both(self.inside(block), self.inside(near)))
            def _():
                self.copy(way, hop, block, near).start()

    def keep(self):
        return pltpu.make_async_copy(self.src, self.out.at[self.me], self.local)

    def arrive(self, hop):
        for way, sign, block, near in self.each(hop + 1):

            @pl.when(self.inside(block))
            def _():
                self.copy(way, hop, block, near).wait_recv()

        if hop + 1 < self.stop:
            self.launch(hop + 1)

    def finish(self):
        for hop in range(self.first, self.stop):
            for way, sign, block, near in self.each(hop):

                @pl.when(both(self.inside(block), self.inside(near)))
                def _():
                    self.copy(way, hop, block, near).wait_send()


class LineSum:
    def __init__(self, n, part, out, got, mine, passed, send, recv, load, first=0, stop=None, tail=None, prev=None):
        self.n, self.part, self.out = n, part, out
        self.got, self.mine, self.passed = got, mine, passed
        self.send, self.recv, self.load = send, recv, load
        self.first, self.stop = first, n - 1 if stop is None else stop
        self.tail, self.prev = tail, prev
        self.me = lax.axis_index("seq")

    @staticmethod
    def scratch(n, rows, width, first=0, stop=None):
        stop = n - 1 if stop is None else stop
        return [
            pltpu.VMEM((2, stop - first + (first > 0), rows, width), HALF),
            pltpu.VMEM((2, rows, width), HALF),
            pltpu.VMEM((2, max(stop - max(first, 1), 1), rows, width), HALF),
            pltpu.SemaphoreType.DMA((2, n - 1)),
            pltpu.SemaphoreType.DMA((2, n - 1)),
            pltpu.SemaphoreType.DMA((2, 2)),
        ]

    def inside(self, position):
        return both(position >= 0, position < self.n)

    def each(self, step):
        reach = self.n - 1 - step
        for way, sign in ((0, 1), (1, -1)):
            yield way, self.me + sign * reach, self.me + sign, self.me - sign

    def slot(self, way, step):
        return self.passed.at[way, max(step - max(self.first, 1), 0)]

    def copy(self, way, step, src, near):
        if self.tail is not None and step == self.stop - 1:
            dst = self.tail.at[way]
        else:
            dst = self.got.at[way, step - self.first]
        return pltpu.make_async_remote_copy(
            src_ref=src,
            dst_ref=dst,
            send_sem=self.send.at[way, step],
            recv_sem=self.recv.at[way, step],
            device_id=on_line(near),
            device_id_type=MESH,
        )

    def round(self, step):
        for way, owner, near, behind in self.each(step):
            if step == 0:

                @pl.when(self.inside(owner))
                def _():
                    self.copy(way, step, self.part(owner), near).start()

                continue

            @pl.when(both(self.inside(owner), jnp.logical_not(self.inside(behind))))
            def _():
                self.copy(way, step, self.part(owner), near).start()

            @pl.when(both(self.inside(owner), self.inside(behind)))
            def _():
                fetch = pltpu.make_async_copy(
                    self.part(owner), self.mine.at[way], self.load.at[way, 0]
                )
                fetch.start()
                slot = self.slot(way, step)
                if step == self.first:
                    index = self.stop - self.first
                    held = pltpu.make_async_copy(
                        self.prev.at[way], self.got.at[way, index], self.load.at[way, 1]
                    )
                    held.start()
                    held.wait()
                else:
                    index = step - 1 - self.first
                    self.copy(way, step - 1, slot, near).wait_recv()
                fetch.wait()
                total = self.mine[way].astype(SINGLE) + self.got[way, index].astype(SINGLE)
                self.passed[way, step - max(self.first, 1)] = total.astype(HALF)
                self.copy(way, step, slot, near).start()

    def sent(self):
        for step in range(self.first, self.stop):
            for way, owner, near, behind in self.each(step):

                @pl.when(self.inside(owner))
                def _():
                    self.copy(way, step, self.slot(way, step), near).wait_send()

    def close(self):
        last = self.stop - 1
        for way, owner, near, behind in self.each(last + 1):

            @pl.when(both(self.inside(owner), self.inside(behind)))
            def _():
                self.copy(way, last, self.slot(way, last), near).wait_recv()

        self.sent()

    def finish(self):
        last = self.n - 2
        fetch = pltpu.make_async_copy(self.part(self.me), self.mine.at[0], self.load.at[0, 0])
        fetch.start()
        fetch.wait()
        self.out[...] = self.mine[0].astype(SINGLE)
        for way, owner, near, behind in self.each(last):

            @pl.when(self.inside(behind))
            def _():
                self.copy(way, last, self.slot(way, last), near).wait_recv()
                self.out[...] += self.got[way, last - self.first].astype(SINGLE)

        self.sent()


def at_rows(ref):
    return lambda owner: ref.at[owner]


def at_step(step, when, action):
    @pl.when(step == when)
    def _():
        action()


def to_group(my, dp, offset, src, dst, send, recv):
    peer = lax.rem(my + offset, dp)
    return pltpu.make_async_remote_copy(
        src_ref=src if src.shape == dst.shape[1:] else src.at[peer],
        dst_ref=dst.at[my],
        send_sem=send.at[offset - 1],
        recv_sem=recv.at[offset - 1],
        device_id={"dp": peer},
        device_id_type=MESH,
    )


def to_line(me, n, offset, src, dst, send, recv):
    peer = lax.rem(me + offset, n)
    return pltpu.make_async_remote_copy(
        src_ref=src if src.shape == dst.shape[1:] else src.at[peer],
        dst_ref=dst.at[me],
        send_sem=send.at[offset - 1],
        recv_sem=recv.at[offset - 1],
        device_id=on_line(peer),
        device_id_type=MESH,
    )


def start_kernel(
    n, dp, x_ref, cond_ref, ada_ref, ada_bias, proj_bias, fc2_bias, length_ref, qkv_ref, fc1_ref,
    x_all, side_all, acts, mods, shifts, qkv_all, fc1_all,
    act_ref, part, parts, row, a_send, a_recv, p_send, p_recv, s_send, s_recv, *sems,
):
    me, my = lax.axis_index("seq"), lax.axis_index("dp")
    depth, _, cols = ada_ref.shape
    width = x_ref.shape[1]
    greet(n, "all", "all")
    gather = LineGather(n, x_ref, x_all, *sems[:3])
    qkv = GroupGather(qkv_ref, qkv_all, *sems[3:8])
    fc1 = GroupGather(fc1_ref, fc1_all, *sems[8:13])
    gather.begin()
    cond = cond_ref[...].astype(SINGLE)
    act = (cond / (1.0 + jnp.exp(-cond))).astype(HALF).astype(SINGLE)
    act_ref[...] = jnp.zeros_like(act_ref)
    for k in range(dp):
        act_ref[k, :, :depth] = act[:, k * depth : (k + 1) * depth]
    others = range(1, dp)
    act_go = [to_group(my, dp, k, act_ref, acts, a_send, a_recv) for k in others]
    for copy in act_go:
        copy.start()
    gather.keep().start()
    acts[my] = act_ref[my]
    for copy in act_go:
        copy.wait_recv()
    rows = acts[:, 0, :depth].astype(HALF)
    for t in range(2):
        product = nn_dot(rows, ada_ref[:, t, :])
        for k in range(dp):
            part[k, :, t * cols : (t + 1) * cols] = product[k : k + 1]
    part_go = [to_group(my, dp, k, part, parts, p_send, p_recv) for k in others]
    for copy in part_go:
        copy.start()
    parts[my] = part[my]
    place = 0
    for ref in (ada_bias, proj_bias, fc2_bias):
        for t in range(2):
            size = ref.shape[1]
            row[:, place : place + size] = ref[t : t + 1].astype(SINGLE)
            place += size
    row[:, place:] = jnp.full((1, LANES), length_ref[0, 0].astype(SINGLE))
    for copy in part_go:
        copy.wait_recv()
    qkv.begin()
    fc1.begin()
    row[:, : 2 * cols] += jnp.sum(parts[...], axis=0)
    row_go = [to_line(me, n, k, row, side_all, s_send, s_recv) for k in range(1, n)]
    for copy in row_go:
        copy.start()
    side_all[me] = row[...]
    for hop in range(max(n - 1, qkv.phases)):
        if hop < n - 1:
            gather.arrive(hop)
        if hop < qkv.phases:
            qkv.arrive(hop)
            fc1.arrive(hop)
    for copy in row_go:
        copy.wait()
    mods[...] = jnp.zeros_like(mods)
    piece = math.gcd(cols, width)
    share = proj_bias.shape[1]
    for z in range(n):
        for t in range(2):
            for start in range(0, cols, piece):
                to, at = divmod(z * cols + start, width)
                mods[t, to : to + 1, at : at + piece] = side_all[
                    z, :, t * cols + start : t * cols + start + piece
                ]
        for k in range(4):
            start = 2 * cols + k * share
            shifts[k : k + 1, z * share : (z + 1) * share] = side_all[z, :, start : start + share]
    for copy in act_go + part_go:
        copy.wait_send()
    gather.keep().wait()
    gather.finish()
    qkv.finish()
    fc1.finish()


def start(n, dp, x_loc, cond, ada, ada_bias, proj_bias, fc2_bias, length, qkv, fc1):
    rows, width = x_loc.shape
    depth, _, cols = ada.shape
    span = 2 * cols + 4 * proj_bias.shape[1] + LANES
    anywhere = pl.BlockSpec(memory_space=pl.ANY)
    inner = pl.BlockSpec(memory_space=pltpu.VMEM)
    scalar = pl.BlockSpec(memory_space=pltpu.SMEM)
    return pl.pallas_call(
        functools.partial(start_kernel, n, dp),
        in_specs=[inner] * 6 + [scalar, inner, inner],
        out_specs=[anywhere, inner, inner, inner, inner, anywhere, anywhere],
        out_shape=[
            jax.ShapeDtypeStruct((n, rows, width), HALF),
            jax.ShapeDtypeStruct((n, 1, span), SINGLE),
            jax.ShapeDtypeStruct((dp, 1, up(depth, LANES)), SINGLE),
            jax.ShapeDtypeStruct((2, 8, width), SINGLE),
            jax.ShapeDtypeStruct((4, width), SINGLE),
            jax.ShapeDtypeStruct((dp,) + qkv.shape, HALF),
            jax.ShapeDtypeStruct((dp,) + fc1.shape, HALF),
        ],
        scratch_shapes=[
            pltpu.VMEM((dp, 1, up(depth, LANES)), SINGLE),
            pltpu.VMEM((dp, 1, 2 * cols), SINGLE),
            pltpu.VMEM((dp, 1, 2 * cols), SINGLE),
            pltpu.VMEM((1, span), SINGLE),
            pltpu.SemaphoreType.DMA((dp - 1,)),
            pltpu.SemaphoreType.DMA((dp - 1,)),
            pltpu.SemaphoreType.DMA((dp - 1,)),
            pltpu.SemaphoreType.DMA((dp - 1,)),
            pltpu.SemaphoreType.DMA((n - 1,)),
            pltpu.SemaphoreType.DMA((n - 1,)),
        ]
        + LineGather.scratch(n)
        + GroupGather.scratch(dp)
        + GroupGather.scratch(dp),
        compiler_params=remote(1),
        cost_estimate=cost(10**6, 100 * MEGA),
        name="start",
    )(x_loc, cond, ada, ada_bias, proj_bias, fc2_bias, length, qkv, fc1)


def qkv_kernel(img, x_ref, mod_ref, w_ref, b_ref, a_ref, o_ref):
    wide = o_ref.shape[2]
    for t, sl in ((0, slice(0, img)), (1, slice(img, x_ref.shape[1]))):
        normed, _ = layer_norm(x_ref[0, sl].astype(SINGLE))
        a = (normed * (1.0 + mod_ref[t, 1:2]) + mod_ref[t, 0:1]).astype(HALF)
        a_ref[0, sl] = a
        o_ref[0, sl] = (
            nn_dot(a, w_ref[:, t * wide : (t + 1) * wide]) + b_ref[t : t + 1]
        ).astype(HALF)


def project_qkv(n, img, x_all, mods, weight, bias):
    _, rows, width = x_all.shape
    wide = weight.shape[1] // 2
    return pl.pallas_call(
        functools.partial(qkv_kernel, img),
        grid=(n,),
        in_specs=[
            rows_spec(rows, width),
            whole(mods.shape),
            whole(weight.shape, True),
            whole(bias.shape),
        ],
        out_specs=[rows_spec(rows, width), rows_spec(rows, wide)],
        out_shape=[
            jax.ShapeDtypeStruct((n, rows, width), HALF),
            jax.ShapeDtypeStruct((n, rows, wide), HALF),
        ],
        compiler_params=params(),
        cost_estimate=cost(2 * n * rows * width * wide, 30 * MEGA),
        name="project_qkv",
    )(x_all, mods, weight, bias)


def halves(shape):
    lane = lax.broadcasted_iota(jnp.int32, shape, len(shape) - 1)
    return lane < HD


def attn_kernel(
    n, q_ref, k_ref, v_ref, mask_ref, e_ref, p_ref, o_ref, lse_ref, e_near, mix_ref, p_all,
    o_buf, o_send, o_recv, o_local, *sems,
):
    pair, block = pl.program_id(0), pl.program_id(1)
    pairs = pl.num_programs(0)
    step = pair * n + block
    me = lax.axis_index("seq")
    count, rows, _ = k_ref.shape
    gather = LineGather(n, e_ref, None, *sems[:3], first=0, stop=1, land=e_near)
    proj = GroupGather(p_ref, p_all, *sems[3:])

    def begin():
        greet(n, "all", "paths")
        gather.begin()
        proj.begin()

    at_step(step, 0, begin)
    queries = q_ref[0] * HALF(1.0 / math.sqrt(HD))
    keys = k_ref[...].reshape(n * rows, LANES)
    values = v_ref[...].reshape(n * rows, LANES)
    first = halves(queries.shape)
    outs, logs = [], []
    for head in range(2):
        own = first if head == 0 else jnp.logical_not(first)
        scores = nt_dot(jnp.where(own, queries, HALF(0)), keys) + mask_ref[...]
        maxima = jnp.max(scores, axis=-1, keepdims=True)
        raised = jnp.exp(scores - maxima)
        totals = jnp.sum(raised, axis=-1, keepdims=True)
        weights = (raised * (1.0 / totals)).astype(HALF)
        outs.append(nn_dot(weights, values))
        logs.append(maxima + jnp.log(totals))
    mixed = jnp.where(first, outs[0], outs[1]).astype(HALF)
    o_ref[0] = mixed
    o_buf[pair, block] = mixed
    lse_ref[0] = jnp.where(first, logs[0], logs[1])
    static_pairs = o_buf.shape[0]

    def columns(sender, which):
        start = (sender * static_pairs + which) * LANES
        return mix_ref.at[:, pl.ds(pl.multiple_of(start, LANES), LANES)]

    def away(which, offset):
        peer = lax.rem(me + offset, n)
        return pltpu.make_async_remote_copy(
            src_ref=o_buf.at[which, peer],
            dst_ref=columns(me, which),
            send_sem=o_send.at[which, offset - 1],
            recv_sem=o_recv.at[which, offset - 1],
            device_id=on_line(peer),
            device_id_type=MESH,
        )

    for offset in range(1, n):

        @pl.when(block == lax.rem(me + offset, n))
        def _():
            away(pair, offset).start()

    @pl.when(block == me)
    def _():
        pltpu.make_async_copy(o_buf.at[pair, me], columns(me, pair), o_local.at[pair]).start()

    last = static_pairs * n - 1
    for phase in range(proj.phases):
        at_step(step, min(last, 5 * phase + 5), functools.partial(proj.arrive, phase))

    def finish():
        gather.arrive(0)
        proj.finish()
        for which in range(static_pairs):
            pltpu.make_async_copy(o_buf.at[which, me], columns(me, which), o_local.at[which]).wait()
            for offset in range(1, n):
                away(which, offset).wait()
        gather.finish()

    at_step(step, last, finish)


def attend(n, dp, qkv, mask, e_loc, proj):
    _, rows, wide = qkv.shape
    width = e_loc.shape[1]
    pairs = wide // 3 // LANES
    total = n * rows
    block = pl.BlockSpec((1, rows, LANES), lambda h, s: (s, 0, h))
    anywhere = pl.BlockSpec(memory_space=pl.ANY)
    return pl.pallas_call(
        functools.partial(attn_kernel, n),
        grid=(pairs, n),
        in_specs=[
            block,
            pl.BlockSpec((n, rows, LANES), lambda h, s: (0, 0, pairs + h)),
            pl.BlockSpec((n, rows, LANES), lambda h, s: (0, 0, 2 * pairs + h)),
            whole(mask.shape),
            anywhere,
            whole(proj.shape, True),
        ],
        out_specs=[block, block, anywhere, anywhere, anywhere],
        out_shape=[
            jax.ShapeDtypeStruct((n, rows, pairs * LANES), HALF),
            jax.ShapeDtypeStruct((n, rows, pairs * LANES), SINGLE),
            jax.ShapeDtypeStruct((2, rows, width), HALF),
            jax.ShapeDtypeStruct((rows, n * pairs * LANES), HALF),
            jax.ShapeDtypeStruct((dp,) + proj.shape, HALF),
        ],
        scratch_shapes=[
            pltpu.VMEM((pairs, n, rows, LANES), HALF),
            pltpu.SemaphoreType.DMA((pairs, n - 1)),
            pltpu.SemaphoreType.DMA((pairs, n - 1)),
            pltpu.SemaphoreType.DMA((pairs,)),
        ]
        + LineGather.scratch(n)
        + GroupGather.scratch(dp),
        compiler_params=remote(2),
        cost_estimate=cost(2 * 2 * 4 * pairs * total * total * LANES, 20 * MEGA, 2 * pairs * total * total),
        name="attend",
    )(qkv, qkv, qkv, mask, e_loc, proj)


def attn_back_kernel(
    lines, img, pairs, q_ref, k_ref, v_ref, o_ref, g_ref, lse_ref, mask_ref, y_ref, l_ref, r_ref,
    dq_ref, dk_ref, dv_ref, qb_ref, vb_ref, p_ref, tail,
    acc_ref, lse_row, delta_row, turned, *scratch,
):
    linear = pl.program_id(0)
    ahead = 2 * lines
    attn_steps = pairs * lines
    last = ahead + attn_steps - 1
    step = lax.rem(lax.max(linear - ahead, 0), lines)
    n, rows, _ = q_ref.shape
    total = n * rows
    line = LineSum(lines, at_rows(y_ref), None, *scratch, stop=lines - 2, tail=tail)

    def begin():
        greet(lines, "near")
        line.round(0)

    at_step(linear, 0, begin)
    for t, sl in ((0, slice(0, img)), (1, slice(img, rows))):

        @pl.when(linear == 0)
        def _():
            turned[:, sl] = l_ref[sl].T

        @pl.when(both(linear < ahead, lax.rem(linear, 2) == t))
        def _():
            p_ref[...] = nn_dot(turned[:, sl], r_ref[sl]).astype(HALF).reshape(p_ref.shape)

    @pl.when(linear >= ahead)
    def _():
        grads = g_ref[...].reshape(total, LANES)
        queries = q_ref[...].reshape(total, LANES) * HALF(1.0 / math.sqrt(HD))

        @pl.when(step == 0)
        def _():
            acc_ref[...] = jnp.zeros_like(acc_ref)
            product = grads.astype(SINGLE) * o_ref[...].reshape(total, LANES).astype(SINGLE)
            flipped = product.T
            logs = lse_ref[...].reshape(total, LANES).T
            for head in range(2):
                delta_row[head : head + 1] = jnp.sum(
                    flipped[head * HD : (head + 1) * HD], axis=0, keepdims=True
                )
                lse_row[head : head + 1] = logs[head * HD : head * HD + 1]
            vb_ref[0] = jnp.zeros_like(vb_ref[0])

        keys, values = k_ref[0], v_ref[0]
        first = halves(keys.shape)
        mask = mask_ref[0][:, 0:1]
        dks, dvs = [], []
        for head in range(2):
            own = first if head == 0 else jnp.logical_not(first)
            key_own = jnp.where(own, keys, HALF(0))
            scores = nt_dot(key_own, queries)
            probs = jnp.exp((scores - lse_row[head : head + 1]) + mask)
            grad_prob = nt_dot(jnp.where(own, values, HALF(0)), grads)
            grad_score = (probs * (grad_prob - delta_row[head : head + 1])).astype(HALF)
            dvs.append(nn_dot(probs.astype(HALF), grads))
            dks.append(nn_dot(grad_score, queries))
            acc_ref[...] += tn_dot(grad_score, key_own)
        dk_ref[0] = jnp.where(first, dks[0], dks[1]).astype(HALF)
        dv = jnp.where(first, dvs[0], dvs[1])
        dv_ref[0] = dv.astype(HALF)
        vb_ref[0, 0:1] += jnp.sum(dv[:img], axis=0, keepdims=True)
        vb_ref[0, 1:2] += jnp.sum(dv[img:], axis=0, keepdims=True)

        @pl.when(step == lines - 1)
        def _():
            dq = (acc_ref[...] * (1.0 / math.sqrt(HD))).reshape(n, rows, LANES)
            dq_ref[...] = dq.astype(HALF)
            qb_ref[0, 0:1] = jnp.sum(jnp.sum(dq[:, :img], axis=0), axis=0, keepdims=True)
            qb_ref[0, 1:2] = jnp.sum(jnp.sum(dq[:, img:], axis=0), axis=0, keepdims=True)

    for hop in range(1, lines - 2):
        at_step(linear, min(last, ahead + 5 * hop), functools.partial(line.round, hop))

    at_step(linear, last, line.close)


def attend_back(n, dp, img, qkv, mixture, grad_mix, lse, mask_col, out_parts, grad_attn, mix_loc):
    _, rows, wide = qkv.shape
    pairs = wide // 3 // LANES
    total = n * rows
    lw = pairs * LANES
    ahead = 2 * n
    steps = pairs * n
    width = out_parts.shape[2]
    depth = width // dp

    def place(k):
        return lax.rem(lax.max(k - ahead, 0), n)

    def head(k):
        return lax.div(lax.max(k - ahead, 0), n)

    full = pl.BlockSpec((n, rows, LANES), lambda k: (0, 0, head(k)))

    def block(base):
        return pl.BlockSpec((1, rows, LANES), lambda k: (place(k), 0, base + head(k)))

    bias = pl.BlockSpec((1, 2, LANES), lambda k: (head(k), 0, 0))
    anywhere = pl.BlockSpec(memory_space=pl.ANY)
    return pl.pallas_call(
        functools.partial(attn_back_kernel, n, img, pairs),
        grid=(ahead + steps,),
        in_specs=[
            full,
            block(pairs),
            block(2 * pairs),
            full,
            full,
            full,
            pl.BlockSpec((1, rows, LANES), lambda k: (place(k), 0, 0)),
            anywhere,
            whole(grad_attn.shape, True),
            pl.BlockSpec((rows, lw), lambda k: (0, lax.min(lax.div(k, 2), n - 1))),
        ],
        out_specs=[
            full,
            block(0),
            block(0),
            bias,
            bias,
            pl.BlockSpec((dp, 1, depth, lw), lambda k: (0, lax.min(k, ahead - 1), 0, 0)),
            anywhere,
        ],
        out_shape=[jax.ShapeDtypeStruct((n, rows, lw), HALF)] * 3
        + [jax.ShapeDtypeStruct((pairs, 2, LANES), SINGLE)] * 2
        + [
            jax.ShapeDtypeStruct((dp, 2 * n, depth, lw), HALF),
            jax.ShapeDtypeStruct((2, rows, width), HALF),
        ],
        scratch_shapes=[
            pltpu.VMEM((total, LANES), SINGLE),
            pltpu.VMEM((2, total), SINGLE),
            pltpu.VMEM((2, total), SINGLE),
            pltpu.VMEM((width, rows), HALF),
        ]
        + LineSum.scratch(n, rows, width, stop=n - 2),
        compiler_params=remote(3, 62),
        cost_estimate=cost(2 * 5 * 4 * pairs * total * total * LANES, 30 * MEGA, 2 * pairs * total * total),
        name="attend_back",
    )(qkv, qkv, qkv, mixture, grad_mix, lse, mask_col, out_parts, grad_attn, mix_loc)


def proj_columns(w_ref, z, t):
    dp, _, _, depth, heads = w_ref.shape
    return w_ref[:, z, t].reshape(dp * depth, heads)


def middle_kernel(
    n, img, mix_ref, x_ref, w_ref, b_ref, mod_ref, fc2_ref, y_ref, m_ref, all_ref, fc2_all, own, *sems
):
    greet(n, "near", "paths")
    fc2 = GroupGather(fc2_ref, fc2_all, *sems[3:])
    fc2.begin()
    lw = mix_ref.shape[1] // n
    heads = w_ref.shape[4]
    for t, sl in ((0, slice(0, img)), (1, slice(img, x_ref.shape[0]))):
        attn = b_ref[t : t + 1]
        for z in range(n):
            attn = attn + nt_dot(mix_ref[sl, z * lw : z * lw + heads], proj_columns(w_ref, z, t))
        y_ref[sl] = attn
        middle = x_ref[sl].astype(SINGLE) + mod_ref[t, 2:3] * attn
        m_ref[sl] = middle
        normed, _ = layer_norm(middle)
        own[sl] = (normed * (1.0 + mod_ref[t, 4:5]) + mod_ref[t, 3:4]).astype(HALF)
    gather = LineGather(n, own, all_ref, *sems[:3])
    gather.begin()
    gather.keep().start()
    for hop in range(max(n - 1, fc2.phases)):
        if hop < fc2.phases:
            fc2.arrive(hop)
        if hop < n - 1:
            gather.arrive(hop)
    gather.keep().wait()
    gather.finish()
    fc2.finish()


def middle_rows(n, dp, img, mixture, x_loc, weight, bias, mods, fc2):
    rows, width = x_loc.shape
    inner = pl.BlockSpec(memory_space=pltpu.VMEM)
    anywhere = pl.BlockSpec(memory_space=pl.ANY)
    return pl.pallas_call(
        functools.partial(middle_kernel, n, img),
        in_specs=[inner] * 6,
        out_specs=[inner, inner, anywhere, anywhere],
        out_shape=[
            jax.ShapeDtypeStruct((rows, width), SINGLE),
            jax.ShapeDtypeStruct((rows, width), SINGLE),
            jax.ShapeDtypeStruct((n, rows, width), HALF),
            jax.ShapeDtypeStruct((dp,) + fc2.shape, HALF),
        ],
        scratch_shapes=[pltpu.VMEM((rows, width), HALF)]
        + LineGather.scratch(n)
        + GroupGather.scratch(dp),
        compiler_params=remote(4),
        cost_estimate=cost(2 * rows * width * width, 100 * MEGA),
        name="middle_rows",
    )(mixture, x_loc, weight, bias, mods, fc2)


def by_distance(me, n, count):
    low = lax.min(me, n - 1 - me)
    near = lax.select(lax.rem(count, 2) == 1, lax.div(count + 1, 2), -lax.div(count, 2))
    far = lax.select(me < n - 1 - me, count - low, low - count)
    return me + lax.select(count <= 2 * low, near, far)


def mlp_kernel(n, img, tile, b_ref, e_loc, e_near, mod_ref, w1_ref, b1_ref, w2_ref,
    g_ref, dz_ref, dy_ref, db_ref, y_ref, sum_ref, gate_ref, acc_ref, out_ref, e_all, near_sem, *sems):
    step = pl.program_id(0)
    me = lax.axis_index("seq")
    owner = by_distance(me, n, step)
    e_ref = e_all.at[pl.ds(owner, 1)]
    gather = LineGather(n, e_near, e_all, *sems, first=1)
    own = pltpu.make_async_copy(e_loc, e_all.at[me], near_sem.at[2])

    def nears(action):
        for way, sign in ((0, 1), (1, -1)):
            block = me - sign

            @pl.when(both(block >= 0, block < n))
            def _():
                action(
                    pltpu.make_async_copy(e_near.at[way], e_all.at[block], near_sem.at[way])
                )

    def begin():
        greet(n, "near")
        gather.begin()
        own.start()
        nears(lambda copy: copy.start())
        own.wait()
        nears(lambda copy: copy.wait())

    at_step(step, 0, begin)
    for hop in range(1, n - 1):
        at_step(step, hop + 1, functools.partial(gather.arrive, hop))
    at_step(step, n - 1, gather.finish)
    units = g_ref.shape[2]

    @pl.when(step == 0)
    def _():
        sum_ref[...] = jnp.zeros_like(sum_ref)
        gate_ref[...] = jnp.zeros_like(gate_ref)

    for t, sl in ((0, slice(0, img)), (1, slice(img, b_ref.shape[1]))):
        rows = b_ref[0, sl]
        grad = (mod_ref[t, 5:6] * e_ref[0, sl].astype(SINGLE)).astype(HALF)
        dy_ref[0, sl] = grad

        for k in range(units // tile):
            here = slice(k * tile, (k + 1) * tile)
            cols = slice(t * units + k * tile, t * units + (k + 1) * tile)
            w1 = w1_ref[:, cols]
            pre = nn_dot(rows, w1) + b1_ref[t : t + 1, here]
            hidden, slope = gelu_both(pre)
            hidden = hidden.astype(HALF)
            g_ref[0, sl, here] = hidden
            w2 = w2_ref[:, t, :, here].reshape(-1, tile)
            out = nt_dot(hidden, w2)
            dz = nn_dot(grad, w2) * slope
            sum_ref[t : t + 1, here] += jnp.sum(dz, axis=0, keepdims=True)
            dzh = dz.astype(HALF)
            dz_ref[0, sl, here] = dzh
            part = nt_dot(dzh, w1)
            if k == 0:
                acc_ref[sl] = part
                out_ref[sl] = out
            else:
                acc_ref[sl] += part
                out_ref[sl] += out
        db_ref[0, sl] = acc_ref[sl].astype(HALF)
        out = out_ref[sl]
        y_ref[0, sl] = out.astype(HALF)
        gate_ref[t : t + 1] += jnp.sum(out * e_ref[0, sl].astype(SINGLE), axis=0, keepdims=True)


def feed_forward(n, img, mlp_in, e_loc, e_near, mods, w1, b1, w2):
    rows, width = mlp_in.shape[1:]
    units = w1.shape[1] // 2
    tile = min(768, units)
    while units % tile:
        tile -= LANES

    def owned(columns):
        return pl.BlockSpec(
            (1, rows, columns), lambda k: (by_distance(lax.axis_index("seq"), n, k), 0, 0)
        )

    return pl.pallas_call(
        functools.partial(mlp_kernel, n, img, tile),
        grid=(n,),
        in_specs=[
            owned(width),
            pl.BlockSpec(memory_space=pl.ANY),
            pl.BlockSpec(memory_space=pl.ANY),
            whole(mods.shape),
            whole(w1.shape, True),
            whole(b1.shape),
            whole(w2.shape, True),
        ],
        out_specs=[
            owned(units),
            owned(units),
            owned(width),
            owned(width),
            owned(width),
            whole((2, units)),
            whole((2, width)),
        ],
        out_shape=[
            jax.ShapeDtypeStruct((n, rows, units), HALF),
            jax.ShapeDtypeStruct((n, rows, units), HALF),
            jax.ShapeDtypeStruct((n, rows, width), HALF),
            jax.ShapeDtypeStruct((n, rows, width), HALF),
            jax.ShapeDtypeStruct((n, rows, width), HALF),
            jax.ShapeDtypeStruct((2, units), SINGLE),
            jax.ShapeDtypeStruct((2, width), SINGLE),
        ],
        scratch_shapes=[
            pltpu.VMEM((rows, width), SINGLE),
            pltpu.VMEM((rows, width), SINGLE),
            pltpu.VMEM((n, rows, width), HALF),
            pltpu.SemaphoreType.DMA((3,)),
        ]
        + LineGather.scratch(n),
        compiler_params=remote(9, 60),
        cost_estimate=cost(6 * n * rows * width * units, 50 * MEGA, n * rows * units),
        name="feed_forward",
    )(mlp_in, e_loc, e_near, mods, w1, b1, w2)


def grads_kernel(n, img, plan, rounds, *refs):
    lefts = max(p[0] for p in plan) + 1
    rights = max(p[1] for p in plan) + 1
    l_refs, r_refs = refs[:lefts], refs[lefts : lefts + rights]
    rest = refs[lefts + rights :]
    step = pl.program_id(0)
    if rounds:
        parts, o_ref, tail, turned = rest[:4]
        line = LineSum(n, at_rows(parts), None, *rest[4:], stop=n - 2, tail=tail)

        def begin():
            greet(n, "near")
            line.round(0)

        at_step(step, 0, begin)
    else:
        o_ref, turned = rest
    tile = 512 if o_ref.shape[3] % 512 == 0 else 2 * LANES
    before = None
    for k, (left, right, stream) in enumerate(plan):

        @pl.when(step == k)
        def _():
            l_ref, r_ref = l_refs[left], r_refs[right]
            count, rows, _ = l_ref.shape
            sl = slice(0, img) if stream == 0 else slice(img, rows)
            size = count * (sl.stop - sl.start)
            if before != (left, stream):
                turned[:, :size] = l_ref[:, sl].reshape(size, l_ref.shape[2]).T
            for column in range(0, o_ref.shape[3], tile):
                values = r_ref[:, sl, column : column + tile].reshape(size, tile)
                product = nn_dot(turned[:, :size], values).astype(HALF)
                o_ref[:, 0, :, column : column + tile] = product.reshape(
                    o_ref.shape[0], o_ref.shape[2], tile
                )

        before = (left, stream)
    if rounds:
        for hop, when in enumerate(rounds):
            at_step(step, when, functools.partial(line.round, hop + 1))
        at_step(step, len(plan) - 1, line.close)


def weight_grads(n, dp, img, lefts, rights, plan, rounds, parts, collective, name):
    rows, depth = lefts[0].shape[1:]
    wide = rights[0].shape[2]
    anywhere = pl.BlockSpec(memory_space=pl.ANY)
    block = (dp, 1, depth // dp, wide)
    longest = max(up(n * img, LANES), up(n * (rows - img), LANES))
    return pl.pallas_call(
        functools.partial(grads_kernel, n, img, plan, rounds),
        grid=(len(plan),),
        in_specs=[whole(a.shape, True) for a in (*lefts, *rights)] + [anywhere],
        out_specs=[pl.BlockSpec(block, lambda k: (0, k, 0, 0)), anywhere],
        out_shape=[
            jax.ShapeDtypeStruct((dp, len(plan), depth // dp, wide), HALF),
            jax.ShapeDtypeStruct((2,) + parts.shape[1:], HALF),
        ],
        scratch_shapes=[pltpu.VMEM((depth, longest), HALF)]
        + LineSum.scratch(n, *parts.shape[1:], stop=n - 2),
        compiler_params=remote(collective, 60),
        cost_estimate=cost(2 * n * rows * depth * len(plan) * wide // 2, 60 * MEGA),
        name=name,
    )(*lefts, *rights, parts)


def middle_back_kernel(
    n, img, part_ref, prev_ref, m_ref, y_ref, e_ref, w_ref, mod_ref, dm_ref, dy_ref, sum_ref, all_ref,
    db_ref, mix, send, recv, local, *line_scratch,
):
    me = lax.axis_index("seq")
    rows, width = m_ref.shape
    heads = w_ref.shape[4]
    streams = ((0, slice(0, img)), (1, slice(img, rows)))
    greet(n, "all")
    line = LineSum(n, at_rows(part_ref), db_ref, *line_scratch, first=n - 2, prev=prev_ref)
    line.round(n - 2)
    if mix.shape[2] > heads:
        mix[...] = jnp.zeros_like(mix)
    line.finish()
    for t, sl in streams:
        grad_in = db_ref[sl]
        normed, inv_std = layer_norm(m_ref[sl])
        upstream = e_ref[sl].astype(SINGLE)
        grad_middle = upstream + norm_back(normed, inv_std, grad_in * (1.0 + mod_ref[t, 4:5]))
        dm_ref[sl] = grad_middle
        grad_attn = mod_ref[t, 2:3] * grad_middle
        dy_ref[sl] = grad_attn.astype(HALF)

        def total(value):
            return jnp.sum(value, axis=0, keepdims=True)

        sum_ref[t, 0:1] = total(grad_middle * y_ref[sl])
        sum_ref[t, 1:2] = total(grad_in)
        sum_ref[t, 2:3] = total(grad_in * normed)
        sum_ref[t, 3:4] = total(grad_attn)
        sum_ref[t, 4:5] = total(upstream)

    def exchange(peer, block):
        return pltpu.make_async_remote_copy(
            src_ref=mix.at[peer],
            dst_ref=all_ref.at[block],
            send_sem=send.at[peer],
            recv_sem=recv.at[block],
            device_id=on_line(peer),
            device_id_type=MESH,
        )

    keep = pltpu.make_async_copy(mix.at[me], all_ref.at[me], local)
    for peer in range(n):
        for t, sl in streams:
            mix[peer, sl, :heads] = nn_dot(dy_ref[sl], proj_columns(w_ref, peer, t)).astype(HALF)

        @pl.when(peer != me)
        def _():
            exchange(peer, me).start()

        @pl.when(peer == me)
        def _():
            keep.start()

    for peer in range(n):

        @pl.when(peer != me)
        def _():
            exchange(peer, peer).wait()

    keep.wait()


def middle_back(n, img, parts, prev, middle, attn_out, cot, weight, mods, lwp):
    rows, width = middle.shape
    inner = pl.BlockSpec(memory_space=pltpu.VMEM)
    anywhere = pl.BlockSpec(memory_space=pl.ANY)
    return pl.pallas_call(
        functools.partial(middle_back_kernel, n, img),
        in_specs=[anywhere, anywhere] + [inner] * 5,
        out_specs=[inner, inner, inner, anywhere],
        out_shape=[
            jax.ShapeDtypeStruct((rows, width), SINGLE),
            jax.ShapeDtypeStruct((rows, width), HALF),
            jax.ShapeDtypeStruct((2, 8, width), SINGLE),
            jax.ShapeDtypeStruct((n, rows, lwp), HALF),
        ],
        scratch_shapes=[
            pltpu.VMEM((rows, width), SINGLE),
            pltpu.VMEM((n, rows, lwp), HALF),
            pltpu.SemaphoreType.DMA((n,)),
            pltpu.SemaphoreType.DMA((n,)),
            pltpu.SemaphoreType.DMA,
        ]
        + LineSum.scratch(n, rows, width, first=n - 2),
        compiler_params=remote(5),
        cost_estimate=cost(2 * rows * width * width, 60 * MEGA),
        name="middle_back",
    )(parts, prev, middle, attn_out, cot, weight, mods)


def attn_in_kernel(
    n, img, dq_ref, dk_ref, dv_ref, x_ref, a_ref, w_ref, y_ref, prev_ref, p_ref,
    da_ref, sum_ref, g_ref, y_sum, p_rest, turned, *scratch,
):
    step = pl.program_id(0)
    count, rows, lw = dq_ref.shape
    line = LineSum(n, at_rows(y_ref), y_sum, *scratch[:6], first=n - 2, prev=prev_ref)
    group = GroupSum(p_ref, *scratch[6:])
    streams = ((0, slice(0, img)), (1, slice(img, rows)))

    def begin():
        greet(n, "near", "paths")
        group.begin()
        line.round(n - 2)
        sum_ref[...] = jnp.zeros_like(sum_ref)

    at_step(step, 0, begin)

    @pl.when(step < n)
    def _():
        here = lax.min(step, n - 1)
        for t, sl in streams:
            part = None
            for c, ref in enumerate((dq_ref, dk_ref, dv_ref)):
                start = (3 * t + c) * lw
                term = nt_dot(ref[here, sl], w_ref[:, start : start + lw])
                part = term if part is None else part + term
            da_ref[0, sl] = part.astype(HALF)
            normed, _ = layer_norm(x_ref[0, sl].astype(SINGLE))
            sum_ref[t, 0:1] += jnp.sum(part, axis=0, keepdims=True)
            sum_ref[t, 1:2] += jnp.sum(part * normed, axis=0, keepdims=True)

    for t, sl in streams:
        size = count * (sl.stop - sl.start)
        for c, ref in enumerate((dq_ref, dk_ref, dv_ref)):

            @pl.when(step == n + 3 * t + c)
            def _():
                if c == 0:
                    turned[:, :size] = a_ref[:, sl].reshape(size, a_ref.shape[2]).T
                g_ref[...] = nn_dot(turned[:, :size], ref[:, sl].reshape(size, lw)).astype(HALF)

    for number in range(group.phases - 1):
        at_step(step, min(n + 5, 1 + 5 * number), functools.partial(group.step, number))

    def finish():
        line.finish()
        group.close(p_rest)

    at_step(step, n + 5, finish)


def attn_in_back(n, img, dq, dk, dv, x_all, attn_in, weight, out_parts, running, proj):
    _, rows, lw = dq.shape
    width = x_all.shape[2]
    anywhere = pl.BlockSpec(memory_space=pl.ANY)
    row = pl.BlockSpec((1, rows, width), lambda k: (lax.min(k, n - 1), 0, 0))
    longest = max(up(n * img, LANES), up(n * (rows - img), LANES))
    return pl.pallas_call(
        functools.partial(attn_in_kernel, n, img),
        grid=(n + 6,),
        in_specs=[whole(dq.shape, True)] * 3
        + [row, whole(attn_in.shape, True), whole(weight.shape, True)]
        + [anywhere] * 3,
        out_specs=[
            row,
            whole((2, 2, width)),
            pl.BlockSpec((width, lw), lambda k: (0, lax.max(k - n, 0))),
            whole((rows, width), True),
            whole((2, 2) + proj.shape[2:], True),
        ],
        out_shape=[
            jax.ShapeDtypeStruct((n, rows, width), HALF),
            jax.ShapeDtypeStruct((2, 2, width), SINGLE),
            jax.ShapeDtypeStruct((width, 6 * lw), HALF),
            jax.ShapeDtypeStruct((rows, width), SINGLE),
            jax.ShapeDtypeStruct((2, 2) + proj.shape[2:], HALF),
        ],
        scratch_shapes=[pltpu.VMEM((width, longest), HALF)]
        + LineSum.scratch(n, rows, width, first=n - 2)
        + GroupSum.scratch(proj.shape[0], *proj.shape[2:]),
        compiler_params=remote(10, 62),
        cost_estimate=cost(12 * n * rows * width * lw, 30 * MEGA),
        name="attn_in_back",
    )(dq, dk, dv, x_all, attn_in, weight, out_parts, running, proj)


def end_kernel(
    n, dp, cut, parts, qkv_part, p_rest, packed, extra, ada_ref,
    sum_ref, qkv_sum, p_own, every, cond_ref,
    z_got, row, c_part, c_got, c_all, z_send, z_recv, e_send, e_recv, c_send, c_recv, a_send, a_recv,
    *scratch,
):
    me, my = lax.axis_index("seq"), lax.axis_index("dp")
    depth = ada_ref.shape[0]
    span = packed.shape[2]
    greet(n, "all", "all")
    line = LineSum(n, at_rows(parts), sum_ref, *scratch[:6])
    group = GroupSum(qkv_part, *scratch[6:15])
    proj = GroupLast(p_rest, *scratch[15:])
    mates, others = range(1, n), range(1, dp)
    z_go = [to_line(me, n, k, packed, z_got, z_send, z_recv) for k in mates]
    for copy in z_go:
        copy.start()
    group.begin()
    proj.begin()
    line.round(0)
    z_got[me] = packed[me]
    for copy in z_go:
        copy.wait_recv()
    row[:, :span] = jnp.sum(z_got[...], axis=0)
    row[:, span:] = extra[...]
    e_go = [to_group(my, dp, k, row, every, e_send, e_recv) for k in others]
    for copy in e_go:
        copy.start()
    every[my] = row[...]
    group.step(0)
    for copy in e_go:
        copy.wait_recv()
    cols = cut // 2
    product = nt_dot(every[:, 0, :cols].astype(HALF), ada_ref[:, 0, :])
    product = product + nt_dot(every[:, 0, cols:cut].astype(HALF), ada_ref[:, 1, :])
    c_part[...] = jnp.zeros_like(c_part)
    for k in range(dp):
        c_part[k, :, :depth] = product[k : k + 1]
    c_go = [to_group(my, dp, k, c_part, c_got, c_send, c_recv) for k in others]
    for copy in c_go:
        copy.start()
    c_got[my] = c_part[my]
    a_go = [to_line(me, n, k, c_got, c_all, a_send, a_recv) for k in mates]
    for hop in range(1, n - 1):
        line.round(hop)
        if hop == 1:
            for copy in c_go:
                copy.wait_recv()
            for copy in a_go:
                copy.start()
            c_all[me] = c_got[...]
        if hop < group.phases:
            group.step(hop)
    for number in range(max(n - 1, 1), group.phases):
        group.step(number)
    for copy in a_go:
        copy.wait_recv()
    cond_ref[...] = jnp.sum(c_all[...], axis=0)
    group.finish(qkv_sum)

    def store(half, value):
        p_own[half] = value.astype(HALF)

    proj.finish(store)
    line.finish()
    for copy in z_go + e_go + c_go + a_go:
        copy.wait_send()


def end(n, dp, cut, parts, qkv_part, proj_rest, packed, extra, ada):
    rows, width = parts.shape[1:]
    depth = up(ada.shape[0], LANES)
    span = packed.shape[2] + extra.shape[1]
    inner = pl.BlockSpec(memory_space=pltpu.VMEM)
    anywhere = pl.BlockSpec(memory_space=pl.ANY)
    sems = [n - 1, n - 1, dp - 1, dp - 1, dp - 1, dp - 1, n - 1, n - 1]
    return pl.pallas_call(
        functools.partial(end_kernel, n, dp, cut),
        in_specs=[anywhere, anywhere, inner, inner, inner, inner],
        out_specs=[inner] * 5,
        out_shape=[
            jax.ShapeDtypeStruct((rows, width), SINGLE),
            jax.ShapeDtypeStruct(qkv_part.shape[1:], SINGLE),
            jax.ShapeDtypeStruct(proj_rest.shape[1:], HALF),
            jax.ShapeDtypeStruct((dp, 1, span), SINGLE),
            jax.ShapeDtypeStruct((dp, 1, depth), SINGLE),
        ],
        scratch_shapes=[
            pltpu.VMEM(packed.shape, SINGLE),
            pltpu.VMEM((1, span), SINGLE),
            pltpu.VMEM((dp, 1, depth), SINGLE),
            pltpu.VMEM((dp, 1, depth), SINGLE),
            pltpu.VMEM((n, dp, 1, depth), SINGLE),
        ]
        + [pltpu.SemaphoreType.DMA((k,)) for k in sems]
        + LineSum.scratch(n, rows, width)
        + GroupSum.scratch(dp, *qkv_part.shape[2:])
        + GroupLast.scratch(*proj_rest.shape[2:]),
        compiler_params=remote(7, 60),
        cost_estimate=cost(10**6, 100 * MEGA),
        name="end",
    )(parts, qkv_part, proj_rest, packed, extra, ada)


def rows_kernel(img, slots, da_ref, dm_ref, x_ref, m_ref, y_ref, mod_ref, shift_ref, live_ref, io_ref, to_ref, ig_ref, tg_ref):
    for t, sl, out_ref, grad_ref in (
        (0, slice(0, img), io_ref, ig_ref),
        (1, slice(img, x_ref.shape[0]), to_ref, tg_ref),
    ):
        keep = out_ref.shape[1]
        live = live_ref[sl]
        value = m_ref[sl] + mod_ref[t, 5:6] * (y_ref[sl] + shift_ref[t : t + 1])
        out_ref[0] = (value * live).astype(HALF)[:keep]
        normed, inv_std = layer_norm(x_ref[sl].astype(SINGLE))
        grad = dm_ref[sl] + norm_back(normed, inv_std, da_ref[sl] * (1.0 + mod_ref[t, 1:2]))
        grad_ref[0] = (grad * live)[:keep]


def rows_out(img, slots, grad_attn_in, grad_middle, x_loc, middle, mlp_sum, mods, fc2_shift, live):
    width = x_loc.shape[1]
    return pl.pallas_call(
        functools.partial(rows_kernel, img, slots),
        out_shape=[
            jax.ShapeDtypeStruct((1, img, width), HALF),
            jax.ShapeDtypeStruct((1, slots, width), HALF),
            jax.ShapeDtypeStruct((1, img, width), SINGLE),
            jax.ShapeDtypeStruct((1, slots, width), SINGLE),
        ],
        compiler_params=params(),
        cost_estimate=cost(10**6, 14 * MEGA),
        name="rows_out",
    )(grad_attn_in, grad_middle, x_loc, middle, mlp_sum, mods, fc2_shift, live)


def body(
    image_tokens,
    text_tokens,
    text_lengths,
    conditioning,
    ada_weight,
    ada_bias,
    qkv_weight,
    qv_bias,
    proj_weight,
    proj_bias,
    fc1_weight,
    fc1_bias,
    fc2_weight,
    fc2_bias,
    image_cotangent,
    text_cotangent,
):
    n = lax.axis_size("seq")
    dp = lax.axis_size("dp")
    img, width = image_tokens.shape[1:]
    slots = text_tokens.shape[1]
    pad = up(slots, 16)
    rows = img + pad
    depth = qkv_weight.shape[0]
    lw = qkv_weight.shape[3]
    lwp = up(lw, LANES)
    units = fc1_weight.shape[2]
    mod_cols = ada_weight.shape[2]
    my_seq = lax.axis_index("dp")

    def stacked(image, text):
        return jnp.concatenate([image, jnp.pad(text, ((0, pad - slots), (0, 0)))], axis=0)

    length = text_lengths[0, 0]
    live_text = (jnp.arange(slots, dtype=jnp.int32) < length)[:, None]
    x_loc = stacked(image_tokens[0], text_tokens[0])
    e_loc = stacked(
        image_cotangent[0], jnp.where(live_text, text_cotangent[0], jnp.zeros((), HALF))
    )

    def split(shard):
        return shard.reshape(2, -1, shard.shape[-1])

    qkv_local = jnp.pad(qkv_weight, ((0, 0), (0, 0), (0, 0), (0, lwp - lw))).reshape(depth, 6 * lwp)
    share = proj_weight.shape[0]
    fc1_local = fc1_weight.reshape(depth, 2 * units)

    cond_float = conditioning.astype(SINGLE)
    bias_cols = proj_bias.shape[1]
    cut = 2 * mod_cols
    proj_line = lax.all_gather(proj_weight.transpose(1, 2, 0), "seq", axis=0, tiled=False)
    x_all, side_all, acts, mods, shifts, qkv_full, fc1_full = start(
        n,
        dp,
        x_loc,
        conditioning,
        ada_weight,
        ada_bias,
        proj_bias,
        fc2_bias,
        text_lengths,
        split(qkv_local),
        split(fc1_local),
    )
    qkv_full = qkv_full.reshape(width, 6 * lwp)
    fc1_full = fc1_full.reshape(width, 2 * units)
    act_slice = acts[:, 0, :depth].astype(HALF)
    proj_shift, fc2_shift = shifts[:2], shifts[2:]
    lengths_all = side_all[:, 0, cut + 4 * bias_cols]

    slot = jnp.arange(rows, dtype=SINGLE)[None, :] - img
    live = jnp.logical_or(slot < 0, jnp.logical_and(slot < lengths_all[:, None], slot < slots))
    mask = jnp.where(live, SINGLE(0), SINGLE(MASKED))
    mask_row = mask.reshape(1, n * rows)
    mask_col = jnp.broadcast_to(mask[:, :, None], (n, rows, LANES))
    live_loc = jnp.concatenate(
        [jnp.ones((img, 1), SINGLE), jnp.pad(live_text.astype(SINGLE), ((0, pad - slots), (0, 0)))]
    )

    bias_rows = jnp.stack(
        [qv_bias[:, 0], jnp.zeros_like(qv_bias[:, 0]), qv_bias[:, 1]], axis=1
    ).astype(SINGLE)
    bias_rows = jnp.pad(bias_rows, ((0, 0), (0, 0), (0, lwp - lw))).reshape(2, 3 * lwp)
    attn_in, qkv_rows = project_qkv(n, img, x_all, mods, qkv_full, bias_rows)
    mixture, lse, e_near, mix_loc, proj_full = attend(
        n, dp, qkv_rows, mask_row, e_loc, proj_line.reshape(2, -1, share)
    )
    proj_full = proj_full.reshape(dp, n, 2, depth, share)

    attn_out, middle, mlp_in, fc2_full = middle_rows(
        n, dp, img, mix_loc, x_loc, proj_full, proj_shift, mods, fc2_weight.transpose(1, 2, 0)
    )
    hidden, grad_pre, grad_mlp, mlp_in_part, mlp_out_part, fc1_bias_part, gate_two_part = (
        feed_forward(
            n, img, mlp_in, e_loc, e_near, mods, fc1_full, fc1_bias.astype(SINGLE), fc2_full
        )
    )
    fc_plan = [(w, w, t) for w in range(2) for t in range(2)]
    fc_rounds = [(k + 1) * 4 // (n - 2) for k in range(n - 3)]
    fc_part, running = weight_grads(
        n, dp, img, (mlp_in, grad_mlp), (grad_pre, hidden), fc_plan, fc_rounds, mlp_in_part, 6, "fc_grads"
    )
    fc_sum = lax.psum_scatter(
        fc_part.reshape(dp * 4 * depth, units), "dp", scatter_dimension=0, tiled=True
    ).reshape(4, depth, units)

    grad_middle, grad_attn, sums, grad_mix = middle_back(
        n, img, mlp_in_part, running, middle, attn_out, e_loc, proj_full, mods, lwp
    )
    grad_q, grad_k, grad_v, q_bias_part, v_bias_part, proj_part, out_running = attend_back(
        n, dp, img, qkv_rows, mixture, grad_mix, lse, mask_col, mlp_out_part, grad_attn, mix_loc
    )
    attn_in_part, mod_one, qkv_part, mlp_sum, proj_rest = attn_in_back(
        n,
        img,
        grad_q,
        grad_k,
        grad_v,
        x_all,
        attn_in,
        qkv_full,
        mlp_out_part,
        out_running,
        proj_part.reshape(dp, 2, n * depth, lwp),
    )
    fc_own = fc_sum.astype(SINGLE)

    upstream_sum = sums[:, 4]
    gate_two = gate_two_part + fc2_shift * upstream_sum
    mod_grads = jnp.stack(
        [mod_one[:, 0], mod_one[:, 1], sums[:, 0], sums[:, 1], sums[:, 2], gate_two], axis=1
    ).reshape(2, n, mod_cols)
    rest = jnp.stack([sums[:, 3], mods[:, 5] * upstream_sum]).reshape(4, n, bias_cols)
    packed = jnp.concatenate(
        [
            mod_grads.transpose(1, 0, 2).reshape(n, -1),
            rest.transpose(1, 0, 2).reshape(n, -1),
        ],
        axis=1,
    )
    q_bias = q_bias_part.transpose(1, 0, 2).reshape(2, lwp)[:, :lw]
    v_bias = v_bias_part.transpose(1, 0, 2).reshape(2, lwp)[:, :lw]
    extra = jnp.concatenate(
        [jnp.stack([q_bias, v_bias], axis=1).reshape(-1), fc1_bias_part.reshape(-1)]
    )
    grad_attn_in, qkv_sum, proj_own, every, cond_sum = end(
        n,
        dp,
        cut,
        attn_in_part,
        qkv_part.reshape(dp, 2, depth // 2, 6 * lwp),
        proj_rest,
        packed[:, None],
        extra[None],
        ada_weight,
    )
    proj_own, fc_sum = lax.optimization_barrier((proj_own, fc_sum))
    proj_sum = lax.psum_scatter(
        proj_own.reshape(n * 2 * depth, lwp), "seq", scatter_dimension=0, tiled=True
    ).reshape(2, depth, lwp)
    every = every[:, 0]
    total = jnp.sum(every, axis=0)

    image_out, text_out, image_grad, text_grad = rows_out(
        img, slots, grad_attn_in, grad_middle, x_loc, middle, mlp_sum, mods, fc2_shift, live_loc
    )

    mod_half = every[:, :cut].astype(HALF).reshape(dp, 2, mod_cols)
    ada_grad = jnp.einsum("nd,ntc->dtc", act_slice, mod_half, preferred_element_type=SINGLE)
    ada_bias_grad = total[:cut].reshape(2, mod_cols)
    proj_bias_grad = total[cut : cut + 2 * bias_cols].reshape(2, bias_cols)
    fc2_bias_grad = total[cut + 2 * bias_cols : cut + 4 * bias_cols].reshape(2, bias_cols)
    after = cut + 4 * bias_cols
    qv_bias_grad = total[after : after + 4 * lw].reshape(2, 2, lw)
    fc1_bias_grad = total[after + 4 * lw :].reshape(2, units)
    cond_grad = cond_sum[:, 0, :depth].reshape(1, width) * silu_slope(cond_float)

    qkv_grad = qkv_sum.reshape(depth, 2, 3, lwp)[..., :lw]
    fc1_grad = fc_own[:2].transpose(1, 0, 2)
    fc2_grad = fc_own[2:].transpose(2, 0, 1)
    proj_grad = proj_sum.astype(SINGLE)[..., :share].transpose(2, 0, 1)
    return (
        image_out,
        text_out,
        image_grad,
        text_grad,
        cond_grad,
        ada_grad,
        ada_bias_grad,
        qkv_grad,
        qv_bias_grad,
        proj_grad,
        proj_bias_grad,
        fc1_grad,
        fc1_bias_grad,
        fc2_grad,
        fc2_bias_grad,
    )


def solution(mesh):
    in_specs = (
        P("dp", "seq", None),
        P("dp", "seq", None),
        P("dp", "seq"),
        P("dp", None),
        P("dp", None, "seq"),
        P(None, "seq"),
        P("dp", None, None, "seq"),
        P(None, None, "seq"),
        P("seq", None, "dp"),
        P(None, "seq"),
        P("dp", None, "seq"),
        P(None, "seq"),
        P("seq", None, "dp"),
        P(None, "seq"),
        P("dp", "seq", None),
        P("dp", "seq", None),
    )
    out_specs = (
        P("dp", "seq", None),
        P("dp", "seq", None),
        P("dp", "seq", None),
        P("dp", "seq", None),
        P("dp", None),
        P("dp", None, "seq"),
        P(None, "seq"),
        P("dp", None, None, "seq"),
        P(None, None, "seq"),
        P("seq", None, "dp"),
        P(None, "seq"),
        P("dp", None, "seq"),
        P(None, "seq"),
        P("seq", None, "dp"),
        P(None, "seq"),
    )
    return jax.shard_map(body, mesh=mesh, in_specs=in_specs, out_specs=out_specs, check_vma=False)
```

```python
import functools
import math

import jax
import jax.numpy as jnp
from jax import lax
from jax.experimental import pallas as pl
from jax.experimental.pallas import tpu as pltpu
from jax.sharding import PartitionSpec as P

HD = 64
LANES = 128
EPSILON = 1e-06
GELU_ROOT = math.sqrt(2.0 / math.pi)
GELU_CUBE = 0.044715
MASKED = -1e30
SINGLE = jnp.float32
HALF = jnp.bfloat16
MEGA = 2**20


def up(value, multiple):
    return -(-value // multiple) * multiple


def params(limit=56):
    return pltpu.CompilerParams(vmem_limit_bytes=limit * MEGA)


def remote(collective, limit=56):
    return pltpu.CompilerParams(
        collective_id=collective, has_side_effects=True, vmem_limit_bytes=limit * MEGA
    )


def cost(flops, nbytes, trans=0):
    return pl.CostEstimate(flops=int(flops), bytes_accessed=int(nbytes), transcendentals=int(trans))


def nt_dot(a, b):
    return lax.dot_general(a, b, (((1,), (1,)), ((), ())), preferred_element_type=SINGLE)


def tn_dot(a, b):
    return lax.dot_general(a, b, (((0,), (0,)), ((), ())), preferred_element_type=SINGLE)


def nn_dot(a, b):
    return jnp.dot(a, b, preferred_element_type=SINGLE)


def layer_norm(values):
    center = values - jnp.mean(values, axis=-1, keepdims=True)
    inv_std = lax.rsqrt(jnp.mean(center * center, axis=-1, keepdims=True) + EPSILON)
    return (center * inv_std, inv_std)


def norm_back(normed, inv_std, upstream):
    first = jnp.mean(upstream, axis=-1, keepdims=True)
    second = jnp.mean(upstream * normed, axis=-1, keepdims=True)
    return inv_std * (upstream - first - normed * second)


def gelu_both(values):
    square = values * values
    inner = GELU_ROOT * (values + GELU_CUBE * square * values)
    tangent = jnp.tanh(inner)
    half = 0.5 * (1.0 + tangent)
    slope = half + 0.5 * values * (1.0 - tangent * tangent) * GELU_ROOT * (
        1.0 + 3.0 * GELU_CUBE * square
    )
    return values * half, slope


def silu_slope(values):
    sigma = jax.nn.sigmoid(values)
    return sigma + values * sigma * (1.0 - sigma)


def whole(shape, single=False):
    zeros = (0,) * len(shape)
    if single:
        return pl.BlockSpec(shape, lambda *_: zeros, pipeline_mode=pl.Buffered(1))
    return pl.BlockSpec(shape, lambda *_: zeros)


def rows_spec(rows, width):
    return pl.BlockSpec((1, rows, width), lambda s: (s, 0, 0))


MESH = pl.DeviceIdType.MESH


def on_line(position):
    return {"seq": position}


def both(first, second):
    return jnp.logical_and(first, second)


def flip(value, mask):
    bit = 1
    while bit <= mask:
        if mask & bit:
            value = value + bit - 2 * bit * lax.rem(lax.div(value, bit), 2)
        bit *= 2
    return value


def greet(n, line=None, group=None):
    me, my = lax.axis_index("seq"), lax.axis_index("dp")
    dp = lax.axis_size("dp")
    barrier = pltpu.get_barrier_semaphore()
    peers = []
    if line == "all":
        peers += [on_line(lax.rem(me + offset, n)) for offset in range(1, n)]
    if group == "all":
        peers += [{"dp": lax.rem(my + offset, dp)} for offset in range(1, dp)]
    if group == "paths":
        peers += [{"dp": flip(my, 1)}] + [{"dp": flip(my, mask)} for mask in masks_of(dp)]
    for peer in peers:
        pl.semaphore_signal(barrier, inc=1, device_id=peer, device_id_type=MESH)
    if line == "near":
        for sign in (1, -1):
            near = me + sign

            @pl.when(both(near >= 0, near < n))
            def _():
                pl.semaphore_signal(barrier, inc=1, device_id=on_line(near), device_id_type=MESH)

    count = len(peers)
    if line == "near":
        count = count + lax.min(me, 1) + lax.min(n - 1 - me, 1)
    pl.semaphore_wait(barrier, count)


def masks_of(dp):
    masks, bit = [], 2
    while bit < dp:
        masks.append(bit)
        bit *= 2
    return masks


class GroupGather:
    def __init__(self, src, out, send, recv, pass_send, pass_recv, local):
        self.src, self.out = src, out
        self.send, self.recv, self.local = send, recv, local
        self.pass_send, self.pass_recv = pass_send, pass_recv
        self.my = lax.axis_index("dp")
        masks = masks_of(out.shape[0])
        self.orders = (masks, masks[::-1])
        self.phases = len(masks)

    @staticmethod
    def scratch(dp):
        return [pltpu.SemaphoreType.DMA((2, dp // 2)) for _ in range(4)] + [
            pltpu.SemaphoreType.DMA
        ]

    def span(self, half, count):
        mask = 0
        for k in range(self.phases):
            if count >> k & 1:
                mask |= self.orders[half][k]
        return mask

    def copy(self, half, phase, count, block):
        src = self.src.at[half] if count == 0 else self.out.at[block, half]
        index = 2**phase - 1 + count
        return pltpu.make_async_remote_copy(
            src_ref=src,
            dst_ref=self.out.at[block, half],
            send_sem=self.send.at[half, index],
            recv_sem=self.recv.at[half, index],
            device_id={"dp": flip(self.my, self.orders[half][phase])},
            device_id_type=MESH,
        )

    def hand(self, half, index, block, own=False):
        src = self.src.at[half] if own else self.out.at[block, half]
        return pltpu.make_async_remote_copy(
            src_ref=src,
            dst_ref=self.out.at[block, half],
            send_sem=self.pass_send.at[half, index],
            recv_sem=self.pass_recv.at[half, index],
            device_id={"dp": flip(self.my, 1)},
            device_id_type=MESH,
        )

    def begin(self):
        for phase in range(self.phases):
            for half in range(2):
                self.copy(half, phase, 0, self.my).start()
        for half in range(2):
            self.hand(half, 0, self.my, True).start()
        pltpu.make_async_copy(self.src, self.out.at[self.my], self.local).start()

    def arrive(self, phase):
        for half in range(2):
            mask = self.orders[half][phase]
            for count in range(2**phase):
                block = flip(self.my, mask ^ self.span(half, count))
                self.copy(half, phase, count, block).wait_recv()
            if phase + 1 < self.phases:
                for count in range(1, 2 ** (phase + 1)):
                    block = flip(self.my, self.span(half, count))
                    self.copy(half, phase + 1, count, block).start()
            for count in range(2**phase):
                block = flip(self.my, mask ^ self.span(half, count))
                self.hand(half, 2**phase + count, block).start()

    def finish(self):
        pltpu.make_async_copy(self.src, self.out.at[self.my], self.local).wait()
        other = flip(self.my, 1)
        for half in range(2):
            self.hand(half, 0, other, True).wait()
            for phase in range(self.phases):
                mask = self.orders[half][phase]
                for count in range(2**phase):
                    self.copy(half, phase, count, self.my).wait_send()
                    block = flip(other, mask ^ self.span(half, count))
                    self.hand(half, 2**phase + count, block).wait()


class GroupSum:
    def __init__(self, part, got, hold, passed, came, pass_send, pass_recv, send, recv, load):
        self.part, self.got, self.hold, self.passed, self.came = part, got, hold, passed, came
        self.pass_send, self.pass_recv = pass_send, pass_recv
        self.send, self.recv, self.load = send, recv, load
        self.my = lax.axis_index("dp")
        self.dp = part.shape[0]
        masks = masks_of(self.dp)
        self.orders = (masks, masks[::-1])
        self.phases = len(masks)

    @staticmethod
    def scratch(dp, rows, width):
        half = dp // 2
        return [
            pltpu.VMEM((2, half, rows, width), HALF),
            pltpu.VMEM((2, half, rows, width), HALF),
            pltpu.VMEM((2, half - 1, rows, width), HALF),
            pltpu.VMEM((2, half - 1, rows, width), HALF),
        ] + [pltpu.SemaphoreType.DMA((2, half)) for _ in range(5)]

    def span(self, half, count):
        mask = 0
        for k in range(self.phases):
            if count >> k & 1:
                mask |= self.orders[half][k]
        return mask

    def hand(self, half, count):
        block = flip(self.my, 1 ^ self.span(half, count))
        return pltpu.make_async_remote_copy(
            src_ref=self.part.at[block, half],
            dst_ref=self.got.at[half, count],
            send_sem=self.pass_send.at[half, count],
            recv_sem=self.pass_recv.at[half, count],
            device_id={"dp": flip(self.my, 1)},
            device_id_type=MESH,
        )

    def fetch(self, half, count):
        block = flip(self.my, self.span(half, count))
        return pltpu.make_async_copy(
            self.part.at[block, half], self.hold.at[half, count], self.load.at[half, count]
        )

    def copy(self, half, phase, index):
        return pltpu.make_async_remote_copy(
            src_ref=self.passed.at[half, 2**phase + index - 1],
            dst_ref=self.came.at[half, 2**phase - 1 + index],
            send_sem=self.send.at[half, 2**phase - 1 + index],
            recv_sem=self.recv.at[half, 2**phase - 1 + index],
            device_id={"dp": flip(self.my, self.orders[half][phase])},
            device_id_type=MESH,
        )

    def every(self):
        return [(half, count) for half in range(2) for count in range(self.dp // 2)]

    def begin(self):
        for half, count in self.every():
            self.hand(half, count).start()
            if self.hold is not None:
                self.fetch(half, count).start()

    def value(self, half, count, phase):
        if self.hold is None:
            mine = self.part[flip(self.my, self.span(half, count)), half]
        else:
            mine = self.hold[half, count]
        total = mine.astype(SINGLE) + self.got[half, count].astype(SINGLE)
        for later in range(phase, self.phases):
            total = total + self.came[half, 2**later - 1 + count].astype(SINGLE)
        return total

    def step(self, number):
        if number == 0:
            for half, count in self.every():
                if self.hold is not None:
                    self.fetch(half, count).wait()
                self.hand(half, count).wait_recv()
        else:
            self.took(self.phases - number)
        phase = self.phases - 1 - number
        for half in range(2):
            for index in range(2**phase):
                count = 2**phase + index
                self.passed[half, count - 1] = self.value(half, count, phase + 1).astype(HALF)
                self.copy(half, phase, index).start()

    def took(self, phase):
        for half in range(2):
            for index in range(2**phase):
                self.copy(half, phase, index).wait_recv()

    def finish(self, store):
        self.took(0)
        for half in range(2):
            store(half, self.value(half, 0, 0))
        self.sent(0)

    def sent(self, first):
        for half, count in self.every():
            self.hand(half, count).wait_send()
        for phase in range(first, self.phases):
            for half in range(2):
                for index in range(2**phase):
                    self.copy(half, phase, index).wait_send()


class LineGather:
    def __init__(self, n, src, out, send, recv, local, first=0, stop=None, land=None):
        self.n, self.src, self.out, self.land = n, src, out, land
        self.send, self.recv, self.local = send, recv, local
        self.first, self.stop = first, n - 1 if stop is None else stop
        self.me = lax.axis_index("seq")

    @staticmethod
    def scratch(n):
        return [
            pltpu.SemaphoreType.DMA((2, n - 1)),
            pltpu.SemaphoreType.DMA((2, n - 1)),
            pltpu.SemaphoreType.DMA,
        ]

    def inside(self, position):
        return both(position >= 0, position < self.n)

    def copy(self, way, hop, block, near):
        if hop > self.first:
            src = self.out.at[block]
        else:
            src = self.src if hop == 0 else self.src.at[way]
        return pltpu.make_async_remote_copy(
            src_ref=src,
            dst_ref=self.out.at[block] if self.land is None else self.land.at[way],
            send_sem=self.send.at[way, hop],
            recv_sem=self.recv.at[way, hop],
            device_id=on_line(near),
            device_id_type=MESH,
        )

    def each(self, hop):
        for way, sign in ((0, 1), (1, -1)):
            yield way, sign, self.me - sign * hop, self.me + sign

    def begin(self):
        self.launch(self.first)

    def launch(self, hop):
        for way, sign, block, near in self.each(hop):

            @pl.when(both(self.inside(block), self.inside(near)))
            def _():
                self.copy(way, hop, block, near).start()

    def keep(self):
        return pltpu.make_async_copy(self.src, self.out.at[self.me], self.local)

    def arrive(self, hop):
        for way, sign, block, near in self.each(hop + 1):

            @pl.when(self.inside(block))
            def _():
                self.copy(way, hop, block, near).wait_recv()

        if hop + 1 < self.stop:
            self.launch(hop + 1)

    def finish(self):
        for hop in range(self.first, self.stop):
            for way, sign, block, near in self.each(hop):

                @pl.when(both(self.inside(block), self.inside(near)))
                def _():
                    self.copy(way, hop, block, near).wait_send()


class LineSum:
    def __init__(self, n, part, out, got, mine, passed, send, recv, load, first=0, stop=None, tail=None, prev=None):
        self.n, self.part, self.out = n, part, out
        self.got, self.mine, self.passed = got, mine, passed
        self.send, self.recv, self.load = send, recv, load
        self.first, self.stop = first, n - 1 if stop is None else stop
        self.tail, self.prev = tail, prev
        self.me = lax.axis_index("seq")

    @staticmethod
    def scratch(n, rows, width, first=0, stop=None):
        stop = n - 1 if stop is None else stop
        return [
            pltpu.VMEM((2, stop - first + (first > 0), rows, width), HALF),
            pltpu.VMEM((2, rows, width), HALF),
            pltpu.VMEM((2, max(stop - max(first, 1), 1), rows, width), HALF),
            pltpu.SemaphoreType.DMA((2, n - 1)),
            pltpu.SemaphoreType.DMA((2, n - 1)),
            pltpu.SemaphoreType.DMA((2, 2)),
        ]

    def inside(self, position):
        return both(position >= 0, position < self.n)

    def each(self, step):
        reach = self.n - 1 - step
        for way, sign in ((0, 1), (1, -1)):
            yield way, self.me + sign * reach, self.me + sign, self.me - sign

    def slot(self, way, step):
        return self.passed.at[way, max(step - max(self.first, 1), 0)]

    def copy(self, way, step, src, near):
        if self.tail is not None and step == self.stop - 1:
            dst = self.tail.at[way]
        else:
            dst = self.got.at[way, step - self.first]
        return pltpu.make_async_remote_copy(
            src_ref=src,
            dst_ref=dst,
            send_sem=self.send.at[way, step],
            recv_sem=self.recv.at[way, step],
            device_id=on_line(near),
            device_id_type=MESH,
        )

    def round(self, step):
        for way, owner, near, behind in self.each(step):
            if step == 0:

                @pl.when(self.inside(owner))
                def _():
                    self.copy(way, step, self.part(owner), near).start()

                continue

            @pl.when(both(self.inside(owner), jnp.logical_not(self.inside(behind))))
            def _():
                self.copy(way, step, self.part(owner), near).start()

            @pl.when(both(self.inside(owner), self.inside(behind)))
            def _():
                fetch = pltpu.make_async_copy(
                    self.part(owner), self.mine.at[way], self.load.at[way, 0]
                )
                fetch.start()
                slot = self.slot(way, step)
                if step == self.first:
                    index = self.stop - self.first
                    held = pltpu.make_async_copy(
                        self.prev.at[way], self.got.at[way, index], self.load.at[way, 1]
                    )
                    held.start()
                    held.wait()
                else:
                    index = step - 1 - self.first
                    self.copy(way, step - 1, slot, near).wait_recv()
                fetch.wait()
                total = self.mine[way].astype(SINGLE) + self.got[way, index].astype(SINGLE)
                self.passed[way, step - max(self.first, 1)] = total.astype(HALF)
                self.copy(way, step, slot, near).start()

    def sent(self):
        for step in range(self.first, self.stop):
            for way, owner, near, behind in self.each(step):

                @pl.when(self.inside(owner))
                def _():
                    self.copy(way, step, self.slot(way, step), near).wait_send()

    def close(self):
        last = self.stop - 1
        for way, owner, near, behind in self.each(last + 1):

            @pl.when(both(self.inside(owner), self.inside(behind)))
            def _():
                self.copy(way, last, self.slot(way, last), near).wait_recv()

        self.sent()

    def finish(self):
        last = self.n - 2
        fetch = pltpu.make_async_copy(self.part(self.me), self.mine.at[0], self.load.at[0, 0])
        fetch.start()
        fetch.wait()
        self.out[...] = self.mine[0].astype(SINGLE)
        for way, owner, near, behind in self.each(last):

            @pl.when(self.inside(behind))
            def _():
                self.copy(way, last, self.slot(way, last), near).wait_recv()
                self.out[...] += self.got[way, last - self.first].astype(SINGLE)

        self.sent()


def at_rows(ref):
    return lambda owner: ref.at[owner]


def at_step(step, when, action):
    @pl.when(step == when)
    def _():
        action()


def to_group(my, dp, offset, src, dst, send, recv):
    peer = lax.rem(my + offset, dp)
    return pltpu.make_async_remote_copy(
        src_ref=src if src.shape == dst.shape[1:] else src.at[peer],
        dst_ref=dst.at[my],
        send_sem=send.at[offset - 1],
        recv_sem=recv.at[offset - 1],
        device_id={"dp": peer},
        device_id_type=MESH,
    )


def to_line(me, n, offset, src, dst, send, recv):
    peer = lax.rem(me + offset, n)
    return pltpu.make_async_remote_copy(
        src_ref=src if src.shape == dst.shape[1:] else src.at[peer],
        dst_ref=dst.at[me],
        send_sem=send.at[offset - 1],
        recv_sem=recv.at[offset - 1],
        device_id=on_line(peer),
        device_id_type=MESH,
    )


def start_kernel(
    n, dp, x_ref, cond_ref, ada_ref, ada_bias, proj_bias, fc2_bias, length_ref, qkv_ref, fc1_ref,
    x_all, side_all, acts, mods, shifts, qkv_all, fc1_all,
    act_ref, part, parts, row, a_send, a_recv, p_send, p_recv, s_send, s_recv, *sems,
):
    me, my = lax.axis_index("seq"), lax.axis_index("dp")
    depth, _, cols = ada_ref.shape
    width = x_ref.shape[1]
    greet(n, "all", "all")
    gather = LineGather(n, x_ref, x_all, *sems[:3])
    qkv = GroupGather(qkv_ref, qkv_all, *sems[3:8])
    fc1 = GroupGather(fc1_ref, fc1_all, *sems[8:13])
    gather.begin()
    cond = cond_ref[...].astype(SINGLE)
    act = (cond / (1.0 + jnp.exp(-cond))).astype(HALF).astype(SINGLE)
    act_ref[...] = jnp.zeros_like(act_ref)
    for k in range(dp):
        act_ref[k, :, :depth] = act[:, k * depth : (k + 1) * depth]
    others = range(1, dp)
    act_go = [to_group(my, dp, k, act_ref, acts, a_send, a_recv) for k in others]
    for copy in act_go:
        copy.start()
    gather.keep().start()
    acts[my] = act_ref[my]
    for copy in act_go:
        copy.wait_recv()
    rows = acts[:, 0, :depth].astype(HALF)
    for t in range(2):
        product = nn_dot(rows, ada_ref[:, t, :])
        for k in range(dp):
            part[k, :, t * cols : (t + 1) * cols] = product[k : k + 1]
    part_go = [to_group(my, dp, k, part, parts, p_send, p_recv) for k in others]
    for copy in part_go:
        copy.start()
    parts[my] = part[my]
    place = 0
    for ref in (ada_bias, proj_bias, fc2_bias):
        for t in range(2):
            size = ref.shape[1]
            row[:, place : place + size] = ref[t : t + 1].astype(SINGLE)
            place += size
    row[:, place:] = jnp.full((1, LANES), length_ref[0, 0].astype(SINGLE))
    for copy in part_go:
        copy.wait_recv()
    qkv.begin()
    fc1.begin()
    row[:, : 2 * cols] += jnp.sum(parts[...], axis=0)
    row_go = [to_line(me, n, k, row, side_all, s_send, s_recv) for k in range(1, n)]
    for copy in row_go:
        copy.start()
    side_all[me] = row[...]
    for hop in range(max(n - 1, qkv.phases)):
        if hop < n - 1:
            gather.arrive(hop)
        if hop < qkv.phases:
            qkv.arrive(hop)
            fc1.arrive(hop)
    for copy in row_go:
        copy.wait()
    mods[...] = jnp.zeros_like(mods)
    piece = math.gcd(cols, width)
    share = proj_bias.shape[1]
    for z in range(n):
        for t in range(2):
            for start in range(0, cols, piece):
                to, at = divmod(z * cols + start, width)
                mods[t, to : to + 1, at : at + piece] = side_all[
                    z, :, t * cols + start : t * cols + start + piece
                ]
        for k in range(4):
            start = 2 * cols + k * share
            shifts[k : k + 1, z * share : (z + 1) * share] = side_all[z, :, start : start + share]
    for copy in act_go + part_go:
        copy.wait_send()
    gather.keep().wait()
    gather.finish()
    qkv.finish()
    fc1.finish()


def start(n, dp, x_loc, cond, ada, ada_bias, proj_bias, fc2_bias, length, qkv, fc1):
    rows, width = x_loc.shape
    depth, _, cols = ada.shape
    span = 2 * cols + 4 * proj_bias.shape[1] + LANES
    anywhere = pl.BlockSpec(memory_space=pl.ANY)
    inner = pl.BlockSpec(memory_space=pltpu.VMEM)
    scalar = pl.BlockSpec(memory_space=pltpu.SMEM)
    return pl.pallas_call(
        functools.partial(start_kernel, n, dp),
        in_specs=[inner] * 6 + [scalar, inner, inner],
        out_specs=[anywhere, inner, inner, inner, inner, anywhere, anywhere],
        out_shape=[
            jax.ShapeDtypeStruct((n, rows, width), HALF),
            jax.ShapeDtypeStruct((n, 1, span), SINGLE),
            jax.ShapeDtypeStruct((dp, 1, up(depth, LANES)), SINGLE),
            jax.ShapeDtypeStruct((2, 8, width), SINGLE),
            jax.ShapeDtypeStruct((4, width), SINGLE),
            jax.ShapeDtypeStruct((dp,) + qkv.shape, HALF),
            jax.ShapeDtypeStruct((dp,) + fc1.shape, HALF),
        ],
        scratch_shapes=[
            pltpu.VMEM((dp, 1, up(depth, LANES)), SINGLE),
            pltpu.VMEM((dp, 1, 2 * cols), SINGLE),
            pltpu.VMEM((dp, 1, 2 * cols), SINGLE),
            pltpu.VMEM((1, span), SINGLE),
            pltpu.SemaphoreType.DMA((dp - 1,)),
            pltpu.SemaphoreType.DMA((dp - 1,)),
            pltpu.SemaphoreType.DMA((dp - 1,)),
            pltpu.SemaphoreType.DMA((dp - 1,)),
            pltpu.SemaphoreType.DMA((n - 1,)),
            pltpu.SemaphoreType.DMA((n - 1,)),
        ]
        + LineGather.scratch(n)
        + GroupGather.scratch(dp)
        + GroupGather.scratch(dp),
        compiler_params=remote(1),
        cost_estimate=cost(10**6, 100 * MEGA),
        name="start",
    )(x_loc, cond, ada, ada_bias, proj_bias, fc2_bias, length, qkv, fc1)


def qkv_kernel(img, x_ref, mod_ref, w_ref, b_ref, a_ref, o_ref):
    wide = o_ref.shape[2]
    for t, sl in ((0, slice(0, img)), (1, slice(img, x_ref.shape[1]))):
        normed, _ = layer_norm(x_ref[0, sl].astype(SINGLE))
        a = (normed * (1.0 + mod_ref[t, 1:2]) + mod_ref[t, 0:1]).astype(HALF)
        a_ref[0, sl] = a
        o_ref[0, sl] = (
            nn_dot(a, w_ref[:, t * wide : (t + 1) * wide]) + b_ref[t : t + 1]
        ).astype(HALF)


def project_qkv(n, img, x_all, mods, weight, bias):
    _, rows, width = x_all.shape
    wide = weight.shape[1] // 2
    return pl.pallas_call(
        functools.partial(qkv_kernel, img),
        grid=(n,),
        in_specs=[
            rows_spec(rows, width),
            whole(mods.shape),
            whole(weight.shape, True),
            whole(bias.shape),
        ],
        out_specs=[rows_spec(rows, width), rows_spec(rows, wide)],
        out_shape=[
            jax.ShapeDtypeStruct((n, rows, width), HALF),
            jax.ShapeDtypeStruct((n, rows, wide), HALF),
        ],
        compiler_params=params(),
        cost_estimate=cost(2 * n * rows * width * wide, 30 * MEGA),
        name="project_qkv",
    )(x_all, mods, weight, bias)


def halves(shape):
    lane = lax.broadcasted_iota(jnp.int32, shape, len(shape) - 1)
    return lane < HD


def attn_kernel(
    n, q_ref, k_ref, v_ref, mask_ref, e_ref, p_ref, o_ref, lse_ref, e_near, mix_ref, p_all,
    o_buf, o_send, o_recv, o_local, *sems,
):
    pair, block = pl.program_id(0), pl.program_id(1)
    pairs = pl.num_programs(0)
    step = pair * n + block
    me = lax.axis_index("seq")
    count, rows, _ = k_ref.shape
    gather = LineGather(n, e_ref, None, *sems[:3], first=0, stop=1, land=e_near)
    proj = GroupGather(p_ref, p_all, *sems[3:])

    def begin():
        greet(n, "all", "paths")
        gather.begin()
        proj.begin()

    at_step(step, 0, begin)
    queries = q_ref[0] * HALF(1.0 / math.sqrt(HD))
    keys = k_ref[...].reshape(n * rows, LANES)
    values = v_ref[...].reshape(n * rows, LANES)
    first = halves(queries.shape)
    zero = HALF(0)
    pair_rows = jnp.concatenate([jnp.where(first, queries, zero), jnp.where(first, zero, queries)])
    scores = nt_dot(pair_rows, keys) + mask_ref[...]
    maxima = jnp.max(scores, axis=-1, keepdims=True)
    raised = jnp.exp(scores - maxima)
    totals = jnp.sum(raised, axis=-1, keepdims=True)
    weights = (raised * (1.0 / totals)).astype(HALF)
    outs = nn_dot(weights, values)
    logs = maxima + jnp.log(totals)
    mixed = jnp.where(first, outs[:rows], outs[rows:]).astype(HALF)
    o_ref[0] = mixed
    o_buf[pair, block] = mixed
    lse_ref[0] = jnp.where(first, logs[:rows], logs[rows:])
    static_pairs = o_buf.shape[0]

    def columns(sender, which):
        start = (sender * static_pairs + which) * LANES
        return mix_ref.at[:, pl.ds(pl.multiple_of(start, LANES), LANES)]

    def away(which, offset):
        peer = lax.rem(me + offset, n)
        return pltpu.make_async_remote_copy(
            src_ref=o_buf.at[which, peer],
            dst_ref=columns(me, which),
            send_sem=o_send.at[which, offset - 1],
            recv_sem=o_recv.at[which, offset - 1],
            device_id=on_line(peer),
            device_id_type=MESH,
        )

    for offset in range(1, n):

        @pl.when(block == lax.rem(me + offset, n))
        def _():
            away(pair, offset).start()

    @pl.when(block == me)
    def _():
        pltpu.make_async_copy(o_buf.at[pair, me], columns(me, pair), o_local.at[pair]).start()

    last = static_pairs * n - 1
    for phase in range(proj.phases):
        at_step(step, min(last, 5 * phase + 5), functools.partial(proj.arrive, phase))

    def finish():
        gather.arrive(0)
        proj.finish()
        for which in range(static_pairs):
            pltpu.make_async_copy(o_buf.at[which, me], columns(me, which), o_local.at[which]).wait()
            for offset in range(1, n):
                away(which, offset).wait()
        gather.finish()

    at_step(step, last, finish)


def attend(n, dp, qkv, mask, e_loc, proj):
    _, rows, wide = qkv.shape
    width = e_loc.shape[1]
    pairs = wide // 3 // LANES
    total = n * rows
    block = pl.BlockSpec((1, rows, LANES), lambda h, s: (s, 0, h))
    anywhere = pl.BlockSpec(memory_space=pl.ANY)
    return pl.pallas_call(
        functools.partial(attn_kernel, n),
        grid=(pairs, n),
        in_specs=[
            block,
            pl.BlockSpec((n, rows, LANES), lambda h, s: (0, 0, pairs + h)),
            pl.BlockSpec((n, rows, LANES), lambda h, s: (0, 0, 2 * pairs + h)),
            whole(mask.shape),
            anywhere,
            whole(proj.shape, True),
        ],
        out_specs=[block, block, anywhere, anywhere, anywhere],
        out_shape=[
            jax.ShapeDtypeStruct((n, rows, pairs * LANES), HALF),
            jax.ShapeDtypeStruct((n, rows, pairs * LANES), SINGLE),
            jax.ShapeDtypeStruct((2, rows, width), HALF),
            jax.ShapeDtypeStruct((rows, n * pairs * LANES), HALF),
            jax.ShapeDtypeStruct((dp,) + proj.shape, HALF),
        ],
        scratch_shapes=[
            pltpu.VMEM((pairs, n, rows, LANES), HALF),
            pltpu.SemaphoreType.DMA((pairs, n - 1)),
            pltpu.SemaphoreType.DMA((pairs, n - 1)),
            pltpu.SemaphoreType.DMA((pairs,)),
        ]
        + LineGather.scratch(n)
        + GroupGather.scratch(dp),
        compiler_params=remote(2),
        cost_estimate=cost(2 * 2 * 4 * pairs * total * total * LANES, 20 * MEGA, 2 * pairs * total * total),
        name="attend",
    )(qkv, qkv, qkv, mask, e_loc, proj)


def attn_back_kernel(
    lines, img, pairs, q_ref, k_ref, v_ref, o_ref, g_ref, lse_ref, mask_ref, y_ref, l_ref, r_ref,
    dq_ref, dk_ref, dv_ref, qb_ref, vb_ref, p_ref, tail,
    acc_ref, lse_row, delta_row, turned, *scratch,
):
    linear = pl.program_id(0)
    ahead = 2 * lines
    attn_steps = pairs * lines
    last = ahead + attn_steps - 1
    step = lax.rem(lax.max(linear - ahead, 0), lines)
    n, rows, _ = q_ref.shape
    total = n * rows
    line = LineSum(lines, at_rows(y_ref), None, *scratch, stop=lines - 2, tail=tail)

    def begin():
        greet(lines, "near")
        line.round(0)

    at_step(linear, 0, begin)
    for t, sl in ((0, slice(0, img)), (1, slice(img, rows))):

        @pl.when(linear == 0)
        def _():
            turned[:, sl] = l_ref[sl].T

        @pl.when(both(linear < ahead, lax.rem(linear, 2) == t))
        def _():
            p_ref[...] = nn_dot(turned[:, sl], r_ref[sl]).astype(HALF).reshape(p_ref.shape)

    @pl.when(linear >= ahead)
    def _():
        grads = g_ref[...].reshape(total, LANES)
        queries = q_ref[...].reshape(total, LANES) * HALF(1.0 / math.sqrt(HD))

        @pl.when(step == 0)
        def _():
            acc_ref[...] = jnp.zeros_like(acc_ref)
            product = grads.astype(SINGLE) * o_ref[...].reshape(total, LANES).astype(SINGLE)
            flipped = product.T
            logs = lse_ref[...].reshape(total, LANES).T
            for head in range(2):
                delta_row[head : head + 1] = jnp.sum(
                    flipped[head * HD : (head + 1) * HD], axis=0, keepdims=True
                )
                lse_row[head : head + 1] = logs[head * HD : head * HD + 1]
            vb_ref[0] = jnp.zeros_like(vb_ref[0])

        keys, values = k_ref[0], v_ref[0]
        first = halves(keys.shape)
        mask = mask_ref[0][:, 0:1]
        zero = HALF(0)

        def pair(value):
            return jnp.concatenate([jnp.where(first, value, zero), jnp.where(first, zero, value)])

        def by_head(row):
            return row[...].reshape(2, 1, total)

        key_pair = pair(keys)
        scores = nt_dot(key_pair, queries).reshape(2, rows, total)
        probs = jnp.exp((scores - by_head(lse_row)) + mask)
        grad_prob = nt_dot(pair(values), grads).reshape(2, rows, total)
        grad_score = (probs * (grad_prob - by_head(delta_row))).astype(HALF)
        grad_score = grad_score.reshape(2 * rows, total)
        dvs = nn_dot(probs.astype(HALF).reshape(2 * rows, total), grads)
        dks = nn_dot(grad_score, queries)
        acc_ref[...] += tn_dot(grad_score, key_pair)
        dk_ref[0] = jnp.where(first, dks[:rows], dks[rows:]).astype(HALF)
        dv = jnp.where(first, dvs[:rows], dvs[rows:])
        dv_ref[0] = dv.astype(HALF)
        vb_ref[0, 0:1] += jnp.sum(dv[:img], axis=0, keepdims=True)
        vb_ref[0, 1:2] += jnp.sum(dv[img:], axis=0, keepdims=True)

        @pl.when(step == lines - 1)
        def _():
            dq = (acc_ref[...] * (1.0 / math.sqrt(HD))).reshape(n, rows, LANES)
            dq_ref[...] = dq.astype(HALF)
            qb_ref[0, 0:1] = jnp.sum(jnp.sum(dq[:, :img], axis=0), axis=0, keepdims=True)
            qb_ref[0, 1:2] = jnp.sum(jnp.sum(dq[:, img:], axis=0), axis=0, keepdims=True)

    for hop in range(1, lines - 2):
        at_step(linear, min(last, ahead + 5 * hop), functools.partial(line.round, hop))

    at_step(linear, last, line.close)


def attend_back(n, dp, img, qkv, mixture, grad_mix, lse, mask_col, out_parts, grad_attn, mix_loc):
    _, rows, wide = qkv.shape
    pairs = wide // 3 // LANES
    total = n * rows
    lw = pairs * LANES
    ahead = 2 * n
    steps = pairs * n
    width = out_parts.shape[2]
    depth = width // dp

    def place(k):
        return lax.rem(lax.max(k - ahead, 0), n)

    def head(k):
        return lax.div(lax.max(k - ahead, 0), n)

    full = pl.BlockSpec((n, rows, LANES), lambda k: (0, 0, head(k)))

    def block(base):
        return pl.BlockSpec((1, rows, LANES), lambda k: (place(k), 0, base + head(k)))

    bias = pl.BlockSpec((1, 2, LANES), lambda k: (head(k), 0, 0))
    anywhere = pl.BlockSpec(memory_space=pl.ANY)
    return pl.pallas_call(
        functools.partial(attn_back_kernel, n, img, pairs),
        grid=(ahead + steps,),
        in_specs=[
            full,
            block(pairs),
            block(2 * pairs),
            full,
            full,
            full,
            pl.BlockSpec((1, rows, LANES), lambda k: (place(k), 0, 0)),
            anywhere,
            whole(grad_attn.shape, True),
            pl.BlockSpec((rows, lw), lambda k: (0, lax.min(lax.div(k, 2), n - 1))),
        ],
        out_specs=[
            full,
            block(0),
            block(0),
            bias,
            bias,
            pl.BlockSpec((dp, 1, depth, lw), lambda k: (0, lax.min(k, ahead - 1), 0, 0)),
            anywhere,
        ],
        out_shape=[jax.ShapeDtypeStruct((n, rows, lw), HALF)] * 3
        + [jax.ShapeDtypeStruct((pairs, 2, LANES), SINGLE)] * 2
        + [
            jax.ShapeDtypeStruct((dp, 2 * n, depth, lw), HALF),
            jax.ShapeDtypeStruct((2, rows, width), HALF),
        ],
        scratch_shapes=[
            pltpu.VMEM((total, LANES), SINGLE),
            pltpu.VMEM((2, total), SINGLE),
            pltpu.VMEM((2, total), SINGLE),
            pltpu.VMEM((width, rows), HALF),
        ]
        + LineSum.scratch(n, rows, width, stop=n - 2),
        compiler_params=remote(3, 62),
        cost_estimate=cost(2 * 5 * 4 * pairs * total * total * LANES, 30 * MEGA, 2 * pairs * total * total),
        name="attend_back",
    )(qkv, qkv, qkv, mixture, grad_mix, lse, mask_col, out_parts, grad_attn, mix_loc)


def proj_columns(w_ref, z, t):
    dp, _, _, depth, heads = w_ref.shape
    return w_ref[:, z, t].reshape(dp * depth, heads)


def middle_kernel(
    n, img, mix_ref, x_ref, w_ref, b_ref, mod_ref, fc2_ref, y_ref, m_ref, all_ref, fc2_all, own, *sems
):
    greet(n, "near", "paths")
    fc2 = GroupGather(fc2_ref, fc2_all, *sems[3:])
    fc2.begin()
    lw = mix_ref.shape[1] // n
    heads = w_ref.shape[4]
    for t, sl in ((0, slice(0, img)), (1, slice(img, x_ref.shape[0]))):
        attn = b_ref[t : t + 1]
        for z in range(n):
            attn = attn + nt_dot(mix_ref[sl, z * lw : z * lw + heads], proj_columns(w_ref, z, t))
        y_ref[sl] = attn
        middle = x_ref[sl].astype(SINGLE) + mod_ref[t, 2:3] * attn
        m_ref[sl] = middle
        normed, _ = layer_norm(middle)
        own[sl] = (normed * (1.0 + mod_ref[t, 4:5]) + mod_ref[t, 3:4]).astype(HALF)
    gather = LineGather(n, own, all_ref, *sems[:3])
    gather.begin()
    gather.keep().start()
    for hop in range(max(n - 1, fc2.phases)):
        if hop < fc2.phases:
            fc2.arrive(hop)
        if hop < n - 1:
            gather.arrive(hop)
    gather.keep().wait()
    gather.finish()
    fc2.finish()


def middle_rows(n, dp, img, mixture, x_loc, weight, bias, mods, fc2):
    rows, width = x_loc.shape
    inner = pl.BlockSpec(memory_space=pltpu.VMEM)
    anywhere = pl.BlockSpec(memory_space=pl.ANY)
    return pl.pallas_call(
        functools.partial(middle_kernel, n, img),
        in_specs=[inner] * 6,
        out_specs=[inner, inner, anywhere, anywhere],
        out_shape=[
            jax.ShapeDtypeStruct((rows, width), SINGLE),
            jax.ShapeDtypeStruct((rows, width), SINGLE),
            jax.ShapeDtypeStruct((n, rows, width), HALF),
            jax.ShapeDtypeStruct((dp,) + fc2.shape, HALF),
        ],
        scratch_shapes=[pltpu.VMEM((rows, width), HALF)]
        + LineGather.scratch(n)
        + GroupGather.scratch(dp),
        compiler_params=remote(4),
        cost_estimate=cost(2 * rows * width * width, 100 * MEGA),
        name="middle_rows",
    )(mixture, x_loc, weight, bias, mods, fc2)


def by_distance(me, n, count):
    low = lax.min(me, n - 1 - me)
    near = lax.select(lax.rem(count, 2) == 1, lax.div(count + 1, 2), -lax.div(count, 2))
    far = lax.select(me < n - 1 - me, count - low, low - count)
    return me + lax.select(count <= 2 * low, near, far)


def mlp_kernel(n, img, tile, b_ref, e_loc, e_near, mod_ref, w1_ref, b1_ref, w2_ref,
    g_ref, dz_ref, dy_ref, db_ref, y_ref, sum_ref, gate_ref, acc_ref, out_ref, e_all, near_sem, *sems):
    step = pl.program_id(0)
    me = lax.axis_index("seq")
    owner = by_distance(me, n, step)
    e_ref = e_all.at[pl.ds(owner, 1)]
    gather = LineGather(n, e_near, e_all, *sems, first=1)
    own = pltpu.make_async_copy(e_loc, e_all.at[me], near_sem.at[2])

    def nears(action):
        for way, sign in ((0, 1), (1, -1)):
            block = me - sign

            @pl.when(both(block >= 0, block < n))
            def _():
                action(
                    pltpu.make_async_copy(e_near.at[way], e_all.at[block], near_sem.at[way])
                )

    def begin():
        greet(n, "near")
        gather.begin()
        own.start()
        nears(lambda copy: copy.start())
        own.wait()
        nears(lambda copy: copy.wait())

    at_step(step, 0, begin)
    for hop in range(1, n - 1):
        at_step(step, hop + 1, functools.partial(gather.arrive, hop))
    at_step(step, n - 1, gather.finish)
    units = g_ref.shape[2]

    @pl.when(step == 0)
    def _():
        sum_ref[...] = jnp.zeros_like(sum_ref)
        gate_ref[...] = jnp.zeros_like(gate_ref)

    for t, sl in ((0, slice(0, img)), (1, slice(img, b_ref.shape[1]))):
        rows = b_ref[0, sl]
        grad = (mod_ref[t, 5:6] * e_ref[0, sl].astype(SINGLE)).astype(HALF)
        dy_ref[0, sl] = grad

        for k in range(units // tile):
            here = slice(k * tile, (k + 1) * tile)
            cols = slice(t * units + k * tile, t * units + (k + 1) * tile)
            w1 = w1_ref[:, cols]
            pre = nn_dot(rows, w1) + b1_ref[t : t + 1, here]
            hidden, slope = gelu_both(pre)
            hidden = hidden.astype(HALF)
            g_ref[0, sl, here] = hidden
            w2 = w2_ref[:, t, :, here].reshape(-1, tile)
            out = nt_dot(hidden, w2)
            dz = nn_dot(grad, w2) * slope
            sum_ref[t : t + 1, here] += jnp.sum(dz, axis=0, keepdims=True)
            dzh = dz.astype(HALF)
            dz_ref[0, sl, here] = dzh
            part = nt_dot(dzh, w1)
            if k == 0:
                acc_ref[sl] = part
                out_ref[sl] = out
            else:
                acc_ref[sl] += part
                out_ref[sl] += out
        db_ref[0, sl] = acc_ref[sl].astype(HALF)
        out = out_ref[sl]
        y_ref[0, sl] = out.astype(HALF)
        gate_ref[t : t + 1] += jnp.sum(out * e_ref[0, sl].astype(SINGLE), axis=0, keepdims=True)


def feed_forward(n, img, mlp_in, e_loc, e_near, mods, w1, b1, w2):
    rows, width = mlp_in.shape[1:]
    units = w1.shape[1] // 2
    tile = min(768, units)
    while units % tile:
        tile -= LANES

    def owned(columns):
        return pl.BlockSpec(
            (1, rows, columns), lambda k: (by_distance(lax.axis_index("seq"), n, k), 0, 0)
        )

    return pl.pallas_call(
        functools.partial(mlp_kernel, n, img, tile),
        grid=(n,),
        in_specs=[
            owned(width),
            pl.BlockSpec(memory_space=pl.ANY),
            pl.BlockSpec(memory_space=pl.ANY),
            whole(mods.shape),
            whole(w1.shape, True),
            whole(b1.shape),
            whole(w2.shape, True),
        ],
        out_specs=[
            owned(units),
            owned(units),
            owned(width),
            owned(width),
            owned(width),
            whole((2, units)),
            whole((2, width)),
        ],
        out_shape=[
            jax.ShapeDtypeStruct((n, rows, units), HALF),
            jax.ShapeDtypeStruct((n, rows, units), HALF),
            jax.ShapeDtypeStruct((n, rows, width), HALF),
            jax.ShapeDtypeStruct((n, rows, width), HALF),
            jax.ShapeDtypeStruct((n, rows, width), HALF),
            jax.ShapeDtypeStruct((2, units), SINGLE),
            jax.ShapeDtypeStruct((2, width), SINGLE),
        ],
        scratch_shapes=[
            pltpu.VMEM((rows, width), SINGLE),
            pltpu.VMEM((rows, width), SINGLE),
            pltpu.VMEM((n, rows, width), HALF),
            pltpu.SemaphoreType.DMA((3,)),
        ]
        + LineGather.scratch(n),
        compiler_params=remote(9, 60),
        cost_estimate=cost(6 * n * rows * width * units, 50 * MEGA, n * rows * units),
        name="feed_forward",
    )(mlp_in, e_loc, e_near, mods, w1, b1, w2)


def grads_kernel(n, img, plan, rounds, *refs):
    lefts = max(p[0] for p in plan) + 1
    rights = max(p[1] for p in plan) + 1
    l_refs, r_refs = refs[:lefts], refs[lefts : lefts + rights]
    rest = refs[lefts + rights :]
    step = pl.program_id(0)
    if rounds:
        parts, o_ref, tail, turned = rest[:4]
        line = LineSum(n, at_rows(parts), None, *rest[4:], stop=n - 2, tail=tail)

        def begin():
            greet(n, "near")
            line.round(0)

        at_step(step, 0, begin)
    else:
        o_ref, turned = rest
    tile = 512 if o_ref.shape[3] % 512 == 0 else 2 * LANES
    before = None
    for k, (left, right, stream) in enumerate(plan):

        @pl.when(step == k)
        def _():
            l_ref, r_ref = l_refs[left], r_refs[right]
            count, rows, _ = l_ref.shape
            sl = slice(0, img) if stream == 0 else slice(img, rows)
            size = count * (sl.stop - sl.start)
            if before != (left, stream):
                turned[:, :size] = l_ref[:, sl].reshape(size, l_ref.shape[2]).T
            for column in range(0, o_ref.shape[3], tile):
                values = r_ref[:, sl, column : column + tile].reshape(size, tile)
                product = nn_dot(turned[:, :size], values).astype(HALF)
                o_ref[:, 0, :, column : column + tile] = product.reshape(
                    o_ref.shape[0], o_ref.shape[2], tile
                )

        before = (left, stream)
    if rounds:
        for hop, when in enumerate(rounds):
            at_step(step, when, functools.partial(line.round, hop + 1))
        at_step(step, len(plan) - 1, line.close)


def weight_grads(n, dp, img, lefts, rights, plan, rounds, parts, collective, name):
    rows, depth = lefts[0].shape[1:]
    wide = rights[0].shape[2]
    anywhere = pl.BlockSpec(memory_space=pl.ANY)
    block = (dp, 1, depth // dp, wide)
    longest = max(up(n * img, LANES), up(n * (rows - img), LANES))
    return pl.pallas_call(
        functools.partial(grads_kernel, n, img, plan, rounds),
        grid=(len(plan),),
        in_specs=[whole(a.shape, True) for a in (*lefts, *rights)] + [anywhere],
        out_specs=[pl.BlockSpec(block, lambda k: (0, k, 0, 0)), anywhere],
        out_shape=[
            jax.ShapeDtypeStruct((dp, len(plan), depth // dp, wide), HALF),
            jax.ShapeDtypeStruct((2,) + parts.shape[1:], HALF),
        ],
        scratch_shapes=[pltpu.VMEM((depth, longest), HALF)]
        + LineSum.scratch(n, *parts.shape[1:], stop=n - 2),
        compiler_params=remote(collective, 60),
        cost_estimate=cost(2 * n * rows * depth * len(plan) * wide // 2, 60 * MEGA),
        name=name,
    )(*lefts, *rights, parts)


def middle_back_kernel(
    n, img, part_ref, prev_ref, m_ref, y_ref, e_ref, w_ref, mod_ref, dm_ref, dy_ref, sum_ref, all_ref,
    db_ref, mix, send, recv, local, *line_scratch,
):
    me = lax.axis_index("seq")
    rows, width = m_ref.shape
    heads = w_ref.shape[4]
    streams = ((0, slice(0, img)), (1, slice(img, rows)))
    greet(n, "all")
    line = LineSum(n, at_rows(part_ref), db_ref, *line_scratch, first=n - 2, prev=prev_ref)
    line.round(n - 2)
    if mix.shape[2] > heads:
        mix[...] = jnp.zeros_like(mix)
    line.finish()
    for t, sl in streams:
        grad_in = db_ref[sl]
        normed, inv_std = layer_norm(m_ref[sl])
        upstream = e_ref[sl].astype(SINGLE)
        grad_middle = upstream + norm_back(normed, inv_std, grad_in * (1.0 + mod_ref[t, 4:5]))
        dm_ref[sl] = grad_middle
        grad_attn = mod_ref[t, 2:3] * grad_middle
        dy_ref[sl] = grad_attn.astype(HALF)

        def total(value):
            return jnp.sum(value, axis=0, keepdims=True)

        sum_ref[t, 0:1] = total(grad_middle * y_ref[sl])
        sum_ref[t, 1:2] = total(grad_in)
        sum_ref[t, 2:3] = total(grad_in * normed)
        sum_ref[t, 3:4] = total(grad_attn)
        sum_ref[t, 4:5] = total(upstream)

    def exchange(peer, block):
        return pltpu.make_async_remote_copy(
            src_ref=mix.at[peer],
            dst_ref=all_ref.at[block],
            send_sem=send.at[peer],
            recv_sem=recv.at[block],
            device_id=on_line(peer),
            device_id_type=MESH,
        )

    keep = pltpu.make_async_copy(mix.at[me], all_ref.at[me], local)
    for peer in range(n):
        for t, sl in streams:
            mix[peer, sl, :heads] = nn_dot(dy_ref[sl], proj_columns(w_ref, peer, t)).astype(HALF)

        @pl.when(peer != me)
        def _():
            exchange(peer, me).start()

        @pl.when(peer == me)
        def _():
            keep.start()

    for peer in range(n):

        @pl.when(peer != me)
        def _():
            exchange(peer, peer).wait()

    keep.wait()


def middle_back(n, img, parts, prev, middle, attn_out, cot, weight, mods, lwp):
    rows, width = middle.shape
    inner = pl.BlockSpec(memory_space=pltpu.VMEM)
    anywhere = pl.BlockSpec(memory_space=pl.ANY)
    return pl.pallas_call(
        functools.partial(middle_back_kernel, n, img),
        in_specs=[anywhere, anywhere] + [inner] * 5,
        out_specs=[inner, inner, inner, anywhere],
        out_shape=[
            jax.ShapeDtypeStruct((rows, width), SINGLE),
            jax.ShapeDtypeStruct((rows, width), HALF),
            jax.ShapeDtypeStruct((2, 8, width), SINGLE),
            jax.ShapeDtypeStruct((n, rows, lwp), HALF),
        ],
        scratch_shapes=[
            pltpu.VMEM((rows, width), SINGLE),
            pltpu.VMEM((n, rows, lwp), HALF),
            pltpu.SemaphoreType.DMA((n,)),
            pltpu.SemaphoreType.DMA((n,)),
            pltpu.SemaphoreType.DMA,
        ]
        + LineSum.scratch(n, rows, width, first=n - 2),
        compiler_params=remote(5),
        cost_estimate=cost(2 * rows * width * width, 60 * MEGA),
        name="middle_back",
    )(parts, prev, middle, attn_out, cot, weight, mods)


def attn_in_kernel(
    n, img, dq_ref, dk_ref, dv_ref, x_ref, a_ref, w_ref, y_ref, prev_ref,
    da_ref, sum_ref, g_ref, y_sum, turned, *scratch,
):
    step = pl.program_id(0)
    count, rows, lw = dq_ref.shape
    line = LineSum(n, at_rows(y_ref), y_sum, *scratch, first=n - 2, prev=prev_ref)
    streams = ((0, slice(0, img)), (1, slice(img, rows)))

    def begin():
        greet(n, "near")
        line.round(n - 2)
        sum_ref[...] = jnp.zeros_like(sum_ref)

    at_step(step, 0, begin)

    @pl.when(step < n)
    def _():
        here = lax.min(step, n - 1)
        for t, sl in streams:
            part = None
            for c, ref in enumerate((dq_ref, dk_ref, dv_ref)):
                start = (3 * t + c) * lw
                term = nt_dot(ref[here, sl], w_ref[:, start : start + lw])
                part = term if part is None else part + term
            da_ref[0, sl] = part.astype(HALF)
            normed, _ = layer_norm(x_ref[0, sl].astype(SINGLE))
            sum_ref[t, 0:1] += jnp.sum(part, axis=0, keepdims=True)
            sum_ref[t, 1:2] += jnp.sum(part * normed, axis=0, keepdims=True)

    for t, sl in streams:
        size = count * (sl.stop - sl.start)
        for c, ref in enumerate((dq_ref, dk_ref, dv_ref)):

            @pl.when(step == n + 3 * t + c)
            def _():
                if c == 0:
                    turned[:, :size] = a_ref[:, sl].reshape(size, a_ref.shape[2]).T
                g_ref[...] = nn_dot(turned[:, :size], ref[:, sl].reshape(size, lw)).astype(HALF)

    at_step(step, n + 5, line.finish)


def attn_in_back(n, img, dq, dk, dv, x_all, attn_in, weight, out_parts, running):
    _, rows, lw = dq.shape
    width = x_all.shape[2]
    anywhere = pl.BlockSpec(memory_space=pl.ANY)
    row = pl.BlockSpec((1, rows, width), lambda k: (lax.min(k, n - 1), 0, 0))
    longest = max(up(n * img, LANES), up(n * (rows - img), LANES))
    return pl.pallas_call(
        functools.partial(attn_in_kernel, n, img),
        grid=(n + 6,),
        in_specs=[whole(dq.shape, True)] * 3
        + [row, whole(attn_in.shape, True), whole(weight.shape, True)]
        + [anywhere] * 2,
        out_specs=[
            row,
            whole((2, 2, width)),
            pl.BlockSpec((width, lw), lambda k: (0, lax.max(k - n, 0))),
            whole((rows, width), True),
        ],
        out_shape=[
            jax.ShapeDtypeStruct((n, rows, width), HALF),
            jax.ShapeDtypeStruct((2, 2, width), SINGLE),
            jax.ShapeDtypeStruct((width, 6 * lw), HALF),
            jax.ShapeDtypeStruct((rows, width), SINGLE),
        ],
        scratch_shapes=[pltpu.VMEM((width, longest), HALF)]
        + LineSum.scratch(n, rows, width, first=n - 2),
        compiler_params=remote(10, 62),
        cost_estimate=cost(12 * n * rows * width * lw, 30 * MEGA),
        name="attn_in_back",
    )(dq, dk, dv, x_all, attn_in, weight, out_parts, running)


def end_kernel(
    n, dp, cut, parts, qkv_part, p_ref, packed, extra, ada_ref, acts,
    sum_ref, qkv_sum, p_own, every, cond_ref, ada_grad,
    z_got, row, c_part, c_got, c_all, z_send, z_recv, e_send, e_recv, c_send, c_recv, a_send, a_recv,
    *scratch,
):
    me, my = lax.axis_index("seq"), lax.axis_index("dp")
    depth = ada_ref.shape[0]
    span = packed.shape[2]
    greet(n, "all", "all")
    line = LineSum(n, at_rows(parts), sum_ref, *scratch[:6])
    group = GroupSum(qkv_part, *scratch[6:15])
    proj = GroupSum(p_ref, *scratch[15:])
    mates, others = range(1, n), range(1, dp)
    z_go = [to_line(me, n, k, packed, z_got, z_send, z_recv) for k in mates]
    for copy in z_go:
        copy.start()
    line.round(0)
    proj.begin()
    group.begin()
    z_got[me] = packed[me]
    for copy in z_go:
        copy.wait_recv()
    row[:, :span] = jnp.sum(z_got[...], axis=0)
    row[:, span:] = extra[...]
    e_go = [to_group(my, dp, k, row, every, e_send, e_recv) for k in others]
    for copy in e_go:
        copy.start()
    every[my] = row[...]
    proj.step(0)
    group.step(0)
    for copy in e_go:
        copy.wait_recv()
    cols = cut // 2
    halves_of = [every[:, 0, t * cols : (t + 1) * cols].astype(HALF) for t in range(2)]
    product = nt_dot(halves_of[0], ada_ref[:, 0, :]) + nt_dot(halves_of[1], ada_ref[:, 1, :])
    c_part[...] = jnp.zeros_like(c_part)
    for k in range(dp):
        c_part[k, :, :depth] = product[k : k + 1]
    c_go = [to_group(my, dp, k, c_part, c_got, c_send, c_recv) for k in others]
    for copy in c_go:
        copy.start()
    c_got[my] = c_part[my]
    act_rows = acts[:, 0, :depth].astype(HALF)
    for t in range(2):
        ada_grad[:, t, :] = tn_dot(act_rows, halves_of[t])
    for hop in range(1, n - 1):
        line.round(hop)
    for number in range(1, group.phases):
        proj.step(number)
        group.step(number)
    for copy in c_go:
        copy.wait_recv()
    a_go = [to_line(me, n, k, c_got, c_all, a_send, a_recv) for k in mates]
    for copy in a_go:
        copy.start()
    c_all[me] = c_got[...]
    for copy in a_go:
        copy.wait_recv()
    cond_ref[...] = jnp.sum(c_all[...], axis=0)
    rows, _, _, wide = qkv_sum.shape

    def store_proj(half, value):
        p_own[half] = value.astype(HALF)

    def store_qkv(half, value):
        own = slice(half * rows // 2, (half + 1) * rows // 2)
        for k in range(6):
            qkv_sum[own, k % 3, k // 3, :] = value[:, k * wide : (k + 1) * wide]

    proj.finish(store_proj)
    group.finish(store_qkv)
    line.finish()
    for copy in z_go + e_go + c_go + a_go:
        copy.wait_send()


def end(n, dp, cut, parts, qkv_part, proj_part, packed, extra, ada, acts):
    rows, width = parts.shape[1:]
    depth = up(ada.shape[0], LANES)
    span = packed.shape[2] + extra.shape[1]
    inner = pl.BlockSpec(memory_space=pltpu.VMEM)
    anywhere = pl.BlockSpec(memory_space=pl.ANY)
    sems = [n - 1, n - 1, dp - 1, dp - 1, dp - 1, dp - 1, n - 1, n - 1]
    return pl.pallas_call(
        functools.partial(end_kernel, n, dp, cut),
        in_specs=[anywhere, anywhere, anywhere, inner, inner, inner, inner],
        out_specs=[inner] * 6,
        out_shape=[
            jax.ShapeDtypeStruct((rows, width), SINGLE),
            jax.ShapeDtypeStruct((ada.shape[0], 3, 2, qkv_part.shape[3] // 6), SINGLE),
            jax.ShapeDtypeStruct(proj_part.shape[1:], HALF),
            jax.ShapeDtypeStruct((dp, 1, span), SINGLE),
            jax.ShapeDtypeStruct((dp, 1, depth), SINGLE),
            jax.ShapeDtypeStruct(ada.shape, SINGLE),
        ],
        scratch_shapes=[
            pltpu.VMEM(packed.shape, SINGLE),
            pltpu.VMEM((1, span), SINGLE),
            pltpu.VMEM((dp, 1, depth), SINGLE),
            pltpu.VMEM((dp, 1, depth), SINGLE),
            pltpu.VMEM((n, dp, 1, depth), SINGLE),
        ]
        + [pltpu.SemaphoreType.DMA((k,)) for k in sems]
        + LineSum.scratch(n, rows, width)
        + GroupSum.scratch(dp, *qkv_part.shape[2:])
        + GroupSum.scratch(dp, *proj_part.shape[2:]),
        compiler_params=remote(7, 62),
        cost_estimate=cost(10**6, 100 * MEGA),
        name="end",
    )(parts, qkv_part, proj_part, packed, extra, ada, acts)


def rows_kernel(img, slots, da_ref, dm_ref, x_ref, m_ref, y_ref, mod_ref, shift_ref, live_ref, io_ref, to_ref, ig_ref, tg_ref):
    for t, sl, out_ref, grad_ref in (
        (0, slice(0, img), io_ref, ig_ref),
        (1, slice(img, x_ref.shape[0]), to_ref, tg_ref),
    ):
        keep = out_ref.shape[1]
        live = live_ref[sl]
        value = m_ref[sl] + mod_ref[t, 5:6] * (y_ref[sl] + shift_ref[t : t + 1])
        out_ref[0] = (value * live).astype(HALF)[:keep]
        normed, inv_std = layer_norm(x_ref[sl].astype(SINGLE))
        grad = dm_ref[sl] + norm_back(normed, inv_std, da_ref[sl] * (1.0 + mod_ref[t, 1:2]))
        grad_ref[0] = (grad * live)[:keep]


def rows_out(img, slots, grad_attn_in, grad_middle, x_loc, middle, mlp_sum, mods, fc2_shift, live):
    width = x_loc.shape[1]
    return pl.pallas_call(
        functools.partial(rows_kernel, img, slots),
        out_shape=[
            jax.ShapeDtypeStruct((1, img, width), HALF),
            jax.ShapeDtypeStruct((1, slots, width), HALF),
            jax.ShapeDtypeStruct((1, img, width), SINGLE),
            jax.ShapeDtypeStruct((1, slots, width), SINGLE),
        ],
        compiler_params=params(),
        cost_estimate=cost(10**6, 14 * MEGA),
        name="rows_out",
    )(grad_attn_in, grad_middle, x_loc, middle, mlp_sum, mods, fc2_shift, live)


def body(
    image_tokens,
    text_tokens,
    text_lengths,
    conditioning,
    ada_weight,
    ada_bias,
    qkv_weight,
    qv_bias,
    proj_weight,
    proj_bias,
    fc1_weight,
    fc1_bias,
    fc2_weight,
    fc2_bias,
    image_cotangent,
    text_cotangent,
):
    n = lax.axis_size("seq")
    dp = lax.axis_size("dp")
    img, width = image_tokens.shape[1:]
    slots = text_tokens.shape[1]
    pad = up(slots, 16)
    rows = img + pad
    depth = qkv_weight.shape[0]
    lw = qkv_weight.shape[3]
    lwp = up(lw, LANES)
    units = fc1_weight.shape[2]
    mod_cols = ada_weight.shape[2]
    my_seq = lax.axis_index("dp")

    def stacked(image, text):
        return jnp.concatenate([image, jnp.pad(text, ((0, pad - slots), (0, 0)))], axis=0)

    length = text_lengths[0, 0]
    live_text = (jnp.arange(slots, dtype=jnp.int32) < length)[:, None]
    x_loc = stacked(image_tokens[0], text_tokens[0])
    e_loc = stacked(
        image_cotangent[0], jnp.where(live_text, text_cotangent[0], jnp.zeros((), HALF))
    )

    def split(shard):
        return shard.reshape(2, -1, shard.shape[-1])

    qkv_local = jnp.pad(qkv_weight, ((0, 0), (0, 0), (0, 0), (0, lwp - lw))).reshape(depth, 6 * lwp)
    share = proj_weight.shape[0]
    fc1_local = fc1_weight.reshape(depth, 2 * units)

    cond_float = conditioning.astype(SINGLE)
    bias_cols = proj_bias.shape[1]
    cut = 2 * mod_cols
    proj_line = lax.all_gather(proj_weight.transpose(1, 2, 0), "seq", axis=0, tiled=False)
    x_all, side_all, acts, mods, shifts, qkv_full, fc1_full = start(
        n,
        dp,
        x_loc,
        conditioning,
        ada_weight,
        ada_bias,
        proj_bias,
        fc2_bias,
        text_lengths,
        split(qkv_local),
        split(fc1_local),
    )
    qkv_full = qkv_full.reshape(width, 6 * lwp)
    fc1_full = fc1_full.reshape(width, 2 * units)
    proj_shift, fc2_shift = shifts[:2], shifts[2:]
    lengths_all = side_all[:, 0, cut + 4 * bias_cols]

    slot = jnp.arange(rows, dtype=SINGLE)[None, :] - img
    live = jnp.logical_or(slot < 0, jnp.logical_and(slot < lengths_all[:, None], slot < slots))
    mask = jnp.where(live, SINGLE(0), SINGLE(MASKED))
    mask_row = mask.reshape(1, n * rows)
    mask_col = jnp.broadcast_to(mask[:, :, None], (n, rows, LANES))
    live_loc = jnp.concatenate(
        [jnp.ones((img, 1), SINGLE), jnp.pad(live_text.astype(SINGLE), ((0, pad - slots), (0, 0)))]
    )

    bias_rows = jnp.stack(
        [qv_bias[:, 0], jnp.zeros_like(qv_bias[:, 0]), qv_bias[:, 1]], axis=1
    ).astype(SINGLE)
    bias_rows = jnp.pad(bias_rows, ((0, 0), (0, 0), (0, lwp - lw))).reshape(2, 3 * lwp)
    attn_in, qkv_rows = project_qkv(n, img, x_all, mods, qkv_full, bias_rows)
    mixture, lse, e_near, mix_loc, proj_full = attend(
        n, dp, qkv_rows, mask_row, e_loc, proj_line.reshape(2, -1, share)
    )
    proj_full = proj_full.reshape(dp, n, 2, depth, share)

    attn_out, middle, mlp_in, fc2_full = middle_rows(
        n, dp, img, mix_loc, x_loc, proj_full, proj_shift, mods, fc2_weight.transpose(1, 2, 0)
    )
    hidden, grad_pre, grad_mlp, mlp_in_part, mlp_out_part, fc1_bias_part, gate_two_part = (
        feed_forward(
            n, img, mlp_in, e_loc, e_near, mods, fc1_full, fc1_bias.astype(SINGLE), fc2_full
        )
    )
    fc_plan = [(w, w, t) for w in range(2) for t in range(2)]
    fc_rounds = [(k + 1) * 4 // (n - 2) for k in range(n - 3)]
    fc_part, running = weight_grads(
        n, dp, img, (mlp_in, grad_mlp), (grad_pre, hidden), fc_plan, fc_rounds, mlp_in_part, 6, "fc_grads"
    )
    fc_sum = lax.psum_scatter(
        fc_part.reshape(dp * 4 * depth, units), "dp", scatter_dimension=0, tiled=True
    ).reshape(4, depth, units)

    grad_middle, grad_attn, sums, grad_mix = middle_back(
        n, img, mlp_in_part, running, middle, attn_out, e_loc, proj_full, mods, lwp
    )
    grad_q, grad_k, grad_v, q_bias_part, v_bias_part, proj_part, out_running = attend_back(
        n, dp, img, qkv_rows, mixture, grad_mix, lse, mask_col, mlp_out_part, grad_attn, mix_loc
    )
    attn_in_part, mod_one, qkv_part, mlp_sum = attn_in_back(
        n,
        img,
        grad_q,
        grad_k,
        grad_v,
        x_all,
        attn_in,
        qkv_full,
        mlp_out_part,
        out_running,
    )
    fc_own = fc_sum.astype(SINGLE)

    upstream_sum = sums[:, 4]
    gate_two = gate_two_part + fc2_shift * upstream_sum
    mod_grads = jnp.stack(
        [mod_one[:, 0], mod_one[:, 1], sums[:, 0], sums[:, 1], sums[:, 2], gate_two], axis=1
    ).reshape(2, n, mod_cols)
    rest = jnp.stack([sums[:, 3], mods[:, 5] * upstream_sum]).reshape(4, n, bias_cols)
    packed = jnp.concatenate(
        [
            mod_grads.transpose(1, 0, 2).reshape(n, -1),
            rest.transpose(1, 0, 2).reshape(n, -1),
        ],
        axis=1,
    )
    q_bias = q_bias_part.transpose(1, 0, 2).reshape(2, lwp)[:, :lw]
    v_bias = v_bias_part.transpose(1, 0, 2).reshape(2, lwp)[:, :lw]
    extra = jnp.concatenate(
        [jnp.stack([q_bias, v_bias], axis=1).reshape(-1), fc1_bias_part.reshape(-1)]
    )
    grad_attn_in, qkv_sum, proj_own, every, cond_sum, ada_grad = end(
        n,
        dp,
        cut,
        attn_in_part,
        qkv_part.reshape(dp, 2, depth // 2, 6 * lwp),
        proj_part.reshape(dp, 2, n * depth, lwp),
        packed[:, None],
        extra[None],
        ada_weight,
        acts,
    )
    proj_own, fc_sum = lax.optimization_barrier((proj_own, fc_sum))
    proj_sum = lax.psum_scatter(
        proj_own.reshape(n * 2 * depth, lwp), "seq", scatter_dimension=0, tiled=True
    ).reshape(2, depth, lwp)
    every = every[:, 0]
    total = jnp.sum(every, axis=0)

    image_out, text_out, image_grad, text_grad = rows_out(
        img, slots, grad_attn_in, grad_middle, x_loc, middle, mlp_sum, mods, fc2_shift, live_loc
    )

    ada_bias_grad = total[:cut].reshape(2, mod_cols)
    proj_bias_grad = total[cut : cut + 2 * bias_cols].reshape(2, bias_cols)
    fc2_bias_grad = total[cut + 2 * bias_cols : cut + 4 * bias_cols].reshape(2, bias_cols)
    after = cut + 4 * bias_cols
    qv_bias_grad = total[after : after + 4 * lw].reshape(2, 2, lw)
    fc1_bias_grad = total[after + 4 * lw :].reshape(2, units)
    cond_grad = cond_sum[:, 0, :depth].reshape(1, width) * silu_slope(cond_float)

    qkv_grad = qkv_sum[..., :lw].transpose(0, 2, 1, 3)
    fc1_grad = fc_own[:2].transpose(1, 0, 2)
    fc2_grad = fc_own[2:].transpose(2, 0, 1)
    proj_grad = proj_sum.astype(SINGLE)[..., :share].transpose(2, 0, 1)
    return (
        image_out,
        text_out,
        image_grad,
        text_grad,
        cond_grad,
        ada_grad,
        ada_bias_grad,
        qkv_grad,
        qv_bias_grad,
        proj_grad,
        proj_bias_grad,
        fc1_grad,
        fc1_bias_grad,
        fc2_grad,
        fc2_bias_grad,
    )


def solution(mesh):
    in_specs = (
        P("dp", "seq", None),
        P("dp", "seq", None),
        P("dp", "seq"),
        P("dp", None),
        P("dp", None, "seq"),
        P(None, "seq"),
        P("dp", None, None, "seq"),
        P(None, None, "seq"),
        P("seq", None, "dp"),
        P(None, "seq"),
        P("dp", None, "seq"),
        P(None, "seq"),
        P("seq", None, "dp"),
        P(None, "seq"),
        P("dp", "seq", None),
        P("dp", "seq", None),
    )
    out_specs = (
        P("dp", "seq", None),
        P("dp", "seq", None),
        P("dp", "seq", None),
        P("dp", "seq", None),
        P("dp", None),
        P("dp", None, "seq"),
        P(None, "seq"),
        P("dp", None, None, "seq"),
        P(None, None, "seq"),
        P("seq", None, "dp"),
        P(None, "seq"),
        P("dp", None, "seq"),
        P(None, "seq"),
        P("seq", None, "dp"),
        P(None, "seq"),
    )
    return jax.shard_map(body, mesh=mesh, in_specs=in_specs, out_specs=out_specs, check_vma=False)
```

```python
import functools
import math

import jax
import jax.numpy as jnp
from jax import lax
from jax.experimental import pallas as pl
from jax.experimental.pallas import tpu as pltpu
from jax.sharding import PartitionSpec as P

HD = 64
LANES = 128
EPSILON = 1e-06
GELU_ROOT = math.sqrt(2.0 / math.pi)
GELU_CUBE = 0.044715
MASKED = -1e30
SINGLE = jnp.float32
HALF = jnp.bfloat16
MEGA = 2**20


def up(value, multiple):
    return -(-value // multiple) * multiple


def params(limit=56):
    return pltpu.CompilerParams(vmem_limit_bytes=limit * MEGA)


def remote(collective, limit=56):
    return pltpu.CompilerParams(
        collective_id=collective, has_side_effects=True, vmem_limit_bytes=limit * MEGA
    )


def cost(flops, nbytes, trans=0):
    return pl.CostEstimate(flops=int(flops), bytes_accessed=int(nbytes), transcendentals=int(trans))


def nt_dot(a, b):
    return lax.dot_general(a, b, (((1,), (1,)), ((), ())), preferred_element_type=SINGLE)


def tn_dot(a, b):
    return lax.dot_general(a, b, (((0,), (0,)), ((), ())), preferred_element_type=SINGLE)


def nn_dot(a, b):
    return jnp.dot(a, b, preferred_element_type=SINGLE)


def layer_norm(values):
    center = values - jnp.mean(values, axis=-1, keepdims=True)
    inv_std = lax.rsqrt(jnp.mean(center * center, axis=-1, keepdims=True) + EPSILON)
    return (center * inv_std, inv_std)


def norm_back(normed, inv_std, upstream):
    first = jnp.mean(upstream, axis=-1, keepdims=True)
    second = jnp.mean(upstream * normed, axis=-1, keepdims=True)
    return inv_std * (upstream - first - normed * second)


def gelu_both(values):
    square = values * values
    inner = GELU_ROOT * (values + GELU_CUBE * square * values)
    tangent = jnp.tanh(inner)
    half = 0.5 * (1.0 + tangent)
    slope = half + 0.5 * values * (1.0 - tangent * tangent) * GELU_ROOT * (
        1.0 + 3.0 * GELU_CUBE * square
    )
    return values * half, slope


def silu_slope(values):
    sigma = jax.nn.sigmoid(values)
    return sigma + values * sigma * (1.0 - sigma)


def whole(shape, single=False):
    zeros = (0,) * len(shape)
    if single:
        return pl.BlockSpec(shape, lambda *_: zeros, pipeline_mode=pl.Buffered(1))
    return pl.BlockSpec(shape, lambda *_: zeros)


def rows_spec(rows, width):
    return pl.BlockSpec((1, rows, width), lambda s: (s, 0, 0))


MESH = pl.DeviceIdType.MESH


def on_line(position):
    return {"seq": position}


def both(first, second):
    return jnp.logical_and(first, second)


def flip(value, mask):
    bit = 1
    while bit <= mask:
        if mask & bit:
            value = value + bit - 2 * bit * lax.rem(lax.div(value, bit), 2)
        bit *= 2
    return value


def greet(n, line=None, group=None):
    me, my = lax.axis_index("seq"), lax.axis_index("dp")
    dp = lax.axis_size("dp")
    barrier = pltpu.get_barrier_semaphore()
    peers = []
    if line == "all":
        peers += [on_line(lax.rem(me + offset, n)) for offset in range(1, n)]
    if group == "all":
        peers += [{"dp": lax.rem(my + offset, dp)} for offset in range(1, dp)]
    if group == "paths":
        peers += [{"dp": flip(my, 1)}] + [{"dp": flip(my, mask)} for mask in masks_of(dp)]
    for peer in peers:
        pl.semaphore_signal(barrier, inc=1, device_id=peer, device_id_type=MESH)
    if line == "near":
        for sign in (1, -1):
            near = me + sign

            @pl.when(both(near >= 0, near < n))
            def _():
                pl.semaphore_signal(barrier, inc=1, device_id=on_line(near), device_id_type=MESH)

    count = len(peers)
    if line == "near":
        count = count + lax.min(me, 1) + lax.min(n - 1 - me, 1)
    pl.semaphore_wait(barrier, count)


def masks_of(dp):
    masks, bit = [], 2
    while bit < dp:
        masks.append(bit)
        bit *= 2
    return masks


class GroupGather:
    def __init__(self, src, out, send, recv, pass_send, pass_recv, local):
        self.src, self.out = src, out
        self.send, self.recv, self.local = send, recv, local
        self.pass_send, self.pass_recv = pass_send, pass_recv
        self.my = lax.axis_index("dp")
        masks = masks_of(out.shape[0])
        self.orders = (masks, masks[::-1])
        self.phases = len(masks)

    @staticmethod
    def scratch(dp):
        return [pltpu.SemaphoreType.DMA((2, dp // 2)) for _ in range(4)] + [
            pltpu.SemaphoreType.DMA
        ]

    def span(self, half, count):
        mask = 0
        for k in range(self.phases):
            if count >> k & 1:
                mask |= self.orders[half][k]
        return mask

    def copy(self, half, phase, count, block):
        src = self.src.at[half] if count == 0 else self.out.at[block, half]
        index = 2**phase - 1 + count
        return pltpu.make_async_remote_copy(
            src_ref=src,
            dst_ref=self.out.at[block, half],
            send_sem=self.send.at[half, index],
            recv_sem=self.recv.at[half, index],
            device_id={"dp": flip(self.my, self.orders[half][phase])},
            device_id_type=MESH,
        )

    def hand(self, half, index, block, own=False):
        src = self.src.at[half] if own else self.out.at[block, half]
        return pltpu.make_async_remote_copy(
            src_ref=src,
            dst_ref=self.out.at[block, half],
            send_sem=self.pass_send.at[half, index],
            recv_sem=self.pass_recv.at[half, index],
            device_id={"dp": flip(self.my, 1)},
            device_id_type=MESH,
        )

    def begin(self):
        for phase in range(self.phases):
            for half in range(2):
                self.copy(half, phase, 0, self.my).start()
        for half in range(2):
            self.hand(half, 0, self.my, True).start()
        pltpu.make_async_copy(self.src, self.out.at[self.my], self.local).start()

    def arrive(self, phase):
        for half in range(2):
            mask = self.orders[half][phase]
            for count in range(2**phase):
                block = flip(self.my, mask ^ self.span(half, count))
                self.copy(half, phase, count, block).wait_recv()
            if phase + 1 < self.phases:
                for count in range(1, 2 ** (phase + 1)):
                    block = flip(self.my, self.span(half, count))
                    self.copy(half, phase + 1, count, block).start()
            for count in range(2**phase):
                block = flip(self.my, mask ^ self.span(half, count))
                self.hand(half, 2**phase + count, block).start()

    def finish(self):
        pltpu.make_async_copy(self.src, self.out.at[self.my], self.local).wait()
        other = flip(self.my, 1)
        for half in range(2):
            self.hand(half, 0, other, True).wait()
            for phase in range(self.phases):
                mask = self.orders[half][phase]
                for count in range(2**phase):
                    self.copy(half, phase, count, self.my).wait_send()
                    block = flip(other, mask ^ self.span(half, count))
                    self.hand(half, 2**phase + count, block).wait()


class GroupSum:
    def __init__(self, part, got, hold, passed, came, pass_send, pass_recv, send, recv, load):
        self.part, self.got, self.hold, self.passed, self.came = part, got, hold, passed, came
        self.pass_send, self.pass_recv = pass_send, pass_recv
        self.send, self.recv, self.load = send, recv, load
        self.my = lax.axis_index("dp")
        self.dp = part.shape[0]
        masks = masks_of(self.dp)
        self.orders = (masks, masks[::-1])
        self.phases = len(masks)

    @staticmethod
    def scratch(dp, rows, width):
        half = dp // 2
        return [
            pltpu.VMEM((2, half, rows, width), HALF),
            pltpu.VMEM((2, half, rows, width), HALF),
            pltpu.VMEM((2, half - 1, rows, width), HALF),
            pltpu.VMEM((2, half - 1, rows, width), HALF),
        ] + [pltpu.SemaphoreType.DMA((2, half)) for _ in range(5)]

    def span(self, half, count):
        mask = 0
        for k in range(self.phases):
            if count >> k & 1:
                mask |= self.orders[half][k]
        return mask

    def hand(self, half, count):
        block = flip(self.my, 1 ^ self.span(half, count))
        return pltpu.make_async_remote_copy(
            src_ref=self.part.at[block, half],
            dst_ref=self.got.at[half, count],
            send_sem=self.pass_send.at[half, count],
            recv_sem=self.pass_recv.at[half, count],
            device_id={"dp": flip(self.my, 1)},
            device_id_type=MESH,
        )

    def fetch(self, half, count):
        block = flip(self.my, self.span(half, count))
        return pltpu.make_async_copy(
            self.part.at[block, half], self.hold.at[half, count], self.load.at[half, count]
        )

    def copy(self, half, phase, index):
        return pltpu.make_async_remote_copy(
            src_ref=self.passed.at[half, 2**phase + index - 1],
            dst_ref=self.came.at[half, 2**phase - 1 + index],
            send_sem=self.send.at[half, 2**phase - 1 + index],
            recv_sem=self.recv.at[half, 2**phase - 1 + index],
            device_id={"dp": flip(self.my, self.orders[half][phase])},
            device_id_type=MESH,
        )

    def every(self):
        return [(half, count) for half in range(2) for count in range(self.dp // 2)]

    def begin(self):
        for half, count in self.every():
            self.hand(half, count).start()
            if self.hold is not None:
                self.fetch(half, count).start()

    def value(self, half, count, phase):
        if self.hold is None:
            mine = self.part[flip(self.my, self.span(half, count)), half]
        else:
            mine = self.hold[half, count]
        total = mine.astype(SINGLE) + self.got[half, count].astype(SINGLE)
        for later in range(phase, self.phases):
            total = total + self.came[half, 2**later - 1 + count].astype(SINGLE)
        return total

    def step(self, number):
        if number == 0:
            for half, count in self.every():
                if self.hold is not None:
                    self.fetch(half, count).wait()
                self.hand(half, count).wait_recv()
        else:
            self.took(self.phases - number)
        phase = self.phases - 1 - number
        for half in range(2):
            for index in range(2**phase):
                count = 2**phase + index
                self.passed[half, count - 1] = self.value(half, count, phase + 1).astype(HALF)
                self.copy(half, phase, index).start()

    def took(self, phase):
        for half in range(2):
            for index in range(2**phase):
                self.copy(half, phase, index).wait_recv()

    def finish(self, store):
        self.took(0)
        for half in range(2):
            store(half, self.value(half, 0, 0))
        self.sent(0)

    def sent(self, first):
        for half, count in self.every():
            self.hand(half, count).wait_send()
        for phase in range(first, self.phases):
            for half in range(2):
                for index in range(2**phase):
                    self.copy(half, phase, index).wait_send()


class LineGather:
    def __init__(self, n, src, out, send, recv, local, first=0, stop=None, land=None):
        self.n, self.src, self.out, self.land = n, src, out, land
        self.send, self.recv, self.local = send, recv, local
        self.first, self.stop = first, n - 1 if stop is None else stop
        self.me = lax.axis_index("seq")

    @staticmethod
    def scratch(n):
        return [
            pltpu.SemaphoreType.DMA((2, n - 1)),
            pltpu.SemaphoreType.DMA((2, n - 1)),
            pltpu.SemaphoreType.DMA,
        ]

    def inside(self, position):
        return both(position >= 0, position < self.n)

    def copy(self, way, hop, block, near):
        if hop > self.first:
            src = self.out.at[block]
        else:
            src = self.src if hop == 0 else self.src.at[way]
        return pltpu.make_async_remote_copy(
            src_ref=src,
            dst_ref=self.out.at[block] if self.land is None else self.land.at[way],
            send_sem=self.send.at[way, hop],
            recv_sem=self.recv.at[way, hop],
            device_id=on_line(near),
            device_id_type=MESH,
        )

    def each(self, hop):
        for way, sign in ((0, 1), (1, -1)):
            yield way, sign, self.me - sign * hop, self.me + sign

    def begin(self):
        self.launch(self.first)

    def launch(self, hop):
        for way, sign, block, near in self.each(hop):

            @pl.when(both(self.inside(block), self.inside(near)))
            def _():
                self.copy(way, hop, block, near).start()

    def keep(self):
        return pltpu.make_async_copy(self.src, self.out.at[self.me], self.local)

    def arrive(self, hop):
        for way, sign, block, near in self.each(hop + 1):

            @pl.when(self.inside(block))
            def _():
                self.copy(way, hop, block, near).wait_recv()

        if hop + 1 < self.stop:
            self.launch(hop + 1)

    def finish(self):
        for hop in range(self.first, self.stop):
            for way, sign, block, near in self.each(hop):

                @pl.when(both(self.inside(block), self.inside(near)))
                def _():
                    self.copy(way, hop, block, near).wait_send()


class LineSum:
    def __init__(self, n, part, out, got, mine, passed, send, recv, load, first=0, stop=None, tail=None, prev=None):
        self.n, self.part, self.out = n, part, out
        self.got, self.mine, self.passed = got, mine, passed
        self.send, self.recv, self.load = send, recv, load
        self.first, self.stop = first, n - 1 if stop is None else stop
        self.tail, self.prev = tail, prev
        self.me = lax.axis_index("seq")

    @staticmethod
    def scratch(n, rows, width, first=0, stop=None):
        stop = n - 1 if stop is None else stop
        return [
            pltpu.VMEM((2, stop - first + (first > 0), rows, width), HALF),
            pltpu.VMEM((2, rows, width), HALF),
            pltpu.VMEM((2, max(stop - max(first, 1), 1), rows, width), HALF),
            pltpu.SemaphoreType.DMA((2, n - 1)),
            pltpu.SemaphoreType.DMA((2, n - 1)),
            pltpu.SemaphoreType.DMA((2, 2)),
        ]

    def inside(self, position):
        return both(position >= 0, position < self.n)

    def each(self, step):
        reach = self.n - 1 - step
        for way, sign in ((0, 1), (1, -1)):
            yield way, self.me + sign * reach, self.me + sign, self.me - sign

    def slot(self, way, step):
        return self.passed.at[way, max(step - max(self.first, 1), 0)]

    def copy(self, way, step, src, near):
        if self.tail is not None and step == self.stop - 1:
            dst = self.tail.at[way]
        else:
            dst = self.got.at[way, step - self.first]
        return pltpu.make_async_remote_copy(
            src_ref=src,
            dst_ref=dst,
            send_sem=self.send.at[way, step],
            recv_sem=self.recv.at[way, step],
            device_id=on_line(near),
            device_id_type=MESH,
        )

    def round(self, step):
        for way, owner, near, behind in self.each(step):
            if step == 0:

                @pl.when(self.inside(owner))
                def _():
                    self.copy(way, step, self.part(owner), near).start()

                continue

            @pl.when(both(self.inside(owner), jnp.logical_not(self.inside(behind))))
            def _():
                self.copy(way, step, self.part(owner), near).start()

            @pl.when(both(self.inside(owner), self.inside(behind)))
            def _():
                fetch = pltpu.make_async_copy(
                    self.part(owner), self.mine.at[way], self.load.at[way, 0]
                )
                fetch.start()
                slot = self.slot(way, step)
                if step == self.first:
                    index = self.stop - self.first
                    held = pltpu.make_async_copy(
                        self.prev.at[way], self.got.at[way, index], self.load.at[way, 1]
                    )
                    held.start()
                    held.wait()
                else:
                    index = step - 1 - self.first
                    self.copy(way, step - 1, slot, near).wait_recv()
                fetch.wait()
                total = self.mine[way].astype(SINGLE) + self.got[way, index].astype(SINGLE)
                self.passed[way, step - max(self.first, 1)] = total.astype(HALF)
                self.copy(way, step, slot, near).start()

    def sent(self):
        for step in range(self.first, self.stop):
            for way, owner, near, behind in self.each(step):

                @pl.when(self.inside(owner))
                def _():
                    self.copy(way, step, self.slot(way, step), near).wait_send()

    def close(self):
        last = self.stop - 1
        for way, owner, near, behind in self.each(last + 1):

            @pl.when(both(self.inside(owner), self.inside(behind)))
            def _():
                self.copy(way, last, self.slot(way, last), near).wait_recv()

        self.sent()

    def finish(self):
        last = self.n - 2
        fetch = pltpu.make_async_copy(self.part(self.me), self.mine.at[0], self.load.at[0, 0])
        fetch.start()
        fetch.wait()
        self.out[...] = self.mine[0].astype(SINGLE)
        for way, owner, near, behind in self.each(last):

            @pl.when(self.inside(behind))
            def _():
                self.copy(way, last, self.slot(way, last), near).wait_recv()
                self.out[...] += self.got[way, last - self.first].astype(SINGLE)

        self.sent()


def at_rows(ref):
    return lambda owner: ref.at[owner]


def at_step(step, when, action):
    @pl.when(step == when)
    def _():
        action()


def to_group(my, dp, offset, src, dst, send, recv):
    peer = lax.rem(my + offset, dp)
    return pltpu.make_async_remote_copy(
        src_ref=src if src.shape == dst.shape[1:] else src.at[peer],
        dst_ref=dst.at[my],
        send_sem=send.at[offset - 1],
        recv_sem=recv.at[offset - 1],
        device_id={"dp": peer},
        device_id_type=MESH,
    )


def to_line(me, n, offset, src, dst, send, recv):
    peer = lax.rem(me + offset, n)
    return pltpu.make_async_remote_copy(
        src_ref=src if src.shape == dst.shape[1:] else src.at[peer],
        dst_ref=dst.at[me],
        send_sem=send.at[offset - 1],
        recv_sem=recv.at[offset - 1],
        device_id=on_line(peer),
        device_id_type=MESH,
    )


def start_kernel(
    n, dp, x_ref, cond_ref, ada_ref, ada_bias, proj_bias, fc2_bias, length_ref, qkv_ref, fc1_ref,
    x_all, side_all, acts, mods, shifts, qkv_all, fc1_all,
    act_ref, part, parts, row, a_send, a_recv, p_send, p_recv, s_send, s_recv, *sems,
):
    me, my = lax.axis_index("seq"), lax.axis_index("dp")
    depth, _, cols = ada_ref.shape
    width = x_ref.shape[1]
    greet(n, "all", "all")
    gather = LineGather(n, x_ref, x_all, *sems[:3])
    qkv = GroupGather(qkv_ref, qkv_all, *sems[3:8])
    fc1 = GroupGather(fc1_ref, fc1_all, *sems[8:13])
    gather.begin()
    cond = cond_ref[...].astype(SINGLE)
    act = (cond / (1.0 + jnp.exp(-cond))).astype(HALF).astype(SINGLE)
    act_ref[...] = jnp.zeros_like(act_ref)
    for k in range(dp):
        act_ref[k, :, :depth] = act[:, k * depth : (k + 1) * depth]
    others = range(1, dp)
    act_go = [to_group(my, dp, k, act_ref, acts, a_send, a_recv) for k in others]
    for copy in act_go:
        copy.start()
    gather.keep().start()
    acts[my] = act_ref[my]
    for copy in act_go:
        copy.wait_recv()
    rows = acts[:, 0, :depth].astype(HALF)
    for t in range(2):
        product = nn_dot(rows, ada_ref[:, t, :])
        for k in range(dp):
            part[k, :, t * cols : (t + 1) * cols] = product[k : k + 1]
    part_go = [to_group(my, dp, k, part, parts, p_send, p_recv) for k in others]
    for copy in part_go:
        copy.start()
    parts[my] = part[my]
    place = 0
    for ref in (ada_bias, proj_bias, fc2_bias):
        for t in range(2):
            size = ref.shape[1]
            row[:, place : place + size] = ref[t : t + 1].astype(SINGLE)
            place += size
    row[:, place:] = jnp.full((1, LANES), length_ref[0, 0].astype(SINGLE))
    for copy in part_go:
        copy.wait_recv()
    qkv.begin()
    fc1.begin()
    row[:, : 2 * cols] += jnp.sum(parts[...], axis=0)
    row_go = [to_line(me, n, k, row, side_all, s_send, s_recv) for k in range(1, n)]
    for copy in row_go:
        copy.start()
    side_all[me] = row[...]
    for hop in range(max(n - 1, qkv.phases)):
        if hop < n - 1:
            gather.arrive(hop)
        if hop < qkv.phases:
            qkv.arrive(hop)
            fc1.arrive(hop)
    for copy in row_go:
        copy.wait()
    mods[...] = jnp.zeros_like(mods)
    piece = math.gcd(cols, width)
    share = proj_bias.shape[1]
    for z in range(n):
        for t in range(2):
            for start in range(0, cols, piece):
                to, at = divmod(z * cols + start, width)
                mods[t, to : to + 1, at : at + piece] = side_all[
                    z, :, t * cols + start : t * cols + start + piece
                ]
        for k in range(4):
            start = 2 * cols + k * share
            shifts[k : k + 1, z * share : (z + 1) * share] = side_all[z, :, start : start + share]
    for copy in act_go + part_go:
        copy.wait_send()
    gather.keep().wait()
    gather.finish()
    qkv.finish()
    fc1.finish()


def start(n, dp, x_loc, cond, ada, ada_bias, proj_bias, fc2_bias, length, qkv, fc1):
    rows, width = x_loc.shape
    depth, _, cols = ada.shape
    span = 2 * cols + 4 * proj_bias.shape[1] + LANES
    anywhere = pl.BlockSpec(memory_space=pl.ANY)
    inner = pl.BlockSpec(memory_space=pltpu.VMEM)
    scalar = pl.BlockSpec(memory_space=pltpu.SMEM)
    return pl.pallas_call(
        functools.partial(start_kernel, n, dp),
        in_specs=[inner] * 6 + [scalar, inner, inner],
        out_specs=[anywhere, inner, inner, inner, inner, anywhere, anywhere],
        out_shape=[
            jax.ShapeDtypeStruct((n, rows, width), HALF),
            jax.ShapeDtypeStruct((n, 1, span), SINGLE),
            jax.ShapeDtypeStruct((dp, 1, up(depth, LANES)), SINGLE),
            jax.ShapeDtypeStruct((2, 8, width), SINGLE),
            jax.ShapeDtypeStruct((4, width), SINGLE),
            jax.ShapeDtypeStruct((dp,) + qkv.shape, HALF),
            jax.ShapeDtypeStruct((dp,) + fc1.shape, HALF),
        ],
        scratch_shapes=[
            pltpu.VMEM((dp, 1, up(depth, LANES)), SINGLE),
            pltpu.VMEM((dp, 1, 2 * cols), SINGLE),
            pltpu.VMEM((dp, 1, 2 * cols), SINGLE),
            pltpu.VMEM((1, span), SINGLE),
            pltpu.SemaphoreType.DMA((dp - 1,)),
            pltpu.SemaphoreType.DMA((dp - 1,)),
            pltpu.SemaphoreType.DMA((dp - 1,)),
            pltpu.SemaphoreType.DMA((dp - 1,)),
            pltpu.SemaphoreType.DMA((n - 1,)),
            pltpu.SemaphoreType.DMA((n - 1,)),
        ]
        + LineGather.scratch(n)
        + GroupGather.scratch(dp)
        + GroupGather.scratch(dp),
        compiler_params=remote(1),
        cost_estimate=cost(10**6, 100 * MEGA),
        name="start",
    )(x_loc, cond, ada, ada_bias, proj_bias, fc2_bias, length, qkv, fc1)


def qkv_kernel(img, x_ref, mod_ref, w_ref, b_ref, a_ref, o_ref):
    wide = o_ref.shape[2]
    for t, sl in ((0, slice(0, img)), (1, slice(img, x_ref.shape[1]))):
        normed, _ = layer_norm(x_ref[0, sl].astype(SINGLE))
        a = (normed * (1.0 + mod_ref[t, 1:2]) + mod_ref[t, 0:1]).astype(HALF)
        a_ref[0, sl] = a
        o_ref[0, sl] = (
            nn_dot(a, w_ref[:, t * wide : (t + 1) * wide]) + b_ref[t : t + 1]
        ).astype(HALF)


def project_qkv(n, img, x_all, mods, weight, bias):
    _, rows, width = x_all.shape
    wide = weight.shape[1] // 2
    return pl.pallas_call(
        functools.partial(qkv_kernel, img),
        grid=(n,),
        in_specs=[
            rows_spec(rows, width),
            whole(mods.shape),
            whole(weight.shape, True),
            whole(bias.shape),
        ],
        out_specs=[rows_spec(rows, width), rows_spec(rows, wide)],
        out_shape=[
            jax.ShapeDtypeStruct((n, rows, width), HALF),
            jax.ShapeDtypeStruct((n, rows, wide), HALF),
        ],
        compiler_params=params(),
        cost_estimate=cost(2 * n * rows * width * wide, 30 * MEGA),
        name="project_qkv",
    )(x_all, mods, weight, bias)


def halves(shape):
    lane = lax.broadcasted_iota(jnp.int32, shape, len(shape) - 1)
    return lane < HD


def attn_kernel(
    n, q_ref, k_ref, v_ref, mask_ref, e_ref, p_ref, o_ref, lse_ref, e_near, mix_ref, p_all,
    o_buf, o_send, o_recv, o_local, *sems,
):
    pair, block = pl.program_id(0), pl.program_id(1)
    pairs = pl.num_programs(0)
    step = pair * n + block
    me = lax.axis_index("seq")
    count, rows, _ = k_ref.shape
    gather = LineGather(n, e_ref, None, *sems[:3], first=0, stop=1, land=e_near)
    proj = GroupGather(p_ref, p_all, *sems[3:])

    def begin():
        greet(n, "all", "paths")
        gather.begin()
        proj.begin()

    at_step(step, 0, begin)
    queries = q_ref[0] * HALF(1.0 / math.sqrt(HD))
    keys = k_ref[...].reshape(n * rows, LANES)
    values = v_ref[...].reshape(n * rows, LANES)
    first = halves(queries.shape)
    zero = HALF(0)
    pair_rows = jnp.concatenate([jnp.where(first, queries, zero), jnp.where(first, zero, queries)])
    scores = nt_dot(pair_rows, keys) + mask_ref[...]
    maxima = jnp.max(scores, axis=-1, keepdims=True)
    raised = jnp.exp(scores - maxima)
    totals = jnp.sum(raised, axis=-1, keepdims=True)
    weights = (raised * (1.0 / totals)).astype(HALF)
    outs = nn_dot(weights, values)
    logs = maxima + jnp.log(totals)
    mixed = jnp.where(first, outs[:rows], outs[rows:]).astype(HALF)
    o_ref[0] = mixed
    o_buf[pair, block] = mixed
    lse_ref[0] = jnp.where(first, logs[:rows], logs[rows:])
    static_pairs = o_buf.shape[0]

    def columns(sender, which):
        start = (sender * static_pairs + which) * LANES
        return mix_ref.at[:, pl.ds(pl.multiple_of(start, LANES), LANES)]

    def away(which, offset):
        peer = lax.rem(me + offset, n)
        return pltpu.make_async_remote_copy(
            src_ref=o_buf.at[which, peer],
            dst_ref=columns(me, which),
            send_sem=o_send.at[which, offset - 1],
            recv_sem=o_recv.at[which, offset - 1],
            device_id=on_line(peer),
            device_id_type=MESH,
        )

    for offset in range(1, n):

        @pl.when(block == lax.rem(me + offset, n))
        def _():
            away(pair, offset).start()

    @pl.when(block == me)
    def _():
        pltpu.make_async_copy(o_buf.at[pair, me], columns(me, pair), o_local.at[pair]).start()

    last = static_pairs * n - 1
    for phase in range(proj.phases):
        at_step(step, min(last, 5 * phase + 5), functools.partial(proj.arrive, phase))

    def finish():
        gather.arrive(0)
        proj.finish()
        for which in range(static_pairs):
            pltpu.make_async_copy(o_buf.at[which, me], columns(me, which), o_local.at[which]).wait()
            for offset in range(1, n):
                away(which, offset).wait()
        gather.finish()

    at_step(step, last, finish)


def attend(n, dp, qkv, mask, e_loc, proj):
    _, rows, wide = qkv.shape
    width = e_loc.shape[1]
    pairs = wide // 3 // LANES
    total = n * rows
    block = pl.BlockSpec((1, rows, LANES), lambda h, s: (s, 0, h))
    anywhere = pl.BlockSpec(memory_space=pl.ANY)
    return pl.pallas_call(
        functools.partial(attn_kernel, n),
        grid=(pairs, n),
        in_specs=[
            block,
            pl.BlockSpec((n, rows, LANES), lambda h, s: (0, 0, pairs + h)),
            pl.BlockSpec((n, rows, LANES), lambda h, s: (0, 0, 2 * pairs + h)),
            whole(mask.shape),
            anywhere,
            whole(proj.shape, True),
        ],
        out_specs=[block, block, anywhere, anywhere, anywhere],
        out_shape=[
            jax.ShapeDtypeStruct((n, rows, pairs * LANES), HALF),
            jax.ShapeDtypeStruct((n, rows, pairs * LANES), SINGLE),
            jax.ShapeDtypeStruct((2, rows, width), HALF),
            jax.ShapeDtypeStruct((rows, n * pairs * LANES), HALF),
            jax.ShapeDtypeStruct((dp,) + proj.shape, HALF),
        ],
        scratch_shapes=[
            pltpu.VMEM((pairs, n, rows, LANES), HALF),
            pltpu.SemaphoreType.DMA((pairs, n - 1)),
            pltpu.SemaphoreType.DMA((pairs, n - 1)),
            pltpu.SemaphoreType.DMA((pairs,)),
        ]
        + LineGather.scratch(n)
        + GroupGather.scratch(dp),
        compiler_params=remote(2),
        cost_estimate=cost(2 * 2 * 4 * pairs * total * total * LANES, 20 * MEGA, 2 * pairs * total * total),
        name="attend",
    )(qkv, qkv, qkv, mask, e_loc, proj)


def attn_back_kernel(
    lines, img, pairs, q_ref, k_ref, v_ref, o_ref, g_ref, lse_ref, mask_ref, y_ref, l_ref, r_ref,
    dq_ref, dk_ref, dv_ref, qb_ref, vb_ref, p_ref, tail,
    acc_ref, lse_row, delta_row, turned, *scratch,
):
    linear = pl.program_id(0)
    ahead = 2 * lines
    attn_steps = pairs * lines
    last = ahead + attn_steps - 1
    step = lax.rem(lax.max(linear - ahead, 0), lines)
    n, rows, _ = q_ref.shape
    total = n * rows
    line = LineSum(lines, at_rows(y_ref), None, *scratch, stop=lines - 2, tail=tail)

    def begin():
        greet(lines, "near")
        line.round(0)

    at_step(linear, 0, begin)
    for t, sl in ((0, slice(0, img)), (1, slice(img, rows))):

        @pl.when(linear == 0)
        def _():
            turned[:, sl] = l_ref[sl].T

        @pl.when(both(linear < ahead, lax.rem(linear, 2) == t))
        def _():
            p_ref[...] = nn_dot(turned[:, sl], r_ref[sl]).astype(HALF).reshape(p_ref.shape)

    @pl.when(linear >= ahead)
    def _():
        grads = g_ref[...].reshape(total, LANES)
        queries = q_ref[...].reshape(total, LANES) * HALF(1.0 / math.sqrt(HD))

        @pl.when(step == 0)
        def _():
            acc_ref[...] = jnp.zeros_like(acc_ref)
            product = grads.astype(SINGLE) * o_ref[...].reshape(total, LANES).astype(SINGLE)
            flipped = product.T
            logs = lse_ref[...].reshape(total, LANES).T
            for head in range(2):
                delta_row[head : head + 1] = jnp.sum(
                    flipped[head * HD : (head + 1) * HD], axis=0, keepdims=True
                )
                lse_row[head : head + 1] = logs[head * HD : head * HD + 1]
            vb_ref[0] = jnp.zeros_like(vb_ref[0])

        keys, values = k_ref[0], v_ref[0]
        first = halves(keys.shape)
        mask = mask_ref[0][:, 0:1]
        zero = HALF(0)

        def pair(value):
            return jnp.concatenate([jnp.where(first, value, zero), jnp.where(first, zero, value)])

        def by_head(row):
            return row[...].reshape(2, 1, total)

        key_pair = pair(keys)
        scores = nt_dot(key_pair, queries).reshape(2, rows, total)
        probs = jnp.exp((scores - by_head(lse_row)) + mask)
        grad_prob = nt_dot(pair(values), grads).reshape(2, rows, total)
        grad_score = (probs * (grad_prob - by_head(delta_row))).astype(HALF)
        grad_score = grad_score.reshape(2 * rows, total)
        dvs = nn_dot(probs.astype(HALF).reshape(2 * rows, total), grads)
        dks = nn_dot(grad_score, queries)
        acc_ref[...] += tn_dot(grad_score, key_pair)
        dk_ref[0] = jnp.where(first, dks[:rows], dks[rows:]).astype(HALF)
        dv = jnp.where(first, dvs[:rows], dvs[rows:])
        dv_ref[0] = dv.astype(HALF)
        vb_ref[0, 0:1] += jnp.sum(dv[:img], axis=0, keepdims=True)
        vb_ref[0, 1:2] += jnp.sum(dv[img:], axis=0, keepdims=True)

        @pl.when(step == lines - 1)
        def _():
            dq = (acc_ref[...] * (1.0 / math.sqrt(HD))).reshape(n, rows, LANES)
            dq_ref[...] = dq.astype(HALF)
            qb_ref[0, 0:1] = jnp.sum(jnp.sum(dq[:, :img], axis=0), axis=0, keepdims=True)
            qb_ref[0, 1:2] = jnp.sum(jnp.sum(dq[:, img:], axis=0), axis=0, keepdims=True)

    for hop in range(1, lines - 2):
        at_step(linear, min(last, ahead + 5 * hop), functools.partial(line.round, hop))

    at_step(linear, last, line.close)


def attend_back(n, dp, img, qkv, mixture, grad_mix, lse, mask_col, out_parts, grad_attn, mix_loc):
    _, rows, wide = qkv.shape
    pairs = wide // 3 // LANES
    total = n * rows
    lw = pairs * LANES
    ahead = 2 * n
    steps = pairs * n
    width = out_parts.shape[2]
    depth = width // dp

    def place(k):
        return lax.rem(lax.max(k - ahead, 0), n)

    def head(k):
        return lax.div(lax.max(k - ahead, 0), n)

    full = pl.BlockSpec((n, rows, LANES), lambda k: (0, 0, head(k)))

    def block(base):
        return pl.BlockSpec((1, rows, LANES), lambda k: (place(k), 0, base + head(k)))

    bias = pl.BlockSpec((1, 2, LANES), lambda k: (head(k), 0, 0))
    anywhere = pl.BlockSpec(memory_space=pl.ANY)
    return pl.pallas_call(
        functools.partial(attn_back_kernel, n, img, pairs),
        grid=(ahead + steps,),
        in_specs=[
            full,
            block(pairs),
            block(2 * pairs),
            full,
            full,
            full,
            pl.BlockSpec((1, rows, LANES), lambda k: (place(k), 0, 0)),
            anywhere,
            whole(grad_attn.shape, True),
            pl.BlockSpec((rows, lw), lambda k: (0, lax.min(lax.div(k, 2), n - 1))),
        ],
        out_specs=[
            full,
            block(0),
            block(0),
            bias,
            bias,
            pl.BlockSpec((dp, 1, depth, lw), lambda k: (0, lax.min(k, ahead - 1), 0, 0)),
            anywhere,
        ],
        out_shape=[jax.ShapeDtypeStruct((n, rows, lw), HALF)] * 3
        + [jax.ShapeDtypeStruct((pairs, 2, LANES), SINGLE)] * 2
        + [
            jax.ShapeDtypeStruct((dp, 2 * n, depth, lw), HALF),
            jax.ShapeDtypeStruct((2, rows, width), HALF),
        ],
        scratch_shapes=[
            pltpu.VMEM((total, LANES), SINGLE),
            pltpu.VMEM((2, total), SINGLE),
            pltpu.VMEM((2, total), SINGLE),
            pltpu.VMEM((width, rows), HALF),
        ]
        + LineSum.scratch(n, rows, width, stop=n - 2),
        compiler_params=remote(3, 62),
        cost_estimate=cost(2 * 5 * 4 * pairs * total * total * LANES, 30 * MEGA, 2 * pairs * total * total),
        name="attend_back",
    )(qkv, qkv, qkv, mixture, grad_mix, lse, mask_col, out_parts, grad_attn, mix_loc)


def proj_columns(w_ref, z, t):
    dp, _, _, depth, heads = w_ref.shape
    return w_ref[:, z, t].reshape(dp * depth, heads)


def middle_kernel(
    n, img, mix_ref, x_ref, w_ref, b_ref, mod_ref, fc2_ref, y_ref, m_ref, all_ref, fc2_all, own, *sems
):
    greet(n, "near", "paths")
    fc2 = GroupGather(fc2_ref, fc2_all, *sems[3:])
    fc2.begin()
    lw = mix_ref.shape[1] // n
    heads = w_ref.shape[4]
    for t, sl in ((0, slice(0, img)), (1, slice(img, x_ref.shape[0]))):
        attn = b_ref[t : t + 1]
        for z in range(n):
            attn = attn + nt_dot(mix_ref[sl, z * lw : z * lw + heads], proj_columns(w_ref, z, t))
        y_ref[sl] = attn
        middle = x_ref[sl].astype(SINGLE) + mod_ref[t, 2:3] * attn
        m_ref[sl] = middle
        normed, _ = layer_norm(middle)
        own[sl] = (normed * (1.0 + mod_ref[t, 4:5]) + mod_ref[t, 3:4]).astype(HALF)
    gather = LineGather(n, own, all_ref, *sems[:3])
    gather.begin()
    gather.keep().start()
    for hop in range(max(n - 1, fc2.phases)):
        if hop < fc2.phases:
            fc2.arrive(hop)
        if hop < n - 1:
            gather.arrive(hop)
    gather.keep().wait()
    gather.finish()
    fc2.finish()


def middle_rows(n, dp, img, mixture, x_loc, weight, bias, mods, fc2):
    rows, width = x_loc.shape
    inner = pl.BlockSpec(memory_space=pltpu.VMEM)
    anywhere = pl.BlockSpec(memory_space=pl.ANY)
    return pl.pallas_call(
        functools.partial(middle_kernel, n, img),
        in_specs=[inner] * 6,
        out_specs=[inner, inner, anywhere, anywhere],
        out_shape=[
            jax.ShapeDtypeStruct((rows, width), SINGLE),
            jax.ShapeDtypeStruct((rows, width), SINGLE),
            jax.ShapeDtypeStruct((n, rows, width), HALF),
            jax.ShapeDtypeStruct((dp,) + fc2.shape, HALF),
        ],
        scratch_shapes=[pltpu.VMEM((rows, width), HALF)]
        + LineGather.scratch(n)
        + GroupGather.scratch(dp),
        compiler_params=remote(4),
        cost_estimate=cost(2 * rows * width * width, 100 * MEGA),
        name="middle_rows",
    )(mixture, x_loc, weight, bias, mods, fc2)


def by_distance(me, n, count):
    low = lax.min(me, n - 1 - me)
    near = lax.select(lax.rem(count, 2) == 1, lax.div(count + 1, 2), -lax.div(count, 2))
    far = lax.select(me < n - 1 - me, count - low, low - count)
    return me + lax.select(count <= 2 * low, near, far)


def mlp_kernel(n, img, tile, b_ref, e_loc, e_near, mod_ref, w1_far, b1_ref, w2_far,
    g_ref, dz_ref, dy_ref, db_ref, y_ref, sum_ref, gate_ref, acc_ref, out_ref, e_all, near_sem,
    w1_ref, w2_ref, w_sem, *sems):
    step = pl.program_id(0)
    me = lax.axis_index("seq")
    owner = by_distance(me, n, step)
    e_ref = e_all.at[pl.ds(owner, 1)]
    gather = LineGather(n, e_near, e_all, *sems, first=1)
    own = pltpu.make_async_copy(e_loc, e_all.at[me], near_sem.at[2])
    wide = g_ref.shape[2]

    def weights(t):
        cols = pl.ds(t * wide, wide)
        return (
            pltpu.make_async_copy(w1_far.at[:, cols], w1_ref.at[:, cols], w_sem.at[t, 0]),
            pltpu.make_async_copy(w2_far.at[:, t], w2_ref.at[:, t], w_sem.at[t, 1]),
        )

    def weights_in(t):
        for copy in weights(t):
            copy.wait()

    def nears(action):
        for way, sign in ((0, 1), (1, -1)):
            block = me - sign

            @pl.when(both(block >= 0, block < n))
            def _():
                action(
                    pltpu.make_async_copy(e_near.at[way], e_all.at[block], near_sem.at[way])
                )

    def begin():
        greet(n, "near")
        gather.begin()
        own.start()
        nears(lambda copy: copy.start())
        for t in range(2):
            for copy in weights(t):
                copy.start()
        own.wait()
        nears(lambda copy: copy.wait())

    at_step(step, 0, begin)
    for hop in range(1, n - 1):
        at_step(step, hop + 1, functools.partial(gather.arrive, hop))
    at_step(step, n - 1, gather.finish)
    units = g_ref.shape[2]

    @pl.when(step == 0)
    def _():
        sum_ref[...] = jnp.zeros_like(sum_ref)
        gate_ref[...] = jnp.zeros_like(gate_ref)

    for t, sl in ((0, slice(0, img)), (1, slice(img, b_ref.shape[1]))):
        at_step(step, 0, functools.partial(weights_in, t))
        rows = b_ref[0, sl]
        grad = (mod_ref[t, 5:6] * e_ref[0, sl].astype(SINGLE)).astype(HALF)
        dy_ref[0, sl] = grad

        for k in range(units // tile):
            here = slice(k * tile, (k + 1) * tile)
            cols = slice(t * units + k * tile, t * units + (k + 1) * tile)
            w1 = w1_ref[:, cols]
            pre = nn_dot(rows, w1) + b1_ref[t : t + 1, here]
            hidden, slope = gelu_both(pre)
            hidden = hidden.astype(HALF)
            g_ref[0, sl, here] = hidden
            w2 = w2_ref[:, t, :, here].reshape(-1, tile)
            out = nt_dot(hidden, w2)
            dz = nn_dot(grad, w2) * slope
            sum_ref[t : t + 1, here] += jnp.sum(dz, axis=0, keepdims=True)
            dzh = dz.astype(HALF)
            dz_ref[0, sl, here] = dzh
            part = nt_dot(dzh, w1)
            if k == 0:
                acc_ref[sl] = part
                out_ref[sl] = out
            else:
                acc_ref[sl] += part
                out_ref[sl] += out
        db_ref[0, sl] = acc_ref[sl].astype(HALF)
        out = out_ref[sl]
        y_ref[0, sl] = out.astype(HALF)
        gate_ref[t : t + 1] += jnp.sum(out * e_ref[0, sl].astype(SINGLE), axis=0, keepdims=True)


def feed_forward(n, img, mlp_in, e_loc, e_near, mods, w1, b1, w2):
    rows, width = mlp_in.shape[1:]
    units = w1.shape[1] // 2
    tile = min(768, units)
    while units % tile:
        tile -= LANES

    def owned(columns):
        return pl.BlockSpec(
            (1, rows, columns), lambda k: (by_distance(lax.axis_index("seq"), n, k), 0, 0)
        )

    return pl.pallas_call(
        functools.partial(mlp_kernel, n, img, tile),
        grid=(n,),
        in_specs=[
            owned(width),
            pl.BlockSpec(memory_space=pl.ANY),
            pl.BlockSpec(memory_space=pl.ANY),
            whole(mods.shape),
            pl.BlockSpec(memory_space=pl.ANY),
            whole(b1.shape),
            pl.BlockSpec(memory_space=pl.ANY),
        ],
        out_specs=[
            owned(units),
            owned(units),
            owned(width),
            owned(width),
            owned(width),
            whole((2, units)),
            whole((2, width)),
        ],
        out_shape=[
            jax.ShapeDtypeStruct((n, rows, units), HALF),
            jax.ShapeDtypeStruct((n, rows, units), HALF),
            jax.ShapeDtypeStruct((n, rows, width), HALF),
            jax.ShapeDtypeStruct((n, rows, width), HALF),
            jax.ShapeDtypeStruct((n, rows, width), HALF),
            jax.ShapeDtypeStruct((2, units), SINGLE),
            jax.ShapeDtypeStruct((2, width), SINGLE),
        ],
        scratch_shapes=[
            pltpu.VMEM((rows, width), SINGLE),
            pltpu.VMEM((rows, width), SINGLE),
            pltpu.VMEM((n, rows, width), HALF),
            pltpu.SemaphoreType.DMA((3,)),
            pltpu.VMEM(w1.shape, HALF),
            pltpu.VMEM(w2.shape, HALF),
            pltpu.SemaphoreType.DMA((2, 2)),
        ]
        + LineGather.scratch(n),
        compiler_params=remote(9, 60),
        cost_estimate=cost(6 * n * rows * width * units, 50 * MEGA, n * rows * units),
        name="feed_forward",
    )(mlp_in, e_loc, e_near, mods, w1, b1, w2)


def grads_kernel(n, img, plan, rounds, *refs):
    lefts = max(p[0] for p in plan) + 1
    rights = max(p[1] for p in plan) + 1
    count = lefts + rights
    far, rest = refs[:count], refs[count:]
    held, loaded, rest = rest[-count - 1 : -1], rest[-1], rest[: -count - 1]
    l_refs, r_refs = held[:lefts], held[lefts:]
    copies = [pltpu.make_async_copy(far[k], held[k], loaded.at[k]) for k in range(count)]
    step = pl.program_id(0)
    parts, o_ref, tail, turned = rest[:4]
    line = LineSum(n, at_rows(parts), None, *rest[4:], stop=n - 2, tail=tail)

    def begin():
        greet(n, "near")
        line.round(0)
        for left, right, stream in plan:
            if stream == 0:
                copies[left].start()
                copies[lefts + right].start()

    at_step(step, 0, begin)
    for hop, when in enumerate(rounds):
        at_step(step, when, functools.partial(line.round, hop + 1))
    tile = 512 if o_ref.shape[3] % 512 == 0 else 2 * LANES
    before = None
    for k, (left, right, stream) in enumerate(plan):

        @pl.when(step == k)
        def _():
            l_ref, r_ref = l_refs[left], r_refs[right]
            if stream == 0:
                copies[left].wait()
                copies[lefts + right].wait()
            count, rows, _ = l_ref.shape
            sl = slice(0, img) if stream == 0 else slice(img, rows)
            size = count * (sl.stop - sl.start)
            if before != (left, stream):
                turned[:, :size] = l_ref[:, sl].reshape(size, l_ref.shape[2]).T
            for column in range(0, o_ref.shape[3], tile):
                values = r_ref[:, sl, column : column + tile].reshape(size, tile)
                product = nn_dot(turned[:, :size], values).astype(HALF)
                o_ref[:, 0, :, column : column + tile] = product.reshape(
                    o_ref.shape[0], o_ref.shape[2], tile
                )

        before = (left, stream)
    at_step(step, len(plan) - 1, line.close)


def weight_grads(n, dp, img, lefts, rights, plan, rounds, parts, collective, name):
    rows, depth = lefts[0].shape[1:]
    wide = rights[0].shape[2]
    anywhere = pl.BlockSpec(memory_space=pl.ANY)
    block = (dp, 1, depth // dp, wide)
    longest = max(up(n * img, LANES), up(n * (rows - img), LANES))
    return pl.pallas_call(
        functools.partial(grads_kernel, n, img, plan, rounds),
        grid=(len(plan),),
        in_specs=[anywhere] * (len(lefts) + len(rights) + 1),
        out_specs=[pl.BlockSpec(block, lambda k: (0, k, 0, 0)), anywhere],
        out_shape=[
            jax.ShapeDtypeStruct((dp, len(plan), depth // dp, wide), HALF),
            jax.ShapeDtypeStruct((2,) + parts.shape[1:], HALF),
        ],
        scratch_shapes=[pltpu.VMEM((depth, longest), HALF)]
        + LineSum.scratch(n, *parts.shape[1:], stop=n - 2)
        + [pltpu.VMEM(a.shape, HALF) for a in (*lefts, *rights)]
        + [pltpu.SemaphoreType.DMA((len(lefts) + len(rights),))],
        compiler_params=remote(collective, 60),
        cost_estimate=cost(2 * n * rows * depth * len(plan) * wide // 2, 60 * MEGA),
        name=name,
    )(*lefts, *rights, parts)


def middle_back_kernel(
    n, img, part_ref, prev_ref, m_ref, y_ref, e_ref, w_ref, mod_ref, dm_ref, dy_ref, sum_ref, all_ref,
    db_ref, mix, send, recv, local, *line_scratch,
):
    me = lax.axis_index("seq")
    rows, width = m_ref.shape
    heads = w_ref.shape[4]
    streams = ((0, slice(0, img)), (1, slice(img, rows)))
    greet(n, "all")
    line = LineSum(n, at_rows(part_ref), db_ref, *line_scratch, first=n - 2, prev=prev_ref)
    line.round(n - 2)
    if mix.shape[2] > heads:
        mix[...] = jnp.zeros_like(mix)
    line.finish()
    for t, sl in streams:
        grad_in = db_ref[sl]
        normed, inv_std = layer_norm(m_ref[sl])
        upstream = e_ref[sl].astype(SINGLE)
        grad_middle = upstream + norm_back(normed, inv_std, grad_in * (1.0 + mod_ref[t, 4:5]))
        dm_ref[sl] = grad_middle
        grad_attn = mod_ref[t, 2:3] * grad_middle
        dy_ref[sl] = grad_attn.astype(HALF)

        def total(value):
            return jnp.sum(value, axis=0, keepdims=True)

        sum_ref[t, 0:1] = total(grad_middle * y_ref[sl])
        sum_ref[t, 1:2] = total(grad_in)
        sum_ref[t, 2:3] = total(grad_in * normed)
        sum_ref[t, 3:4] = total(grad_attn)
        sum_ref[t, 4:5] = total(upstream)

    def exchange(peer, block):
        return pltpu.make_async_remote_copy(
            src_ref=mix.at[peer],
            dst_ref=all_ref.at[block],
            send_sem=send.at[peer],
            recv_sem=recv.at[block],
            device_id=on_line(peer),
            device_id_type=MESH,
        )

    keep = pltpu.make_async_copy(mix.at[me], all_ref.at[me], local)
    for peer in range(n):
        for t, sl in streams:
            mix[peer, sl, :heads] = nn_dot(dy_ref[sl], proj_columns(w_ref, peer, t)).astype(HALF)

        @pl.when(peer != me)
        def _():
            exchange(peer, me).start()

        @pl.when(peer == me)
        def _():
            keep.start()

    for peer in range(n):

        @pl.when(peer != me)
        def _():
            exchange(peer, peer).wait()

    keep.wait()


def middle_back(n, img, parts, prev, middle, attn_out, cot, weight, mods, lwp):
    rows, width = middle.shape
    inner = pl.BlockSpec(memory_space=pltpu.VMEM)
    anywhere = pl.BlockSpec(memory_space=pl.ANY)
    return pl.pallas_call(
        functools.partial(middle_back_kernel, n, img),
        in_specs=[anywhere, anywhere] + [inner] * 5,
        out_specs=[inner, inner, inner, anywhere],
        out_shape=[
            jax.ShapeDtypeStruct((rows, width), SINGLE),
            jax.ShapeDtypeStruct((rows, width), HALF),
            jax.ShapeDtypeStruct((2, 8, width), SINGLE),
            jax.ShapeDtypeStruct((n, rows, lwp), HALF),
        ],
        scratch_shapes=[
            pltpu.VMEM((rows, width), SINGLE),
            pltpu.VMEM((n, rows, lwp), HALF),
            pltpu.SemaphoreType.DMA((n,)),
            pltpu.SemaphoreType.DMA((n,)),
            pltpu.SemaphoreType.DMA,
        ]
        + LineSum.scratch(n, rows, width, first=n - 2),
        compiler_params=remote(5),
        cost_estimate=cost(2 * rows * width * width, 60 * MEGA),
        name="middle_back",
    )(parts, prev, middle, attn_out, cot, weight, mods)


def attn_in_kernel(
    n, img, dq_ref, dk_ref, dv_ref, x_ref, a_ref, w_ref, y_ref, prev_ref,
    da_ref, sum_ref, g_ref, y_sum, turned, *scratch,
):
    step = pl.program_id(0)
    count, rows, lw = dq_ref.shape
    line = LineSum(n, at_rows(y_ref), y_sum, *scratch, first=n - 2, prev=prev_ref)
    streams = ((0, slice(0, img)), (1, slice(img, rows)))

    def begin():
        greet(n, "near")
        line.round(n - 2)
        sum_ref[...] = jnp.zeros_like(sum_ref)

    at_step(step, 0, begin)

    @pl.when(step < n)
    def _():
        here = lax.min(step, n - 1)
        for t, sl in streams:
            part = None
            for c, ref in enumerate((dq_ref, dk_ref, dv_ref)):
                start = (3 * t + c) * lw
                term = nt_dot(ref[here, sl], w_ref[:, start : start + lw])
                part = term if part is None else part + term
            da_ref[0, sl] = part.astype(HALF)
            normed, _ = layer_norm(x_ref[0, sl].astype(SINGLE))
            sum_ref[t, 0:1] += jnp.sum(part, axis=0, keepdims=True)
            sum_ref[t, 1:2] += jnp.sum(part * normed, axis=0, keepdims=True)

    for t, sl in streams:
        size = count * (sl.stop - sl.start)
        for c, ref in enumerate((dq_ref, dk_ref, dv_ref)):

            @pl.when(step == n + 3 * t + c)
            def _():
                if c == 0:
                    turned[:, :size] = a_ref[:, sl].reshape(size, a_ref.shape[2]).T
                g_ref[...] = nn_dot(turned[:, :size], ref[:, sl].reshape(size, lw)).astype(HALF)

    at_step(step, n + 5, line.finish)


def attn_in_back(n, img, dq, dk, dv, x_all, attn_in, weight, out_parts, running):
    _, rows, lw = dq.shape
    width = x_all.shape[2]
    anywhere = pl.BlockSpec(memory_space=pl.ANY)
    row = pl.BlockSpec((1, rows, width), lambda k: (lax.min(k, n - 1), 0, 0))
    longest = max(up(n * img, LANES), up(n * (rows - img), LANES))
    return pl.pallas_call(
        functools.partial(attn_in_kernel, n, img),
        grid=(n + 6,),
        in_specs=[whole(dq.shape, True)] * 3
        + [row, whole(attn_in.shape, True), whole(weight.shape, True)]
        + [anywhere] * 2,
        out_specs=[
            row,
            whole((2, 2, width)),
            pl.BlockSpec((width, lw), lambda k: (0, lax.max(k - n, 0))),
            whole((rows, width), True),
        ],
        out_shape=[
            jax.ShapeDtypeStruct((n, rows, width), HALF),
            jax.ShapeDtypeStruct((2, 2, width), SINGLE),
            jax.ShapeDtypeStruct((width, 6 * lw), HALF),
            jax.ShapeDtypeStruct((rows, width), SINGLE),
        ],
        scratch_shapes=[pltpu.VMEM((width, longest), HALF)]
        + LineSum.scratch(n, rows, width, first=n - 2),
        compiler_params=remote(10, 62),
        cost_estimate=cost(12 * n * rows * width * lw, 30 * MEGA),
        name="attn_in_back",
    )(dq, dk, dv, x_all, attn_in, weight, out_parts, running)


def end_kernel(
    n, dp, cut, parts, qkv_part, p_ref, packed, extra, ada_ref, acts,
    sum_ref, qkv_sum, p_own, every, cond_ref, ada_grad,
    z_got, row, c_part, c_got, c_all, z_send, z_recv, e_send, e_recv, c_send, c_recv, a_send, a_recv,
    *scratch,
):
    me, my = lax.axis_index("seq"), lax.axis_index("dp")
    depth = ada_ref.shape[0]
    span = packed.shape[2]
    greet(n, "all", "all")
    line = LineSum(n, at_rows(parts), sum_ref, *scratch[:6])
    group = GroupSum(qkv_part, *scratch[6:15])
    proj = GroupSum(p_ref, *scratch[15:])
    mates, others = range(1, n), range(1, dp)
    z_go = [to_line(me, n, k, packed, z_got, z_send, z_recv) for k in mates]
    for copy in z_go:
        copy.start()
    line.round(0)
    proj.begin()
    group.begin()
    z_got[me] = packed[me]
    for copy in z_go:
        copy.wait_recv()
    row[:, :span] = jnp.sum(z_got[...], axis=0)
    row[:, span:] = extra[...]
    e_go = [to_group(my, dp, k, row, every, e_send, e_recv) for k in others]
    for copy in e_go:
        copy.start()
    every[my] = row[...]
    proj.step(0)
    group.step(0)
    for copy in e_go:
        copy.wait_recv()
    cols = cut // 2
    halves_of = [every[:, 0, t * cols : (t + 1) * cols].astype(HALF) for t in range(2)]
    product = nt_dot(halves_of[0], ada_ref[:, 0, :]) + nt_dot(halves_of[1], ada_ref[:, 1, :])
    c_part[...] = jnp.zeros_like(c_part)
    for k in range(dp):
        c_part[k, :, :depth] = product[k : k + 1]
    c_go = [to_group(my, dp, k, c_part, c_got, c_send, c_recv) for k in others]
    for copy in c_go:
        copy.start()
    c_got[my] = c_part[my]
    act_rows = acts[:, 0, :depth].astype(HALF)
    for t in range(2):
        ada_grad[:, t, :] = tn_dot(act_rows, halves_of[t])
    for hop in range(1, n - 1):
        line.round(hop)
    for number in range(1, group.phases):
        proj.step(number)
        group.step(number)
    for copy in c_go:
        copy.wait_recv()
    a_go = [to_line(me, n, k, c_got, c_all, a_send, a_recv) for k in mates]
    for copy in a_go:
        copy.start()
    c_all[me] = c_got[...]
    for copy in a_go:
        copy.wait_recv()
    cond_ref[...] = jnp.sum(c_all[...], axis=0)
    rows, _, _, wide = qkv_sum.shape

    def store_proj(half, value):
        p_own[half] = value.astype(HALF)

    def store_qkv(half, value):
        own = slice(half * rows // 2, (half + 1) * rows // 2)
        for k in range(6):
            qkv_sum[own, k % 3, k // 3, :] = value[:, k * wide : (k + 1) * wide]

    proj.finish(store_proj)
    group.finish(store_qkv)
    line.finish()
    for copy in z_go + e_go + c_go + a_go:
        copy.wait_send()


def end(n, dp, cut, parts, qkv_part, proj_part, packed, extra, ada, acts):
    rows, width = parts.shape[1:]
    depth = up(ada.shape[0], LANES)
    span = packed.shape[2] + extra.shape[1]
    inner = pl.BlockSpec(memory_space=pltpu.VMEM)
    anywhere = pl.BlockSpec(memory_space=pl.ANY)
    sems = [n - 1, n - 1, dp - 1, dp - 1, dp - 1, dp - 1, n - 1, n - 1]
    return pl.pallas_call(
        functools.partial(end_kernel, n, dp, cut),
        in_specs=[anywhere, anywhere, anywhere, inner, inner, inner, inner],
        out_specs=[inner] * 6,
        out_shape=[
            jax.ShapeDtypeStruct((rows, width), SINGLE),
            jax.ShapeDtypeStruct((ada.shape[0], 3, 2, qkv_part.shape[3] // 6), SINGLE),
            jax.ShapeDtypeStruct(proj_part.shape[1:], HALF),
            jax.ShapeDtypeStruct((dp, 1, span), SINGLE),
            jax.ShapeDtypeStruct((dp, 1, depth), SINGLE),
            jax.ShapeDtypeStruct(ada.shape, SINGLE),
        ],
        scratch_shapes=[
            pltpu.VMEM(packed.shape, SINGLE),
            pltpu.VMEM((1, span), SINGLE),
            pltpu.VMEM((dp, 1, depth), SINGLE),
            pltpu.VMEM((dp, 1, depth), SINGLE),
            pltpu.VMEM((n, dp, 1, depth), SINGLE),
        ]
        + [pltpu.SemaphoreType.DMA((k,)) for k in sems]
        + LineSum.scratch(n, rows, width)
        + GroupSum.scratch(dp, *qkv_part.shape[2:])
        + GroupSum.scratch(dp, *proj_part.shape[2:]),
        compiler_params=remote(7, 62),
        cost_estimate=cost(10**6, 100 * MEGA),
        name="end",
    )(parts, qkv_part, proj_part, packed, extra, ada, acts)


def rows_kernel(img, slots, da_ref, dm_ref, x_ref, m_ref, y_ref, mod_ref, shift_ref, live_ref, io_ref, to_ref, ig_ref, tg_ref):
    for t, sl, out_ref, grad_ref in (
        (0, slice(0, img), io_ref, ig_ref),
        (1, slice(img, x_ref.shape[0]), to_ref, tg_ref),
    ):
        keep = out_ref.shape[1]
        live = live_ref[sl]
        value = m_ref[sl] + mod_ref[t, 5:6] * (y_ref[sl] + shift_ref[t : t + 1])
        out_ref[0] = (value * live).astype(HALF)[:keep]
        normed, inv_std = layer_norm(x_ref[sl].astype(SINGLE))
        grad = dm_ref[sl] + norm_back(normed, inv_std, da_ref[sl] * (1.0 + mod_ref[t, 1:2]))
        grad_ref[0] = (grad * live)[:keep]


def rows_out(img, slots, grad_attn_in, grad_middle, x_loc, middle, mlp_sum, mods, fc2_shift, live):
    width = x_loc.shape[1]
    return pl.pallas_call(
        functools.partial(rows_kernel, img, slots),
        out_shape=[
            jax.ShapeDtypeStruct((1, img, width), HALF),
            jax.ShapeDtypeStruct((1, slots, width), HALF),
            jax.ShapeDtypeStruct((1, img, width), SINGLE),
            jax.ShapeDtypeStruct((1, slots, width), SINGLE),
        ],
        compiler_params=params(),
        cost_estimate=cost(10**6, 14 * MEGA),
        name="rows_out",
    )(grad_attn_in, grad_middle, x_loc, middle, mlp_sum, mods, fc2_shift, live)


def body(
    image_tokens,
    text_tokens,
    text_lengths,
    conditioning,
    ada_weight,
    ada_bias,
    qkv_weight,
    qv_bias,
    proj_weight,
    proj_bias,
    fc1_weight,
    fc1_bias,
    fc2_weight,
    fc2_bias,
    image_cotangent,
    text_cotangent,
):
    n = lax.axis_size("seq")
    dp = lax.axis_size("dp")
    img, width = image_tokens.shape[1:]
    slots = text_tokens.shape[1]
    pad = up(slots, 16)
    rows = img + pad
    depth = qkv_weight.shape[0]
    lw = qkv_weight.shape[3]
    lwp = up(lw, LANES)
    units = fc1_weight.shape[2]
    mod_cols = ada_weight.shape[2]
    my_seq = lax.axis_index("dp")

    def stacked(image, text):
        return jnp.concatenate([image, jnp.pad(text, ((0, pad - slots), (0, 0)))], axis=0)

    length = text_lengths[0, 0]
    live_text = (jnp.arange(slots, dtype=jnp.int32) < length)[:, None]
    x_loc = stacked(image_tokens[0], text_tokens[0])
    e_loc = stacked(
        image_cotangent[0], jnp.where(live_text, text_cotangent[0], jnp.zeros((), HALF))
    )

    def split(shard):
        return shard.reshape(2, -1, shard.shape[-1])

    qkv_local = jnp.pad(qkv_weight, ((0, 0), (0, 0), (0, 0), (0, lwp - lw))).reshape(depth, 6 * lwp)
    share = proj_weight.shape[0]
    fc1_local = fc1_weight.reshape(depth, 2 * units)

    cond_float = conditioning.astype(SINGLE)
    bias_cols = proj_bias.shape[1]
    cut = 2 * mod_cols
    proj_line = lax.all_gather(proj_weight.transpose(1, 2, 0), "seq", axis=0, tiled=False)
    x_all, side_all, acts, mods, shifts, qkv_full, fc1_full = start(
        n,
        dp,
        x_loc,
        conditioning,
        ada_weight,
        ada_bias,
        proj_bias,
        fc2_bias,
        text_lengths,
        split(qkv_local),
        split(fc1_local),
    )
    qkv_full = qkv_full.reshape(width, 6 * lwp)
    fc1_full = fc1_full.reshape(width, 2 * units)
    proj_shift, fc2_shift = shifts[:2], shifts[2:]
    lengths_all = side_all[:, 0, cut + 4 * bias_cols]

    slot = jnp.arange(rows, dtype=SINGLE)[None, :] - img
    live = jnp.logical_or(slot < 0, jnp.logical_and(slot < lengths_all[:, None], slot < slots))
    mask = jnp.where(live, SINGLE(0), SINGLE(MASKED))
    mask_row = mask.reshape(1, n * rows)
    mask_col = jnp.broadcast_to(mask[:, :, None], (n, rows, LANES))
    live_loc = jnp.concatenate(
        [jnp.ones((img, 1), SINGLE), jnp.pad(live_text.astype(SINGLE), ((0, pad - slots), (0, 0)))]
    )

    bias_rows = jnp.stack(
        [qv_bias[:, 0], jnp.zeros_like(qv_bias[:, 0]), qv_bias[:, 1]], axis=1
    ).astype(SINGLE)
    bias_rows = jnp.pad(bias_rows, ((0, 0), (0, 0), (0, lwp - lw))).reshape(2, 3 * lwp)
    attn_in, qkv_rows = project_qkv(n, img, x_all, mods, qkv_full, bias_rows)
    mixture, lse, e_near, mix_loc, proj_full = attend(
        n, dp, qkv_rows, mask_row, e_loc, proj_line.reshape(2, -1, share)
    )
    proj_full = proj_full.reshape(dp, n, 2, depth, share)

    attn_out, middle, mlp_in, fc2_full = middle_rows(
        n, dp, img, mix_loc, x_loc, proj_full, proj_shift, mods, fc2_weight.transpose(1, 2, 0)
    )
    hidden, grad_pre, grad_mlp, mlp_in_part, mlp_out_part, fc1_bias_part, gate_two_part = (
        feed_forward(
            n, img, mlp_in, e_loc, e_near, mods, fc1_full, fc1_bias.astype(SINGLE), fc2_full
        )
    )
    fc_plan = [(w, w, t) for w in range(2) for t in range(2)]
    fc_rounds = [(k + 1) * 4 // (n - 2) for k in range(n - 3)]
    fc_part, running = weight_grads(
        n, dp, img, (mlp_in, grad_mlp), (grad_pre, hidden), fc_plan, fc_rounds, mlp_in_part, 6, "fc_grads"
    )
    fc_sum = lax.psum_scatter(
        fc_part.reshape(dp * 4 * depth, units), "dp", scatter_dimension=0, tiled=True
    ).reshape(4, depth, units)

    grad_middle, grad_attn, sums, grad_mix = middle_back(
        n, img, mlp_in_part, running, middle, attn_out, e_loc, proj_full, mods, lwp
    )
    grad_q, grad_k, grad_v, q_bias_part, v_bias_part, proj_part, out_running = attend_back(
        n, dp, img, qkv_rows, mixture, grad_mix, lse, mask_col, mlp_out_part, grad_attn, mix_loc
    )
    attn_in_part, mod_one, qkv_part, mlp_sum = attn_in_back(
        n,
        img,
        grad_q,
        grad_k,
        grad_v,
        x_all,
        attn_in,
        qkv_full,
        mlp_out_part,
        out_running,
    )
    fc_own = fc_sum.astype(SINGLE)

    upstream_sum = sums[:, 4]
    gate_two = gate_two_part + fc2_shift * upstream_sum
    mod_grads = jnp.stack(
        [mod_one[:, 0], mod_one[:, 1], sums[:, 0], sums[:, 1], sums[:, 2], gate_two], axis=1
    ).reshape(2, n, mod_cols)
    rest = jnp.stack([sums[:, 3], mods[:, 5] * upstream_sum]).reshape(4, n, bias_cols)
    packed = jnp.concatenate(
        [
            mod_grads.transpose(1, 0, 2).reshape(n, -1),
            rest.transpose(1, 0, 2).reshape(n, -1),
        ],
        axis=1,
    )
    q_bias = q_bias_part.transpose(1, 0, 2).reshape(2, lwp)[:, :lw]
    v_bias = v_bias_part.transpose(1, 0, 2).reshape(2, lwp)[:, :lw]
    extra = jnp.concatenate(
        [jnp.stack([q_bias, v_bias], axis=1).reshape(-1), fc1_bias_part.reshape(-1)]
    )
    grad_attn_in, qkv_sum, proj_own, every, cond_sum, ada_grad = end(
        n,
        dp,
        cut,
        attn_in_part,
        qkv_part.reshape(dp, 2, depth // 2, 6 * lwp),
        proj_part.reshape(dp, 2, n * depth, lwp),
        packed[:, None],
        extra[None],
        ada_weight,
        acts,
    )
    proj_own, fc_sum = lax.optimization_barrier((proj_own, fc_sum))
    proj_sum = lax.psum_scatter(
        proj_own.reshape(n * 2 * depth, lwp), "seq", scatter_dimension=0, tiled=True
    ).reshape(2, depth, lwp)
    every = every[:, 0]
    total = jnp.sum(every, axis=0)

    image_out, text_out, image_grad, text_grad = rows_out(
        img, slots, grad_attn_in, grad_middle, x_loc, middle, mlp_sum, mods, fc2_shift, live_loc
    )

    ada_bias_grad = total[:cut].reshape(2, mod_cols)
    proj_bias_grad = total[cut : cut + 2 * bias_cols].reshape(2, bias_cols)
    fc2_bias_grad = total[cut + 2 * bias_cols : cut + 4 * bias_cols].reshape(2, bias_cols)
    after = cut + 4 * bias_cols
    qv_bias_grad = total[after : after + 4 * lw].reshape(2, 2, lw)
    fc1_bias_grad = total[after + 4 * lw :].reshape(2, units)
    cond_grad = cond_sum[:, 0, :depth].reshape(1, width) * silu_slope(cond_float)

    qkv_grad = qkv_sum[..., :lw].transpose(0, 2, 1, 3)
    fc1_grad = fc_own[:2].transpose(1, 0, 2)
    fc2_grad = fc_own[2:].transpose(2, 0, 1)
    proj_grad = proj_sum.astype(SINGLE)[..., :share].transpose(2, 0, 1)
    return (
        image_out,
        text_out,
        image_grad,
        text_grad,
        cond_grad,
        ada_grad,
        ada_bias_grad,
        qkv_grad,
        qv_bias_grad,
        proj_grad,
        proj_bias_grad,
        fc1_grad,
        fc1_bias_grad,
        fc2_grad,
        fc2_bias_grad,
    )


def solution(mesh):
    in_specs = (
        P("dp", "seq", None),
        P("dp", "seq", None),
        P("dp", "seq"),
        P("dp", None),
        P("dp", None, "seq"),
        P(None, "seq"),
        P("dp", None, None, "seq"),
        P(None, None, "seq"),
        P("seq", None, "dp"),
        P(None, "seq"),
        P("dp", None, "seq"),
        P(None, "seq"),
        P("seq", None, "dp"),
        P(None, "seq"),
        P("dp", "seq", None),
        P("dp", "seq", None),
    )
    out_specs = (
        P("dp", "seq", None),
        P("dp", "seq", None),
        P("dp", "seq", None),
        P("dp", "seq", None),
        P("dp", None),
        P("dp", None, "seq"),
        P(None, "seq"),
        P("dp", None, None, "seq"),
        P(None, None, "seq"),
        P("seq", None, "dp"),
        P(None, "seq"),
        P("dp", None, "seq"),
        P(None, "seq"),
        P("seq", None, "dp"),
        P(None, "seq"),
    )
    return jax.shard_map(body, mesh=mesh, in_specs=in_specs, out_specs=out_specs, check_vma=False)
```

```python
import functools
import math

import jax
import jax.numpy as jnp
from jax import lax
from jax.experimental import pallas as pl
from jax.experimental.pallas import tpu as pltpu
from jax.sharding import PartitionSpec as P

HD = 64
LANES = 128
EPSILON = 1e-06
GELU_ROOT = math.sqrt(2.0 / math.pi)
GELU_CUBE = 0.044715
MASKED = -1e30
SINGLE = jnp.float32
HALF = jnp.bfloat16
MEGA = 2**20


def up(value, multiple):
    return -(-value // multiple) * multiple


def params(limit=56):
    return pltpu.CompilerParams(vmem_limit_bytes=limit * MEGA)


def remote(collective, limit=56):
    return pltpu.CompilerParams(
        collective_id=collective, has_side_effects=True, vmem_limit_bytes=limit * MEGA
    )


def cost(flops, nbytes, trans=0):
    return pl.CostEstimate(flops=int(flops), bytes_accessed=int(nbytes), transcendentals=int(trans))


def nt_dot(a, b):
    return lax.dot_general(a, b, (((1,), (1,)), ((), ())), preferred_element_type=SINGLE)


def tn_dot(a, b):
    return lax.dot_general(a, b, (((0,), (0,)), ((), ())), preferred_element_type=SINGLE)


def nn_dot(a, b):
    return jnp.dot(a, b, preferred_element_type=SINGLE)


def layer_norm(values):
    center = values - jnp.mean(values, axis=-1, keepdims=True)
    inv_std = lax.rsqrt(jnp.mean(center * center, axis=-1, keepdims=True) + EPSILON)
    return (center * inv_std, inv_std)


def norm_back(normed, inv_std, upstream):
    first = jnp.mean(upstream, axis=-1, keepdims=True)
    second = jnp.mean(upstream * normed, axis=-1, keepdims=True)
    return inv_std * (upstream - first - normed * second)


def gelu_both(values):
    square = values * values
    inner = GELU_ROOT * (values + GELU_CUBE * square * values)
    tangent = jnp.tanh(inner)
    half = 0.5 * (1.0 + tangent)
    slope = half + 0.5 * values * (1.0 - tangent * tangent) * GELU_ROOT * (
        1.0 + 3.0 * GELU_CUBE * square
    )
    return values * half, slope


def silu_slope(values):
    sigma = jax.nn.sigmoid(values)
    return sigma + values * sigma * (1.0 - sigma)


def whole(shape, single=False):
    zeros = (0,) * len(shape)
    if single:
        return pl.BlockSpec(shape, lambda *_: zeros, pipeline_mode=pl.Buffered(1))
    return pl.BlockSpec(shape, lambda *_: zeros)


def rows_spec(rows, width):
    return pl.BlockSpec((1, rows, width), lambda s: (s, 0, 0))


MESH = pl.DeviceIdType.MESH


def on_line(position):
    return {"seq": position}


def both(first, second):
    return jnp.logical_and(first, second)


def flip(value, mask):
    bit = 1
    while bit <= mask:
        if mask & bit:
            value = value + bit - 2 * bit * lax.rem(lax.div(value, bit), 2)
        bit *= 2
    return value


def greet(n, line=None, group=None):
    me, my = lax.axis_index("seq"), lax.axis_index("dp")
    dp = lax.axis_size("dp")
    barrier = pltpu.get_barrier_semaphore()
    peers = []
    if line == "all":
        peers += [on_line(lax.rem(me + offset, n)) for offset in range(1, n)]
    if group == "all":
        peers += [{"dp": lax.rem(my + offset, dp)} for offset in range(1, dp)]
    if group == "paths":
        peers += [{"dp": flip(my, 1)}] + [{"dp": flip(my, mask)} for mask in masks_of(dp)]
    for peer in peers:
        pl.semaphore_signal(barrier, inc=1, device_id=peer, device_id_type=MESH)
    if line == "near":
        for sign in (1, -1):
            near = me + sign

            @pl.when(both(near >= 0, near < n))
            def _():
                pl.semaphore_signal(barrier, inc=1, device_id=on_line(near), device_id_type=MESH)

    count = len(peers)
    if line == "near":
        count = count + lax.min(me, 1) + lax.min(n - 1 - me, 1)
    pl.semaphore_wait(barrier, count)


def masks_of(dp):
    masks, bit = [], 2
    while bit < dp:
        masks.append(bit)
        bit *= 2
    return masks


class GroupGather:
    def __init__(self, src, out, send, recv, pass_send, pass_recv, local):
        self.src, self.out = src, out
        self.send, self.recv, self.local = send, recv, local
        self.pass_send, self.pass_recv = pass_send, pass_recv
        self.my = lax.axis_index("dp")
        masks = masks_of(out.shape[0])
        self.orders = (masks, masks[::-1])
        self.phases = len(masks)

    @staticmethod
    def scratch(dp):
        return [pltpu.SemaphoreType.DMA((2, dp // 2)) for _ in range(4)] + [
            pltpu.SemaphoreType.DMA
        ]

    def span(self, half, count):
        mask = 0
        for k in range(self.phases):
            if count >> k & 1:
                mask |= self.orders[half][k]
        return mask

    def copy(self, half, phase, count, block):
        src = self.src.at[half] if count == 0 else self.out.at[block, half]
        index = 2**phase - 1 + count
        return pltpu.make_async_remote_copy(
            src_ref=src,
            dst_ref=self.out.at[block, half],
            send_sem=self.send.at[half, index],
            recv_sem=self.recv.at[half, index],
            device_id={"dp": flip(self.my, self.orders[half][phase])},
            device_id_type=MESH,
        )

    def hand(self, half, index, block, own=False):
        src = self.src.at[half] if own else self.out.at[block, half]
        return pltpu.make_async_remote_copy(
            src_ref=src,
            dst_ref=self.out.at[block, half],
            send_sem=self.pass_send.at[half, index],
            recv_sem=self.pass_recv.at[half, index],
            device_id={"dp": flip(self.my, 1)},
            device_id_type=MESH,
        )

    def begin(self):
        for phase in range(self.phases):
            for half in range(2):
                self.copy(half, phase, 0, self.my).start()
        for half in range(2):
            self.hand(half, 0, self.my, True).start()
        pltpu.make_async_copy(self.src, self.out.at[self.my], self.local).start()

    def arrive(self, phase):
        for half in range(2):
            mask = self.orders[half][phase]
            for count in range(2**phase):
                block = flip(self.my, mask ^ self.span(half, count))
                self.copy(half, phase, count, block).wait_recv()
            if phase + 1 < self.phases:
                for count in range(1, 2 ** (phase + 1)):
                    block = flip(self.my, self.span(half, count))
                    self.copy(half, phase + 1, count, block).start()
            for count in range(2**phase):
                block = flip(self.my, mask ^ self.span(half, count))
                self.hand(half, 2**phase + count, block).start()

    def finish(self):
        pltpu.make_async_copy(self.src, self.out.at[self.my], self.local).wait()
        other = flip(self.my, 1)
        for half in range(2):
            self.hand(half, 0, other, True).wait()
            for phase in range(self.phases):
                mask = self.orders[half][phase]
                for count in range(2**phase):
                    self.copy(half, phase, count, self.my).wait_send()
                    block = flip(other, mask ^ self.span(half, count))
                    self.hand(half, 2**phase + count, block).wait()


class GroupSum:
    def __init__(self, part, got, hold, passed, came, pass_send, pass_recv, send, recv, load):
        self.part, self.got, self.hold, self.passed, self.came = part, got, hold, passed, came
        self.pass_send, self.pass_recv = pass_send, pass_recv
        self.send, self.recv, self.load = send, recv, load
        self.my = lax.axis_index("dp")
        self.dp = part.shape[0]
        masks = masks_of(self.dp)
        self.orders = (masks, masks[::-1])
        self.phases = len(masks)

    @staticmethod
    def scratch(dp, rows, width):
        half = dp // 2
        return [
            pltpu.VMEM((2, half, rows, width), HALF),
            pltpu.VMEM((2, half, rows, width), HALF),
            pltpu.VMEM((2, half - 1, rows, width), HALF),
            pltpu.VMEM((2, half - 1, rows, width), HALF),
        ] + [pltpu.SemaphoreType.DMA((2, half)) for _ in range(5)]

    def span(self, half, count):
        mask = 0
        for k in range(self.phases):
            if count >> k & 1:
                mask |= self.orders[half][k]
        return mask

    def hand(self, half, count):
        block = flip(self.my, 1 ^ self.span(half, count))
        return pltpu.make_async_remote_copy(
            src_ref=self.part.at[block, half],
            dst_ref=self.got.at[half, count],
            send_sem=self.pass_send.at[half, count],
            recv_sem=self.pass_recv.at[half, count],
            device_id={"dp": flip(self.my, 1)},
            device_id_type=MESH,
        )

    def fetch(self, half, count):
        block = flip(self.my, self.span(half, count))
        return pltpu.make_async_copy(
            self.part.at[block, half], self.hold.at[half, count], self.load.at[half, count]
        )

    def copy(self, half, phase, index):
        return pltpu.make_async_remote_copy(
            src_ref=self.passed.at[half, 2**phase + index - 1],
            dst_ref=self.came.at[half, 2**phase - 1 + index],
            send_sem=self.send.at[half, 2**phase - 1 + index],
            recv_sem=self.recv.at[half, 2**phase - 1 + index],
            device_id={"dp": flip(self.my, self.orders[half][phase])},
            device_id_type=MESH,
        )

    def every(self):
        return [(half, count) for half in range(2) for count in range(self.dp // 2)]

    def begin(self):
        for half, count in self.every():
            self.hand(half, count).start()
            if self.hold is not None:
                self.fetch(half, count).start()

    def value(self, half, count, phase):
        if self.hold is None:
            mine = self.part[flip(self.my, self.span(half, count)), half]
        else:
            mine = self.hold[half, count]
        total = mine.astype(SINGLE) + self.got[half, count].astype(SINGLE)
        for later in range(phase, self.phases):
            total = total + self.came[half, 2**later - 1 + count].astype(SINGLE)
        return total

    def step(self, number):
        if number == 0:
            for half, count in self.every():
                if self.hold is not None:
                    self.fetch(half, count).wait()
                self.hand(half, count).wait_recv()
        else:
            self.took(self.phases - number)
        phase = self.phases - 1 - number
        for half in range(2):
            for index in range(2**phase):
                count = 2**phase + index
                self.passed[half, count - 1] = self.value(half, count, phase + 1).astype(HALF)
                self.copy(half, phase, index).start()

    def took(self, phase):
        for half in range(2):
            for index in range(2**phase):
                self.copy(half, phase, index).wait_recv()

    def finish(self, store):
        self.took(0)
        for half in range(2):
            store(half, self.value(half, 0, 0))
        self.sent(0)

    def sent(self, first):
        for half, count in self.every():
            self.hand(half, count).wait_send()
        for phase in range(first, self.phases):
            for half in range(2):
                for index in range(2**phase):
                    self.copy(half, phase, index).wait_send()


class LineGather:
    def __init__(self, n, src, out, send, recv, local, first=0, stop=None, land=None):
        self.n, self.src, self.out, self.land = n, src, out, land
        self.send, self.recv, self.local = send, recv, local
        self.first, self.stop = first, n - 1 if stop is None else stop
        self.me = lax.axis_index("seq")

    @staticmethod
    def scratch(n):
        return [
            pltpu.SemaphoreType.DMA((2, n - 1)),
            pltpu.SemaphoreType.DMA((2, n - 1)),
            pltpu.SemaphoreType.DMA,
        ]

    def inside(self, position):
        return both(position >= 0, position < self.n)

    def copy(self, way, hop, block, near):
        if hop > self.first:
            src = self.out.at[block]
        else:
            src = self.src if hop == 0 else self.src.at[way]
        return pltpu.make_async_remote_copy(
            src_ref=src,
            dst_ref=self.out.at[block] if self.land is None else self.land.at[way],
            send_sem=self.send.at[way, hop],
            recv_sem=self.recv.at[way, hop],
            device_id=on_line(near),
            device_id_type=MESH,
        )

    def each(self, hop):
        for way, sign in ((0, 1), (1, -1)):
            yield way, sign, self.me - sign * hop, self.me + sign

    def begin(self):
        self.launch(self.first)

    def launch(self, hop):
        for way, sign, block, near in self.each(hop):

            @pl.when(both(self.inside(block), self.inside(near)))
            def _():
                self.copy(way, hop, block, near).start()

    def keep(self):
        return pltpu.make_async_copy(self.src, self.out.at[self.me], self.local)

    def arrive(self, hop):
        for way, sign, block, near in self.each(hop + 1):

            @pl.when(self.inside(block))
            def _():
                self.copy(way, hop, block, near).wait_recv()

        if hop + 1 < self.stop:
            self.launch(hop + 1)

    def finish(self):
        for hop in range(self.first, self.stop):
            for way, sign, block, near in self.each(hop):

                @pl.when(both(self.inside(block), self.inside(near)))
                def _():
                    self.copy(way, hop, block, near).wait_send()


class LineSum:
    def __init__(self, n, part, out, got, mine, passed, send, recv, load, first=0, stop=None, tail=None, prev=None):
        self.n, self.part, self.out = n, part, out
        self.got, self.mine, self.passed = got, mine, passed
        self.send, self.recv, self.load = send, recv, load
        self.first, self.stop = first, n - 1 if stop is None else stop
        self.tail, self.prev = tail, prev
        self.me = lax.axis_index("seq")

    @staticmethod
    def scratch(n, rows, width, first=0, stop=None):
        stop = n - 1 if stop is None else stop
        return [
            pltpu.VMEM((2, stop - first + (first > 0), rows, width), HALF),
            pltpu.VMEM((2, rows, width), HALF),
            pltpu.VMEM((2, max(stop - max(first, 1), 1), rows, width), HALF),
            pltpu.SemaphoreType.DMA((2, n - 1)),
            pltpu.SemaphoreType.DMA((2, n - 1)),
            pltpu.SemaphoreType.DMA((2, 2)),
        ]

    def inside(self, position):
        return both(position >= 0, position < self.n)

    def each(self, step):
        reach = self.n - 1 - step
        for way, sign in ((0, 1), (1, -1)):
            yield way, self.me + sign * reach, self.me + sign, self.me - sign

    def slot(self, way, step):
        return self.passed.at[way, max(step - max(self.first, 1), 0)]

    def copy(self, way, step, src, near):
        if self.tail is not None and step == self.stop - 1:
            dst = self.tail.at[way]
        else:
            dst = self.got.at[way, step - self.first]
        return pltpu.make_async_remote_copy(
            src_ref=src,
            dst_ref=dst,
            send_sem=self.send.at[way, step],
            recv_sem=self.recv.at[way, step],
            device_id=on_line(near),
            device_id_type=MESH,
        )

    def round(self, step):
        for way, owner, near, behind in self.each(step):
            if step == 0:

                @pl.when(self.inside(owner))
                def _():
                    self.copy(way, step, self.part(owner), near).start()

                continue

            @pl.when(both(self.inside(owner), jnp.logical_not(self.inside(behind))))
            def _():
                self.copy(way, step, self.part(owner), near).start()

            @pl.when(both(self.inside(owner), self.inside(behind)))
            def _():
                fetch = pltpu.make_async_copy(
                    self.part(owner), self.mine.at[way], self.load.at[way, 0]
                )
                fetch.start()
                slot = self.slot(way, step)
                if step == self.first:
                    index = self.stop - self.first
                    held = pltpu.make_async_copy(
                        self.prev.at[way], self.got.at[way, index], self.load.at[way, 1]
                    )
                    held.start()
                    held.wait()
                else:
                    index = step - 1 - self.first
                    self.copy(way, step - 1, slot, near).wait_recv()
                fetch.wait()
                total = self.mine[way].astype(SINGLE) + self.got[way, index].astype(SINGLE)
                self.passed[way, step - max(self.first, 1)] = total.astype(HALF)
                self.copy(way, step, slot, near).start()

    def sent(self):
        for step in range(self.first, self.stop):
            for way, owner, near, behind in self.each(step):

                @pl.when(self.inside(owner))
                def _():
                    self.copy(way, step, self.slot(way, step), near).wait_send()

    def close(self):
        last = self.stop - 1
        for way, owner, near, behind in self.each(last + 1):

            @pl.when(both(self.inside(owner), self.inside(behind)))
            def _():
                self.copy(way, last, self.slot(way, last), near).wait_recv()

        self.sent()

    def finish(self):
        last = self.n - 2
        fetch = pltpu.make_async_copy(self.part(self.me), self.mine.at[0], self.load.at[0, 0])
        fetch.start()
        fetch.wait()
        self.out[...] = self.mine[0].astype(SINGLE)
        for way, owner, near, behind in self.each(last):

            @pl.when(self.inside(behind))
            def _():
                self.copy(way, last, self.slot(way, last), near).wait_recv()
                self.out[...] += self.got[way, last - self.first].astype(SINGLE)

        self.sent()


def at_rows(ref):
    return lambda owner: ref.at[owner]


def at_step(step, when, action):
    @pl.when(step == when)
    def _():
        action()


def to_group(my, dp, offset, src, dst, send, recv):
    peer = lax.rem(my + offset, dp)
    return pltpu.make_async_remote_copy(
        src_ref=src if src.shape == dst.shape[1:] else src.at[peer],
        dst_ref=dst.at[my],
        send_sem=send.at[offset - 1],
        recv_sem=recv.at[offset - 1],
        device_id={"dp": peer},
        device_id_type=MESH,
    )


def to_line(me, n, offset, src, dst, send, recv):
    peer = lax.rem(me + offset, n)
    return pltpu.make_async_remote_copy(
        src_ref=src if src.shape == dst.shape[1:] else src.at[peer],
        dst_ref=dst.at[me],
        send_sem=send.at[offset - 1],
        recv_sem=recv.at[offset - 1],
        device_id=on_line(peer),
        device_id_type=MESH,
    )


def start_kernel(
    n, dp, x_ref, cond_ref, ada_ref, ada_bias, proj_bias, fc2_bias, length_ref, qkv_ref, fc1_ref,
    x_all, side_all, acts, mods, shifts, qkv_all, fc1_all,
    act_ref, part, parts, row, a_send, a_recv, p_send, p_recv, s_send, s_recv, *sems,
):
    me, my = lax.axis_index("seq"), lax.axis_index("dp")
    depth, _, cols = ada_ref.shape
    width = x_ref.shape[1]
    greet(n, "all", "all")
    gather = LineGather(n, x_ref, x_all, *sems[:3])
    qkv = GroupGather(qkv_ref, qkv_all, *sems[3:8])
    fc1 = GroupGather(fc1_ref, fc1_all, *sems[8:13])
    gather.begin()
    cond = cond_ref[...].astype(SINGLE)
    act = (cond / (1.0 + jnp.exp(-cond))).astype(HALF).astype(SINGLE)
    act_ref[...] = jnp.zeros_like(act_ref)
    for k in range(dp):
        act_ref[k, :, :depth] = act[:, k * depth : (k + 1) * depth]
    others = range(1, dp)
    act_go = [to_group(my, dp, k, act_ref, acts, a_send, a_recv) for k in others]
    for copy in act_go:
        copy.start()
    gather.keep().start()
    acts[my] = act_ref[my]
    for copy in act_go:
        copy.wait_recv()
    rows = acts[:, 0, :depth].astype(HALF)
    for t in range(2):
        product = nn_dot(rows, ada_ref[:, t, :])
        for k in range(dp):
            part[k, :, t * cols : (t + 1) * cols] = product[k : k + 1]
    part_go = [to_group(my, dp, k, part, parts, p_send, p_recv) for k in others]
    for copy in part_go:
        copy.start()
    parts[my] = part[my]
    place = 0
    for ref in (ada_bias, proj_bias, fc2_bias):
        for t in range(2):
            size = ref.shape[1]
            row[:, place : place + size] = ref[t : t + 1].astype(SINGLE)
            place += size
    row[:, place:] = jnp.full((1, LANES), length_ref[0, 0].astype(SINGLE))
    for copy in part_go:
        copy.wait_recv()
    qkv.begin()
    fc1.begin()
    row[:, : 2 * cols] += jnp.sum(parts[...], axis=0)
    row_go = [to_line(me, n, k, row, side_all, s_send, s_recv) for k in range(1, n)]
    for copy in row_go:
        copy.start()
    side_all[me] = row[...]
    for hop in range(max(n - 1, qkv.phases)):
        if hop < n - 1:
            gather.arrive(hop)
        if hop < qkv.phases:
            qkv.arrive(hop)
            fc1.arrive(hop)
    for copy in row_go:
        copy.wait()
    mods[...] = jnp.zeros_like(mods)
    piece = math.gcd(cols, width)
    share = proj_bias.shape[1]
    for z in range(n):
        for t in range(2):
            for start in range(0, cols, piece):
                to, at = divmod(z * cols + start, width)
                mods[t, to : to + 1, at : at + piece] = side_all[
                    z, :, t * cols + start : t * cols + start + piece
                ]
        for k in range(4):
            start = 2 * cols + k * share
            shifts[k : k + 1, z * share : (z + 1) * share] = side_all[z, :, start : start + share]
    for copy in act_go + part_go:
        copy.wait_send()
    gather.keep().wait()
    gather.finish()
    qkv.finish()
    fc1.finish()


def start(n, dp, x_loc, cond, ada, ada_bias, proj_bias, fc2_bias, length, qkv, fc1):
    rows, width = x_loc.shape
    depth, _, cols = ada.shape
    span = 2 * cols + 4 * proj_bias.shape[1] + LANES
    anywhere = pl.BlockSpec(memory_space=pl.ANY)
    inner = pl.BlockSpec(memory_space=pltpu.VMEM)
    scalar = pl.BlockSpec(memory_space=pltpu.SMEM)
    return pl.pallas_call(
        functools.partial(start_kernel, n, dp),
        in_specs=[inner] * 6 + [scalar, inner, inner],
        out_specs=[anywhere, inner, inner, inner, inner, anywhere, anywhere],
        out_shape=[
            jax.ShapeDtypeStruct((n, rows, width), HALF),
            jax.ShapeDtypeStruct((n, 1, span), SINGLE),
            jax.ShapeDtypeStruct((dp, 1, up(depth, LANES)), SINGLE),
            jax.ShapeDtypeStruct((2, 8, width), SINGLE),
            jax.ShapeDtypeStruct((4, width), SINGLE),
            jax.ShapeDtypeStruct((dp,) + qkv.shape, HALF),
            jax.ShapeDtypeStruct((dp,) + fc1.shape, HALF),
        ],
        scratch_shapes=[
            pltpu.VMEM((dp, 1, up(depth, LANES)), SINGLE),
            pltpu.VMEM((dp, 1, 2 * cols), SINGLE),
            pltpu.VMEM((dp, 1, 2 * cols), SINGLE),
            pltpu.VMEM((1, span), SINGLE),
            pltpu.SemaphoreType.DMA((dp - 1,)),
            pltpu.SemaphoreType.DMA((dp - 1,)),
            pltpu.SemaphoreType.DMA((dp - 1,)),
            pltpu.SemaphoreType.DMA((dp - 1,)),
            pltpu.SemaphoreType.DMA((n - 1,)),
            pltpu.SemaphoreType.DMA((n - 1,)),
        ]
        + LineGather.scratch(n)
        + GroupGather.scratch(dp)
        + GroupGather.scratch(dp),
        compiler_params=remote(1),
        cost_estimate=cost(10**6, 100 * MEGA),
        name="start",
    )(x_loc, cond, ada, ada_bias, proj_bias, fc2_bias, length, qkv, fc1)


def qkv_kernel(img, x_ref, mod_ref, w_ref, b_ref, a_ref, o_ref):
    wide = o_ref.shape[2]
    for t, sl in ((0, slice(0, img)), (1, slice(img, x_ref.shape[1]))):
        normed, _ = layer_norm(x_ref[0, sl].astype(SINGLE))
        a = (normed * (1.0 + mod_ref[t, 1:2]) + mod_ref[t, 0:1]).astype(HALF)
        a_ref[0, sl] = a
        o_ref[0, sl] = (
            nn_dot(a, w_ref[:, t * wide : (t + 1) * wide]) + b_ref[t : t + 1]
        ).astype(HALF)


def project_qkv(n, img, x_all, mods, weight, bias):
    _, rows, width = x_all.shape
    wide = weight.shape[1] // 2
    return pl.pallas_call(
        functools.partial(qkv_kernel, img),
        grid=(n,),
        in_specs=[
            rows_spec(rows, width),
            whole(mods.shape),
            whole(weight.shape, True),
            whole(bias.shape),
        ],
        out_specs=[rows_spec(rows, width), rows_spec(rows, wide)],
        out_shape=[
            jax.ShapeDtypeStruct((n, rows, width), HALF),
            jax.ShapeDtypeStruct((n, rows, wide), HALF),
        ],
        compiler_params=params(),
        cost_estimate=cost(2 * n * rows * width * wide, 30 * MEGA),
        name="project_qkv",
    )(x_all, mods, weight, bias)


def halves(shape):
    lane = lax.broadcasted_iota(jnp.int32, shape, len(shape) - 1)
    return lane < HD


def attn_kernel(
    n, q_ref, k_ref, v_ref, mask_ref, e_ref, p_ref, o_ref, lse_ref, e_near, mix_ref, p_all,
    o_buf, o_send, o_recv, o_local, *sems,
):
    pair, block = pl.program_id(0), pl.program_id(1)
    pairs = pl.num_programs(0)
    step = pair * n + block
    me = lax.axis_index("seq")
    count, rows, _ = k_ref.shape
    gather = LineGather(n, e_ref, None, *sems[:3], first=0, stop=1, land=e_near)
    proj = GroupGather(p_ref, p_all, *sems[3:])

    def begin():
        greet(n, "all", "paths")
        gather.begin()
        proj.begin()

    at_step(step, 0, begin)
    queries = q_ref[0] * HALF(1.0 / math.sqrt(HD))
    keys = k_ref[...].reshape(n * rows, LANES)
    values = v_ref[...].reshape(n * rows, LANES)
    first = halves(queries.shape)
    zero = HALF(0)
    pair_rows = jnp.concatenate([jnp.where(first, queries, zero), jnp.where(first, zero, queries)])
    scores = nt_dot(pair_rows, keys) + mask_ref[...]
    maxima = jnp.max(scores, axis=-1, keepdims=True)
    raised = jnp.exp(scores - maxima)
    totals = jnp.sum(raised, axis=-1, keepdims=True)
    weights = (raised * (1.0 / totals)).astype(HALF)
    outs = nn_dot(weights, values)
    logs = maxima + jnp.log(totals)
    mixed = jnp.where(first, outs[:rows], outs[rows:]).astype(HALF)
    o_ref[0] = mixed
    o_buf[pair, block] = mixed
    lse_ref[0] = jnp.where(first, logs[:rows], logs[rows:])
    static_pairs = o_buf.shape[0]

    def columns(sender, which):
        start = (sender * static_pairs + which) * LANES
        return mix_ref.at[:, pl.ds(pl.multiple_of(start, LANES), LANES)]

    def away(which, offset):
        peer = lax.rem(me + offset, n)
        return pltpu.make_async_remote_copy(
            src_ref=o_buf.at[which, peer],
            dst_ref=columns(me, which),
            send_sem=o_send.at[which, offset - 1],
            recv_sem=o_recv.at[which, offset - 1],
            device_id=on_line(peer),
            device_id_type=MESH,
        )

    for offset in range(1, n):

        @pl.when(block == lax.rem(me + offset, n))
        def _():
            away(pair, offset).start()

    @pl.when(block == me)
    def _():
        pltpu.make_async_copy(o_buf.at[pair, me], columns(me, pair), o_local.at[pair]).start()

    last = static_pairs * n - 1
    for phase in range(proj.phases):
        at_step(step, min(last, 5 * phase + 5), functools.partial(proj.arrive, phase))

    def finish():
        gather.arrive(0)
        proj.finish()
        for which in range(static_pairs):
            pltpu.make_async_copy(o_buf.at[which, me], columns(me, which), o_local.at[which]).wait()
            for offset in range(1, n):
                away(which, offset).wait()
        gather.finish()

    at_step(step, last, finish)


def attend(n, dp, qkv, mask, e_loc, proj):
    _, rows, wide = qkv.shape
    width = e_loc.shape[1]
    pairs = wide // 3 // LANES
    total = n * rows
    block = pl.BlockSpec((1, rows, LANES), lambda h, s: (s, 0, h))
    anywhere = pl.BlockSpec(memory_space=pl.ANY)
    return pl.pallas_call(
        functools.partial(attn_kernel, n),
        grid=(pairs, n),
        in_specs=[
            block,
            pl.BlockSpec((n, rows, LANES), lambda h, s: (0, 0, pairs + h)),
            pl.BlockSpec((n, rows, LANES), lambda h, s: (0, 0, 2 * pairs + h)),
            whole(mask.shape),
            anywhere,
            whole(proj.shape, True),
        ],
        out_specs=[block, block, anywhere, anywhere, anywhere],
        out_shape=[
            jax.ShapeDtypeStruct((n, rows, pairs * LANES), HALF),
            jax.ShapeDtypeStruct((n, rows, pairs * LANES), SINGLE),
            jax.ShapeDtypeStruct((2, rows, width), HALF),
            jax.ShapeDtypeStruct((rows, n * pairs * LANES), HALF),
            jax.ShapeDtypeStruct((dp,) + proj.shape, HALF),
        ],
        scratch_shapes=[
            pltpu.VMEM((pairs, n, rows, LANES), HALF),
            pltpu.SemaphoreType.DMA((pairs, n - 1)),
            pltpu.SemaphoreType.DMA((pairs, n - 1)),
            pltpu.SemaphoreType.DMA((pairs,)),
        ]
        + LineGather.scratch(n)
        + GroupGather.scratch(dp),
        compiler_params=remote(2),
        cost_estimate=cost(2 * 2 * 4 * pairs * total * total * LANES, 20 * MEGA, 2 * pairs * total * total),
        name="attend",
    )(qkv, qkv, qkv, mask, e_loc, proj)


def attn_back_kernel(
    lines, img, pairs, q_ref, k_ref, v_ref, o_ref, g_ref, lse_ref, mask_ref, y_ref, l_ref, r_ref,
    dq_ref, dk_ref, dv_ref, qb_ref, vb_ref, p_ref, tail,
    acc_ref, lse_row, delta_row, turned, *scratch,
):
    linear = pl.program_id(0)
    ahead = 2 * lines
    attn_steps = pairs * lines
    last = ahead + attn_steps - 1
    step = lax.rem(lax.max(linear - ahead, 0), lines)
    n, rows, _ = q_ref.shape
    total = n * rows
    line = LineSum(lines, at_rows(y_ref), None, *scratch, stop=lines - 2, tail=tail)

    def begin():
        greet(lines, "near")
        line.round(0)

    at_step(linear, 0, begin)
    for t, sl in ((0, slice(0, img)), (1, slice(img, rows))):

        @pl.when(linear == 0)
        def _():
            turned[:, sl] = l_ref[sl].T

        @pl.when(both(linear < ahead, lax.rem(linear, 2) == t))
        def _():
            p_ref[...] = nn_dot(turned[:, sl], r_ref[sl]).astype(HALF).reshape(p_ref.shape)

    @pl.when(linear >= ahead)
    def _():
        grads = g_ref[...].reshape(total, LANES)
        queries = q_ref[...].reshape(total, LANES) * HALF(1.0 / math.sqrt(HD))

        @pl.when(step == 0)
        def _():
            acc_ref[...] = jnp.zeros_like(acc_ref)
            product = grads.astype(SINGLE) * o_ref[...].reshape(total, LANES).astype(SINGLE)
            flipped = product.T
            logs = lse_ref[...].reshape(total, LANES).T
            for head in range(2):
                delta_row[head : head + 1] = jnp.sum(
                    flipped[head * HD : (head + 1) * HD], axis=0, keepdims=True
                )
                lse_row[head : head + 1] = logs[head * HD : head * HD + 1]
            vb_ref[0] = jnp.zeros_like(vb_ref[0])

        keys, values = k_ref[0], v_ref[0]
        first = halves(keys.shape)
        mask = mask_ref[0][:, 0:1]
        zero = HALF(0)

        def pair(value):
            return jnp.concatenate([jnp.where(first, value, zero), jnp.where(first, zero, value)])

        def by_head(row):
            return row[...].reshape(2, 1, total)

        key_pair = pair(keys)
        scores = nt_dot(key_pair, queries).reshape(2, rows, total)
        probs = jnp.exp((scores - by_head(lse_row)) + mask)
        grad_prob = nt_dot(pair(values), grads).reshape(2, rows, total)
        grad_score = (probs * (grad_prob - by_head(delta_row))).astype(HALF)
        grad_score = grad_score.reshape(2 * rows, total)
        dvs = nn_dot(probs.astype(HALF).reshape(2 * rows, total), grads)
        dks = nn_dot(grad_score, queries)
        acc_ref[...] += tn_dot(grad_score, key_pair)
        dk_ref[0] = jnp.where(first, dks[:rows], dks[rows:]).astype(HALF)
        dv = jnp.where(first, dvs[:rows], dvs[rows:])
        dv_ref[0] = dv.astype(HALF)
        vb_ref[0, 0:1] += jnp.sum(dv[:img], axis=0, keepdims=True)
        vb_ref[0, 1:2] += jnp.sum(dv[img:], axis=0, keepdims=True)

        @pl.when(step == lines - 1)
        def _():
            dq = (acc_ref[...] * (1.0 / math.sqrt(HD))).reshape(n, rows, LANES)
            dq_ref[...] = dq.astype(HALF)
            qb_ref[0, 0:1] = jnp.sum(jnp.sum(dq[:, :img], axis=0), axis=0, keepdims=True)
            qb_ref[0, 1:2] = jnp.sum(jnp.sum(dq[:, img:], axis=0), axis=0, keepdims=True)

    for hop in range(1, lines - 2):
        at_step(linear, min(last, ahead + 5 * hop), functools.partial(line.round, hop))

    at_step(linear, last, line.close)


def attend_back(n, dp, img, qkv, mixture, grad_mix, lse, mask_col, out_parts, grad_attn, mix_loc):
    _, rows, wide = qkv.shape
    pairs = wide // 3 // LANES
    total = n * rows
    lw = pairs * LANES
    ahead = 2 * n
    steps = pairs * n
    width = out_parts.shape[2]
    depth = width // dp

    def place(k):
        return lax.rem(lax.max(k - ahead, 0), n)

    def head(k):
        return lax.div(lax.max(k - ahead, 0), n)

    full = pl.BlockSpec((n, rows, LANES), lambda k: (0, 0, head(k)))

    def block(base):
        return pl.BlockSpec((1, rows, LANES), lambda k: (place(k), 0, base + head(k)))

    bias = pl.BlockSpec((1, 2, LANES), lambda k: (head(k), 0, 0))
    anywhere = pl.BlockSpec(memory_space=pl.ANY)
    return pl.pallas_call(
        functools.partial(attn_back_kernel, n, img, pairs),
        grid=(ahead + steps,),
        in_specs=[
            full,
            block(pairs),
            block(2 * pairs),
            full,
            full,
            full,
            pl.BlockSpec((1, rows, LANES), lambda k: (place(k), 0, 0)),
            anywhere,
            whole(grad_attn.shape, True),
            pl.BlockSpec((rows, lw), lambda k: (0, lax.min(lax.div(k, 2), n - 1))),
        ],
        out_specs=[
            full,
            block(0),
            block(0),
            bias,
            bias,
            pl.BlockSpec((dp, 1, depth, lw), lambda k: (0, lax.min(k, ahead - 1), 0, 0)),
            anywhere,
        ],
        out_shape=[jax.ShapeDtypeStruct((n, rows, lw), HALF)] * 3
        + [jax.ShapeDtypeStruct((pairs, 2, LANES), SINGLE)] * 2
        + [
            jax.ShapeDtypeStruct((dp, 2 * n, depth, lw), HALF),
            jax.ShapeDtypeStruct((2, rows, width), HALF),
        ],
        scratch_shapes=[
            pltpu.VMEM((total, LANES), SINGLE),
            pltpu.VMEM((2, total), SINGLE),
            pltpu.VMEM((2, total), SINGLE),
            pltpu.VMEM((width, rows), HALF),
        ]
        + LineSum.scratch(n, rows, width, stop=n - 2),
        compiler_params=remote(3, 62),
        cost_estimate=cost(2 * 5 * 4 * pairs * total * total * LANES, 30 * MEGA, 2 * pairs * total * total),
        name="attend_back",
    )(qkv, qkv, qkv, mixture, grad_mix, lse, mask_col, out_parts, grad_attn, mix_loc)


def proj_columns(w_ref, z, t):
    dp, _, _, depth, heads = w_ref.shape
    return w_ref[:, z, t].reshape(dp * depth, heads)


def middle_kernel(
    n, img, mix_ref, x_ref, w_ref, b_ref, mod_ref, fc2_ref, y_ref, m_ref, all_ref, fc2_all, own, *sems
):
    greet(n, "near", "paths")
    fc2 = GroupGather(fc2_ref, fc2_all, *sems[3:])
    fc2.begin()
    lw = mix_ref.shape[1] // n
    heads = w_ref.shape[4]
    for t, sl in ((0, slice(0, img)), (1, slice(img, x_ref.shape[0]))):
        attn = b_ref[t : t + 1]
        for z in range(n):
            attn = attn + nt_dot(mix_ref[sl, z * lw : z * lw + heads], proj_columns(w_ref, z, t))
        y_ref[sl] = attn
        middle = x_ref[sl].astype(SINGLE) + mod_ref[t, 2:3] * attn
        m_ref[sl] = middle
        normed, _ = layer_norm(middle)
        own[sl] = (normed * (1.0 + mod_ref[t, 4:5]) + mod_ref[t, 3:4]).astype(HALF)
    gather = LineGather(n, own, all_ref, *sems[:3])
    gather.begin()
    gather.keep().start()
    for hop in range(max(n - 1, fc2.phases)):
        if hop < fc2.phases:
            fc2.arrive(hop)
        if hop < n - 1:
            gather.arrive(hop)
    gather.keep().wait()
    gather.finish()
    fc2.finish()


def middle_rows(n, dp, img, mixture, x_loc, weight, bias, mods, fc2):
    rows, width = x_loc.shape
    inner = pl.BlockSpec(memory_space=pltpu.VMEM)
    anywhere = pl.BlockSpec(memory_space=pl.ANY)
    return pl.pallas_call(
        functools.partial(middle_kernel, n, img),
        in_specs=[inner] * 6,
        out_specs=[inner, inner, anywhere, anywhere],
        out_shape=[
            jax.ShapeDtypeStruct((rows, width), SINGLE),
            jax.ShapeDtypeStruct((rows, width), SINGLE),
            jax.ShapeDtypeStruct((n, rows, width), HALF),
            jax.ShapeDtypeStruct((dp,) + fc2.shape, HALF),
        ],
        scratch_shapes=[pltpu.VMEM((rows, width), HALF)]
        + LineGather.scratch(n)
        + GroupGather.scratch(dp),
        compiler_params=remote(4),
        cost_estimate=cost(2 * rows * width * width, 100 * MEGA),
        name="middle_rows",
    )(mixture, x_loc, weight, bias, mods, fc2)


def by_distance(me, n, count):
    low = lax.min(me, n - 1 - me)
    near = lax.select(lax.rem(count, 2) == 1, lax.div(count + 1, 2), -lax.div(count, 2))
    far = lax.select(me < n - 1 - me, count - low, low - count)
    return me + lax.select(count <= 2 * low, near, far)


def mlp_kernel(n, img, tile, b_ref, e_loc, e_near, mod_ref, w1_far, b1_ref, w2_far,
    g_ref, dz_ref, dy_ref, db_ref, y_ref, sum_ref, gate_ref, acc_ref, out_ref, e_all, near_sem,
    w1_ref, w2_ref, w_sem, *sems):
    step = pl.program_id(0)
    me = lax.axis_index("seq")
    owner = by_distance(me, n, step)
    e_ref = e_all.at[pl.ds(owner, 1)]
    gather = LineGather(n, e_near, e_all, *sems, first=1)
    own = pltpu.make_async_copy(e_loc, e_all.at[me], near_sem.at[2])
    wide = g_ref.shape[2]

    def weights(t):
        cols = pl.ds(t * wide, wide)
        return (
            pltpu.make_async_copy(w1_far.at[:, cols], w1_ref.at[:, cols], w_sem.at[t, 0]),
            pltpu.make_async_copy(w2_far.at[:, t], w2_ref.at[:, t], w_sem.at[t, 1]),
        )

    def weights_in(t):
        for copy in weights(t):
            copy.wait()

    def nears(action):
        for way, sign in ((0, 1), (1, -1)):
            block = me - sign

            @pl.when(both(block >= 0, block < n))
            def _():
                action(
                    pltpu.make_async_copy(e_near.at[way], e_all.at[block], near_sem.at[way])
                )

    def begin():
        greet(n, "near")
        gather.begin()
        own.start()
        nears(lambda copy: copy.start())
        for t in range(2):
            for copy in weights(t):
                copy.start()
        own.wait()
        nears(lambda copy: copy.wait())

    at_step(step, 0, begin)
    for hop in range(1, n - 1):
        at_step(step, hop + 1, functools.partial(gather.arrive, hop))
    at_step(step, n - 1, gather.finish)
    units = g_ref.shape[2]

    @pl.when(step == 0)
    def _():
        sum_ref[...] = jnp.zeros_like(sum_ref)
        gate_ref[...] = jnp.zeros_like(gate_ref)

    for t, sl in ((0, slice(0, img)), (1, slice(img, b_ref.shape[1]))):
        at_step(step, 0, functools.partial(weights_in, t))
        rows = b_ref[0, sl]
        grad = (mod_ref[t, 5:6] * e_ref[0, sl].astype(SINGLE)).astype(HALF)
        dy_ref[0, sl] = grad

        for k in range(units // tile):
            here = slice(k * tile, (k + 1) * tile)
            cols = slice(t * units + k * tile, t * units + (k + 1) * tile)
            w1 = w1_ref[:, cols]
            pre = nn_dot(rows, w1) + b1_ref[t : t + 1, here]
            hidden, slope = gelu_both(pre)
            hidden = hidden.astype(HALF)
            g_ref[0, sl, here] = hidden
            w2 = w2_ref[:, t, :, here].reshape(-1, tile)
            out = nt_dot(hidden, w2)
            dz = nn_dot(grad, w2) * slope
            sum_ref[t : t + 1, here] += jnp.sum(dz, axis=0, keepdims=True)
            dzh = dz.astype(HALF)
            dz_ref[0, sl, here] = dzh
            part = nt_dot(dzh, w1)
            if k == 0:
                acc_ref[sl] = part
                out_ref[sl] = out
            else:
                acc_ref[sl] += part
                out_ref[sl] += out
        db_ref[0, sl] = acc_ref[sl].astype(HALF)
        out = out_ref[sl]
        y_ref[0, sl] = out.astype(HALF)
        gate_ref[t : t + 1] += jnp.sum(out * e_ref[0, sl].astype(SINGLE), axis=0, keepdims=True)


def feed_forward(n, img, mlp_in, e_loc, e_near, mods, w1, b1, w2):
    rows, width = mlp_in.shape[1:]
    units = w1.shape[1] // 2
    tile = min(768, units)
    while units % tile:
        tile -= LANES

    def owned(columns):
        return pl.BlockSpec(
            (1, rows, columns), lambda k: (by_distance(lax.axis_index("seq"), n, k), 0, 0)
        )

    return pl.pallas_call(
        functools.partial(mlp_kernel, n, img, tile),
        grid=(n,),
        in_specs=[
            owned(width),
            pl.BlockSpec(memory_space=pl.ANY),
            pl.BlockSpec(memory_space=pl.ANY),
            whole(mods.shape),
            pl.BlockSpec(memory_space=pl.ANY),
            whole(b1.shape),
            pl.BlockSpec(memory_space=pl.ANY),
        ],
        out_specs=[
            owned(units),
            owned(units),
            owned(width),
            owned(width),
            owned(width),
            whole((2, units)),
            whole((2, width)),
        ],
        out_shape=[
            jax.ShapeDtypeStruct((n, rows, units), HALF),
            jax.ShapeDtypeStruct((n, rows, units), HALF),
            jax.ShapeDtypeStruct((n, rows, width), HALF),
            jax.ShapeDtypeStruct((n, rows, width), HALF),
            jax.ShapeDtypeStruct((n, rows, width), HALF),
            jax.ShapeDtypeStruct((2, units), SINGLE),
            jax.ShapeDtypeStruct((2, width), SINGLE),
        ],
        scratch_shapes=[
            pltpu.VMEM((rows, width), SINGLE),
            pltpu.VMEM((rows, width), SINGLE),
            pltpu.VMEM((n, rows, width), HALF),
            pltpu.SemaphoreType.DMA((3,)),
            pltpu.VMEM(w1.shape, HALF),
            pltpu.VMEM(w2.shape, HALF),
            pltpu.SemaphoreType.DMA((2, 2)),
        ]
        + LineGather.scratch(n),
        compiler_params=remote(9, 60),
        cost_estimate=cost(6 * n * rows * width * units, 50 * MEGA, n * rows * units),
        name="feed_forward",
    )(mlp_in, e_loc, e_near, mods, w1, b1, w2)


def grads_kernel(n, img, plan, rounds, *refs):
    lefts = max(p[0] for p in plan) + 1
    rights = max(p[1] for p in plan) + 1
    count = lefts + rights
    far, rest = refs[:count], refs[count:]
    held, loaded, rest = rest[-count - 1 : -1], rest[-1], rest[: -count - 1]
    l_refs, r_refs = held[:lefts], held[lefts:]
    copies = [pltpu.make_async_copy(far[k], held[k], loaded.at[k]) for k in range(count)]
    step = pl.program_id(0)
    parts, o_ref, tail, turned = rest[:4]
    line = LineSum(n, at_rows(parts), None, *rest[4:], stop=n - 2, tail=tail)

    def begin():
        greet(n, "near")
        line.round(0)
        for left, right, stream in plan:
            if stream == 0:
                copies[left].start()
                copies[lefts + right].start()

    at_step(step, 0, begin)
    for hop, when in enumerate(rounds):
        at_step(step, when, functools.partial(line.round, hop + 1))
    tile = 512 if o_ref.shape[3] % 512 == 0 else 2 * LANES
    before = None
    for k, (left, right, stream) in enumerate(plan):

        @pl.when(step == k)
        def _():
            l_ref, r_ref = l_refs[left], r_refs[right]
            if stream == 0:
                copies[left].wait()
                copies[lefts + right].wait()
            count, rows, _ = l_ref.shape
            sl = slice(0, img) if stream == 0 else slice(img, rows)
            size = count * (sl.stop - sl.start)
            if before != (left, stream):
                turned[:, :size] = l_ref[:, sl].reshape(size, l_ref.shape[2]).T
            for column in range(0, o_ref.shape[3], tile):
                values = r_ref[:, sl, column : column + tile].reshape(size, tile)
                product = nn_dot(turned[:, :size], values).astype(HALF)
                o_ref[:, 0, :, column : column + tile] = product.reshape(
                    o_ref.shape[0], o_ref.shape[2], tile
                )

        before = (left, stream)
    at_step(step, len(plan) - 1, line.close)


def weight_grads(n, dp, img, lefts, rights, plan, rounds, parts, collective, name):
    rows, depth = lefts[0].shape[1:]
    wide = rights[0].shape[2]
    anywhere = pl.BlockSpec(memory_space=pl.ANY)
    block = (dp, 1, depth // dp, wide)
    longest = max(up(n * img, LANES), up(n * (rows - img), LANES))
    return pl.pallas_call(
        functools.partial(grads_kernel, n, img, plan, rounds),
        grid=(len(plan),),
        in_specs=[anywhere] * (len(lefts) + len(rights) + 1),
        out_specs=[pl.BlockSpec(block, lambda k: (0, k, 0, 0)), anywhere],
        out_shape=[
            jax.ShapeDtypeStruct((dp, len(plan), depth // dp, wide), HALF),
            jax.ShapeDtypeStruct((2,) + parts.shape[1:], HALF),
        ],
        scratch_shapes=[pltpu.VMEM((depth, longest), HALF)]
        + LineSum.scratch(n, *parts.shape[1:], stop=n - 2)
        + [pltpu.VMEM(a.shape, HALF) for a in (*lefts, *rights)]
        + [pltpu.SemaphoreType.DMA((len(lefts) + len(rights),))],
        compiler_params=remote(collective, 60),
        cost_estimate=cost(2 * n * rows * depth * len(plan) * wide // 2, 60 * MEGA),
        name=name,
    )(*lefts, *rights, parts)


def middle_back_kernel(
    n, img, part_ref, prev_ref, m_ref, y_ref, e_ref, w_far, mod_ref, dm_ref, dy_ref, sum_ref, all_ref,
    db_ref, mix, send, recv, local, w_ref, w_sem, *line_scratch,
):
    me = lax.axis_index("seq")
    rows, width = m_ref.shape
    heads = w_ref.shape[4]
    streams = ((0, slice(0, img)), (1, slice(img, rows)))
    greet(n, "all")
    line = LineSum(n, at_rows(part_ref), db_ref, *line_scratch, first=n - 2, prev=prev_ref)
    line.round(n - 2)
    weights = pltpu.make_async_copy(w_far, w_ref, w_sem)
    weights.start()
    if mix.shape[2] > heads:
        mix[...] = jnp.zeros_like(mix)
    line.finish()
    for t, sl in streams:
        grad_in = db_ref[sl]
        normed, inv_std = layer_norm(m_ref[sl])
        upstream = e_ref[sl].astype(SINGLE)
        grad_middle = upstream + norm_back(normed, inv_std, grad_in * (1.0 + mod_ref[t, 4:5]))
        dm_ref[sl] = grad_middle
        grad_attn = mod_ref[t, 2:3] * grad_middle
        dy_ref[sl] = grad_attn.astype(HALF)

        def total(value):
            return jnp.sum(value, axis=0, keepdims=True)

        sum_ref[t, 0:1] = total(grad_middle * y_ref[sl])
        sum_ref[t, 1:2] = total(grad_in)
        sum_ref[t, 2:3] = total(grad_in * normed)
        sum_ref[t, 3:4] = total(grad_attn)
        sum_ref[t, 4:5] = total(upstream)

    def exchange(peer, block):
        return pltpu.make_async_remote_copy(
            src_ref=mix.at[peer],
            dst_ref=all_ref.at[block],
            send_sem=send.at[peer],
            recv_sem=recv.at[block],
            device_id=on_line(peer),
            device_id_type=MESH,
        )

    keep = pltpu.make_async_copy(mix.at[me], all_ref.at[me], local)
    weights.wait()
    for peer in range(n):
        for t, sl in streams:
            mix[peer, sl, :heads] = nn_dot(dy_ref[sl], proj_columns(w_ref, peer, t)).astype(HALF)

        @pl.when(peer != me)
        def _():
            exchange(peer, me).start()

        @pl.when(peer == me)
        def _():
            keep.start()

    for peer in range(n):

        @pl.when(peer != me)
        def _():
            exchange(peer, peer).wait()

    keep.wait()


def middle_back(n, img, parts, prev, middle, attn_out, cot, weight, mods, lwp):
    rows, width = middle.shape
    inner = pl.BlockSpec(memory_space=pltpu.VMEM)
    anywhere = pl.BlockSpec(memory_space=pl.ANY)
    return pl.pallas_call(
        functools.partial(middle_back_kernel, n, img),
        in_specs=[anywhere, anywhere] + [inner] * 3 + [anywhere, inner],
        out_specs=[inner, inner, inner, anywhere],
        out_shape=[
            jax.ShapeDtypeStruct((rows, width), SINGLE),
            jax.ShapeDtypeStruct((rows, width), HALF),
            jax.ShapeDtypeStruct((2, 8, width), SINGLE),
            jax.ShapeDtypeStruct((n, rows, lwp), HALF),
        ],
        scratch_shapes=[
            pltpu.VMEM((rows, width), SINGLE),
            pltpu.VMEM((n, rows, lwp), HALF),
            pltpu.SemaphoreType.DMA((n,)),
            pltpu.SemaphoreType.DMA((n,)),
            pltpu.SemaphoreType.DMA,
            pltpu.VMEM(weight.shape, HALF),
            pltpu.SemaphoreType.DMA,
        ]
        + LineSum.scratch(n, rows, width, first=n - 2),
        compiler_params=remote(5),
        cost_estimate=cost(2 * rows * width * width, 60 * MEGA),
        name="middle_back",
    )(parts, prev, middle, attn_out, cot, weight, mods)


def attn_in_kernel(
    n, img, dq_ref, dk_ref, dv_ref, x_ref, a_ref, w_ref, y_ref, prev_ref,
    da_ref, sum_ref, g_ref, y_sum, turned, *scratch,
):
    step = pl.program_id(0)
    count, rows, lw = dq_ref.shape
    line = LineSum(n, at_rows(y_ref), y_sum, *scratch, first=n - 2, prev=prev_ref)
    streams = ((0, slice(0, img)), (1, slice(img, rows)))

    def begin():
        greet(n, "near")
        line.round(n - 2)
        sum_ref[...] = jnp.zeros_like(sum_ref)

    at_step(step, 0, begin)

    @pl.when(step < n)
    def _():
        here = lax.min(step, n - 1)
        for t, sl in streams:
            part = None
            for c, ref in enumerate((dq_ref, dk_ref, dv_ref)):
                start = (3 * t + c) * lw
                term = nt_dot(ref[here, sl], w_ref[:, start : start + lw])
                part = term if part is None else part + term
            da_ref[0, sl] = part.astype(HALF)
            normed, _ = layer_norm(x_ref[0, sl].astype(SINGLE))
            sum_ref[t, 0:1] += jnp.sum(part, axis=0, keepdims=True)
            sum_ref[t, 1:2] += jnp.sum(part * normed, axis=0, keepdims=True)

    for t, sl in streams:
        size = count * (sl.stop - sl.start)
        for c, ref in enumerate((dq_ref, dk_ref, dv_ref)):

            @pl.when(step == n + 3 * t + c)
            def _():
                if c == 0:
                    turned[:, :size] = a_ref[:, sl].reshape(size, a_ref.shape[2]).T
                g_ref[...] = nn_dot(turned[:, :size], ref[:, sl].reshape(size, lw)).astype(HALF)

    at_step(step, n + 5, line.finish)


def attn_in_back(n, img, dq, dk, dv, x_all, attn_in, weight, out_parts, running):
    _, rows, lw = dq.shape
    width = x_all.shape[2]
    anywhere = pl.BlockSpec(memory_space=pl.ANY)
    row = pl.BlockSpec((1, rows, width), lambda k: (lax.min(k, n - 1), 0, 0))
    longest = max(up(n * img, LANES), up(n * (rows - img), LANES))
    return pl.pallas_call(
        functools.partial(attn_in_kernel, n, img),
        grid=(n + 6,),
        in_specs=[whole(dq.shape, True)] * 3
        + [row, whole(attn_in.shape, True), whole(weight.shape, True)]
        + [anywhere] * 2,
        out_specs=[
            row,
            whole((2, 2, width)),
            pl.BlockSpec((width, lw), lambda k: (0, lax.max(k - n, 0))),
            whole((rows, width), True),
        ],
        out_shape=[
            jax.ShapeDtypeStruct((n, rows, width), HALF),
            jax.ShapeDtypeStruct((2, 2, width), SINGLE),
            jax.ShapeDtypeStruct((width, 6 * lw), HALF),
            jax.ShapeDtypeStruct((rows, width), SINGLE),
        ],
        scratch_shapes=[pltpu.VMEM((width, longest), HALF)]
        + LineSum.scratch(n, rows, width, first=n - 2),
        compiler_params=remote(10, 62),
        cost_estimate=cost(12 * n * rows * width * lw, 30 * MEGA),
        name="attn_in_back",
    )(dq, dk, dv, x_all, attn_in, weight, out_parts, running)


def end_kernel(
    n, dp, cut, parts, qkv_part, p_ref, packed, extra, ada_ref, acts,
    sum_ref, qkv_sum, p_own, every, cond_ref, ada_grad,
    z_got, row, c_part, c_got, c_all, z_send, z_recv, e_send, e_recv, c_send, c_recv, a_send, a_recv,
    *scratch,
):
    me, my = lax.axis_index("seq"), lax.axis_index("dp")
    depth = ada_ref.shape[0]
    span = packed.shape[2]
    greet(n, "all", "all")
    line = LineSum(n, at_rows(parts), sum_ref, *scratch[:6])
    group = GroupSum(qkv_part, *scratch[6:15])
    proj = GroupSum(p_ref, *scratch[15:])
    mates, others = range(1, n), range(1, dp)
    z_go = [to_line(me, n, k, packed, z_got, z_send, z_recv) for k in mates]
    for copy in z_go:
        copy.start()
    line.round(0)
    proj.begin()
    group.begin()
    z_got[me] = packed[me]
    for copy in z_go:
        copy.wait_recv()
    row[:, :span] = jnp.sum(z_got[...], axis=0)
    row[:, span:] = extra[...]
    e_go = [to_group(my, dp, k, row, every, e_send, e_recv) for k in others]
    for copy in e_go:
        copy.start()
    every[my] = row[...]
    proj.step(0)
    group.step(0)
    for copy in e_go:
        copy.wait_recv()
    cols = cut // 2
    halves_of = [every[:, 0, t * cols : (t + 1) * cols].astype(HALF) for t in range(2)]
    product = nt_dot(halves_of[0], ada_ref[:, 0, :]) + nt_dot(halves_of[1], ada_ref[:, 1, :])
    c_part[...] = jnp.zeros_like(c_part)
    for k in range(dp):
        c_part[k, :, :depth] = product[k : k + 1]
    c_go = [to_group(my, dp, k, c_part, c_got, c_send, c_recv) for k in others]
    for copy in c_go:
        copy.start()
    c_got[my] = c_part[my]
    act_rows = acts[:, 0, :depth].astype(HALF)
    for t in range(2):
        ada_grad[:, t, :] = tn_dot(act_rows, halves_of[t])
    for hop in range(1, n - 1):
        line.round(hop)
    for number in range(1, group.phases):
        proj.step(number)
        group.step(number)
    for copy in c_go:
        copy.wait_recv()
    a_go = [to_line(me, n, k, c_got, c_all, a_send, a_recv) for k in mates]
    for copy in a_go:
        copy.start()
    c_all[me] = c_got[...]
    for copy in a_go:
        copy.wait_recv()
    cond_ref[...] = jnp.sum(c_all[...], axis=0)
    rows, _, _, wide = qkv_sum.shape

    def store_proj(half, value):
        p_own[half] = value.astype(HALF)

    def store_qkv(half, value):
        own = slice(half * rows // 2, (half + 1) * rows // 2)
        for k in range(6):
            qkv_sum[own, k % 3, k // 3, :] = value[:, k * wide : (k + 1) * wide]

    proj.finish(store_proj)
    group.finish(store_qkv)
    line.finish()
    for copy in z_go + e_go + c_go + a_go:
        copy.wait_send()


def end(n, dp, cut, parts, qkv_part, proj_part, packed, extra, ada, acts):
    rows, width = parts.shape[1:]
    depth = up(ada.shape[0], LANES)
    span = packed.shape[2] + extra.shape[1]
    inner = pl.BlockSpec(memory_space=pltpu.VMEM)
    anywhere = pl.BlockSpec(memory_space=pl.ANY)
    sems = [n - 1, n - 1, dp - 1, dp - 1, dp - 1, dp - 1, n - 1, n - 1]
    return pl.pallas_call(
        functools.partial(end_kernel, n, dp, cut),
        in_specs=[anywhere, anywhere, anywhere, inner, inner, inner, inner],
        out_specs=[inner] * 6,
        out_shape=[
            jax.ShapeDtypeStruct((rows, width), SINGLE),
            jax.ShapeDtypeStruct((ada.shape[0], 3, 2, qkv_part.shape[3] // 6), SINGLE),
            jax.ShapeDtypeStruct(proj_part.shape[1:], HALF),
            jax.ShapeDtypeStruct((dp, 1, span), SINGLE),
            jax.ShapeDtypeStruct((dp, 1, depth), SINGLE),
            jax.ShapeDtypeStruct(ada.shape, SINGLE),
        ],
        scratch_shapes=[
            pltpu.VMEM(packed.shape, SINGLE),
            pltpu.VMEM((1, span), SINGLE),
            pltpu.VMEM((dp, 1, depth), SINGLE),
            pltpu.VMEM((dp, 1, depth), SINGLE),
            pltpu.VMEM((n, dp, 1, depth), SINGLE),
        ]
        + [pltpu.SemaphoreType.DMA((k,)) for k in sems]
        + LineSum.scratch(n, rows, width)
        + GroupSum.scratch(dp, *qkv_part.shape[2:])
        + GroupSum.scratch(dp, *proj_part.shape[2:]),
        compiler_params=remote(7, 62),
        cost_estimate=cost(10**6, 100 * MEGA),
        name="end",
    )(parts, qkv_part, proj_part, packed, extra, ada, acts)


def rows_kernel(img, slots, da_ref, dm_ref, x_ref, m_ref, y_ref, mod_ref, shift_ref, live_ref, io_ref, to_ref, ig_ref, tg_ref):
    for t, sl, out_ref, grad_ref in (
        (0, slice(0, img), io_ref, ig_ref),
        (1, slice(img, x_ref.shape[0]), to_ref, tg_ref),
    ):
        keep = out_ref.shape[1]
        live = live_ref[sl]
        value = m_ref[sl] + mod_ref[t, 5:6] * (y_ref[sl] + shift_ref[t : t + 1])
        out_ref[0] = (value * live).astype(HALF)[:keep]
        normed, inv_std = layer_norm(x_ref[sl].astype(SINGLE))
        grad = dm_ref[sl] + norm_back(normed, inv_std, da_ref[sl] * (1.0 + mod_ref[t, 1:2]))
        grad_ref[0] = (grad * live)[:keep]


def rows_out(img, slots, grad_attn_in, grad_middle, x_loc, middle, mlp_sum, mods, fc2_shift, live):
    width = x_loc.shape[1]
    return pl.pallas_call(
        functools.partial(rows_kernel, img, slots),
        out_shape=[
            jax.ShapeDtypeStruct((1, img, width), HALF),
            jax.ShapeDtypeStruct((1, slots, width), HALF),
            jax.ShapeDtypeStruct((1, img, width), SINGLE),
            jax.ShapeDtypeStruct((1, slots, width), SINGLE),
        ],
        compiler_params=params(),
        cost_estimate=cost(10**6, 14 * MEGA),
        name="rows_out",
    )(grad_attn_in, grad_middle, x_loc, middle, mlp_sum, mods, fc2_shift, live)


def body(
    image_tokens,
    text_tokens,
    text_lengths,
    conditioning,
    ada_weight,
    ada_bias,
    qkv_weight,
    qv_bias,
    proj_weight,
    proj_bias,
    fc1_weight,
    fc1_bias,
    fc2_weight,
    fc2_bias,
    image_cotangent,
    text_cotangent,
):
    n = lax.axis_size("seq")
    dp = lax.axis_size("dp")
    img, width = image_tokens.shape[1:]
    slots = text_tokens.shape[1]
    pad = up(slots, 16)
    rows = img + pad
    depth = qkv_weight.shape[0]
    lw = qkv_weight.shape[3]
    lwp = up(lw, LANES)
    units = fc1_weight.shape[2]
    mod_cols = ada_weight.shape[2]
    my_seq = lax.axis_index("dp")

    def stacked(image, text):
        return jnp.concatenate([image, jnp.pad(text, ((0, pad - slots), (0, 0)))], axis=0)

    length = text_lengths[0, 0]
    live_text = (jnp.arange(slots, dtype=jnp.int32) < length)[:, None]
    x_loc = stacked(image_tokens[0], text_tokens[0])
    e_loc = stacked(
        image_cotangent[0], jnp.where(live_text, text_cotangent[0], jnp.zeros((), HALF))
    )

    def split(shard):
        return shard.reshape(2, -1, shard.shape[-1])

    qkv_local = jnp.pad(qkv_weight, ((0, 0), (0, 0), (0, 0), (0, lwp - lw))).reshape(depth, 6 * lwp)
    share = proj_weight.shape[0]
    fc1_local = fc1_weight.reshape(depth, 2 * units)

    cond_float = conditioning.astype(SINGLE)
    bias_cols = proj_bias.shape[1]
    cut = 2 * mod_cols
    proj_line = lax.all_gather(proj_weight.transpose(1, 2, 0), "seq", axis=0, tiled=False)
    x_all, side_all, acts, mods, shifts, qkv_full, fc1_full = start(
        n,
        dp,
        x_loc,
        conditioning,
        ada_weight,
        ada_bias,
        proj_bias,
        fc2_bias,
        text_lengths,
        split(qkv_local),
        split(fc1_local),
    )
    qkv_full = qkv_full.reshape(width, 6 * lwp)
    fc1_full = fc1_full.reshape(width, 2 * units)
    proj_shift, fc2_shift = shifts[:2], shifts[2:]
    lengths_all = side_all[:, 0, cut + 4 * bias_cols]

    slot = jnp.arange(rows, dtype=SINGLE)[None, :] - img
    live = jnp.logical_or(slot < 0, jnp.logical_and(slot < lengths_all[:, None], slot < slots))
    mask = jnp.where(live, SINGLE(0), SINGLE(MASKED))
    mask_row = mask.reshape(1, n * rows)
    mask_col = jnp.broadcast_to(mask[:, :, None], (n, rows, LANES))
    live_loc = jnp.concatenate(
        [jnp.ones((img, 1), SINGLE), jnp.pad(live_text.astype(SINGLE), ((0, pad - slots), (0, 0)))]
    )

    bias_rows = jnp.stack(
        [qv_bias[:, 0], jnp.zeros_like(qv_bias[:, 0]), qv_bias[:, 1]], axis=1
    ).astype(SINGLE)
    bias_rows = jnp.pad(bias_rows, ((0, 0), (0, 0), (0, lwp - lw))).reshape(2, 3 * lwp)
    attn_in, qkv_rows = project_qkv(n, img, x_all, mods, qkv_full, bias_rows)
    mixture, lse, e_near, mix_loc, proj_full = attend(
        n, dp, qkv_rows, mask_row, e_loc, proj_line.reshape(2, -1, share)
    )
    proj_full = proj_full.reshape(dp, n, 2, depth, share)

    attn_out, middle, mlp_in, fc2_full = middle_rows(
        n, dp, img, mix_loc, x_loc, proj_full, proj_shift, mods, fc2_weight.transpose(1, 2, 0)
    )
    hidden, grad_pre, grad_mlp, mlp_in_part, mlp_out_part, fc1_bias_part, gate_two_part = (
        feed_forward(
            n, img, mlp_in, e_loc, e_near, mods, fc1_full, fc1_bias.astype(SINGLE), fc2_full
        )
    )
    fc_plan = [(w, w, t) for w in range(2) for t in range(2)]
    fc_rounds = [(k + 1) * 4 // (n - 2) for k in range(n - 3)]
    fc_part, running = weight_grads(
        n, dp, img, (mlp_in, grad_mlp), (grad_pre, hidden), fc_plan, fc_rounds, mlp_in_part, 6, "fc_grads"
    )
    fc_sum = lax.psum_scatter(
        fc_part.reshape(dp * 4 * depth, units), "dp", scatter_dimension=0, tiled=True
    ).reshape(4, depth, units)

    grad_middle, grad_attn, sums, grad_mix = middle_back(
        n, img, mlp_in_part, running, middle, attn_out, e_loc, proj_full, mods, lwp
    )
    grad_q, grad_k, grad_v, q_bias_part, v_bias_part, proj_part, out_running = attend_back(
        n, dp, img, qkv_rows, mixture, grad_mix, lse, mask_col, mlp_out_part, grad_attn, mix_loc
    )
    attn_in_part, mod_one, qkv_part, mlp_sum = attn_in_back(
        n,
        img,
        grad_q,
        grad_k,
        grad_v,
        x_all,
        attn_in,
        qkv_full,
        mlp_out_part,
        out_running,
    )
    fc_own = fc_sum.astype(SINGLE)

    upstream_sum = sums[:, 4]
    gate_two = gate_two_part + fc2_shift * upstream_sum
    mod_grads = jnp.stack(
        [mod_one[:, 0], mod_one[:, 1], sums[:, 0], sums[:, 1], sums[:, 2], gate_two], axis=1
    ).reshape(2, n, mod_cols)
    rest = jnp.stack([sums[:, 3], mods[:, 5] * upstream_sum]).reshape(4, n, bias_cols)
    packed = jnp.concatenate(
        [
            mod_grads.transpose(1, 0, 2).reshape(n, -1),
            rest.transpose(1, 0, 2).reshape(n, -1),
        ],
        axis=1,
    )
    q_bias = q_bias_part.transpose(1, 0, 2).reshape(2, lwp)[:, :lw]
    v_bias = v_bias_part.transpose(1, 0, 2).reshape(2, lwp)[:, :lw]
    extra = jnp.concatenate(
        [jnp.stack([q_bias, v_bias], axis=1).reshape(-1), fc1_bias_part.reshape(-1)]
    )
    grad_attn_in, qkv_sum, proj_own, every, cond_sum, ada_grad = end(
        n,
        dp,
        cut,
        attn_in_part,
        qkv_part.reshape(dp, 2, depth // 2, 6 * lwp),
        proj_part.reshape(dp, 2, n * depth, lwp),
        packed[:, None],
        extra[None],
        ada_weight,
        acts,
    )
    proj_own, fc_sum = lax.optimization_barrier((proj_own, fc_sum))
    proj_sum = lax.psum_scatter(
        proj_own.reshape(n * 2 * depth, lwp), "seq", scatter_dimension=0, tiled=True
    ).reshape(2, depth, lwp)
    every = every[:, 0]
    total = jnp.sum(every, axis=0)

    image_out, text_out, image_grad, text_grad = rows_out(
        img, slots, grad_attn_in, grad_middle, x_loc, middle, mlp_sum, mods, fc2_shift, live_loc
    )

    ada_bias_grad = total[:cut].reshape(2, mod_cols)
    proj_bias_grad = total[cut : cut + 2 * bias_cols].reshape(2, bias_cols)
    fc2_bias_grad = total[cut + 2 * bias_cols : cut + 4 * bias_cols].reshape(2, bias_cols)
    after = cut + 4 * bias_cols
    qv_bias_grad = total[after : after + 4 * lw].reshape(2, 2, lw)
    fc1_bias_grad = total[after + 4 * lw :].reshape(2, units)
    cond_grad = cond_sum[:, 0, :depth].reshape(1, width) * silu_slope(cond_float)

    qkv_grad = qkv_sum[..., :lw].transpose(0, 2, 1, 3)
    fc1_grad = fc_own[:2].transpose(1, 0, 2)
    fc2_grad = fc_own[2:].transpose(2, 0, 1)
    proj_grad = proj_sum.astype(SINGLE)[..., :share].transpose(2, 0, 1)
    return (
        image_out,
        text_out,
        image_grad,
        text_grad,
        cond_grad,
        ada_grad,
        ada_bias_grad,
        qkv_grad,
        qv_bias_grad,
        proj_grad,
        proj_bias_grad,
        fc1_grad,
        fc1_bias_grad,
        fc2_grad,
        fc2_bias_grad,
    )


def solution(mesh):
    in_specs = (
        P("dp", "seq", None),
        P("dp", "seq", None),
        P("dp", "seq"),
        P("dp", None),
        P("dp", None, "seq"),
        P(None, "seq"),
        P("dp", None, None, "seq"),
        P(None, None, "seq"),
        P("seq", None, "dp"),
        P(None, "seq"),
        P("dp", None, "seq"),
        P(None, "seq"),
        P("seq", None, "dp"),
        P(None, "seq"),
        P("dp", "seq", None),
        P("dp", "seq", None),
    )
    out_specs = (
        P("dp", "seq", None),
        P("dp", "seq", None),
        P("dp", "seq", None),
        P("dp", "seq", None),
        P("dp", None),
        P("dp", None, "seq"),
        P(None, "seq"),
        P("dp", None, None, "seq"),
        P(None, None, "seq"),
        P("seq", None, "dp"),
        P(None, "seq"),
        P("dp", None, "seq"),
        P(None, "seq"),
        P("seq", None, "dp"),
        P(None, "seq"),
    )
    return jax.shard_map(body, mesh=mesh, in_specs=in_specs, out_specs=out_specs, check_vma=False)
```
